512 devices in a mesh: dp: 32 (over z, core), tensor: 16 (over y, x).
Axes of the slice: x: 4, y: 4, z: 16, core: 2. Of those that a mesh axis runs over, the one named last changes fastest.
Arguments:
- hidden: bfloat16 [8192, 4096], P(('dp', 'tensor')), may hold values from -3.6 to 3.6
- lengths: int32 [32, 32], P('dp'), may hold values from 1 to 80, 256 in all within a row
- positives: int32 [256], replicated, may hold values from 0 to 767, as said below
- negatives: int32 [256, 7], replicated, may hold values from 1 to 766, as said below
- in_gain: float32 [4096], replicated, may hold values from 0.25 to 1.75
- wq: bfloat16 [4096, 2048], P(None, 'tensor'), may hold values from -0.09375 to 0.09375
- wkv: bfloat16 [4096, 2048], P(None, 'tensor'), may hold values from -0.09375 to 0.09375
- q_gain: float32 [128], replicated, may hold values from 0.25 to 1.75
- k_gain: float32 [128], replicated, may hold values from 0.25 to 1.75
- wo: bfloat16 [2048, 4096], P('tensor'), may hold values from -0.125 to 0.125
- out_gain: float32 [4096], replicated, may hold values from 0.25 to 1.75
Outputs:
- d_hidden: bfloat16 [8192, 4096], P(('dp', 'tensor'))
- loss: float32 [], replicated
The draws below stay inside these ranges and needn't reach their ends.
Inputs may be any that keep to these rules, and one draw needn't show every extreme that they name: Each group's 32 lengths sum to 256, and one of them is exactly 80. The 256 positives are distinct passages. The 7 hard negatives of a query are distinct, and none of them is any query's positive.
All inputs are finite; a program needn't handle non-finite values.
Results may differ from the reference program's by a relative error of at most 0.023.
Values may be sent and summed in bfloat16 or wider, within the bound.
No kernel may reach another device: no remote copies, remote signals or barrier semaphores. Data moves between devices by JAX's collectives and lax.ppermute only.
A program may use at most 64 MiB of HBM per device.

```python
import math
import jax
import jax.numpy as jnp
import numpy as np
from jax import lax

D = 4096
HD = 128
QH = 16
KVH = 8
TOK_DEV = 256
QDEV = 8
NNEG = 7
NSEQ = 32
LMAX = 80
QALL = 256
PALL = 768
TOKENS = 8192
N_DP = 32


def place_value(order, value, target_labels):
    where_now = jnp.argmax(order == value).astype(jnp.int32)
    return order.at[where_now].set(order[target_labels]).at[target_labels].set(value)


def passage_order(key):
    order = jax.random.permutation(jax.random.fold_in(key, 11), PALL).astype(jnp.int32)
    order = place_value(order, 0, 0)
    order = place_value(order, PALL - 1, QALL - 1)
    order = place_value(order, 1, QALL)
    order = place_value(order, PALL - 2, QALL + 1)
    return order


def draw_positives(key, part):
    order = passage_order(key)
    return order[:QALL].astype(jnp.int32)


def draw_negatives(key, part):
    order = passage_order(key)
    key = jax.random.fold_in(key, 7)
    favour_key, noise_key = jax.random.split(key)
    pool = order[QALL:]
    pool_size = PALL - QALL
    favoured = (pool == 1) | (pool == PALL - 2)
    favour = jnp.where(favoured, 4, jax.random.randint(favour_key, (pool_size,), 0, 4))
    noise = jax.random.randint(noise_key, (QALL, pool_size), 0, 32768)
    score = (favour[None, :] * 65536 + noise) * pool_size + jnp.arange(pool_size, dtype=jnp.int32)[None, :]
    picked = lax.top_k(score.astype(jnp.int32), NNEG)[1]
    return jnp.take(pool, picked).astype(jnp.int32)


def draw_hidden(key, part):
    key = jax.random.fold_in(key, 3)
    row_key, column_key, base_key = jax.random.split(key, 3)
    row_scale = 0.03 * jnp.exp(jax.random.uniform(row_key, (TOKENS, 1), jnp.float32, 0.0, math.log(10.0)))
    column_scale = 0.3 * jnp.exp(jax.random.uniform(column_key, (1, D), jnp.float32, 0.0, math.log(10.0)))
    base = jax.random.truncated_normal(base_key, -4.0, 4.0, (TOKENS, D), jnp.float32)
    return (base * row_scale * column_scale).astype(jnp.bfloat16)


def shard_levels(key, extent, pieces, least, top_value):
    def one(axis_at, shards_of):
        draws = jax.random.uniform(jax.random.fold_in(jax.random.fold_in(key, 6), axis_at), (shards_of,), jnp.float32, least / len(pieces), top_value / len(pieces))
        return jnp.repeat(jnp.exp(draws), extent[axis_at] // shards_of).reshape((-1,) + (1,) * (len(extent) - axis_at - 1))

    factor_of = one(*pieces[0])
    for cut in pieces[1:]:
        factor_of = factor_of * one(*cut)
    return factor_of


def length_profile(amount, total, bound, slope):
    portions = [(1 << 20) // math.isqrt(standing ** slope) + 1 for standing in range(2, amount + 1)]
    rest, counts = total - bound - (amount - 1), [1] * (amount - 1)
    while rest > 0:
        free = [i for i in range(amount - 1) if counts[i] < bound]
        mass, remaining = sum([portions[i] for i in free]), rest
        for i in free:
            addition = min(bound - counts[i], max(1, remaining * portions[i] // mass), rest)
            counts[i] = counts[i] + addition
            rest = rest - addition
    return np.array([bound] + counts)


def uneven_parts(own_key, number_of, total, limit, slope):
    if number_of == 2:
        one = jax.random.randint(own_key, (), max(1, total - limit), min(limit, total - 1) + 1)
        return jnp.stack([one, total - one])
    tallies = jnp.asarray(length_profile(number_of, total, limit, slope), jnp.int32)
    couples = (number_of - 1) // 2
    donor, receiver = tallies[1:1 + 2 * couples:2], tallies[2:2 + 2 * couples:2]
    slack = jnp.minimum(donor - 1, limit - receiver)
    moved = jax.random.randint(jax.random.fold_in(own_key, 1), (couples,), 0, 1 << 20) % (slack + 1)
    tallies = tallies.at[1:1 + 2 * couples:2].set(donor - moved).at[2:2 + 2 * couples:2].set(receiver + moved)
    return tallies[jax.random.permutation(jax.random.fold_in(own_key, 2), number_of)]


def normal_values(rng, extent, scale, most, cuts=(), kind=jnp.bfloat16):
    entries = jax.random.normal(rng, extent, jnp.float32) * scale
    if len(cuts) > 0:
        entries = shard_levels(rng, extent, cuts, -0.22, 0.18) * entries
    return jnp.clip(entries, min=-most, max=most).astype(kind)


def setup_inputs(seed: int = 0) -> dict:
    streams_of = jax.random.split(jax.random.key(seed), 12)
    return {
        "hidden": draw_hidden(jax.random.fold_in(streams_of[11], 71), 0),
        "lengths": jax.vmap(lambda own: uneven_parts(own, NSEQ, TOK_DEV, LMAX, 2))(jax.random.split(streams_of[1], N_DP)).reshape((N_DP, NSEQ)).astype(jnp.int32),
        "positives": draw_positives(jax.random.fold_in(streams_of[11], 71), 0),
        "negatives": draw_negatives(jax.random.fold_in(streams_of[11], 71), 0),
        "in_gain": jnp.clip(1.0 + 0.15 * jax.random.normal(streams_of[4], (D,), jnp.float32), 0.25, 1.75),
        "wq": normal_values(streams_of[5], (D, QH * HD), D ** -0.5, 0.09375, ((1, 16),)),
        "wkv": normal_values(streams_of[6], (D, 2 * KVH * HD), D ** -0.5, 0.09375, ((1, 16),)),
        "q_gain": jnp.clip(1.0 + 0.15 * jax.random.normal(streams_of[7], (HD,), jnp.float32), 0.25, 1.75),
        "k_gain": jnp.clip(1.0 + 0.15 * jax.random.normal(streams_of[8], (HD,), jnp.float32), 0.25, 1.75),
        "wo": normal_values(streams_of[9], (QH * HD, D), (QH * HD) ** -0.5, 0.125, ((0, 16),)),
        "out_gain": jnp.clip(1.0 + 0.15 * jax.random.normal(streams_of[10], (D,), jnp.float32), 0.25, 1.75),
    }


EPSILON = 1e-06
SOFTMAX_TEMPER = 0.05
LOSS_MULTIPLIER = 8192.0
ROPE_BASE = 1000000.0

def rms_scale(tensor):
    return lax.rsqrt(lax.optimization_barrier(jnp.mean(tensor * tensor, axis=-1, keepdims=True)) + EPSILON)

def rope_tables(position, head_width):
    halfway = head_width // 2
    frequency = ROPE_BASE ** (-(jnp.arange(halfway, dtype=jnp.float32) * (2.0 / head_width)))
    angles = position[:, None] * frequency[None, :]
    angles = jnp.concatenate([angles, angles], axis=-1)
    return (jnp.cos(angles), jnp.sin(angles))

def rotate(tensor, cosine, sine):
    halfway = tensor.shape[-1] // 2
    turned = jnp.concatenate([-tensor[..., halfway:], tensor[..., :halfway]], axis=-1)
    return tensor * cosine + turned * sine

def segment_layout(lengths_row, total_tokens):
    seq_ends = jnp.cumsum(lengths_row).astype(jnp.int32)
    starts = seq_ends - lengths_row.astype(jnp.int32)
    token_index = jnp.arange(total_tokens, dtype=jnp.int32)
    inside = (token_index[:, None] >= starts[None, :]) & (token_index[:, None] < seq_ends[None, :])
    offset = lax.optimization_barrier(jnp.sum(jnp.where(inside, starts[None, :], 0), axis=1)).astype(jnp.int32)
    position = (token_index - offset).astype(jnp.float32)
    return (inside, position, (seq_ends - 1).astype(jnp.int32))

def head_forward(raw, gain, cosine, sine):
    inverse = rms_scale(raw)
    unit_form = raw * inverse
    return (unit_form, inverse, rotate(unit_form * gain, cosine, sine))

def norm_backward(grad, unit_form, inverse, gain):
    scaled = grad * gain
    return inverse * (scaled - unit_form * lax.optimization_barrier(jnp.mean(unit_form * scaled, axis=-1, keepdims=True)))

def head_backward(grad_rot, unit_form, inverse, gain, cosine, sine):
    return norm_backward(rotate(grad_rot, cosine, -sine), unit_form, inverse, gain)

def contrast(embeds16, positives, negatives):
    groups = embeds16.shape[0]
    feature_count = embeds16.shape[2]
    query_rows = embeds16[:, :QDEV].reshape(groups * QDEV, feature_count)
    passage_rows = embeds16[:, QDEV:].reshape(-1, feature_count)
    query_total_count = query_rows.shape[0]
    passage_ids = jnp.arange(passage_rows.shape[0], dtype=jnp.int32)
    similarity_logits = jnp.dot(query_rows, passage_rows.T, preferred_element_type=jnp.float32) / SOFTMAX_TEMPER
    positive_hot = positives[:, None] == passage_ids[None, :]
    hard_hot = jnp.any(negatives[:, :, None] == passage_ids[None, None, :], axis=1)
    permitted_mask = jnp.any(positive_hot, axis=0)[None, :] | hard_hot
    weight_params = jnp.where(permitted_mask, jnp.exp(similarity_logits - 1.0 / SOFTMAX_TEMPER), 0.0)
    running_totals = lax.optimization_barrier(jnp.sum(weight_params, axis=1, keepdims=True))
    target_labels = lax.optimization_barrier(jnp.sum(jnp.where(positive_hot, similarity_logits, 0.0), axis=1))
    loss = jnp.mean(jnp.log(running_totals[:, 0]) + 1.0 / SOFTMAX_TEMPER - target_labels)
    scaling_factor = LOSS_MULTIPLIER / (query_total_count * SOFTMAX_TEMPER)
    coef16 = (scaling_factor * (weight_params / running_totals - positive_hot.astype(jnp.float32))).astype(jnp.bfloat16)
    d_queries = jnp.dot(coef16, passage_rows, preferred_element_type=jnp.float32)
    d_passages = jnp.dot(coef16.T, query_rows, preferred_element_type=jnp.float32)
    joined = jnp.concatenate([d_queries.reshape(groups, QDEV, feature_count), d_passages.reshape(groups, -1, feature_count)], axis=1)
    return (loss, joined)

def group_forward(hidden_rows, lengths_row, in_gain, wq, wkv, q_gain, k_gain, wo, out_gain):
    tokens_count = hidden_rows.shape[0]
    inside, position, last = segment_layout(lengths_row, tokens_count)
    hidden32 = hidden_rows.astype(jnp.float32)
    inverse_in = rms_scale(hidden32)
    normed = (hidden32 * inverse_in * in_gain).astype(jnp.bfloat16)
    kv_raw = jnp.dot(normed, wkv, preferred_element_type=jnp.float32).reshape(tokens_count, KVH, 2, HD)
    key_raw = kv_raw[:, :, 0]
    value16 = kv_raw[:, :, 1].astype(jnp.bfloat16)
    cos_key, sin_key = rope_tables(position, HD)
    key_unit, key_inverse, key_rot = head_forward(key_raw, k_gain, cos_key[:, None], sin_key[:, None])
    key16 = key_rot.astype(jnp.bfloat16)
    last_rows = jnp.take(normed, last, axis=0)
    query_raw = jnp.dot(last_rows, wq, preferred_element_type=jnp.float32).reshape(NSEQ, QH, HD)
    cos_query, sin_query = rope_tables(jnp.take(position, last), HD)
    query_unit, query_inverse, query_rot = head_forward(query_raw, q_gain, cos_query[:, None], sin_query[:, None])
    query16 = query_rot.astype(jnp.bfloat16)
    shift = math.sqrt(HD) * jnp.max(q_gain) * jnp.max(k_gain)
    key_heads = jnp.repeat(key16, 2, axis=1).astype(jnp.float32)
    value_heads = jnp.repeat(value16, 2, axis=1).astype(jnp.float32)
    scores = jnp.einsum('shd,thd->sht', query16.astype(jnp.float32), key_heads) / math.sqrt(HD)
    weight_params = jnp.where(inside.T[:, None, :], jnp.exp(scores - shift), 0.0)
    probs = weight_params / lax.optimization_barrier(jnp.sum(weight_params, axis=-1, keepdims=True))
    probs16 = probs.astype(jnp.bfloat16)
    attn16 = jnp.einsum('sht,thd->shd', probs16.astype(jnp.float32), value_heads).astype(jnp.bfloat16).reshape(NSEQ, QH * HD)
    resid = jnp.take(hidden32, last, axis=0) + jnp.dot(attn16, wo, preferred_element_type=jnp.float32)
    resid_inverse = rms_scale(resid)
    resid_unit = resid * resid_inverse
    final = resid_unit * out_gain
    final_inverse = lax.rsqrt(lax.optimization_barrier(jnp.sum(final * final, axis=-1, keepdims=True)) + EPSILON)
    embed = final * final_inverse
    saved = (inverse_in, last, key_unit, key_inverse, key16, value16, query_unit, query_inverse, query16, probs, probs16, resid_unit, resid_inverse, embed, final_inverse, cos_key, sin_key, cos_query, sin_query)
    return (embed.astype(jnp.bfloat16), saved)

def group_backward(hidden_rows, d_embed, saved, in_gain, wq, wkv, q_gain, k_gain, wo, out_gain):
    inverse_in, last, key_unit, key_inverse, key16, value16, query_unit, query_inverse, query16, probs, probs16, resid_unit, resid_inverse, embed, final_inverse, cos_key, sin_key, cos_query, sin_query = saved
    tokens_count = hidden_rows.shape[0]
    hidden32 = hidden_rows.astype(jnp.float32)
    d_final = final_inverse * (d_embed - embed * lax.optimization_barrier(jnp.sum(embed * d_embed, axis=-1, keepdims=True)))
    d_resid = norm_backward(d_final, resid_unit, resid_inverse, out_gain)
    d_attn16 = jnp.dot(d_resid.astype(jnp.bfloat16), wo.T, preferred_element_type=jnp.float32).astype(jnp.bfloat16).reshape(NSEQ, QH, HD)
    key_heads = jnp.repeat(key16, 2, axis=1).astype(jnp.float32)
    value_heads = jnp.repeat(value16, 2, axis=1).astype(jnp.float32)
    d_probs = jnp.einsum('shd,thd->sht', d_attn16.astype(jnp.float32), value_heads)
    d_scores16 = (probs * (d_probs - lax.optimization_barrier(jnp.sum(probs * d_probs, axis=-1, keepdims=True))) / math.sqrt(HD)).astype(jnp.bfloat16)
    d_query_rot = jnp.einsum('sht,thd->shd', d_scores16.astype(jnp.float32), key_heads)
    d_key_heads = jnp.einsum('sht,shd->thd', d_scores16.astype(jnp.float32), query16.astype(jnp.float32))
    d_value_heads = jnp.einsum('sht,shd->thd', probs16.astype(jnp.float32), d_attn16.astype(jnp.float32))
    d_key_rot = lax.optimization_barrier(jnp.sum(d_key_heads.reshape(tokens_count, KVH, 2, HD), axis=2))
    d_value = lax.optimization_barrier(jnp.sum(d_value_heads.reshape(tokens_count, KVH, 2, HD), axis=2))
    d_key_raw = head_backward(d_key_rot, key_unit, key_inverse, k_gain, cos_key[:, None], sin_key[:, None])
    d_query_raw = head_backward(d_query_rot, query_unit, query_inverse, q_gain, cos_query[:, None], sin_query[:, None])
    d_kv16 = jnp.stack([d_key_raw, d_value], axis=2).reshape(tokens_count, QH, HD).astype(jnp.bfloat16)
    d_query16 = d_query_raw.astype(jnp.bfloat16)
    kv_blocks = jnp.transpose(d_kv16, (1, 0, 2))
    wkv_blocks = jnp.transpose(wkv.reshape(D, QH, HD), (1, 0, 2))
    query_blocks = jnp.transpose(d_query16, (1, 0, 2))
    wq_blocks = jnp.transpose(wq.reshape(D, QH, HD), (1, 0, 2))

    def add_block(total, items):
        kv_part, wkv_part, query_part, wq_part = items
        term = jnp.dot(kv_part, wkv_part.T, preferred_element_type=jnp.float32)
        term = term.at[last].add(jnp.dot(query_part, wq_part.T, preferred_element_type=jnp.float32))
        rounded = lax.optimization_barrier(term.astype(jnp.bfloat16))
        return (total + rounded.astype(jnp.float32), None)
    start_total = jnp.zeros((tokens_count, D), jnp.float32)
    d_normed, _ = lax.scan(add_block, start_total, (kv_blocks, wkv_blocks, query_blocks, wq_blocks))
    d_hidden = norm_backward(d_normed, hidden32 * inverse_in, inverse_in, in_gain)
    d_hidden = d_hidden.at[last].add(d_resid)
    return d_hidden.astype(jnp.bfloat16)

def reference(hidden, lengths, positives, negatives, in_gain, wq, wkv, q_gain, k_gain, wo, out_gain):
    groups = hidden.reshape(N_DP, TOK_DEV, D)

    def forward_one(items):
        return group_forward(items[0], items[1], in_gain, wq, wkv, q_gain, k_gain, wo, out_gain)
    embeds, saved = lax.map(forward_one, (groups, lengths))
    loss, d_embeds = contrast(embeds, positives, negatives)

    def backward_one(items):
        return group_backward(items[0], items[1], items[2], in_gain, wq, wkv, q_gain, k_gain, wo, out_gain)
    d_hidden = lax.map(backward_one, (groups, d_embeds, saved))
    return (d_hidden.reshape(TOKENS, D), loss)
```

```python
import math

import jax
import jax.numpy as jnp
from jax import lax
from jax.sharding import PartitionSpec as P

QDEV = 8


EPSILON = 1e-06
SOFTMAX_TEMPER = 0.05
LOSS_MULTIPLIER = 8192.0
ROPE_BASE = 1000000.0


def swapped(value, axis, apart):
    mask = 2**apart
    pairs = [(source, source ^ mask) for source in range(lax.axis_size(axis))]
    return lax.ppermute(value, axis, pairs)


def rms_scale(tensor):
    return lax.rsqrt(jnp.mean(tensor * tensor, axis=-1, keepdims=True) + EPSILON)


def rope_tables(position, head_width):
    halfway = head_width // 2
    frequency = ROPE_BASE ** (-(jnp.arange(halfway, dtype=jnp.float32) * (2.0 / head_width)))
    angles = position[:, None] * frequency[None, :]
    angles = jnp.concatenate([angles, angles], axis=-1)
    return (jnp.cos(angles), jnp.sin(angles))


def rotate(tensor, cosine, sine):
    halfway = tensor.shape[-1] // 2
    turned = jnp.concatenate([-tensor[..., halfway:], tensor[..., :halfway]], axis=-1)
    return tensor * cosine + turned * sine


def segment_layout(lengths_row, total_tokens):
    seq_ends = jnp.cumsum(lengths_row)
    starts = seq_ends - lengths_row
    token_index = jnp.arange(total_tokens, dtype=jnp.int32)
    inside = (token_index[:, None] >= starts[None, :]) & (token_index[:, None] < seq_ends[None, :])
    offset = jnp.sum(jnp.where(inside, starts[None, :], 0), axis=1)
    position = (token_index - offset).astype(jnp.float32)
    return (inside, position, seq_ends - 1)


def head_forward(raw, gain, cosine, sine):
    inverse = rms_scale(raw)
    unit_form = raw * inverse
    return (unit_form, inverse, rotate(unit_form * gain, cosine, sine))


def norm_backward(grad, unit_form, inverse, gain):
    scaled = grad * gain
    return inverse * (scaled - unit_form * jnp.mean(unit_form * scaled, axis=-1, keepdims=True))


def head_backward(grad_rot, unit_form, inverse, gain, cosine, sine):
    return norm_backward(rotate(grad_rot, cosine, -sine), unit_form, inverse, gain)


def exchange(blocks, axis):
    return lax.all_to_all(blocks, axis, 0, 0, tiled=True)


def gather_rows(rows, axis):
    count = lax.axis_size(axis)
    copies = jnp.broadcast_to(rows[None], (count,) + rows.shape)
    return exchange(copies, axis)


def to_lanes(block, lanes):
    rows, width = block.shape
    return block.reshape(rows, width // lanes, lanes).reshape(-1, lanes)


def split16(value):
    parts = []
    rest = value
    for _ in range(3):
        part = rest.astype(jnp.bfloat16)
        parts.append(part)
        rest = rest - part.astype(jnp.float32)
    return parts


def contrast(scaled16, out_gain, positives, negatives):
    groups, sequences, width = scaled16.shape
    tensor_count = lax.axis_size("tensor")
    query_rows = scaled16[:, :QDEV].reshape(groups * QDEV, width)
    passage_rows = scaled16[:, QDEV:].reshape(-1, width)
    query_count, passage_count = query_rows.shape[0], passage_rows.shape[0]
    own_queries = query_count // tensor_count
    features = width * tensor_count

    raw = jnp.dot(query_rows, passage_rows.T, preferred_element_type=jnp.float32)
    rows32 = jnp.concatenate([query_rows, passage_rows]).astype(jnp.float32)
    plain = rows32 / out_gain
    squares = jnp.sum(rows32 * rows32 + plain * plain * (EPSILON / features), axis=1)
    lanes = 128
    logit_rows = own_queries * passage_count // lanes
    packed = jnp.concatenate(
        [
            raw.reshape(tensor_count, own_queries, passage_count // lanes, lanes).reshape(
                tensor_count, logit_rows, lanes
            ),
            jnp.broadcast_to(
                squares.reshape(1, -1, lanes), (tensor_count, squares.shape[0] // lanes, lanes)
            ),
        ],
        axis=1,
    )
    summed = jnp.sum(exchange(packed, "tensor"), axis=0)
    inverse = lax.rsqrt(summed[logit_rows:].reshape(-1) + EPSILON * EPSILON)
    own = lax.axis_index("tensor") * own_queries
    inverse_query = lax.dynamic_slice_in_dim(inverse[:query_count], own, own_queries)
    inverse_passage = inverse[query_count:]
    logits = (
        summed[:logit_rows].reshape(own_queries, passage_count)
        * inverse_query[:, None]
        * inverse_passage[None, :]
        / SOFTMAX_TEMPER
    )

    passage_ids = jnp.arange(passage_count, dtype=jnp.int32)
    any_positive = jnp.any(positives[:, None] == passage_ids[None, :], axis=0)
    own_positives = lax.dynamic_slice_in_dim(positives, own, own_queries)
    own_negatives = lax.dynamic_slice_in_dim(negatives, own, own_queries)
    positive_hot = own_positives[:, None] == passage_ids[None, :]
    hard_hot = jnp.any(own_negatives[:, :, None] == passage_ids[None, None, :], axis=1)
    permitted_mask = any_positive[None, :] | hard_hot
    weight_params = jnp.where(permitted_mask, jnp.exp(logits - 1.0 / SOFTMAX_TEMPER), 0.0)
    totals = jnp.sum(weight_params, axis=1, keepdims=True)
    target_labels = jnp.sum(jnp.where(positive_hot, logits, 0.0), axis=1)
    loss_part = jnp.sum(jnp.log(totals[:, 0]) + 1.0 / SOFTMAX_TEMPER - target_labels)
    scaling_factor = LOSS_MULTIPLIER / (query_count * SOFTMAX_TEMPER)
    coef16 = (
        scaling_factor * (weight_params / totals - positive_hot.astype(jnp.float32))
    ).astype(jnp.bfloat16)
    weighted = coef16.astype(jnp.float32) * logits * SOFTMAX_TEMPER
    along_query = jnp.sum(weighted, axis=1)
    along_passage = jnp.sum(weighted, axis=0)

    small = jnp.concatenate(
        [
            along_passage,
            jnp.pad(jnp.concatenate([along_query, loss_part[None]]), (0, lanes - own_queries - 1)),
        ]
    ).reshape(-1, lanes)
    small_rows = small.shape[0]
    sent = jnp.concatenate([coef16.reshape(-1, lanes)] + split16(small))
    pad = -sent.shape[0] % 16
    sent = jnp.pad(sent, ((0, pad), (0, 0)))
    arrived = gather_rows(sent, "tensor").reshape(tensor_count, -1, lanes)
    coef_all = arrived[:, :logit_rows].reshape(query_count, passage_count)
    parts = arrived[:, logit_rows : logit_rows + 3 * small_rows].astype(jnp.float32)
    small_all = jnp.sum(parts.reshape(tensor_count, 3, small_rows, lanes), axis=1)
    along_passage = jnp.sum(small_all[:, : small_rows - 1], axis=0).reshape(-1)
    along_query = small_all[:, small_rows - 1, :own_queries].reshape(-1)
    loss = jnp.sum(small_all[:, small_rows - 1, own_queries]) / query_count

    embeds16 = (rows32 * inverse[:, None]).astype(jnp.bfloat16)
    d_queries = jnp.dot(
        coef_all, embeds16[query_count:], preferred_element_type=jnp.float32
    )
    d_passages = jnp.dot(
        coef_all.T, embeds16[:query_count], preferred_element_type=jnp.float32
    )
    own_group = lax.axis_index("dp")
    others = sequences - QDEV

    def own_part(of_queries, of_passages):
        return jnp.concatenate(
            [
                lax.dynamic_slice_in_dim(of_queries, own_group * QDEV, QDEV),
                lax.dynamic_slice_in_dim(of_passages, own_group * others, others),
            ]
        )

    return (
        loss,
        own_part(d_queries, d_passages),
        own_part(along_query, along_passage),
        own_part(inverse[:query_count], inverse_passage),
    )


def on_device(
    hidden, lengths, positives, negatives, in_gain, wq, wkv, q_gain, k_gain, wo, out_gain
):
    tensor_count = lax.axis_size("tensor")
    tensor_index = lax.axis_index("tensor")
    own_rows, features = hidden.shape
    tokens_count = own_rows * tensor_count
    head_width = wq.shape[1]
    sequences = lengths.shape[1]
    chunk = features // tensor_count
    root = math.sqrt(head_width)
    is_even = tensor_index % 2 == 0
    hidden32 = hidden.astype(jnp.float32)
    inverse_in = rms_scale(hidden32)
    normed = (hidden32 * inverse_in * in_gain).astype(jnp.bfloat16)
    piece = gather_rows(normed, "tensor").reshape(tokens_count, features)
    own_index = tensor_index * own_rows + jnp.arange(own_rows, dtype=jnp.int32)
    inside, position, last = segment_layout(lengths[0], tokens_count)
    own_last = (last[:, None] == own_index[None, :]).astype(jnp.bfloat16)
    token_index = jnp.arange(tokens_count, dtype=jnp.int32)
    chosen = (last[:, None] == token_index[None, :]).astype(jnp.bfloat16)
    kv_own = jnp.dot(piece, wkv, preferred_element_type=jnp.float32)
    kv_other = swapped(kv_own, "tensor", 0)
    last_rows = jnp.dot(chosen, piece, preferred_element_type=jnp.float32).astype(jnp.bfloat16)
    query_raw = jnp.dot(last_rows, wq, preferred_element_type=jnp.float32)
    key_raw = jnp.where(is_even, kv_own, kv_other)
    value16 = jnp.where(is_even, kv_other, kv_own).astype(jnp.bfloat16)
    cos_key, sin_key = rope_tables(position, head_width)
    key_unit, key_inverse, key_rot = head_forward(key_raw, k_gain, cos_key, sin_key)
    key16 = key_rot.astype(jnp.bfloat16)
    cos_query, sin_query = rope_tables((lengths[0] - 1).astype(jnp.float32), head_width)
    query_unit, query_inverse, query_rot = head_forward(query_raw, q_gain, cos_query, sin_query)
    query16 = query_rot.astype(jnp.bfloat16)
    shift = root * jnp.max(q_gain) * jnp.max(k_gain)
    scores = jnp.dot(query16, key16.T, preferred_element_type=jnp.float32) / root
    weight_params = jnp.where(inside.T, jnp.exp(scores - shift), 0.0)
    probs = weight_params / jnp.sum(weight_params, axis=-1, keepdims=True)
    probs16 = probs.astype(jnp.bfloat16)
    attn16 = jnp.dot(probs16, value16, preferred_element_type=jnp.float32).astype(jnp.bfloat16)
    partial_rows = jnp.dot(attn16, wo, preferred_element_type=jnp.float32) + jnp.dot(
        own_last, hidden, preferred_element_type=jnp.float32
    )
    blocks = partial_rows.astype(jnp.bfloat16).reshape(sequences, tensor_count, chunk)
    arrived = exchange(blocks.transpose(1, 0, 2), "tensor")
    resid = jnp.sum(arrived.astype(jnp.float32), axis=0)
    own_gain = lax.dynamic_slice_in_dim(out_gain, tensor_index * chunk, chunk)
    scaled = resid * own_gain
    everyone = lax.all_gather(scaled.astype(jnp.bfloat16), "dp", axis=0, tiled=True)
    groups = lax.axis_size("dp")
    loss, d_embed, along, inverse = contrast(
        everyone.reshape(groups, sequences, chunk), own_gain, positives, negatives
    )
    inverse, along = inverse[:, None], along[:, None]
    d_resid = inverse * own_gain * (d_embed - scaled * inverse * along) - resid * (
        along * inverse * inverse * (EPSILON / features)
    )
    d_resid16 = gather_rows(d_resid.astype(jnp.bfloat16), "tensor")
    d_resid16 = d_resid16.reshape(tensor_count, sequences, chunk)
    d_resid16 = d_resid16.transpose(1, 0, 2).reshape(sequences, features)
    d_attn16 = jnp.dot(d_resid16, wo.T, preferred_element_type=jnp.float32).astype(jnp.bfloat16)
    d_probs = jnp.dot(d_attn16, value16.T, preferred_element_type=jnp.float32)
    d_scores16 = (
        probs * (d_probs - jnp.sum(probs * d_probs, axis=-1, keepdims=True)) / root
    ).astype(jnp.bfloat16)
    d_query_rot = jnp.dot(d_scores16, key16, preferred_element_type=jnp.float32)
    d_key_rot = jnp.dot(d_scores16.T, query16, preferred_element_type=jnp.float32)
    d_value = jnp.dot(probs16.T, d_attn16, preferred_element_type=jnp.float32)
    d_key_raw = head_backward(d_key_rot, key_unit, key_inverse, k_gain, cos_key, sin_key)
    d_query_raw = head_backward(
        d_query_rot, query_unit, query_inverse, q_gain, cos_query, sin_query
    )
    mine = jnp.where(is_even, d_key_raw, d_value)
    theirs = jnp.where(is_even, d_value, d_key_raw)
    column16 = (mine + swapped(theirs, "tensor", 0)).astype(jnp.bfloat16)
    spread16 = jnp.dot(
        chosen.T, d_query_raw.astype(jnp.bfloat16), preferred_element_type=jnp.float32
    ).astype(jnp.bfloat16)
    product = jnp.dot(column16, wkv.T, preferred_element_type=jnp.float32) + jnp.dot(
        spread16, wq.T, preferred_element_type=jnp.float32
    )
    terms = exchange(product.astype(jnp.bfloat16), "tensor")
    d_normed = jnp.sum(
        terms.reshape(tensor_count, own_rows, features).astype(jnp.float32), axis=0
    )
    d_hidden = norm_backward(d_normed, hidden32 * inverse_in, inverse_in, in_gain)
    d_hidden = d_hidden + jnp.dot(own_last.T, d_resid16, preferred_element_type=jnp.float32)
    return (d_hidden.astype(jnp.bfloat16), loss)


def solution(mesh):
    placed = (
        P(("dp", "tensor"), None),
        P("dp", None),
        P(),
        P(),
        P(),
        P(None, "tensor"),
        P(None, "tensor"),
        P(),
        P(),
        P("tensor", None),
        P(),
    )
    return jax.shard_map(
        on_device,
        mesh=mesh,
        in_specs=placed,
        out_specs=(P(("dp", "tensor"), None), P()),
        check_vma=False,
    )
```

```python
import math

import jax
import jax.numpy as jnp
from jax import lax
from jax.sharding import PartitionSpec as P

QDEV = 8


EPSILON = 1e-06
SOFTMAX_TEMPER = 0.05
LOSS_MULTIPLIER = 8192.0
ROPE_BASE = 1000000.0


def swapped(value, axis, apart):
    mask = 2**apart
    pairs = [(source, source ^ mask) for source in range(lax.axis_size(axis))]
    return lax.ppermute(value, axis, pairs)


def rms_scale(tensor):
    return lax.rsqrt(jnp.mean(tensor * tensor, axis=-1, keepdims=True) + EPSILON)


def rope_tables(position, head_width):
    halfway = head_width // 2
    frequency = ROPE_BASE ** (-(jnp.arange(halfway, dtype=jnp.float32) * (2.0 / head_width)))
    angles = position[:, None] * frequency[None, :]
    angles = jnp.concatenate([angles, angles], axis=-1)
    return (jnp.cos(angles), jnp.sin(angles))


def rotate(tensor, cosine, sine):
    halfway = tensor.shape[-1] // 2
    turned = jnp.concatenate([-tensor[..., halfway:], tensor[..., :halfway]], axis=-1)
    return tensor * cosine + turned * sine


def segment_layout(lengths_row, total_tokens):
    seq_ends = jnp.cumsum(lengths_row)
    starts = seq_ends - lengths_row
    token_index = jnp.arange(total_tokens, dtype=jnp.int32)
    inside = (token_index[:, None] >= starts[None, :]) & (token_index[:, None] < seq_ends[None, :])
    offset = jnp.sum(jnp.where(inside, starts[None, :], 0), axis=1)
    position = (token_index - offset).astype(jnp.float32)
    return (inside, position, seq_ends - 1)


def head_forward(raw, gain, cosine, sine):
    inverse = rms_scale(raw)
    unit_form = raw * inverse
    return (unit_form, inverse, rotate(unit_form * gain, cosine, sine))


def norm_backward(grad, unit_form, inverse, gain):
    scaled = grad * gain
    return inverse * (scaled - unit_form * jnp.mean(unit_form * scaled, axis=-1, keepdims=True))


def head_backward(grad_rot, unit_form, inverse, gain, cosine, sine):
    return norm_backward(rotate(grad_rot, cosine, -sine), unit_form, inverse, gain)


def exchange(blocks, axis):
    return lax.all_to_all(blocks, axis, 0, 0, tiled=True)


def gather_rows(rows, axis):
    count = lax.axis_size(axis)
    return exchange(jnp.broadcast_to(rows[None], (count,) + rows.shape), axis)


def to_tiles(block):
    rows, width = block.shape
    tiles = block.reshape(rows // 8, 8, width // 128, 128).transpose(0, 2, 1, 3)
    return tiles.reshape(rows // 8, width // 16, 128)


def from_tiles(tiles):
    count, height = tiles.shape[:2]
    block = tiles.reshape(count, height // 8, 8, 128).transpose(0, 2, 1, 3)
    return block.reshape(count * 8, height * 16)


def split16(value):
    high = value.astype(jnp.bfloat16)
    return [high, (value - high.astype(jnp.float32)).astype(jnp.bfloat16)]


def contrast(scaled16, out_gain, positives, negatives):
    groups, sequences, width = scaled16.shape
    tensor_count, core_count = lax.axis_size("tensor"), lax.axis_size("core")
    query_rows = scaled16[:, :QDEV].reshape(groups * QDEV, width)
    passage_rows = scaled16[:, QDEV:].reshape(-1, width)
    query_count, passage_count = query_rows.shape[0], passage_rows.shape[0]
    core_queries = query_count // core_count
    own_queries = core_queries // tensor_count
    features = width * tensor_count

    core_start = lax.axis_index("core") * core_queries
    core_rows = lax.dynamic_slice_in_dim(query_rows, core_start, core_queries)
    raw = jnp.dot(core_rows, passage_rows.T, preferred_element_type=jnp.float32)
    rows32 = jnp.concatenate([query_rows, passage_rows]).astype(jnp.float32)
    plain = rows32 / out_gain
    squares = jnp.sum(rows32 * rows32 + plain * plain * (EPSILON / features), axis=1)
    lanes = 128
    logit_rows = own_queries * passage_count // lanes
    packed = jnp.concatenate(
        [
            to_tiles(raw),
            jnp.broadcast_to(
                squares.reshape(1, -1, lanes), (tensor_count, squares.shape[0] // lanes, lanes)
            ),
        ],
        axis=1,
    )
    summed = jnp.sum(exchange(packed, "tensor"), axis=0)
    inverse = lax.rsqrt(summed[logit_rows:].reshape(-1) + EPSILON * EPSILON)
    own = core_start + lax.axis_index("tensor") * own_queries
    inverse_query = lax.dynamic_slice_in_dim(inverse[:query_count], own, own_queries)
    inverse_passage = inverse[query_count:]
    logits = (
        from_tiles(summed[None, :logit_rows])
        * inverse_query[:, None]
        * inverse_passage[None, :]
        / SOFTMAX_TEMPER
    )

    passage_ids = jnp.arange(passage_count, dtype=jnp.int32)
    any_positive = jnp.any(positives[:, None] == passage_ids[None, :], axis=0)
    own_positives = lax.dynamic_slice_in_dim(positives, own, own_queries)
    own_negatives = lax.dynamic_slice_in_dim(negatives, own, own_queries)
    positive_hot = own_positives[:, None] == passage_ids[None, :]
    hard_hot = jnp.any(own_negatives[:, :, None] == passage_ids[None, None, :], axis=1)
    permitted_mask = any_positive[None, :] | hard_hot
    weight_params = jnp.where(permitted_mask, jnp.exp(logits - 1.0 / SOFTMAX_TEMPER), 0.0)
    totals = jnp.sum(weight_params, axis=1, keepdims=True)
    target_labels = jnp.sum(jnp.where(positive_hot, logits, 0.0), axis=1)
    loss_part = jnp.sum(jnp.log(totals[:, 0]) + 1.0 / SOFTMAX_TEMPER - target_labels)
    scaling_factor = LOSS_MULTIPLIER / (query_count * SOFTMAX_TEMPER)
    coef16 = (
        scaling_factor * (weight_params / totals - positive_hot.astype(jnp.float32))
    ).astype(jnp.bfloat16)
    weighted = coef16.astype(jnp.float32) * logits * SOFTMAX_TEMPER
    along_query = jnp.sum(weighted, axis=1)
    along_passage = jnp.sum(weighted, axis=0)

    small = jnp.concatenate(
        [
            along_passage,
            jnp.pad(jnp.concatenate([along_query, loss_part[None]]), (0, lanes - own_queries - 1)),
        ]
    ).reshape(-1, lanes)
    small_rows = small.shape[0]
    sent = jnp.concatenate([to_tiles(coef16)[0]] + split16(small))
    sent = jnp.pad(sent, ((0, -sent.shape[0] % 16), (0, 0)))
    arrived = lax.all_gather(gather_rows(sent, "tensor"), "core", axis=0, tiled=True)
    arrived = arrived.reshape(core_count * tensor_count, -1, lanes)
    coef_all = from_tiles(arrived[:, :logit_rows])
    parts = arrived[:, logit_rows : logit_rows + 2 * small_rows].astype(jnp.float32)
    small_all = parts[:, :small_rows] + parts[:, small_rows:]
    along_passage = jnp.sum(small_all[:, : small_rows - 1], axis=0).reshape(-1)
    along_query = small_all[:, small_rows - 1, :own_queries].reshape(-1)
    loss = jnp.sum(small_all[:, small_rows - 1, own_queries]) / query_count

    embeds16 = (rows32 * inverse[:, None]).astype(jnp.bfloat16)
    d_queries = jnp.dot(
        coef_all, embeds16[query_count:], preferred_element_type=jnp.float32
    )
    d_passages = jnp.dot(
        coef_all.T, embeds16[:query_count], preferred_element_type=jnp.float32
    )
    own_group = lax.axis_index("z") * core_count + lax.axis_index("core")
    others = sequences - QDEV

    def own_part(of_queries, of_passages):
        return jnp.concatenate(
            [
                lax.dynamic_slice_in_dim(of_queries, own_group * QDEV, QDEV),
                lax.dynamic_slice_in_dim(of_passages, own_group * others, others),
            ]
        )

    return (
        loss,
        own_part(d_queries, d_passages),
        own_part(along_query, along_passage),
        own_part(inverse[:query_count], inverse_passage),
    )


def on_device(
    hidden, lengths, positives, negatives, in_gain, wq, wkv, q_gain, k_gain, wo, out_gain
):
    tensor_count = lax.axis_size("tensor")
    tensor_index = lax.axis_index("tensor")
    own_rows, features = hidden.shape
    tokens_count = own_rows * tensor_count
    head_width = wq.shape[1]
    sequences = lengths.shape[1]
    chunk = features // tensor_count
    root = math.sqrt(head_width)
    is_even = tensor_index % 2 == 0
    hidden32 = hidden.astype(jnp.float32)
    inverse_in = rms_scale(hidden32)
    normed = (hidden32 * inverse_in * in_gain).astype(jnp.bfloat16)
    piece = gather_rows(normed, "tensor").reshape(tokens_count, features)
    own_index = tensor_index * own_rows + jnp.arange(own_rows, dtype=jnp.int32)
    inside, position, last = segment_layout(lengths[0], tokens_count)
    own_last = (last[:, None] == own_index[None, :]).astype(jnp.bfloat16)
    token_index = jnp.arange(tokens_count, dtype=jnp.int32)
    chosen = (last[:, None] == token_index[None, :]).astype(jnp.bfloat16)
    weights = jnp.concatenate([wkv, wq], axis=1)
    projected = jnp.dot(piece, weights, preferred_element_type=jnp.float32)
    kv_own = projected[:, :head_width]
    kv_other = swapped(kv_own, "tensor", 0)
    query_raw = jnp.dot(
        chosen.astype(jnp.float32), projected[:, head_width:], precision=lax.Precision.HIGHEST
    )
    key_raw = jnp.where(is_even, kv_own, kv_other)
    value16 = jnp.where(is_even, kv_other, kv_own).astype(jnp.bfloat16)
    cos_key, sin_key = rope_tables(position, head_width)
    key_unit, key_inverse, key_rot = head_forward(key_raw, k_gain, cos_key, sin_key)
    key16 = key_rot.astype(jnp.bfloat16)
    cos_query, sin_query = rope_tables((lengths[0] - 1).astype(jnp.float32), head_width)
    query_unit, query_inverse, query_rot = head_forward(query_raw, q_gain, cos_query, sin_query)
    query16 = query_rot.astype(jnp.bfloat16)
    shift = root * jnp.max(q_gain) * jnp.max(k_gain)
    scores = jnp.dot(query16, key16.T, preferred_element_type=jnp.float32) / root
    weight_params = jnp.where(inside.T, jnp.exp(scores - shift), 0.0)
    probs = weight_params / jnp.sum(weight_params, axis=-1, keepdims=True)
    probs16 = probs.astype(jnp.bfloat16)
    attn16 = jnp.dot(probs16, value16, preferred_element_type=jnp.float32).astype(jnp.bfloat16)
    partial_rows = jnp.dot(attn16, wo, preferred_element_type=jnp.float32) + jnp.dot(
        own_last, hidden, preferred_element_type=jnp.float32
    )
    blocks = partial_rows.astype(jnp.bfloat16).reshape(sequences, tensor_count, chunk)
    arrived = exchange(blocks.transpose(1, 0, 2), "tensor")
    resid = jnp.sum(arrived.astype(jnp.float32), axis=0)
    own_gain = lax.dynamic_slice_in_dim(out_gain, tensor_index * chunk, chunk)
    scaled = resid * own_gain
    same_core = gather_rows(scaled.astype(jnp.bfloat16), "z")
    everyone = lax.all_gather(same_core, "core", axis=1)
    everyone = everyone.reshape(-1, sequences, chunk)
    loss, d_embed, along, inverse = contrast(everyone, own_gain, positives, negatives)
    inverse, along = inverse[:, None], along[:, None]
    d_resid = inverse * own_gain * (d_embed - scaled * inverse * along) - resid * (
        along * inverse * inverse * (EPSILON / features)
    )
    d_resid16 = gather_rows(d_resid.astype(jnp.bfloat16), "tensor")
    d_resid16 = d_resid16.reshape(tensor_count, sequences, chunk)
    d_resid16 = d_resid16.transpose(1, 0, 2).reshape(sequences, features)
    d_attn16 = jnp.dot(d_resid16, wo.T, preferred_element_type=jnp.float32).astype(jnp.bfloat16)
    d_probs = jnp.dot(d_attn16, value16.T, preferred_element_type=jnp.float32)
    d_scores16 = (
        probs * (d_probs - jnp.sum(probs * d_probs, axis=-1, keepdims=True)) / root
    ).astype(jnp.bfloat16)
    d_query_rot = jnp.dot(d_scores16, key16, preferred_element_type=jnp.float32)
    d_key_rot = jnp.dot(d_scores16.T, query16, preferred_element_type=jnp.float32)
    d_value = jnp.dot(probs16.T, d_attn16, preferred_element_type=jnp.float32)
    d_key_raw = head_backward(d_key_rot, key_unit, key_inverse, k_gain, cos_key, sin_key)
    d_query_raw = head_backward(
        d_query_rot, query_unit, query_inverse, q_gain, cos_query, sin_query
    )
    mine = jnp.where(is_even, d_key_raw, d_value)
    theirs = jnp.where(is_even, d_value, d_key_raw)
    column16 = (mine + swapped(theirs, "tensor", 0)).astype(jnp.bfloat16)
    spread16 = jnp.dot(
        chosen.T, d_query_raw.astype(jnp.bfloat16), preferred_element_type=jnp.float32
    ).astype(jnp.bfloat16)
    product = jnp.dot(
        jnp.concatenate([column16, spread16], axis=1),
        weights.T,
        preferred_element_type=jnp.float32,
    )
    terms = exchange(product.astype(jnp.bfloat16), "tensor")
    d_normed = jnp.sum(
        terms.reshape(tensor_count, own_rows, features).astype(jnp.float32), axis=0
    )
    d_hidden = norm_backward(d_normed, hidden32 * inverse_in, inverse_in, in_gain)
    d_hidden = d_hidden + jnp.dot(own_last.T, d_resid16, preferred_element_type=jnp.float32)
    return (d_hidden.astype(jnp.bfloat16), loss)


def solution(mesh):
    z_count = mesh.shape["dp"] // 2
    chips = mesh.devices.reshape(z_count, 2, mesh.shape["tensor"])
    mesh = jax.sharding.Mesh(chips, ("z", "core", "tensor"))
    everywhere = P(("z", "core", "tensor"), None)
    placed = (
        everywhere,
        P(("z", "core"), None),
        P(),
        P(),
        P(),
        P(None, "tensor"),
        P(None, "tensor"),
        P(),
        P(),
        P("tensor", None),
        P(),
    )
    return jax.shard_map(
        on_device, mesh=mesh, in_specs=placed, out_specs=(everywhere, P()), check_vma=False
    )
```

```python
import math

import jax
import jax.numpy as jnp
from jax import lax
from jax.experimental import pallas as pl
from jax.experimental.pallas import tpu as pltpu
from jax.sharding import PartitionSpec as P

QDEV = 8
LANES = 128


EPSILON = 1e-06
SOFTMAX_TEMPER = 0.05
LOSS_MULTIPLIER = 8192.0
ROPE_BASE = 1000000.0


def swapped(value, axis, apart):
    mask = 2**apart
    pairs = [(source, source ^ mask) for source in range(lax.axis_size(axis))]
    return lax.ppermute(value, axis, pairs)


def rms_scale(tensor):
    return lax.rsqrt(jnp.mean(tensor * tensor, axis=-1, keepdims=True) + EPSILON)


def rope_tables(position, head_width):
    halfway = head_width // 2
    frequency = ROPE_BASE ** (-(jnp.arange(halfway, dtype=jnp.float32) * (2.0 / head_width)))
    angles = position[:, None] * frequency[None, :]
    angles = jnp.concatenate([angles, angles], axis=-1)
    return (jnp.cos(angles), jnp.sin(angles))


def rotate(tensor, cosine, sine):
    halfway = tensor.shape[-1] // 2
    turned = jnp.concatenate([-tensor[..., halfway:], tensor[..., :halfway]], axis=-1)
    return tensor * cosine + turned * sine


def segment_layout(lengths_row, total_tokens):
    seq_ends = jnp.cumsum(lengths_row)
    starts = seq_ends - lengths_row
    token_index = jnp.arange(total_tokens, dtype=jnp.int32)
    inside = (token_index[:, None] >= starts[None, :]) & (token_index[:, None] < seq_ends[None, :])
    offset = jnp.sum(jnp.where(inside, starts[None, :], 0), axis=1)
    position = (token_index - offset).astype(jnp.float32)
    return (inside, position, seq_ends - 1)


def head_forward(raw, gain, cosine, sine):
    inverse = rms_scale(raw)
    unit_form = raw * inverse
    return (unit_form, inverse, rotate(unit_form * gain, cosine, sine))


def norm_backward(grad, unit_form, inverse, gain):
    scaled = grad * gain
    return inverse * (scaled - unit_form * jnp.mean(unit_form * scaled, axis=-1, keepdims=True))


def head_backward(grad_rot, unit_form, inverse, gain, cosine, sine):
    return norm_backward(rotate(grad_rot, cosine, -sine), unit_form, inverse, gain)


def exchange(blocks, axis):
    return lax.all_to_all(blocks, axis, 0, 0, tiled=True)


def gather_rows(rows, axis):
    count = lax.axis_size(axis)
    return exchange(jnp.broadcast_to(rows[None], (count,) + rows.shape), axis)


def halves(value):
    high = value.astype(jnp.bfloat16).astype(jnp.float32)
    return jnp.concatenate([high, value - high], axis=0)


def iota(shape, axis):
    return lax.broadcasted_iota(jnp.int32, shape, axis)


def columns_to_lanes(column, out_ref):
    diagonal = iota((LANES, LANES), 0) == iota((LANES, LANES), 1)
    for k in range(column.shape[0] // LANES):
        block = jnp.where(diagonal, column[LANES * k : LANES * (k + 1)], 0.0)
        out_ref[k : k + 1, :] = jnp.sum(block, axis=0, keepdims=True)


def partial_logits_kernel(rows_ref, query_hot_ref, positive_hot_ref, listed_ref, gain_ref, out_ref, held_ref):
    rows = rows_ref[...]
    queries = jnp.dot(query_hot_ref[...], rows, preferred_element_type=jnp.float32)
    positives = jnp.dot(positive_hot_ref[...], rows, preferred_element_type=jnp.float32)
    queries = queries.astype(jnp.bfloat16)
    features = gain_ref.shape[1] * out_ref.shape[0]
    rows32 = rows.astype(jnp.float32)
    plain = rows32 / gain_ref[...]
    squares = jnp.sum(rows32 * rows32, axis=1, keepdims=True) + jnp.sum(
        plain * plain, axis=1, keepdims=True
    ) * (EPSILON / features)
    against = (((1,), (1,)), ((), ()))
    with_positives = lax.dot_general(
        positives.astype(jnp.bfloat16), queries, against, preferred_element_type=jnp.float32
    )
    with_all = lax.dot_general(rows, queries, against, preferred_element_type=jnp.float32)
    row_index = iota(with_all.shape, 0)
    for j in range(8):
        listed = row_index == listed_ref[j : j + 1, :]
        held_ref[j : j + 1, :] = jnp.sum(jnp.where(listed, with_all, 0.0), axis=0, keepdims=True)
        held_ref[8 + j : 9 + j, :] = jnp.sum(
            jnp.where(listed, squares, 0.0), axis=0, keepdims=True
        )
    columns_to_lanes(squares, held_ref.at[16:24])
    count = with_positives.shape[0]
    sent = [with_positives.astype(jnp.bfloat16)]
    for start in (0, 8, 16):
        sent.append(halves(held_ref[start : start + 8, :]).astype(jnp.bfloat16))
    for t in range(out_ref.shape[0]):
        out_ref[t, :count, :] = sent[0]
        for k in range(3):
            out_ref[t, count + 16 * k : count + 16 * (k + 1), :] = sent[k + 1]


def softmax_kernel(core_start_ref, arrived_ref, positive_hot_ref, out_ref, inverse_ref):
    count = positive_hot_ref.shape[0]
    summed = arrived_ref[0].astype(jnp.float32)
    for t in range(1, arrived_ref.shape[0]):
        summed = summed + arrived_ref[t].astype(jnp.float32)

    def small(k):
        block = summed[count + 16 * k : count + 16 * (k + 1)]
        return block[:8] + block[8:]

    inverse_listed = lax.rsqrt(small(1) + EPSILON * EPSILON)
    inverse = lax.rsqrt(small(2) + EPSILON * EPSILON)
    inverse_ref[...] = inverse
    inverse_query = inverse_listed[7:8, :]
    picked = jnp.zeros((count, LANES), jnp.float32)
    for k in range(8):
        hot = positive_hot_ref[:, LANES * k : LANES * (k + 1)].astype(jnp.float32)
        picked = picked + hot * inverse[k : k + 1, :]
    inverse_positive = jnp.sum(picked, axis=1, keepdims=True)
    logits = summed[:count] * inverse_positive * inverse_query / SOFTMAX_TEMPER
    hard = small(0) * inverse_listed * inverse_query / SOFTMAX_TEMPER
    is_hard = iota(hard.shape, 0) < 7
    is_own = iota(logits.shape, 0) == iota(logits.shape, 1) + core_start_ref[0]
    weights = jnp.exp(logits - 1.0 / SOFTMAX_TEMPER)
    hard_weights = jnp.where(is_hard, jnp.exp(hard - 1.0 / SOFTMAX_TEMPER), 0.0)
    totals = jnp.sum(weights, axis=0, keepdims=True) + jnp.sum(hard_weights, axis=0, keepdims=True)
    target = jnp.sum(jnp.where(is_own, logits, 0.0), axis=0, keepdims=True)
    losses = jnp.log(totals) + 1.0 / SOFTMAX_TEMPER - target
    scaling_factor = LOSS_MULTIPLIER / (count * SOFTMAX_TEMPER)

    def rounded(value):
        return value.astype(jnp.bfloat16).astype(jnp.float32)

    coef = rounded(scaling_factor * (weights / totals - is_own.astype(jnp.float32)))
    hard_coef = rounded(scaling_factor * (hard_weights / totals))
    weighted = coef * logits * SOFTMAX_TEMPER
    hard_weighted = jnp.where(is_hard, hard_coef * hard * SOFTMAX_TEMPER, 0.0)
    along_query = jnp.sum(weighted, axis=0, keepdims=True) + jnp.sum(
        hard_weighted, axis=0, keepdims=True
    )
    out_ref[:count, :] = coef
    out_ref[count : count + 8, :] = jnp.where(is_hard, hard_coef, along_query)
    out_ref[count + 8 : count + 16, :] = jnp.where(is_hard, hard_weighted, losses)
    out_ref[count + 16 :, :] = jnp.zeros_like(out_ref[count + 16 :, :])
    columns_to_lanes(jnp.sum(weighted, axis=1, keepdims=True), out_ref.at[count + 16 :])


def resid_grad_kernel(
    group_ref,
    both_ref,
    inverse_ref,
    rows_ref,
    positive_hot_ref,
    query_hot_ref,
    positive_row_ref,
    listed_ref,
    own_listed_ref,
    resid_ref,
    gain_ref,
    out_ref,
    loss_ref,
):
    sequences = resid_ref.shape[0]
    count, total_rows = positive_hot_ref.shape
    first_row = group_ref[0] * sequences
    first_query = group_ref[0] * QDEV
    across = (((1,), (1,)), ((), ()))

    def joined(start, stop):
        return jnp.concatenate([both_ref[0, start:stop, :], both_ref[1, start:stop, :]], axis=1)

    coef = joined(0, count)
    coef16 = coef.astype(jnp.bfloat16)
    hard = joined(count, count + 8)
    hard_weighted = joined(count + 8, count + 16)
    along_passage = both_ref[0, count + 16 : count + 24, :] + both_ref[1, count + 16 : count + 24, :]
    along_passage = jnp.concatenate([along_passage[0:1], along_passage[1:2]], axis=1)
    inverse = jnp.concatenate([inverse_ref[k : k + 1, :] for k in range(8)], axis=1)

    own_row = first_row + iota((sequences, count), 0)
    own_query = (iota((sequences, count), 0) < QDEV) & (
        iota((sequences, count), 1) == first_query + iota((sequences, count), 0)
    )
    own_positive = positive_row_ref[...] == own_row
    to_positives = lax.dot_general(
        own_query.astype(jnp.bfloat16), coef16, across, preferred_element_type=jnp.float32
    )
    to_queries = jnp.dot(
        own_positive.astype(jnp.bfloat16), coef16, preferred_element_type=jnp.float32
    )
    along = jnp.sum(
        jnp.where(own_query, hard[7:8, :], 0.0) + jnp.where(own_positive, along_passage, 0.0),
        axis=1,
        keepdims=True,
    )
    for j in range(7):
        listed = listed_ref[j : j + 1, :] == own_row
        to_queries = to_queries + jnp.where(listed, hard[j : j + 1, :], 0.0)
        along = along + jnp.sum(
            jnp.where(listed, hard_weighted[j : j + 1, :], 0.0), axis=1, keepdims=True
        )
    matrix = jnp.dot(
        to_positives.astype(jnp.bfloat16), positive_hot_ref[...], preferred_element_type=jnp.float32
    ) + jnp.dot(
        to_queries.astype(jnp.bfloat16), query_hot_ref[...], preferred_element_type=jnp.float32
    )
    row_index = iota((sequences, total_rows), 1)
    for j in range(7):
        own_hard = jnp.sum(jnp.where(own_query, hard[j : j + 1, :], 0.0), axis=1, keepdims=True)
        listed = row_index == own_listed_ref[:, j : j + 1]
        matrix = matrix + jnp.where(listed, own_hard, 0.0)
    matrix = matrix * inverse
    high = matrix.astype(jnp.bfloat16)
    low = (matrix - high.astype(jnp.float32)).astype(jnp.bfloat16)
    rows = rows_ref[...]
    d_embed = jnp.dot(high, rows, preferred_element_type=jnp.float32) + jnp.dot(
        low, rows, preferred_element_type=jnp.float32
    )

    is_own_row = row_index == first_row + iota((sequences, total_rows), 0)
    own_inverse = jnp.sum(jnp.where(is_own_row, inverse, 0.0), axis=1, keepdims=True)
    resid = resid_ref[...]
    gain = gain_ref[...]
    features = gain.shape[1] * out_ref.shape[0]
    d_resid = own_inverse * gain * (
        d_embed - resid * gain * own_inverse * along
    ) - resid * (along * own_inverse * own_inverse * (EPSILON / features))
    d_resid16 = d_resid.astype(jnp.bfloat16)
    for t in range(out_ref.shape[0]):
        out_ref[t] = d_resid16
    losses = jnp.sum(hard_weighted[7:8, :], axis=1, keepdims=True)
    loss_ref[...] = jnp.broadcast_to(losses / count, loss_ref.shape)


def kernel_call(body, outs, arrays, scalars=0, scratch=()):
    specs = [pl.BlockSpec(memory_space=pltpu.SMEM)] * scalars
    specs += [pl.BlockSpec(memory_space=pltpu.VMEM)] * (len(arrays) - scalars)
    return pl.pallas_call(
        body,
        out_shape=[jax.ShapeDtypeStruct(shape, dtype) for shape, dtype in outs],
        in_specs=specs,
        out_specs=[pl.BlockSpec(memory_space=pltpu.VMEM)] * len(outs),
        scratch_shapes=list(scratch),
        compiler_params=pltpu.CompilerParams(vmem_limit_bytes=40 * 2**20),
    )(*arrays)


def candidate_tables(positives, negatives, core, group, sequences, core_count):
    others = sequences - QDEV
    query_count = positives.shape[0]
    total_rows = query_count // QDEV * sequences
    core_queries = query_count // core_count

    def row_of(passage):
        return passage // others * sequences + QDEV + passage % others

    queries = jnp.arange(query_count, dtype=jnp.int32)
    query_row = queries // QDEV * sequences + queries % QDEV
    positive_row = row_of(positives)
    rows = jnp.arange(total_rows, dtype=jnp.int32)
    query_hot = (query_row[:, None] == rows[None, :]).astype(jnp.bfloat16)
    positive_hot = (positive_row[:, None] == rows[None, :]).astype(jnp.bfloat16)
    listed = jnp.concatenate([row_of(negatives), query_row[:, None]], axis=1)
    own_listed = lax.dynamic_slice_in_dim(listed, group * QDEV, QDEV)
    own_listed = jnp.pad(
        own_listed, ((0, sequences - QDEV), (0, LANES - listed.shape[1])), constant_values=-1
    )
    core_start = core * core_queries
    return (
        positive_row[None, :],
        query_hot,
        lax.dynamic_slice_in_dim(query_hot, core_start, core_queries),
        positive_hot,
        listed.T,
        lax.dynamic_slice_in_dim(listed, core_start, core_queries).T,
        own_listed,
    )


def contrast(everyone, resid, out_gain, tables, group):
    tensor_count, core_count = lax.axis_size("tensor"), lax.axis_size("core")
    sequences, width = resid.shape
    positive_row, query_hot, core_hot, positive_hot, listed, core_listed, own_listed = tables
    count, total_rows = positive_hot.shape
    rows = everyone.reshape(total_rows, width)
    gain = out_gain[None, :]
    core_queries = core_hot.shape[0]
    core_start = (lax.axis_index("core") * core_queries)[None]
    (sent,) = kernel_call(
        partial_logits_kernel,
        [((tensor_count, count + 48, core_queries), jnp.bfloat16)],
        [rows, core_hot, positive_hot, core_listed, gain],
        scratch=[pltpu.VMEM((24, core_queries), jnp.float32)],
    )
    arrived = exchange(sent, "tensor")
    coefs, inverse = kernel_call(
        softmax_kernel,
        [((count + 24, core_queries), jnp.float32), ((8, LANES), jnp.float32)],
        [core_start, arrived, positive_hot],
        scalars=1,
    )
    both = lax.all_gather(coefs, "core", axis=0)
    d_resid16, loss = kernel_call(
        resid_grad_kernel,
        [((tensor_count, sequences, width), jnp.bfloat16), ((8, LANES), jnp.float32)],
        [
            group[None],
            both,
            inverse,
            rows,
            positive_hot,
            query_hot,
            positive_row,
            listed,
            own_listed,
            resid,
            gain,
        ],
        scalars=1,
    )
    return loss[0, 0], exchange(d_resid16, "tensor")


def on_device(
    hidden, lengths, positives, negatives, in_gain, wq, wkv, q_gain, k_gain, wo, out_gain
):
    tensor_count = lax.axis_size("tensor")
    tensor_index = lax.axis_index("tensor")
    own_rows, features = hidden.shape
    tokens_count = own_rows * tensor_count
    head_width = wq.shape[1]
    sequences = lengths.shape[1]
    chunk = features // tensor_count
    root = math.sqrt(head_width)
    is_even = tensor_index % 2 == 0
    hidden32 = hidden.astype(jnp.float32)
    inverse_in = rms_scale(hidden32)
    normed = (hidden32 * inverse_in * in_gain).astype(jnp.bfloat16)
    core_count = lax.axis_size("core")
    core = lax.axis_index("core")
    group = lax.axis_index("z") * core_count + core
    tables = candidate_tables(positives, negatives, core, group, sequences, core_count)
    piece = gather_rows(normed, "tensor").reshape(tokens_count, features)
    own_index = tensor_index * own_rows + jnp.arange(own_rows, dtype=jnp.int32)
    inside, position, last = segment_layout(lengths[0], tokens_count)
    own_last = (last[:, None] == own_index[None, :]).astype(jnp.bfloat16)
    token_index = jnp.arange(tokens_count, dtype=jnp.int32)
    chosen = (last[:, None] == token_index[None, :]).astype(jnp.bfloat16)
    weights = jnp.concatenate([wkv, wq], axis=1)
    projected = jnp.dot(piece, weights, preferred_element_type=jnp.float32)
    kv_own = projected[:, :head_width]
    kv_other = swapped(kv_own, "tensor", 0)
    query_raw = jnp.dot(
        chosen.astype(jnp.float32), projected[:, head_width:], precision=lax.Precision.HIGHEST
    )
    key_raw = jnp.where(is_even, kv_own, kv_other)
    value16 = jnp.where(is_even, kv_other, kv_own).astype(jnp.bfloat16)
    cos_key, sin_key = rope_tables(position, head_width)
    key_unit, key_inverse, key_rot = head_forward(key_raw, k_gain, cos_key, sin_key)
    key16 = key_rot.astype(jnp.bfloat16)
    cos_query, sin_query = rope_tables((lengths[0] - 1).astype(jnp.float32), head_width)
    query_unit, query_inverse, query_rot = head_forward(query_raw, q_gain, cos_query, sin_query)
    query16 = query_rot.astype(jnp.bfloat16)
    shift = root * jnp.max(q_gain) * jnp.max(k_gain)
    scores = jnp.dot(query16, key16.T, preferred_element_type=jnp.float32) / root
    weight_params = jnp.where(inside.T, jnp.exp(scores - shift), 0.0)
    probs = weight_params / jnp.sum(weight_params, axis=-1, keepdims=True)
    probs16 = probs.astype(jnp.bfloat16)
    attn16 = jnp.dot(probs16, value16, preferred_element_type=jnp.float32).astype(jnp.bfloat16)
    partial_rows = jnp.dot(attn16, wo, preferred_element_type=jnp.float32) + jnp.dot(
        own_last, hidden, preferred_element_type=jnp.float32
    )
    blocks = partial_rows.astype(jnp.bfloat16).reshape(sequences, tensor_count, chunk)
    arrived = exchange(blocks.transpose(1, 0, 2), "tensor")
    resid = jnp.sum(arrived.astype(jnp.float32), axis=0)
    own_gain = lax.dynamic_slice_in_dim(out_gain, tensor_index * chunk, chunk)
    scaled = resid * own_gain
    same_core = gather_rows(scaled.astype(jnp.bfloat16), "z")
    everyone = lax.all_gather(same_core, "core", axis=1)
    loss, d_resid16 = contrast(everyone, resid, own_gain, tables, group)
    d_resid16 = d_resid16.transpose(1, 0, 2).reshape(sequences, features)
    d_attn16 = jnp.dot(d_resid16, wo.T, preferred_element_type=jnp.float32).astype(jnp.bfloat16)
    d_probs = jnp.dot(d_attn16, value16.T, preferred_element_type=jnp.float32)
    d_scores16 = (
        probs * (d_probs - jnp.sum(probs * d_probs, axis=-1, keepdims=True)) / root
    ).astype(jnp.bfloat16)
    d_query_rot = jnp.dot(d_scores16, key16, preferred_element_type=jnp.float32)
    d_key_rot = jnp.dot(d_scores16.T, query16, preferred_element_type=jnp.float32)
    d_value = jnp.dot(probs16.T, d_attn16, preferred_element_type=jnp.float32)
    d_key_raw = head_backward(d_key_rot, key_unit, key_inverse, k_gain, cos_key, sin_key)
    d_query_raw = head_backward(
        d_query_rot, query_unit, query_inverse, q_gain, cos_query, sin_query
    )
    mine = jnp.where(is_even, d_key_raw, d_value)
    theirs = jnp.where(is_even, d_value, d_key_raw)
    column16 = (mine + swapped(theirs, "tensor", 0)).astype(jnp.bfloat16)
    spread16 = jnp.dot(
        chosen.T, d_query_raw.astype(jnp.bfloat16), preferred_element_type=jnp.float32
    ).astype(jnp.bfloat16)
    product = jnp.dot(
        jnp.concatenate([column16, spread16], axis=1),
        weights.T,
        preferred_element_type=jnp.float32,
    )
    terms = exchange(product.astype(jnp.bfloat16), "tensor")
    d_normed = jnp.sum(
        terms.reshape(tensor_count, own_rows, features).astype(jnp.float32), axis=0
    )
    d_hidden = norm_backward(d_normed, hidden32 * inverse_in, inverse_in, in_gain)
    d_hidden = d_hidden + jnp.dot(own_last.T, d_resid16, preferred_element_type=jnp.float32)
    return (d_hidden.astype(jnp.bfloat16), loss)


def solution(mesh):
    z_count = mesh.shape["dp"] // 2
    chips = mesh.devices.reshape(z_count, 2, mesh.shape["tensor"])
    mesh = jax.sharding.Mesh(chips, ("z", "core", "tensor"))
    everywhere = P(("z", "core", "tensor"), None)
    placed = (
        everywhere,
        P(("z", "core"), None),
        P(),
        P(),
        P(),
        P(None, "tensor"),
        P(None, "tensor"),
        P(),
        P(),
        P("tensor", None),
        P(),
    )
    return jax.shard_map(
        on_device, mesh=mesh, in_specs=placed, out_specs=(everywhere, P()), check_vma=False
    )
```

```python
import math

import jax
import jax.numpy as jnp
from jax import lax
from jax.experimental import pallas as pl
from jax.experimental.pallas import tpu as pltpu
from jax.sharding import PartitionSpec as P

QDEV = 8
LANES = 128


EPSILON = 1e-06
SOFTMAX_TEMPER = 0.05
LOSS_MULTIPLIER = 8192.0
ROPE_BASE = 1000000.0


def swapped(value, axis, apart):
    mask = 2**apart
    pairs = [(source, source ^ mask) for source in range(lax.axis_size(axis))]
    return lax.ppermute(value, axis, pairs)


def rms_scale(tensor):
    return lax.rsqrt(jnp.mean(tensor * tensor, axis=-1, keepdims=True) + EPSILON)


def rope_tables(position, head_width):
    halfway = head_width // 2
    frequency = ROPE_BASE ** (-(jnp.arange(halfway, dtype=jnp.float32) * (2.0 / head_width)))
    angles = position[:, None] * frequency[None, :]
    angles = jnp.concatenate([angles, angles], axis=-1)
    return (jnp.cos(angles), jnp.sin(angles))


def segment_layout(lengths_row, total_tokens):
    seq_ends = jnp.cumsum(lengths_row)
    starts = seq_ends - lengths_row
    token_index = jnp.arange(total_tokens, dtype=jnp.int32)
    inside = (token_index[:, None] >= starts[None, :]) & (token_index[:, None] < seq_ends[None, :])
    offset = jnp.sum(jnp.where(inside, starts[None, :], 0), axis=1)
    position = (token_index - offset).astype(jnp.float32)
    return (inside, position, seq_ends - 1)


def norm_backward(grad, unit_form, inverse, gain):
    scaled = grad * gain
    return inverse * (scaled - unit_form * jnp.mean(unit_form * scaled, axis=-1, keepdims=True))


def exchange(blocks, axis):
    return lax.all_to_all(blocks, axis, 0, 0, tiled=True)


def halves(value):
    high = value.astype(jnp.bfloat16).astype(jnp.float32)
    return jnp.concatenate([high, value - high], axis=0)


def iota(shape, axis):
    return lax.broadcasted_iota(jnp.int32, shape, axis)


def columns_to_lanes(column, out_ref):
    diagonal = iota((LANES, LANES), 0) == iota((LANES, LANES), 1)
    for k in range(column.shape[0] // LANES):
        block = jnp.where(diagonal, column[LANES * k : LANES * (k + 1)], 0.0)
        out_ref[k : k + 1, :] = jnp.sum(block, axis=0, keepdims=True)


def partial_logits_kernel(rows_ref, query_hot_ref, positive_hot_ref, listed_ref, gain_ref, out_ref, held_ref):
    rows = rows_ref[...]
    queries = jnp.dot(query_hot_ref[...], rows, preferred_element_type=jnp.float32)
    positives = jnp.dot(positive_hot_ref[...], rows, preferred_element_type=jnp.float32)
    queries = queries.astype(jnp.bfloat16)
    features = gain_ref.shape[1] * out_ref.shape[0]
    rows32 = rows.astype(jnp.float32)
    plain = rows32 / gain_ref[...]
    squares = jnp.sum(rows32 * rows32, axis=1, keepdims=True) + jnp.sum(
        plain * plain, axis=1, keepdims=True
    ) * (EPSILON / features)
    against = (((1,), (1,)), ((), ()))
    with_positives = lax.dot_general(
        positives.astype(jnp.bfloat16), queries, against, preferred_element_type=jnp.float32
    )
    with_all = lax.dot_general(rows, queries, against, preferred_element_type=jnp.float32)
    row_index = iota(with_all.shape, 0)
    for j in range(8):
        listed = row_index == listed_ref[j : j + 1, :]
        held_ref[j : j + 1, :] = jnp.sum(jnp.where(listed, with_all, 0.0), axis=0, keepdims=True)
        held_ref[8 + j : 9 + j, :] = jnp.sum(
            jnp.where(listed, squares, 0.0), axis=0, keepdims=True
        )
    columns_to_lanes(squares, held_ref.at[16:24])
    count = with_positives.shape[0]
    sent = [with_positives.astype(jnp.bfloat16)]
    for start in (0, 8, 16):
        sent.append(halves(held_ref[start : start + 8, :]).astype(jnp.bfloat16))
    for t in range(out_ref.shape[0]):
        out_ref[t, :count, :] = sent[0]
        for k in range(3):
            out_ref[t, count + 16 * k : count + 16 * (k + 1), :] = sent[k + 1]


def softmax_kernel(core_start_ref, arrived_ref, positive_hot_ref, out_ref, inverse_ref):
    count = positive_hot_ref.shape[0]
    summed = arrived_ref[0].astype(jnp.float32)
    for t in range(1, arrived_ref.shape[0]):
        summed = summed + arrived_ref[t].astype(jnp.float32)

    def small(k):
        block = summed[count + 16 * k : count + 16 * (k + 1)]
        return block[:8] + block[8:]

    inverse_listed = lax.rsqrt(small(1) + EPSILON * EPSILON)
    inverse = lax.rsqrt(small(2) + EPSILON * EPSILON)
    inverse_ref[...] = inverse
    inverse_query = inverse_listed[7:8, :]
    picked = jnp.zeros((count, LANES), jnp.float32)
    for k in range(8):
        hot = positive_hot_ref[:, LANES * k : LANES * (k + 1)].astype(jnp.float32)
        picked = picked + hot * inverse[k : k + 1, :]
    inverse_positive = jnp.sum(picked, axis=1, keepdims=True)
    logits = summed[:count] * inverse_positive * inverse_query / SOFTMAX_TEMPER
    hard = small(0) * inverse_listed * inverse_query / SOFTMAX_TEMPER
    is_hard = iota(hard.shape, 0) < 7
    is_own = iota(logits.shape, 0) == iota(logits.shape, 1) + core_start_ref[0]
    weights = jnp.exp(logits - 1.0 / SOFTMAX_TEMPER)
    hard_weights = jnp.where(is_hard, jnp.exp(hard - 1.0 / SOFTMAX_TEMPER), 0.0)
    totals = jnp.sum(weights, axis=0, keepdims=True) + jnp.sum(hard_weights, axis=0, keepdims=True)
    target = jnp.sum(jnp.where(is_own, logits, 0.0), axis=0, keepdims=True)
    losses = jnp.log(totals) + 1.0 / SOFTMAX_TEMPER - target
    scaling_factor = LOSS_MULTIPLIER / (count * SOFTMAX_TEMPER)

    def rounded(value):
        return value.astype(jnp.bfloat16).astype(jnp.float32)

    coef = rounded(scaling_factor * (weights / totals - is_own.astype(jnp.float32)))
    hard_coef = rounded(scaling_factor * (hard_weights / totals))
    weighted = coef * logits * SOFTMAX_TEMPER
    hard_weighted = jnp.where(is_hard, hard_coef * hard * SOFTMAX_TEMPER, 0.0)
    along_query = jnp.sum(weighted, axis=0, keepdims=True) + jnp.sum(
        hard_weighted, axis=0, keepdims=True
    )
    out_ref[:count, :] = coef
    out_ref[count : count + 8, :] = jnp.where(is_hard, hard_coef, along_query)
    out_ref[count + 8 : count + 16, :] = jnp.where(is_hard, hard_weighted, losses)
    out_ref[count + 16 :, :] = jnp.zeros_like(out_ref[count + 16 :, :])
    columns_to_lanes(jnp.sum(weighted, axis=1, keepdims=True), out_ref.at[count + 16 :])


def resid_grad_kernel(
    group_ref,
    both_ref,
    inverse_ref,
    rows_ref,
    positive_hot_ref,
    query_hot_ref,
    positive_row_ref,
    listed_ref,
    own_listed_ref,
    resid_ref,
    gain_ref,
    out_ref,
    loss_ref,
):
    sequences = resid_ref.shape[0]
    count, total_rows = positive_hot_ref.shape
    first_row = group_ref[0] * sequences
    first_query = group_ref[0] * QDEV
    across = (((1,), (1,)), ((), ()))

    def joined(start, stop):
        return jnp.concatenate([both_ref[0, start:stop, :], both_ref[1, start:stop, :]], axis=1)

    coef = joined(0, count)
    coef16 = coef.astype(jnp.bfloat16)
    hard = joined(count, count + 8)
    hard_weighted = joined(count + 8, count + 16)
    along_passage = both_ref[0, count + 16 : count + 24, :] + both_ref[1, count + 16 : count + 24, :]
    along_passage = jnp.concatenate([along_passage[0:1], along_passage[1:2]], axis=1)
    inverse = jnp.concatenate([inverse_ref[k : k + 1, :] for k in range(8)], axis=1)

    own_row = first_row + iota((sequences, count), 0)
    own_query = (iota((sequences, count), 0) < QDEV) & (
        iota((sequences, count), 1) == first_query + iota((sequences, count), 0)
    )
    own_positive = positive_row_ref[...] == own_row
    to_positives = lax.dot_general(
        own_query.astype(jnp.bfloat16), coef16, across, preferred_element_type=jnp.float32
    )
    to_queries = jnp.dot(
        own_positive.astype(jnp.bfloat16), coef16, preferred_element_type=jnp.float32
    )
    along = jnp.sum(
        jnp.where(own_query, hard[7:8, :], 0.0) + jnp.where(own_positive, along_passage, 0.0),
        axis=1,
        keepdims=True,
    )
    for j in range(7):
        listed = listed_ref[j : j + 1, :] == own_row
        to_queries = to_queries + jnp.where(listed, hard[j : j + 1, :], 0.0)
        along = along + jnp.sum(
            jnp.where(listed, hard_weighted[j : j + 1, :], 0.0), axis=1, keepdims=True
        )
    matrix = jnp.dot(
        to_positives.astype(jnp.bfloat16), positive_hot_ref[...], preferred_element_type=jnp.float32
    ) + jnp.dot(
        to_queries.astype(jnp.bfloat16), query_hot_ref[...], preferred_element_type=jnp.float32
    )
    row_index = iota((sequences, total_rows), 1)
    for j in range(7):
        own_hard = jnp.sum(jnp.where(own_query, hard[j : j + 1, :], 0.0), axis=1, keepdims=True)
        listed = row_index == own_listed_ref[:, j : j + 1]
        matrix = matrix + jnp.where(listed, own_hard, 0.0)
    matrix = matrix * inverse
    high = matrix.astype(jnp.bfloat16)
    low = (matrix - high.astype(jnp.float32)).astype(jnp.bfloat16)
    rows = rows_ref[...]
    d_embed = jnp.dot(high, rows, preferred_element_type=jnp.float32) + jnp.dot(
        low, rows, preferred_element_type=jnp.float32
    )

    is_own_row = row_index == first_row + iota((sequences, total_rows), 0)
    own_inverse = jnp.sum(jnp.where(is_own_row, inverse, 0.0), axis=1, keepdims=True)
    resid = resid_ref[...]
    gain = gain_ref[...]
    features = gain.shape[1] * out_ref.shape[0]
    d_resid = own_inverse * gain * (
        d_embed - resid * gain * own_inverse * along
    ) - resid * (along * own_inverse * own_inverse * (EPSILON / features))
    d_resid16 = d_resid.astype(jnp.bfloat16)
    for t in range(out_ref.shape[0]):
        out_ref[t] = d_resid16
    losses = jnp.sum(hard_weighted[7:8, :], axis=1, keepdims=True)
    loss_ref[...] = jnp.broadcast_to(losses / count, loss_ref.shape)


def kernel_call(body, outs, arrays, scalars=0, scratch=()):
    specs = [pl.BlockSpec(memory_space=pltpu.SMEM)] * scalars
    specs += [pl.BlockSpec(memory_space=pltpu.VMEM)] * (len(arrays) - scalars)
    return pl.pallas_call(
        body,
        out_shape=[jax.ShapeDtypeStruct(shape, dtype) for shape, dtype in outs],
        in_specs=specs,
        out_specs=[pl.BlockSpec(memory_space=pltpu.VMEM)] * len(outs),
        scratch_shapes=list(scratch),
        compiler_params=pltpu.CompilerParams(vmem_limit_bytes=24 * 2**20),
    )(*arrays)


def candidate_tables(positives, negatives, core, group, sequences, core_count):
    others = sequences - QDEV
    query_count = positives.shape[0]
    total_rows = query_count // QDEV * sequences
    core_queries = query_count // core_count

    def row_of(passage):
        return passage // others * sequences + QDEV + passage % others

    queries = jnp.arange(query_count, dtype=jnp.int32)
    query_row = queries // QDEV * sequences + queries % QDEV
    positive_row = row_of(positives)
    rows = jnp.arange(total_rows, dtype=jnp.int32)
    query_hot = (query_row[:, None] == rows[None, :]).astype(jnp.bfloat16)
    positive_hot = (positive_row[:, None] == rows[None, :]).astype(jnp.bfloat16)
    listed = jnp.concatenate([row_of(negatives), query_row[:, None]], axis=1)
    own_listed = lax.dynamic_slice_in_dim(listed, group * QDEV, QDEV)
    own_listed = jnp.pad(
        own_listed, ((0, sequences - QDEV), (0, LANES - listed.shape[1])), constant_values=-1
    )
    core_start = core * core_queries
    return (
        positive_row[None, :],
        query_hot,
        lax.dynamic_slice_in_dim(query_hot, core_start, core_queries),
        positive_hot,
        listed.T,
        lax.dynamic_slice_in_dim(listed, core_start, core_queries).T,
        own_listed,
    )


def contrast(everyone, resid, out_gain, tables, group):
    tensor_count, core_count = lax.axis_size("tensor"), lax.axis_size("core")
    sequences, width = resid.shape
    positive_row, query_hot, core_hot, positive_hot, listed, core_listed, own_listed = tables
    count, total_rows = positive_hot.shape
    rows = everyone.reshape(total_rows, width)
    gain = out_gain[None, :]
    core_queries = core_hot.shape[0]
    core_start = (lax.axis_index("core") * core_queries)[None]
    (sent,) = kernel_call(
        partial_logits_kernel,
        [((tensor_count, count + 48, core_queries), jnp.bfloat16)],
        [rows, core_hot, positive_hot, core_listed, gain],
        scratch=[pltpu.VMEM((24, core_queries), jnp.float32)],
    )
    arrived = exchange(sent, "tensor")
    coefs, inverse = kernel_call(
        softmax_kernel,
        [((count + 24, core_queries), jnp.float32), ((8, LANES), jnp.float32)],
        [core_start, arrived, positive_hot],
        scalars=1,
    )
    both = lax.all_gather(coefs, "core", axis=0)
    d_resid16, loss = kernel_call(
        resid_grad_kernel,
        [((tensor_count, sequences, width), jnp.bfloat16), ((8, LANES), jnp.float32)],
        [
            group[None],
            both,
            inverse,
            rows,
            positive_hot,
            query_hot,
            positive_row,
            listed,
            own_listed,
            resid,
            gain,
        ],
        scalars=1,
    )
    return loss[0, 0], exchange(d_resid16, "tensor")


def copied_norm_kernel(hidden_ref, gain_ref, out_ref):
    hidden32 = hidden_ref[...].astype(jnp.float32)
    normed = (hidden32 * rms_scale(hidden32) * gain_ref[...]).astype(jnp.bfloat16)
    for t in range(out_ref.shape[0]):
        out_ref[t] = normed


def projection_kernel(rows_ref, weights_ref, chosen_ref, kv_ref, query_ref):
    width = kv_ref.shape[1]
    projected = jnp.dot(rows_ref[...], weights_ref[...], preferred_element_type=jnp.float32)
    kv_ref[...] = projected[:, :width]
    query_ref[...] = jnp.dot(
        chosen_ref[...].astype(jnp.float32),
        projected[:, width:],
        precision=lax.Precision.HIGHEST,
        preferred_element_type=jnp.float32,
    )


def half_turned(tensor, cosine, signed_sine):
    halfway = tensor.shape[1] // 2
    return tensor * cosine + pltpu.roll(tensor, halfway, 1) * signed_sine


def attention_kernel(
    even_ref,
    own_ref,
    other_ref,
    query_raw_ref,
    key_turn_ref,
    query_turn_ref,
    gains_ref,
    inside_ref,
    own_last_ref,
    hidden_ref,
    wo_ref,
    out_ref,
    key_raw_ref,
    key_ref,
    value_ref,
    query_ref,
    probs_ref,
):
    root = math.sqrt(own_ref.shape[1])
    is_even = even_ref[0] == 1
    own, other = own_ref[...], other_ref[...]
    key_raw = jnp.where(is_even, own, other)
    value16 = jnp.where(is_even, other, own).astype(jnp.bfloat16)
    query_raw = query_raw_ref[...]
    q_gain, k_gain = gains_ref[0:1, :], gains_ref[1:2, :]
    key16 = half_turned(
        key_raw * rms_scale(key_raw) * k_gain, key_turn_ref[0], key_turn_ref[1]
    ).astype(jnp.bfloat16)
    query16 = half_turned(
        query_raw * rms_scale(query_raw) * q_gain, query_turn_ref[0], query_turn_ref[1]
    ).astype(jnp.bfloat16)
    shift = (
        root
        * jnp.max(q_gain, axis=1, keepdims=True)
        * jnp.max(k_gain, axis=1, keepdims=True)
    )
    scores = (
        lax.dot_general(
            query16, key16, (((1,), (1,)), ((), ())), preferred_element_type=jnp.float32
        )
        / root
    )
    weights = jnp.where(inside_ref[...] > 0.0, jnp.exp(scores - shift), 0.0)
    probs = weights / jnp.sum(weights, axis=1, keepdims=True)
    attn16 = jnp.dot(
        probs.astype(jnp.bfloat16), value16, preferred_element_type=jnp.float32
    ).astype(jnp.bfloat16)
    chunk = out_ref.shape[2]
    for t in range(out_ref.shape[0]):
        columns = slice(t * chunk, (t + 1) * chunk)
        block = jnp.dot(attn16, wo_ref[:, columns], preferred_element_type=jnp.float32)
        block = block + jnp.dot(
            own_last_ref[...], hidden_ref[:, columns], preferred_element_type=jnp.float32
        )
        out_ref[t] = block.astype(jnp.bfloat16)
    key_raw_ref[...] = key_raw
    key_ref[...] = key16
    value_ref[...] = value16
    query_ref[...] = query16
    probs_ref[...] = probs


def resid_kernel(arrived_ref, gain_ref, weights_ref, resid_ref, out_ref, weights_out_ref):
    resid = arrived_ref[0].astype(jnp.float32)
    for t in range(1, arrived_ref.shape[0]):
        resid = resid + arrived_ref[t].astype(jnp.float32)
    resid_ref[...] = resid
    scaled16 = (resid * gain_ref[...]).astype(jnp.bfloat16)
    for t in range(out_ref.shape[0]):
        out_ref[t] = scaled16
    weights_out_ref[...] = weights_ref[...]


def gradient_kernel(
    even_ref,
    d_resid_ref,
    wo_t_ref,
    key_raw_ref,
    query_raw_ref,
    key_ref,
    value_ref,
    query_ref,
    probs_ref,
    key_turn_ref,
    query_turn_ref,
    gains_ref,
    chosen_ref,
    own_weights_ref,
    other_weights_ref,
    query_weights_ref,
    out_ref,
):
    root = math.sqrt(key_ref.shape[1])
    is_even = even_ref[0] == 1
    q_gain, k_gain = gains_ref[0:1, :], gains_ref[1:2, :]
    chunk = d_resid_ref.shape[2]
    d_attn = jnp.dot(d_resid_ref[0], wo_t_ref[:chunk, :], preferred_element_type=jnp.float32)
    for t in range(1, d_resid_ref.shape[0]):
        d_attn = d_attn + jnp.dot(
            d_resid_ref[t],
            wo_t_ref[t * chunk : (t + 1) * chunk, :],
            preferred_element_type=jnp.float32,
        )
    d_attn16 = d_attn.astype(jnp.bfloat16)
    probs = probs_ref[...]
    key16, query16 = key_ref[...], query_ref[...]
    d_probs = lax.dot_general(
        d_attn16, value_ref[...], (((1,), (1,)), ((), ())), preferred_element_type=jnp.float32
    )
    d_scores16 = (
        probs * (d_probs - jnp.sum(probs * d_probs, axis=1, keepdims=True)) / root
    ).astype(jnp.bfloat16)
    down = (((0,), (0,)), ((), ()))
    d_query_rot = jnp.dot(d_scores16, key16, preferred_element_type=jnp.float32)
    d_key_rot = lax.dot_general(d_scores16, query16, down, preferred_element_type=jnp.float32)
    d_value = lax.dot_general(
        probs.astype(jnp.bfloat16), d_attn16, down, preferred_element_type=jnp.float32
    )

    def head_gradient(grad_rot, raw, gain, turn_ref):
        inverse = rms_scale(raw)
        turned_back = half_turned(grad_rot, turn_ref[0], -turn_ref[1])
        return norm_backward(turned_back, raw * inverse, inverse, gain)

    d_key = head_gradient(d_key_rot, key_raw_ref[...], k_gain, key_turn_ref)
    d_query = head_gradient(d_query_rot, query_raw_ref[...], q_gain, query_turn_ref)
    own16 = jnp.where(is_even, d_key, d_value).astype(jnp.bfloat16)
    other16 = jnp.where(is_even, d_value, d_key).astype(jnp.bfloat16)
    spread16 = lax.dot_general(
        chosen_ref[...], d_query.astype(jnp.bfloat16), down, preferred_element_type=jnp.float32
    ).astype(jnp.bfloat16)
    for t in range(out_ref.shape[1] // chunk):
        columns = slice(t * chunk, (t + 1) * chunk)
        term = jnp.dot(own16, own_weights_ref[:, columns], preferred_element_type=jnp.float32)
        term = term + jnp.dot(
            other16, other_weights_ref[:, columns], preferred_element_type=jnp.float32
        )
        term = term + jnp.dot(
            spread16, query_weights_ref[:, columns], preferred_element_type=jnp.float32
        )
        out_ref[:, columns] = term.astype(jnp.bfloat16)


def d_hidden_kernel(terms_ref, hidden_ref, gain_ref, last_ref, d_resid_ref, out_ref):
    d_normed = terms_ref[0].astype(jnp.float32)
    for t in range(1, terms_ref.shape[0]):
        d_normed = d_normed + terms_ref[t].astype(jnp.float32)
    hidden32 = hidden_ref[...].astype(jnp.float32)
    inverse = rms_scale(hidden32)
    d_hidden = norm_backward(d_normed, hidden32 * inverse, inverse, gain_ref[...])
    last = last_ref[...]
    chunk = d_resid_ref.shape[2]
    for t in range(d_resid_ref.shape[0]):
        columns = slice(t * chunk, (t + 1) * chunk)
        added = jnp.dot(last, d_resid_ref[t], preferred_element_type=jnp.float32)
        out_ref[:, columns] = (d_hidden[:, columns] + added).astype(jnp.bfloat16)


def turn_tables(position, head_width):
    cosine, sine = rope_tables(position, head_width)
    sign = jnp.where(jnp.arange(head_width) < head_width // 2, -1.0, 1.0)
    return jnp.stack([cosine, sine * sign])


def on_device(
    hidden, lengths, positives, negatives, in_gain, wq, wkv, q_gain, k_gain, wo, out_gain
):
    tensor_count, core_count = lax.axis_size("tensor"), lax.axis_size("core")
    tensor_index, core = lax.axis_index("tensor"), lax.axis_index("core")
    z_count = lax.axis_size("z")
    group = lax.axis_index("z") * core_count + core
    own_rows, features = hidden.shape
    tokens_count = own_rows * tensor_count
    head_width = wq.shape[1]
    sequences = lengths.shape[1]
    chunk = features // tensor_count
    f32, bf16 = jnp.float32, jnp.bfloat16
    is_even = (1 - tensor_index % 2).astype(jnp.int32)[None]
    input_gain = in_gain[None, :]

    (copies,) = kernel_call(
        copied_norm_kernel, [((tensor_count, own_rows, features), bf16)], [hidden, input_gain]
    )
    piece = exchange(copies, "tensor").reshape(tokens_count, features)

    own_index = tensor_index * own_rows + jnp.arange(own_rows, dtype=jnp.int32)
    inside, position, last = segment_layout(lengths[0], tokens_count)
    own_last = (last[:, None] == own_index[None, :]).astype(bf16)
    token_index = jnp.arange(tokens_count, dtype=jnp.int32)
    chosen = (last[:, None] == token_index[None, :]).astype(bf16)
    key_turn = turn_tables(position, head_width)
    query_turn = turn_tables((lengths[0] - 1).astype(f32), head_width)
    gains = jnp.stack([q_gain, k_gain])
    tables = candidate_tables(positives, negatives, core, group, sequences, core_count)
    own_gain = lax.dynamic_slice_in_dim(out_gain, tensor_index * chunk, chunk)

    kv_own, query_raw = kernel_call(
        projection_kernel,
        [((tokens_count, head_width), f32), ((sequences, head_width), f32)],
        [piece, jnp.concatenate([wkv, wq], axis=1), chosen],
    )
    kv_other = swapped(kv_own, "tensor", 0)
    blocks, key_raw, key16, value16, query16, probs = kernel_call(
        attention_kernel,
        [
            ((tensor_count, sequences, chunk), bf16),
            ((tokens_count, head_width), f32),
            ((tokens_count, head_width), bf16),
            ((tokens_count, head_width), bf16),
            ((sequences, head_width), bf16),
            ((sequences, tokens_count), f32),
        ],
        [
            is_even,
            kv_own,
            kv_other,
            query_raw,
            key_turn,
            query_turn,
            gains,
            inside.T.astype(f32),
            own_last,
            hidden,
            wo,
        ],
        scalars=1,
    )
    resid, scaled, own_weights = kernel_call(
        resid_kernel,
        [
            ((sequences, chunk), f32),
            ((z_count, sequences, chunk), bf16),
            ((head_width, features), bf16),
        ],
        [exchange(blocks, "tensor"), own_gain[None, :], wkv.T],
    )
    other_weights = swapped(own_weights, "tensor", 0)
    everyone = lax.all_gather(exchange(scaled, "z"), "core", axis=1)
    loss, d_resid16 = contrast(everyone, resid, own_gain, tables, group)
    (product,) = kernel_call(
        gradient_kernel,
        [((tokens_count, features), bf16)],
        [
            is_even,
            d_resid16,
            wo.T,
            key_raw,
            query_raw,
            key16,
            value16,
            query16,
            probs,
            key_turn,
            query_turn,
            gains,
            chosen,
            own_weights,
            other_weights,
            wq.T,
        ],
        scalars=1,
    )
    terms = exchange(product, "tensor").reshape(tensor_count, own_rows, features)
    (d_hidden,) = kernel_call(
        d_hidden_kernel,
        [((own_rows, features), bf16)],
        [terms, hidden, input_gain, own_last.T, d_resid16],
    )
    return (d_hidden, loss)


def solution(mesh):
    z_count = mesh.shape["dp"] // 2
    chips = mesh.devices.reshape(z_count, 2, mesh.shape["tensor"])
    mesh = jax.sharding.Mesh(chips, ("z", "core", "tensor"))
    everywhere = P(("z", "core", "tensor"), None)
    placed = (
        everywhere,
        P(("z", "core"), None),
        P(),
        P(),
        P(),
        P(None, "tensor"),
        P(None, "tensor"),
        P(),
        P(),
        P("tensor", None),
        P(),
    )
    return jax.shard_map(
        on_device, mesh=mesh, in_specs=placed, out_specs=(everywhere, P()), check_vma=False
    )
```

```python
import functools
import math

import jax
import jax.numpy as jnp
from jax import lax
from jax.experimental import pallas as pl
from jax.experimental.pallas import tpu as pltpu
from jax.sharding import PartitionSpec as P

QDEV = 8
LANES = 128
VMEM_BYTES = 32 * 2**20


EPSILON = 1e-06
SOFTMAX_TEMPER = 0.05
LOSS_MULTIPLIER = 8192.0
ROPE_BASE = 1000000.0


def swapped(value, axis, apart):
    mask = 2**apart
    pairs = [(source, source ^ mask) for source in range(lax.axis_size(axis))]
    return lax.ppermute(value, axis, pairs)


def rms_scale(tensor):
    return lax.rsqrt(jnp.mean(tensor * tensor, axis=-1, keepdims=True) + EPSILON)


def norm_backward(grad, unit_form, inverse, gain):
    scaled = grad * gain
    return inverse * (scaled - unit_form * jnp.mean(unit_form * scaled, axis=-1, keepdims=True))


def exchange(blocks, axis):
    return lax.all_to_all(blocks, axis, 0, 0, tiled=True)


def halves(value):
    high = value.astype(jnp.bfloat16).astype(jnp.float32)
    return jnp.concatenate([high, value - high], axis=0)


def iota(shape, axis):
    return lax.broadcasted_iota(jnp.int32, shape, axis)


def columns_to_lanes(column, out_ref):
    diagonal = iota((LANES, LANES), 0) == iota((LANES, LANES), 1)
    for k in range(column.shape[0] // LANES):
        block = jnp.where(diagonal, column[LANES * k : LANES * (k + 1)], 0.0)
        out_ref[k : k + 1, :] = jnp.sum(block, axis=0, keepdims=True)


def own_core_lanes():
    return pl.ds(pl.multiple_of(lax.axis_index("core") * LANES, LANES), LANES)


def partial_logits_kernel(
    rows_ref, query_hot_ref, positive_hot_ref, listed_all_ref, gain_ref, out_ref, rows_out_ref, held_ref
):
    rows = rows_ref[...]
    rows_out_ref[...] = rows
    listed_ref = listed_all_ref[:8, own_core_lanes()]
    core_hot = query_hot_ref[own_core_lanes(), :]
    queries = jnp.dot(core_hot, rows, preferred_element_type=jnp.float32)
    positives = jnp.dot(positive_hot_ref[...], rows, preferred_element_type=jnp.float32)
    queries = queries.astype(jnp.bfloat16)
    features = gain_ref.shape[1] * out_ref.shape[0]
    rows32 = rows.astype(jnp.float32)
    plain = rows32 / gain_ref[...]
    squares = jnp.sum(rows32 * rows32, axis=1, keepdims=True) + jnp.sum(
        plain * plain, axis=1, keepdims=True
    ) * (EPSILON / features)
    against = (((1,), (1,)), ((), ()))
    with_positives = lax.dot_general(
        positives.astype(jnp.bfloat16), queries, against, preferred_element_type=jnp.float32
    )
    with_all = lax.dot_general(rows, queries, against, preferred_element_type=jnp.float32)
    row_index = iota(with_all.shape, 0)
    for j in range(8):
        listed = row_index == listed_ref[j : j + 1, :]
        held_ref[j : j + 1, :] = jnp.sum(jnp.where(listed, with_all, 0.0), axis=0, keepdims=True)
        held_ref[8 + j : 9 + j, :] = jnp.sum(
            jnp.where(listed, squares, 0.0), axis=0, keepdims=True
        )
    columns_to_lanes(squares, held_ref.at[16:24])
    count = with_positives.shape[0]
    sent = [with_positives.astype(jnp.bfloat16)]
    for start in (0, 8, 16):
        sent.append(halves(held_ref[start : start + 8, :]).astype(jnp.bfloat16))
    for t in range(out_ref.shape[0]):
        out_ref[t, :count, :] = sent[0]
        for k in range(3):
            out_ref[t, count + 16 * k : count + 16 * (k + 1), :] = sent[k + 1]


def softmax_kernel(arrived_ref, positive_hot_ref, out_ref, inverse_ref):
    count = positive_hot_ref.shape[0]
    summed = arrived_ref[0].astype(jnp.float32)
    for t in range(1, arrived_ref.shape[0]):
        summed = summed + arrived_ref[t].astype(jnp.float32)

    def small(k):
        block = summed[count + 16 * k : count + 16 * (k + 1)]
        return block[:8] + block[8:]

    inverse_listed = lax.rsqrt(small(1) + EPSILON * EPSILON)
    inverse = lax.rsqrt(small(2) + EPSILON * EPSILON)
    inverse_ref[...] = inverse
    inverse_query = inverse_listed[7:8, :]
    picked = jnp.zeros((count, LANES), jnp.float32)
    for k in range(8):
        hot = positive_hot_ref[:, LANES * k : LANES * (k + 1)].astype(jnp.float32)
        picked = picked + hot * inverse[k : k + 1, :]
    inverse_positive = jnp.sum(picked, axis=1, keepdims=True)
    logits = summed[:count] * inverse_positive * inverse_query / SOFTMAX_TEMPER
    hard = small(0) * inverse_listed * inverse_query / SOFTMAX_TEMPER
    is_hard = iota(hard.shape, 0) < 7
    is_own = iota(logits.shape, 0) == iota(logits.shape, 1) + lax.axis_index("core") * LANES
    weights = jnp.exp(logits - 1.0 / SOFTMAX_TEMPER)
    hard_weights = jnp.where(is_hard, jnp.exp(hard - 1.0 / SOFTMAX_TEMPER), 0.0)
    totals = jnp.sum(weights, axis=0, keepdims=True) + jnp.sum(hard_weights, axis=0, keepdims=True)
    target = jnp.sum(jnp.where(is_own, logits, 0.0), axis=0, keepdims=True)
    losses = jnp.log(totals) + 1.0 / SOFTMAX_TEMPER - target
    scaling_factor = LOSS_MULTIPLIER / (count * SOFTMAX_TEMPER)

    def rounded(value):
        return value.astype(jnp.bfloat16).astype(jnp.float32)

    coef = rounded(scaling_factor * (weights / totals - is_own.astype(jnp.float32)))
    hard_coef = rounded(scaling_factor * (hard_weights / totals))
    weighted = coef * logits * SOFTMAX_TEMPER
    hard_weighted = jnp.where(is_hard, hard_coef * hard * SOFTMAX_TEMPER, 0.0)
    along_query = jnp.sum(weighted, axis=0, keepdims=True) + jnp.sum(
        hard_weighted, axis=0, keepdims=True
    )
    out_ref[:count, :] = coef
    out_ref[count : count + 8, :] = jnp.where(is_hard, hard_coef, along_query)
    out_ref[count + 8 : count + 16, :] = jnp.where(is_hard, hard_weighted, losses)
    out_ref[count + 16 :, :] = jnp.zeros_like(out_ref[count + 16 :, :])
    columns_to_lanes(jnp.sum(weighted, axis=1, keepdims=True), out_ref.at[count + 16 :])


def resid_grad_kernel(
    both_ref,
    inverse_ref,
    rows_ref,
    positive_hot_ref,
    query_hot_ref,
    listed_ref,
    resid_ref,
    gain_ref,
    out_ref,
    loss_ref,
):
    sequences = resid_ref.shape[0]
    count, total_rows = positive_hot_ref.shape
    group = lax.axis_index("z") * lax.axis_size("core") + lax.axis_index("core")
    first_row = group * sequences
    first_query = group * QDEV
    across = (((1,), (1,)), ((), ()))

    def joined(start, stop):
        return jnp.concatenate([both_ref[0, start:stop, :], both_ref[1, start:stop, :]], axis=1)

    coef = joined(0, count)
    coef16 = coef.astype(jnp.bfloat16)
    hard = joined(count, count + 8)
    hard_weighted = joined(count + 8, count + 16)
    along_passage = both_ref[0, count + 16 : count + 24, :] + both_ref[1, count + 16 : count + 24, :]
    along_passage = jnp.concatenate([along_passage[0:1], along_passage[1:2]], axis=1)
    inverse = jnp.concatenate([inverse_ref[k : k + 1, :] for k in range(8)], axis=1)

    own_row = first_row + iota((sequences, count), 0)
    own_query = (iota((sequences, count), 0) < QDEV) & (
        iota((sequences, count), 1) == first_query + iota((sequences, count), 0)
    )
    own_positive = listed_ref[8:9, :] == own_row
    to_positives = lax.dot_general(
        own_query.astype(jnp.bfloat16), coef16, across, preferred_element_type=jnp.float32
    )
    to_queries = jnp.dot(
        own_positive.astype(jnp.bfloat16), coef16, preferred_element_type=jnp.float32
    )
    along = jnp.sum(
        jnp.where(own_query, hard[7:8, :], 0.0) + jnp.where(own_positive, along_passage, 0.0),
        axis=1,
        keepdims=True,
    )
    for j in range(7):
        listed = listed_ref[j : j + 1, :] == own_row
        to_queries = to_queries + jnp.where(listed, hard[j : j + 1, :], 0.0)
        along = along + jnp.sum(
            jnp.where(listed, hard_weighted[j : j + 1, :], 0.0), axis=1, keepdims=True
        )
    matrix = jnp.dot(
        to_positives.astype(jnp.bfloat16), positive_hot_ref[...], preferred_element_type=jnp.float32
    ) + jnp.dot(
        to_queries.astype(jnp.bfloat16), query_hot_ref[...], preferred_element_type=jnp.float32
    )
    row_index = iota((sequences, total_rows), 1)
    for j in range(7):
        own_hard = jnp.sum(jnp.where(own_query, hard[j : j + 1, :], 0.0), axis=1, keepdims=True)
        own_listed = jnp.where(own_query, listed_ref[j : j + 1, :].astype(jnp.float32), 0.0)
        own_listed = jnp.sum(own_listed, axis=1, keepdims=True).astype(jnp.int32)
        listed = row_index == own_listed
        matrix = matrix + jnp.where(listed, own_hard, 0.0)
    matrix = matrix * inverse
    high = matrix.astype(jnp.bfloat16)
    low = (matrix - high.astype(jnp.float32)).astype(jnp.bfloat16)
    rows = rows_ref[...]
    d_embed = jnp.dot(high, rows, preferred_element_type=jnp.float32) + jnp.dot(
        low, rows, preferred_element_type=jnp.float32
    )

    is_own_row = row_index == first_row + iota((sequences, total_rows), 0)
    own_inverse = jnp.sum(jnp.where(is_own_row, inverse, 0.0), axis=1, keepdims=True)
    resid = resid_ref[...]
    gain = gain_ref[...]
    features = gain.shape[1] * out_ref.shape[0]
    d_resid = own_inverse * gain * (
        d_embed - resid * gain * own_inverse * along
    ) - resid * (along * own_inverse * own_inverse * (EPSILON / features))
    d_resid16 = d_resid.astype(jnp.bfloat16)
    for t in range(out_ref.shape[0]):
        out_ref[t] = d_resid16
    loss_ref[0] = jnp.sum(hard_weighted[7:8, :]) / count


def kernel_call(body, outs, arrays, near=(), near_outs=(), late=(), after=(), scratch=()):
    count = len(arrays)
    far = [i for i in range(count) if i not in near]
    scalar_outs = [i for i in range(len(outs)) if outs[i][0] == (1,)]
    far_outs = [i for i in range(len(outs)) if i not in near_outs and i not in scalar_outs]

    def spec(is_far):
        return pl.BlockSpec(memory_space=pltpu.HBM if is_far else pltpu.VMEM)

    def kernel(*refs):
        given = list(refs[:count])
        start = count + len(after)
        results = list(refs[start : start + len(outs)])
        start += len(outs)
        held_in = refs[start : start + len(far)]
        start += len(far)
        held_out = refs[start : start + len(far_outs)]
        start += len(far_outs)
        semaphores = refs[start]
        copies = {}
        for k, i in enumerate(far):
            copies[i] = pltpu.make_async_copy(given[i], held_in[k], semaphores.at[k])
            copies[i].start()
            given[i] = held_in[k]
        for i in far:
            if i not in late:
                copies[i].wait()

        def ready():
            for i in late:
                copies[i].wait()

        targets = [results[i] for i in far_outs]
        for k, i in enumerate(far_outs):
            results[i] = held_out[k]
        extra = (ready,) if late else ()
        body(*extra, *given, *results, *refs[start + 1 :])
        copies_out = [
            pltpu.make_async_copy(held_out[k], targets[k], semaphores.at[len(far) + k])
            for k in range(len(far_outs))
        ]
        for copy in copies_out:
            copy.start()
        for copy in copies_out:
            copy.wait()

    held = [pltpu.VMEM(arrays[i].shape, arrays[i].dtype) for i in far]
    held += [pltpu.VMEM(*outs[i]) for i in far_outs]
    held.append(pltpu.SemaphoreType.DMA((max(1, len(far) + len(far_outs)),)))
    return pl.pallas_call(
        kernel,
        out_shape=[jax.ShapeDtypeStruct(shape, dtype) for shape, dtype in outs],
        in_specs=[spec(i in far) for i in range(count)] + [pl.BlockSpec(memory_space=pl.ANY)] * len(after),
        out_specs=[
            pl.BlockSpec(memory_space=pltpu.SMEM) if i in scalar_outs else spec(i in far_outs)
            for i in range(len(outs))
        ],
        scratch_shapes=held + list(scratch),
        compiler_params=pltpu.CompilerParams(vmem_limit_bytes=VMEM_BYTES),
    )(*arrays, *after)


def candidate_kernel(positives_ref, negatives_ref, listed_ref, query_hot_ref, positive_hot_ref):
    query_count, total_rows = query_hot_ref.shape
    groups = query_count // QDEV
    sequences = total_rows // groups
    others = sequences - QDEV

    def row_of(passage):
        at = ((passage.astype(jnp.float32) + 0.5) * (1.0 / others)).astype(jnp.int32)
        return passage + at * QDEV + QDEV

    def query_row(query):
        return query + query // QDEV * others

    positive_row = row_of(positives_ref[...])
    count = negatives_ref.shape[0]
    listed_ref[:count, :] = row_of(negatives_ref[...])
    listed_ref[count : count + 1, :] = query_row(iota((1, query_count), 1))
    listed_ref[count + 1 :, :] = jnp.broadcast_to(
        positive_row, (listed_ref.shape[0] - count - 1, query_count)
    )
    shape = (LANES, total_rows)
    diagonal = iota((LANES, LANES), 0) == iota((LANES, LANES), 1)
    for k in range(query_count // LANES):
        rows = slice(LANES * k, LANES * (k + 1))
        query = query_row(iota(shape, 0) + LANES * k)
        query_hot_ref[rows, :] = (query == iota(shape, 1)).astype(jnp.float32).astype(jnp.bfloat16)
        lanes = positive_row[:, rows].astype(jnp.float32)
        column = jnp.sum(jnp.where(diagonal, lanes, 0.0), axis=1, keepdims=True)
        positive_hot_ref[rows, :] = (
            (column.astype(jnp.int32) == iota(shape, 1)).astype(jnp.float32).astype(jnp.bfloat16)
        )


def transpose_kernel(*refs):
    half = len(refs) // 2
    for given_ref, out_ref in zip(refs[:half], refs[half:]):
        given = given_ref[...]
        out_ref[...] = given.T
    if len(refs) > 2 * half:
        refs[-1][0] = jnp.float32(0.0)


def token_kernel(out_ref):
    out_ref[0] = jnp.float32(0.0)


def contrast(everyone, resid, gain, tables, after):
    tensor_count = lax.axis_size("tensor")
    sequences, width = resid.shape
    listed, query_hot, positive_hot = tables
    count, total_rows = positive_hot.shape
    sent, rows = kernel_call(
        partial_logits_kernel,
        [((tensor_count, count + 48, LANES), jnp.bfloat16), ((total_rows, width), jnp.bfloat16)],
        [everyone.reshape(total_rows, width), query_hot, positive_hot, listed, gain],
        near=(0,),
        near_outs=(0,),
        after=after,
        scratch=[pltpu.VMEM((24, LANES), jnp.float32)],
    )
    arrived = exchange(sent, "tensor")
    coefs, inverse = kernel_call(
        softmax_kernel,
        [((count + 24, LANES), jnp.float32), ((8, LANES), jnp.float32)],
        [arrived, positive_hot],
        near=(0,),
        near_outs=(0,),
    )
    both = lax.all_gather(coefs, "core", axis=0)
    d_resid16, loss = kernel_call(
        resid_grad_kernel,
        [((tensor_count, sequences, width), jnp.bfloat16), ((1,), jnp.float32)],
        [both, inverse, rows, positive_hot, query_hot, listed, resid, gain],
        near=(0,),
        near_outs=(0,),
    )
    return loss, exchange(d_resid16, "tensor")


def copied_norm_kernel(hidden_ref, gain_ref, out_ref):
    hidden32 = hidden_ref[...].astype(jnp.float32)
    normed = (hidden32 * rms_scale(hidden32) * gain_ref[...]).astype(jnp.bfloat16)
    height = normed.shape[0]
    for c in range(normed.shape[1] // LANES):
        block = normed[:, LANES * c : LANES * (c + 1)]
        for t in range(out_ref.shape[0]):
            out_ref[t, height * c : height * (c + 1), :] = block


def projection_kernel(rows_ref, kv_weights_ref, query_weights_ref, kv_ref, query_ref):
    tensor_count, tall, _ = rows_ref.shape
    blocks = kv_weights_ref.shape[0] // LANES
    height = tall // blocks

    def block(c):
        part = rows_ref[:, height * c : height * (c + 1), :]
        return part.reshape(tensor_count * height, LANES)

    kv = jnp.zeros(kv_ref.shape, jnp.float32)
    query = jnp.zeros(query_ref.shape, jnp.float32)
    for c in range(0, blocks, 2):
        rows = jnp.concatenate([block(c), block(c + 1)], axis=1)
        columns = slice(LANES * c, LANES * (c + 2))
        kv = kv + jnp.dot(rows, kv_weights_ref[columns, :], preferred_element_type=jnp.float32)
        query = query + jnp.dot(
            rows, query_weights_ref[columns, :], preferred_element_type=jnp.float32
        )
    kv_ref[...] = kv
    query_ref[...] = query


def half_turned(tensor, cosine, signed_sine):
    halfway = tensor.shape[1] // 2
    return tensor * cosine + pltpu.roll(tensor, halfway, 1) * signed_sine


def is_even_tensor():
    return lax.axis_index("tensor") % 2 == 0


def attention_kernel(
    own_ref,
    other_ref,
    query_all_ref,
    layout_ref,
    q_gain_ref,
    k_gain_ref,
    hidden_ref,
    wo_ref,
    out_ref,
    saved_ref,
):
    root = math.sqrt(own_ref.shape[1])
    tokens_count, sequences, own_rows = own_ref.shape[0], out_ref.shape[1], hidden_ref.shape[0]
    at, _ = layout_rows(tokens_count, sequences, own_rows)
    to, _ = saved_rows(tokens_count, sequences)
    is_even = is_even_tensor()
    own, other = own_ref[...], other_ref[...]
    key_raw = jnp.where(is_even, own, other)
    value16 = jnp.where(is_even, other, own).astype(jnp.bfloat16)
    query_raw = jnp.dot(
        unfolded(layout_ref[at["chosen"], :], sequences),
        query_all_ref[...],
        precision=lax.Precision.HIGHEST,
        preferred_element_type=jnp.float32,
    )
    q_gain, k_gain = q_gain_ref[...], k_gain_ref[...]
    key16 = half_turned(
        key_raw * rms_scale(key_raw) * k_gain,
        layout_ref[at["key_cosine"], :],
        layout_ref[at["key_sine"], :],
    ).astype(jnp.bfloat16)
    query16 = half_turned(
        query_raw * rms_scale(query_raw) * q_gain,
        layout_ref[at["query_cosine"], :],
        layout_ref[at["query_sine"], :],
    ).astype(jnp.bfloat16)
    shift = (
        root
        * jnp.max(q_gain, axis=1, keepdims=True)
        * jnp.max(k_gain, axis=1, keepdims=True)
    )
    scores = (
        lax.dot_general(
            query16, key16, (((1,), (1,)), ((), ())), preferred_element_type=jnp.float32
        )
        / root
    )
    inside = unfolded(layout_ref[at["inside"], :], sequences)
    weights = jnp.where(inside > 0.0, jnp.exp(scores - shift), 0.0)
    probs = weights / jnp.sum(weights, axis=1, keepdims=True)
    attn16 = jnp.dot(
        probs.astype(jnp.bfloat16), value16, preferred_element_type=jnp.float32
    ).astype(jnp.bfloat16)
    own_last = layout_ref[at["own_last"], :][:, :own_rows].astype(jnp.bfloat16)
    chunk = out_ref.shape[2]
    for t in range(out_ref.shape[0]):
        columns = slice(t * chunk, (t + 1) * chunk)
        block = jnp.dot(attn16, wo_ref[:, columns], preferred_element_type=jnp.float32)
        block = block + jnp.dot(
            own_last, hidden_ref[:, columns], preferred_element_type=jnp.float32
        )
        out_ref[t] = block.astype(jnp.bfloat16)
    saved_ref[to["key_raw"], :] = key_raw
    saved_ref[to["key"], :] = key16.astype(jnp.float32)
    saved_ref[to["value"], :] = value16.astype(jnp.float32)
    saved_ref[to["query_raw"], :] = query_raw
    saved_ref[to["query"], :] = query16.astype(jnp.float32)
    saved_ref[to["probs"], :] = folded(probs)


def resid_kernel(arrived_ref, gains_ref, resid_ref, out_ref, gain_ref):
    chunk = resid_ref.shape[1]
    start = pl.multiple_of(lax.axis_index("tensor") * chunk, chunk)
    gain = gains_ref[:, pl.ds(start, chunk)]
    gain_ref[...] = gain
    resid = arrived_ref[0].astype(jnp.float32)
    for t in range(1, arrived_ref.shape[0]):
        resid = resid + arrived_ref[t].astype(jnp.float32)
    resid_ref[...] = resid
    scaled16 = (resid * gain).astype(jnp.bfloat16)
    for t in range(out_ref.shape[0]):
        out_ref[t] = scaled16


def gradient_kernel(
    d_resid_ref,
    wo_t_ref,
    saved_ref,
    layout_ref,
    q_gain_ref,
    k_gain_ref,
    own_weights_ref,
    other_weights_ref,
    query_weights_ref,
    out_ref,
    added_ref,
):
    head_width = saved_ref.shape[1]
    root = math.sqrt(head_width)
    sequences = d_resid_ref.shape[1]
    own_rows = added_ref.shape[0]
    tokens_count = own_rows * out_ref.shape[0]
    at, _ = layout_rows(tokens_count, sequences, own_rows)
    to, _ = saved_rows(tokens_count, sequences)
    is_even = is_even_tensor()
    chunk = d_resid_ref.shape[2]
    d_attn = jnp.dot(d_resid_ref[0], wo_t_ref[:chunk, :], preferred_element_type=jnp.float32)
    for t in range(1, d_resid_ref.shape[0]):
        d_attn = d_attn + jnp.dot(
            d_resid_ref[t],
            wo_t_ref[t * chunk : (t + 1) * chunk, :],
            preferred_element_type=jnp.float32,
        )
    d_attn16 = d_attn.astype(jnp.bfloat16)
    probs = unfolded(saved_ref[to["probs"], :], sequences)
    key16 = saved_ref[to["key"], :].astype(jnp.bfloat16)
    query16 = saved_ref[to["query"], :].astype(jnp.bfloat16)
    value16 = saved_ref[to["value"], :].astype(jnp.bfloat16)
    d_probs = lax.dot_general(
        d_attn16, value16, (((1,), (1,)), ((), ())), preferred_element_type=jnp.float32
    )
    d_scores16 = (
        probs * (d_probs - jnp.sum(probs * d_probs, axis=1, keepdims=True)) / root
    ).astype(jnp.bfloat16)
    down = (((0,), (0,)), ((), ()))
    d_query_rot = jnp.dot(d_scores16, key16, preferred_element_type=jnp.float32)
    d_key_rot = lax.dot_general(d_scores16, query16, down, preferred_element_type=jnp.float32)
    d_value = lax.dot_general(
        probs.astype(jnp.bfloat16), d_attn16, down, preferred_element_type=jnp.float32
    )

    def head_gradient(grad_rot, name, gain):
        raw = saved_ref[to[name + "_raw"], :]
        inverse = rms_scale(raw)
        turned_back = half_turned(
            grad_rot, layout_ref[at[name + "_cosine"], :], -layout_ref[at[name + "_sine"], :]
        )
        return norm_backward(turned_back, raw * inverse, inverse, gain)

    d_key = head_gradient(d_key_rot, "key", k_gain_ref[...])
    d_query = head_gradient(d_query_rot, "query", q_gain_ref[...])
    own16 = jnp.where(is_even, d_key, d_value).astype(jnp.bfloat16)
    other16 = jnp.where(is_even, d_value, d_key).astype(jnp.bfloat16)
    spread16 = lax.dot_general(
        unfolded(layout_ref[at["chosen"], :], sequences).astype(jnp.bfloat16),
        d_query.astype(jnp.bfloat16),
        down,
        preferred_element_type=jnp.float32,
    ).astype(jnp.bfloat16)
    last = layout_ref[at["own_last_t"], :][:, :sequences].astype(jnp.bfloat16)
    height = out_ref.shape[1] * LANES // added_ref.shape[1]
    for t in range(added_ref.shape[1] // chunk):
        columns = slice(t * chunk, (t + 1) * chunk)
        added_ref[:, columns] = jnp.dot(last, d_resid_ref[t], preferred_element_type=jnp.float32)
        term = jnp.dot(own16, own_weights_ref[:, columns], preferred_element_type=jnp.float32)
        term = term + jnp.dot(
            other16, other_weights_ref[:, columns], preferred_element_type=jnp.float32
        )
        term = term + jnp.dot(
            spread16, query_weights_ref[:, columns], preferred_element_type=jnp.float32
        )
        term16 = term.astype(jnp.bfloat16)
        for k in range(chunk // LANES):
            c = t * (chunk // LANES) + k
            block = term16[:, LANES * k : LANES * (k + 1)]
            out_ref[:, height * c : height * (c + 1), :] = block.reshape(-1, height, LANES)


def d_hidden_kernel(terms_ref, hidden_ref, gain_ref, added_ref, out_ref):
    d_normed = terms_ref[0].astype(jnp.float32)
    for t in range(1, terms_ref.shape[0]):
        d_normed = d_normed + terms_ref[t].astype(jnp.float32)
    hidden32 = hidden_ref[...].astype(jnp.float32)
    height = hidden32.shape[0]
    d_normed = jnp.concatenate(
        [d_normed[height * c : height * (c + 1)] for c in range(hidden32.shape[1] // LANES)],
        axis=1,
    )
    inverse = rms_scale(hidden32)
    d_hidden = norm_backward(d_normed, hidden32 * inverse, inverse, gain_ref[...])
    out_ref[...] = (d_hidden + added_ref[...]).astype(jnp.bfloat16)


def packed_rows(sizes):
    starts, total = {}, 0
    for name, rows in sizes:
        starts[name] = slice(total, total + rows)
        total += rows
    return starts, total


def layout_rows(tokens_count, sequences, own_rows):
    wide = sequences * tokens_count // LANES
    return packed_rows(
        [
            ("key_cosine", tokens_count),
            ("key_sine", tokens_count),
            ("query_cosine", sequences),
            ("query_sine", sequences),
            ("inside", wide),
            ("chosen", wide),
            ("own_last", sequences),
            ("own_last_t", own_rows),
        ]
    )


def saved_rows(tokens_count, sequences):
    return packed_rows(
        [
            ("key_raw", tokens_count),
            ("key", tokens_count),
            ("value", tokens_count),
            ("query_raw", sequences),
            ("query", sequences),
            ("probs", sequences * tokens_count // LANES),
        ]
    )


def folded(block):
    parts = [block[:, LANES * k : LANES * (k + 1)] for k in range(block.shape[1] // LANES)]
    return jnp.concatenate(parts, axis=0)


def unfolded(block, rows):
    parts = [block[rows * k : rows * (k + 1)] for k in range(block.shape[0] // rows)]
    return jnp.concatenate(parts, axis=1)


def sequence_kernel(lengths_ref, out_ref, *, tokens_count, own_rows):
    sequences = lengths_ref.shape[1]
    at, _ = layout_rows(tokens_count, sequences, own_rows)
    lengths = lengths_ref[...].astype(jnp.float32)
    square = (sequences, sequences)
    ends = jnp.sum(
        jnp.where(iota(square, 1) <= iota(square, 0), lengths, 0.0), axis=1, keepdims=True
    )
    own_length = jnp.sum(
        jnp.where(iota(square, 1) == iota(square, 0), lengths, 0.0), axis=1, keepdims=True
    )
    starts = ends - own_length
    ends_row = jnp.sum(
        jnp.where(iota(square, 0) <= iota(square, 1), own_length, 0.0), axis=0, keepdims=True
    )
    starts_row = ends_row - lengths
    token = iota((sequences, tokens_count), 1).astype(jnp.float32)
    out_ref[at["inside"], :] = folded(((token >= starts) & (token < ends)).astype(jnp.float32))
    out_ref[at["chosen"], :] = folded((token == ends - 1.0).astype(jnp.float32))
    first = (lax.axis_index("tensor") * own_rows).astype(jnp.float32)
    own_token = iota((sequences, LANES), 1).astype(jnp.float32) + first
    own_token = jnp.where(iota((sequences, LANES), 1) < own_rows, own_token, -1.0)
    out_ref[at["own_last"], :] = (own_token == ends - 1.0).astype(jnp.float32)
    own_token = iota((own_rows, sequences), 0).astype(jnp.float32) + first
    own_last_t = (own_token == ends_row - 1.0).astype(jnp.float32)
    out_ref[at["own_last_t"], :] = jnp.concatenate(
        [own_last_t, jnp.zeros((own_rows, LANES - sequences), jnp.float32)], axis=1
    )
    token = iota((tokens_count, sequences), 0).astype(jnp.float32)
    held = (token >= starts_row) & (token < ends_row)
    position = jnp.sum(jnp.where(held, token - starts_row, 0.0), axis=1, keepdims=True)
    lane = iota((1, LANES), 1)
    halfway = LANES // 2
    pair = jnp.where(lane < halfway, lane, lane - halfway).astype(jnp.float32)
    frequency = jnp.exp(pair * (-2.0 / LANES * math.log(ROPE_BASE)))
    sign = jnp.where(lane < halfway, -1.0, 1.0)
    for name, place in (("key", position), ("query", own_length - 1.0)):
        angles = place * frequency
        out_ref[at[name + "_cosine"], :] = jnp.cos(angles)
        out_ref[at[name + "_sine"], :] = jnp.sin(angles) * sign


def on_device(
    hidden, lengths, positives, negatives, in_gain, wq, wkv, q_gain, k_gain, wo, out_gain
):
    tensor_count, z_count = lax.axis_size("tensor"), lax.axis_size("z")
    own_rows, features = hidden.shape
    tokens_count = own_rows * tensor_count
    head_width = wq.shape[1]
    sequences = lengths.shape[1]
    query_count = positives.shape[0]
    total_rows = query_count // QDEV * sequences
    chunk = features // tensor_count
    f32, bf16 = jnp.float32, jnp.bfloat16
    head = (tokens_count, head_width)
    weights_shape = (head_width, features)
    flat = (tensor_count, own_rows * features // LANES, LANES)
    gain_rows = [q_gain[None, :], k_gain[None, :]]

    (copies,) = kernel_call(
        copied_norm_kernel, [(flat, bf16)], [hidden, in_gain[None, :]], near_outs=(0,)
    )
    piece = exchange(copies, "tensor")
    kv_own, query_all = kernel_call(
        projection_kernel,
        [(head, f32), (head, f32)],
        [piece, wkv, wq],
        near=(0,),
        near_outs=(0,),
    )
    kv_other = swapped(kv_own, "tensor", 0)
    (layout,) = kernel_call(
        functools.partial(sequence_kernel, tokens_count=tokens_count, own_rows=own_rows),
        [((layout_rows(tokens_count, sequences, own_rows)[1], LANES), f32)],
        [lengths],
        after=[query_all],
    )
    blocks, saved = kernel_call(
        attention_kernel,
        [
            ((tensor_count, sequences, chunk), bf16),
            ((saved_rows(tokens_count, sequences)[1], LANES), f32),
        ],
        [kv_own, kv_other, query_all, layout, *gain_rows, hidden, wo],
        near=(0, 1),
        near_outs=(0,),
    )
    (own_weights,) = kernel_call(
        transpose_kernel, [(weights_shape, bf16)], [wkv], after=[saved]
    )
    other_weights = swapped(own_weights, "tensor", 0)
    resid, scaled, own_gain = kernel_call(
        resid_kernel,
        [((sequences, chunk), f32), ((z_count, sequences, chunk), bf16), ((1, chunk), f32)],
        [exchange(blocks, "tensor"), out_gain[None, :]],
        near=(0,),
        near_outs=(1,),
    )
    query_weights, wo_t, transposed = kernel_call(
        transpose_kernel,
        [(weights_shape, bf16), ((features, head_width), bf16), ((1,), f32)],
        [wq, wo],
        after=[resid],
    )
    (fetched,) = kernel_call(token_kernel, [((1,), f32)], [], after=[other_weights])
    tables = kernel_call(
        candidate_kernel,
        [
            ((16, query_count), jnp.int32),
            ((query_count, total_rows), bf16),
            ((query_count, total_rows), bf16),
        ],
        [positives[None, :], negatives.T],
        after=[resid],
    )
    everyone = lax.all_gather(exchange(scaled, "z"), "core", axis=1)
    loss, d_resid16 = contrast(
        everyone, resid, own_gain, tables, [transposed, fetched]
    )
    product, added = kernel_call(
        gradient_kernel,
        [(flat, bf16), ((own_rows, features), f32)],
        [
            d_resid16,
            wo_t,
            saved,
            layout,
            *gain_rows,
            own_weights,
            other_weights,
            query_weights,
        ],
        near=(0,),
        near_outs=(0,),
    )
    terms = exchange(product, "tensor")
    (d_hidden,) = kernel_call(
        d_hidden_kernel,
        [((own_rows, features), bf16)],
        [terms, hidden, in_gain[None, :], added],
        near=(0,),
    )
    return (d_hidden, loss[0])


def solution(mesh):
    z_count = mesh.shape["dp"] // 2
    chips = mesh.devices.reshape(z_count, 2, mesh.shape["tensor"])
    mesh = jax.sharding.Mesh(chips, ("z", "core", "tensor"))
    everywhere = P(("z", "core", "tensor"), None)
    placed = (
        everywhere,
        P(("z", "core"), None),
        P(),
        P(),
        P(),
        P(None, "tensor"),
        P(None, "tensor"),
        P(),
        P(),
        P("tensor", None),
        P(),
    )
    return jax.shard_map(
        on_device, mesh=mesh, in_specs=placed, out_specs=(everywhere, P()), check_vma=False
    )
```

```python
import functools
import math

import jax
import jax.numpy as jnp
from jax import lax
from jax.experimental import pallas as pl
from jax.experimental.pallas import tpu as pltpu
from jax.sharding import PartitionSpec as P

QDEV = 8
LANES = 128
VMEM_BYTES = 32 * 2**20


EPSILON = 1e-06
SOFTMAX_TEMPER = 0.05
LOSS_MULTIPLIER = 8192.0
ROPE_BASE = 1000000.0


def swapped(value, axis, apart):
    mask = 2**apart
    pairs = [(source, source ^ mask) for source in range(lax.axis_size(axis))]
    return lax.ppermute(value, axis, pairs)


def rms_scale(tensor):
    return lax.rsqrt(jnp.mean(tensor * tensor, axis=-1, keepdims=True) + EPSILON)


def norm_backward(grad, unit_form, inverse, gain):
    scaled = grad * gain
    return inverse * (scaled - unit_form * jnp.mean(unit_form * scaled, axis=-1, keepdims=True))


def exchange(blocks, axis):
    return lax.all_to_all(blocks, axis, 0, 0, tiled=True)


def halves(value):
    high = value.astype(jnp.bfloat16).astype(jnp.float32)
    return high, value - high


def iota(shape, axis):
    return lax.broadcasted_iota(jnp.int32, shape, axis)


def columns_to_lanes(column, out_ref):
    diagonal = iota((LANES, LANES), 0) == iota((LANES, LANES), 1)
    for k in range(column.shape[0] // LANES):
        block = jnp.where(diagonal, column[LANES * k : LANES * (k + 1)], 0.0)
        out_ref[k : k + 1, :] = jnp.sum(block, axis=0, keepdims=True)


HALF = LANES // 2


def query_block():
    return lax.axis_index("z_pair"), lax.axis_index("core")


def block_lanes(block):
    return pl.ds(pl.multiple_of(block * LANES, LANES), LANES)


def in_first_half(shape):
    return iota(shape, len(shape) - 1) < HALF


def fold_half(first, second, half):
    is_first = in_first_half(first.shape)
    low = jnp.where(is_first, first, pltpu.roll(second, HALF, 1))
    high = jnp.where(is_first, pltpu.roll(first, HALF, 1), second)
    return jnp.where(half == 0, low, high)


def unfold_half(block):
    return block, pltpu.roll(block, HALF, 1)


def own_columns(gains_ref, width):
    start = pl.multiple_of(lax.axis_index("tensor") * width, width)
    return gains_ref[:, pl.ds(start, width)]


def partial_logits_kernel(
    rows_ref, query_hot_ref, positive_hot_ref, listed_all_ref, gains_ref, out_ref, rows_out_ref, held_ref
):
    rows = rows_ref[...]
    rows_out_ref[...] = rows
    query_at, half = query_block()
    listed_ref = listed_all_ref[:8, block_lanes(query_at)]
    block_hot = query_hot_ref[block_lanes(query_at), :]
    queries = jnp.dot(block_hot, rows, preferred_element_type=jnp.float32)
    positives = jnp.dot(positive_hot_ref[...], rows, preferred_element_type=jnp.float32)
    queries = queries.astype(jnp.bfloat16)
    features = gains_ref.shape[1]
    rows32 = rows.astype(jnp.float32)
    plain = rows32 / own_columns(gains_ref, rows.shape[1])
    squares = jnp.sum(rows32 * rows32, axis=1, keepdims=True) + jnp.sum(
        plain * plain, axis=1, keepdims=True
    ) * (EPSILON / features)
    against = (((1,), (1,)), ((), ()))
    with_positives = lax.dot_general(
        positives.astype(jnp.bfloat16), queries, against, preferred_element_type=jnp.float32
    )
    with_all = lax.dot_general(rows, queries, against, preferred_element_type=jnp.float32)
    row_index = iota(with_all.shape, 0)
    for j in range(8):
        listed = row_index == listed_ref[j : j + 1, :]
        held_ref[j : j + 1, :] = jnp.sum(jnp.where(listed, with_all, 0.0), axis=0, keepdims=True)
        held_ref[8 + j : 9 + j, :] = jnp.sum(
            jnp.where(listed, squares, 0.0), axis=0, keepdims=True
        )
    columns_to_lanes(squares, held_ref.at[16:24])
    count = with_positives.shape[0] // 2
    sent = fold_half(with_positives[:count], with_positives[count:], half).astype(jnp.bfloat16)
    high, low = halves(held_ref[0:16, :])
    listed16 = fold_half(high, low, half).astype(jnp.bfloat16)
    squares16 = jnp.concatenate(halves(held_ref[16:24, :])).astype(jnp.bfloat16)
    for t in range(out_ref.shape[0]):
        out_ref[t, :count, :] = sent
        out_ref[t, count : count + 16, :] = listed16
        out_ref[t, count + 16 : count + 32, :] = squares16


def softmax_kernel(arrived_ref, positive_hot_ref, out_ref, inverse_ref):
    count = positive_hot_ref.shape[0]
    summed = arrived_ref[0].astype(jnp.float32)
    for t in range(1, arrived_ref.shape[0]):
        summed = summed + arrived_ref[t].astype(jnp.float32)
    query_at, half = query_block()
    first_query = query_at * LANES + half * HALF
    start = count // 2
    with_positives = jnp.concatenate(unfold_half(summed[:start]), axis=0)
    high, low = unfold_half(summed[start : start + 16])
    hard, listed_squares = high[:8] + low[:8], high[8:] + low[8:]
    squares = summed[start + 16 : start + 24] + summed[start + 24 : start + 32]

    def valid(value, other):
        return jnp.where(in_first_half(value.shape), value, other)

    inverse_listed = lax.rsqrt(valid(listed_squares, 1.0) + EPSILON * EPSILON)
    inverse = lax.rsqrt(squares + EPSILON * EPSILON)
    inverse_ref[...] = inverse
    inverse_query = inverse_listed[7:8, :]
    picked = jnp.zeros((count, LANES), jnp.float32)
    for k in range(8):
        hot = positive_hot_ref[:, LANES * k : LANES * (k + 1)].astype(jnp.float32)
        picked = picked + hot * inverse[k : k + 1, :]
    inverse_positive = jnp.sum(picked, axis=1, keepdims=True)
    logits = valid(with_positives, 0.0) * inverse_positive * inverse_query / SOFTMAX_TEMPER
    hard = valid(hard, 0.0) * inverse_listed * inverse_query / SOFTMAX_TEMPER
    is_hard = iota(hard.shape, 0) < 7
    is_own = iota(logits.shape, 0) == iota(logits.shape, 1) + first_query
    is_own = is_own & in_first_half(logits.shape)
    weights = valid(jnp.exp(logits - 1.0 / SOFTMAX_TEMPER), 1.0)
    hard_weights = jnp.where(is_hard, jnp.exp(hard - 1.0 / SOFTMAX_TEMPER), 0.0)
    totals = jnp.sum(weights, axis=0, keepdims=True) + jnp.sum(hard_weights, axis=0, keepdims=True)
    target = jnp.sum(jnp.where(is_own, logits, 0.0), axis=0, keepdims=True)
    losses = jnp.log(totals) + 1.0 / SOFTMAX_TEMPER - target
    scaling_factor = LOSS_MULTIPLIER / (count * SOFTMAX_TEMPER)

    def rounded(value):
        return value.astype(jnp.bfloat16).astype(jnp.float32)

    coef = rounded(scaling_factor * (weights / totals - is_own.astype(jnp.float32)))
    hard_coef = rounded(scaling_factor * (hard_weights / totals))
    weighted = valid(coef * logits * SOFTMAX_TEMPER, 0.0)
    hard_weighted = jnp.where(is_hard, hard_coef * hard * SOFTMAX_TEMPER, 0.0)
    along_query = jnp.sum(weighted, axis=0, keepdims=True) + jnp.sum(
        hard_weighted, axis=0, keepdims=True
    )
    folded_coef = fold_half(coef[:start], coef[start:], 0)
    folded_hard = fold_half(
        jnp.where(is_hard, hard_coef, along_query), jnp.where(is_hard, hard_weighted, losses), 0
    )
    for k in range(out_ref.shape[0]):
        out_ref[k, :start, :] = folded_coef
        out_ref[k, start : start + 8, :] = folded_hard
        out_ref[k, start + 8 :, :] = jnp.zeros_like(out_ref[k, start + 8 :, :])
        columns_to_lanes(
            jnp.sum(weighted, axis=1, keepdims=True), out_ref.at[k, start + 8 : start + 16]
        )


def resid_grad_kernel(
    both_ref,
    inverse_ref,
    rows_ref,
    positive_hot_ref,
    query_hot_ref,
    listed_ref,
    resid_ref,
    gains_ref,
    out_ref,
    loss_ref,
):
    sequences = resid_ref.shape[0]
    count, total_rows = positive_hot_ref.shape
    z = lax.axis_index("z_far") * lax.axis_size("z_pair") + lax.axis_index("z_pair")
    group = z * lax.axis_size("core") + lax.axis_index("core")
    first_row = group * sequences
    first_query = group * QDEV
    across = (((1,), (1,)), ((), ()))

    def joined(start, stop):
        firsts, seconds = [], []
        for k in (0, 2):
            first, second = both_ref[k, start:stop, :], both_ref[k + 1, start:stop, :]
            firsts.append(fold_half(first, second, 0))
            seconds.append(fold_half(pltpu.roll(first, HALF, 1), pltpu.roll(second, HALF, 1), 0))
        return jnp.concatenate(firsts, axis=1), jnp.concatenate(seconds, axis=1)

    start = count // 2
    coef16 = jnp.concatenate(joined(0, start), axis=0).astype(jnp.bfloat16)
    hard, hard_weighted = joined(start, start + 8)
    along_passage = both_ref[0, start + 8 : start + 16, :]
    for k in range(1, both_ref.shape[0]):
        along_passage = along_passage + both_ref[k, start + 8 : start + 16, :]
    along_passage = jnp.concatenate([along_passage[0:1], along_passage[1:2]], axis=1)
    inverse = jnp.concatenate([inverse_ref[k : k + 1, :] for k in range(8)], axis=1)

    own_row = first_row + iota((sequences, count), 0)
    own_query = (iota((sequences, count), 0) < QDEV) & (
        iota((sequences, count), 1) == first_query + iota((sequences, count), 0)
    )
    own_positive = listed_ref[8:9, :] == own_row
    to_positives = lax.dot_general(
        own_query.astype(jnp.bfloat16), coef16, across, preferred_element_type=jnp.float32
    )
    to_queries = jnp.dot(
        own_positive.astype(jnp.bfloat16), coef16, preferred_element_type=jnp.float32
    )
    along = jnp.sum(
        jnp.where(own_query, hard[7:8, :], 0.0) + jnp.where(own_positive, along_passage, 0.0),
        axis=1,
        keepdims=True,
    )
    for j in range(7):
        listed = listed_ref[j : j + 1, :] == own_row
        to_queries = to_queries + jnp.where(listed, hard[j : j + 1, :], 0.0)
        along = along + jnp.sum(
            jnp.where(listed, hard_weighted[j : j + 1, :], 0.0), axis=1, keepdims=True
        )
    matrix = jnp.dot(
        to_positives.astype(jnp.bfloat16), positive_hot_ref[...], preferred_element_type=jnp.float32
    ) + jnp.dot(
        to_queries.astype(jnp.bfloat16), query_hot_ref[...], preferred_element_type=jnp.float32
    )
    row_index = iota((sequences, total_rows), 1)
    for j in range(7):
        own_hard = jnp.sum(jnp.where(own_query, hard[j : j + 1, :], 0.0), axis=1, keepdims=True)
        own_listed = jnp.where(own_query, listed_ref[j : j + 1, :].astype(jnp.float32), 0.0)
        own_listed = jnp.sum(own_listed, axis=1, keepdims=True).astype(jnp.int32)
        listed = row_index == own_listed
        matrix = matrix + jnp.where(listed, own_hard, 0.0)
    matrix = matrix * inverse
    high = matrix.astype(jnp.bfloat16)
    low = (matrix - high.astype(jnp.float32)).astype(jnp.bfloat16)
    rows = rows_ref[...]
    d_embed = jnp.dot(high, rows, preferred_element_type=jnp.float32) + jnp.dot(
        low, rows, preferred_element_type=jnp.float32
    )

    is_own_row = row_index == first_row + iota((sequences, total_rows), 0)
    own_inverse = jnp.sum(jnp.where(is_own_row, inverse, 0.0), axis=1, keepdims=True)
    resid = resid_ref[...]
    gain = own_columns(gains_ref, resid.shape[1])
    features = gains_ref.shape[1]
    d_resid = own_inverse * gain * (
        d_embed - resid * gain * own_inverse * along
    ) - resid * (along * own_inverse * own_inverse * (EPSILON / features))
    d_resid16 = d_resid.astype(jnp.bfloat16)
    for t in range(out_ref.shape[0]):
        out_ref[t] = d_resid16
    loss_ref[0] = jnp.sum(hard_weighted[7:8, :]) / count


def kernel_call(body, outs, arrays, near=(), near_outs=(), late=(), after=(), scratch=()):
    count = len(arrays)
    far = [i for i in range(count) if i not in near]
    scalar_outs = [i for i in range(len(outs)) if outs[i][0] == (1,)]
    far_outs = [i for i in range(len(outs)) if i not in near_outs and i not in scalar_outs]

    def spec(is_far):
        return pl.BlockSpec(memory_space=pltpu.HBM if is_far else pltpu.VMEM)

    def kernel(*refs):
        given = list(refs[:count])
        start = count + len(after)
        results = list(refs[start : start + len(outs)])
        start += len(outs)
        held_in = refs[start : start + len(far)]
        start += len(far)
        held_out = refs[start : start + len(far_outs)]
        start += len(far_outs)
        semaphores = refs[start]
        copies = {}
        for k, i in enumerate(far):
            copies[i] = pltpu.make_async_copy(given[i], held_in[k], semaphores.at[k])
            copies[i].start()
            given[i] = held_in[k]
        for i in far:
            if i not in late:
                copies[i].wait()

        def ready():
            for i in late:
                copies[i].wait()

        targets = [results[i] for i in far_outs]
        for k, i in enumerate(far_outs):
            results[i] = held_out[k]
        extra = (ready,) if late else ()
        body(*extra, *given, *results, *refs[start + 1 :])
        copies_out = [
            pltpu.make_async_copy(held_out[k], targets[k], semaphores.at[len(far) + k])
            for k in range(len(far_outs))
        ]
        for copy in copies_out:
            copy.start()
        for copy in copies_out:
            copy.wait()

    held = [pltpu.VMEM(arrays[i].shape, arrays[i].dtype) for i in far]
    held += [pltpu.VMEM(*outs[i]) for i in far_outs]
    held.append(pltpu.SemaphoreType.DMA((max(1, len(far) + len(far_outs)),)))
    return pl.pallas_call(
        kernel,
        out_shape=[jax.ShapeDtypeStruct(shape, dtype) for shape, dtype in outs],
        in_specs=[spec(i in far) for i in range(count)] + [pl.BlockSpec(memory_space=pl.ANY)] * len(after),
        out_specs=[
            pl.BlockSpec(memory_space=pltpu.SMEM) if i in scalar_outs else spec(i in far_outs)
            for i in range(len(outs))
        ],
        scratch_shapes=held + list(scratch),
        compiler_params=pltpu.CompilerParams(vmem_limit_bytes=VMEM_BYTES),
    )(*arrays, *after)


def candidate_kernel(positives_ref, negatives_ref, listed_ref, query_hot_ref, positive_hot_ref):
    query_count, total_rows = query_hot_ref.shape
    groups = query_count // QDEV
    sequences = total_rows // groups
    others = sequences - QDEV

    def row_of(passage):
        at = ((passage.astype(jnp.float32) + 0.5) * (1.0 / others)).astype(jnp.int32)
        return passage + at * QDEV + QDEV

    def query_row(query):
        return query + query // QDEV * others

    positive_row = row_of(positives_ref[...])
    count = negatives_ref.shape[0]
    listed_ref[:count, :] = row_of(negatives_ref[...])
    listed_ref[count : count + 1, :] = query_row(iota((1, query_count), 1))
    listed_ref[count + 1 :, :] = jnp.broadcast_to(
        positive_row, (listed_ref.shape[0] - count - 1, query_count)
    )
    shape = (LANES, total_rows)
    diagonal = iota((LANES, LANES), 0) == iota((LANES, LANES), 1)
    for k in range(query_count // LANES):
        rows = slice(LANES * k, LANES * (k + 1))
        query = query_row(iota(shape, 0) + LANES * k)
        query_hot_ref[rows, :] = (query == iota(shape, 1)).astype(jnp.float32).astype(jnp.bfloat16)
        lanes = positive_row[:, rows].astype(jnp.float32)
        column = jnp.sum(jnp.where(diagonal, lanes, 0.0), axis=1, keepdims=True)
        positive_hot_ref[rows, :] = (
            (column.astype(jnp.int32) == iota(shape, 1)).astype(jnp.float32).astype(jnp.bfloat16)
        )


def transpose_kernel(*refs):
    half = len(refs) // 2
    for given_ref, out_ref in zip(refs[:half], refs[half:]):
        given = given_ref[...]
        out_ref[...] = given.T
    if len(refs) > 2 * half:
        refs[-1][0] = jnp.float32(0.0)


def stack_kernel(first_ref, second_ref, out_ref, token_ref):
    rows = first_ref.shape[0]
    out_ref[:rows, :] = first_ref[...]
    out_ref[rows:, :] = second_ref[...]
    token_ref[0] = jnp.float32(0.0)


def contrast(everyone, resid, gains, tables, after):
    tensor_count = lax.axis_size("tensor")
    sequences, width = resid.shape
    listed, query_hot, positive_hot = tables
    count, total_rows = positive_hot.shape
    sent, rows = kernel_call(
        partial_logits_kernel,
        [
            ((tensor_count, count // 2 + 32, LANES), jnp.bfloat16),
            ((total_rows, width), jnp.bfloat16),
        ],
        [everyone.reshape(total_rows, width), query_hot, positive_hot, listed, gains],
        near=(0,),
        near_outs=(0,),
        after=after,
        scratch=[pltpu.VMEM((24, LANES), jnp.float32)],
    )
    arrived = exchange(sent, "tensor")
    coefs, inverse = kernel_call(
        softmax_kernel,
        [((4, count // 2 + 16, LANES), jnp.float32), ((8, LANES), jnp.float32)],
        [arrived, positive_hot],
        near=(0,),
        near_outs=(0,),
    )
    both = exchange(coefs, ("z_pair", "core"))
    d_resid16, loss = kernel_call(
        resid_grad_kernel,
        [((tensor_count, sequences, width), jnp.bfloat16), ((1,), jnp.float32)],
        [both, inverse, rows, positive_hot, query_hot, listed, resid, gains],
        near=(0,),
        near_outs=(0,),
    )
    return loss, exchange(d_resid16, "tensor")


def copied_norm_kernel(hidden_ref, gain_ref, out_ref):
    hidden32 = hidden_ref[...].astype(jnp.float32)
    normed = (hidden32 * rms_scale(hidden32) * gain_ref[...]).astype(jnp.bfloat16)
    height = normed.shape[0]
    for c in range(normed.shape[1] // LANES):
        block = normed[:, LANES * c : LANES * (c + 1)]
        for t in range(out_ref.shape[0]):
            out_ref[t, height * c : height * (c + 1), :] = block


def projection_kernel(rows_ref, kv_weights_ref, query_weights_ref, kv_ref, query_ref):
    tensor_count, tall, _ = rows_ref.shape
    blocks = kv_weights_ref.shape[0] // LANES
    height = tall // blocks

    def block(c):
        part = rows_ref[:, height * c : height * (c + 1), :]
        return part.reshape(tensor_count * height, LANES)

    kv = jnp.zeros(kv_ref.shape, jnp.float32)
    query = jnp.zeros(query_ref.shape, jnp.float32)
    for c in range(0, blocks, 2):
        rows = jnp.concatenate([block(c), block(c + 1)], axis=1)
        columns = slice(LANES * c, LANES * (c + 2))
        kv = kv + jnp.dot(rows, kv_weights_ref[columns, :], preferred_element_type=jnp.float32)
        query = query + jnp.dot(
            rows, query_weights_ref[columns, :], preferred_element_type=jnp.float32
        )
    kv_ref[...] = kv
    query_ref[...] = query


def half_turned(tensor, cosine, signed_sine):
    halfway = tensor.shape[1] // 2
    return tensor * cosine + pltpu.roll(tensor, halfway, 1) * signed_sine


def is_even_tensor():
    return lax.axis_index("tensor") % 2 == 0


def attention_kernel(
    own_ref,
    other_ref,
    query_all_ref,
    layout_ref,
    q_gain_ref,
    k_gain_ref,
    hidden_ref,
    wo_ref,
    out_ref,
    saved_ref,
):
    root = math.sqrt(own_ref.shape[1])
    tokens_count, sequences, own_rows = own_ref.shape[0], out_ref.shape[1], hidden_ref.shape[0]
    at, _ = layout_rows(tokens_count, sequences, own_rows)
    to, _ = saved_rows(tokens_count, sequences)
    is_even = is_even_tensor()
    own, other = own_ref[...], other_ref[...]
    key_raw = jnp.where(is_even, own, other)
    value16 = jnp.where(is_even, other, own).astype(jnp.bfloat16)
    query_raw = jnp.dot(
        unfolded(layout_ref[at["chosen"], :], sequences),
        query_all_ref[...],
        precision=lax.Precision.HIGHEST,
        preferred_element_type=jnp.float32,
    )
    q_gain, k_gain = q_gain_ref[...], k_gain_ref[...]
    key16 = half_turned(
        key_raw * rms_scale(key_raw) * k_gain,
        layout_ref[at["key_cosine"], :],
        layout_ref[at["key_sine"], :],
    ).astype(jnp.bfloat16)
    query16 = half_turned(
        query_raw * rms_scale(query_raw) * q_gain,
        layout_ref[at["query_cosine"], :],
        layout_ref[at["query_sine"], :],
    ).astype(jnp.bfloat16)
    shift = (
        root
        * jnp.max(q_gain, axis=1, keepdims=True)
        * jnp.max(k_gain, axis=1, keepdims=True)
    )
    scores = (
        lax.dot_general(
            query16, key16, (((1,), (1,)), ((), ())), preferred_element_type=jnp.float32
        )
        / root
    )
    inside = unfolded(layout_ref[at["inside"], :], sequences)
    weights = jnp.where(inside > 0.0, jnp.exp(scores - shift), 0.0)
    probs = weights / jnp.sum(weights, axis=1, keepdims=True)
    attn16 = jnp.dot(
        probs.astype(jnp.bfloat16), value16, preferred_element_type=jnp.float32
    ).astype(jnp.bfloat16)
    own_last = layout_ref[at["own_last"], :][:, :own_rows].astype(jnp.bfloat16)
    chunk = out_ref.shape[2]
    for t in range(out_ref.shape[0]):
        columns = slice(t * chunk, (t + 1) * chunk)
        block = jnp.dot(attn16, wo_ref[:, columns], preferred_element_type=jnp.float32)
        block = block + jnp.dot(
            own_last, hidden_ref[:, columns], preferred_element_type=jnp.float32
        )
        out_ref[t] = block.astype(jnp.bfloat16)
    saved_ref[to["key_raw"], :] = key_raw
    saved_ref[to["key"], :] = key16.astype(jnp.float32)
    saved_ref[to["value"], :] = value16.astype(jnp.float32)
    saved_ref[to["query_raw"], :] = query_raw
    saved_ref[to["query"], :] = query16.astype(jnp.float32)
    saved_ref[to["probs"], :] = folded(probs)


def resid_kernel(arrived_ref, gains_ref, resid_ref, out_ref):
    gain = own_columns(gains_ref, resid_ref.shape[1])
    resid = arrived_ref[0].astype(jnp.float32)
    for t in range(1, arrived_ref.shape[0]):
        resid = resid + arrived_ref[t].astype(jnp.float32)
    resid_ref[...] = resid
    scaled16 = (resid * gain).astype(jnp.bfloat16)
    for t in range(out_ref.shape[0]):
        out_ref[t] = scaled16


def gradient_kernel(
    d_resid_ref,
    wo_t_ref,
    saved_ref,
    layout_ref,
    q_gain_ref,
    k_gain_ref,
    both_weights_ref,
    query_weights_ref,
    out_ref,
    added_ref,
):
    head_width = saved_ref.shape[1]
    root = math.sqrt(head_width)
    sequences = d_resid_ref.shape[1]
    own_rows = added_ref.shape[0]
    tokens_count = own_rows * out_ref.shape[0]
    at, _ = layout_rows(tokens_count, sequences, own_rows)
    to, _ = saved_rows(tokens_count, sequences)
    is_even = is_even_tensor()
    chunk = d_resid_ref.shape[2]
    d_attn = jnp.dot(d_resid_ref[0], wo_t_ref[:chunk, :], preferred_element_type=jnp.float32)
    for t in range(1, d_resid_ref.shape[0]):
        d_attn = d_attn + jnp.dot(
            d_resid_ref[t],
            wo_t_ref[t * chunk : (t + 1) * chunk, :],
            preferred_element_type=jnp.float32,
        )
    d_attn16 = d_attn.astype(jnp.bfloat16)
    probs = unfolded(saved_ref[to["probs"], :], sequences)
    key16 = saved_ref[to["key"], :].astype(jnp.bfloat16)
    query16 = saved_ref[to["query"], :].astype(jnp.bfloat16)
    value16 = saved_ref[to["value"], :].astype(jnp.bfloat16)
    d_probs = lax.dot_general(
        d_attn16, value16, (((1,), (1,)), ((), ())), preferred_element_type=jnp.float32
    )
    d_scores16 = (
        probs * (d_probs - jnp.sum(probs * d_probs, axis=1, keepdims=True)) / root
    ).astype(jnp.bfloat16)
    down = (((0,), (0,)), ((), ()))
    d_query_rot = jnp.dot(d_scores16, key16, preferred_element_type=jnp.float32)
    d_key_rot = lax.dot_general(d_scores16, query16, down, preferred_element_type=jnp.float32)
    d_value = lax.dot_general(
        probs.astype(jnp.bfloat16), d_attn16, down, preferred_element_type=jnp.float32
    )

    def head_gradient(grad_rot, name, gain):
        raw = saved_ref[to[name + "_raw"], :]
        inverse = rms_scale(raw)
        turned_back = half_turned(
            grad_rot, layout_ref[at[name + "_cosine"], :], -layout_ref[at[name + "_sine"], :]
        )
        return norm_backward(turned_back, raw * inverse, inverse, gain)

    d_key = head_gradient(d_key_rot, "key", k_gain_ref[...])
    d_query = head_gradient(d_query_rot, "query", q_gain_ref[...])
    own_other16 = jnp.concatenate(
        [jnp.where(is_even, d_key, d_value), jnp.where(is_even, d_value, d_key)], axis=1
    ).astype(jnp.bfloat16)
    spread16 = lax.dot_general(
        unfolded(layout_ref[at["chosen"], :], sequences).astype(jnp.bfloat16),
        d_query.astype(jnp.bfloat16),
        down,
        preferred_element_type=jnp.float32,
    ).astype(jnp.bfloat16)
    last = layout_ref[at["own_last_t"], :][:, :sequences].astype(jnp.bfloat16)
    height = out_ref.shape[1] * LANES // added_ref.shape[1]
    for t in range(added_ref.shape[1] // chunk):
        columns = slice(t * chunk, (t + 1) * chunk)
        added_ref[:, columns] = jnp.dot(last, d_resid_ref[t], preferred_element_type=jnp.float32)
        term = jnp.dot(
            own_other16, both_weights_ref[:, columns], preferred_element_type=jnp.float32
        )
        term = term + jnp.dot(
            spread16, query_weights_ref[:, columns], preferred_element_type=jnp.float32
        )
        term16 = term.astype(jnp.bfloat16)
        for k in range(chunk // LANES):
            c = t * (chunk // LANES) + k
            block = term16[:, LANES * k : LANES * (k + 1)]
            out_ref[:, height * c : height * (c + 1), :] = block.reshape(-1, height, LANES)


def d_hidden_kernel(terms_ref, hidden_ref, gain_ref, added_ref, out_ref):
    d_normed = terms_ref[0].astype(jnp.float32)
    for t in range(1, terms_ref.shape[0]):
        d_normed = d_normed + terms_ref[t].astype(jnp.float32)
    hidden32 = hidden_ref[...].astype(jnp.float32)
    height = hidden32.shape[0]
    d_normed = jnp.concatenate(
        [d_normed[height * c : height * (c + 1)] for c in range(hidden32.shape[1] // LANES)],
        axis=1,
    )
    inverse = rms_scale(hidden32)
    d_hidden = norm_backward(d_normed, hidden32 * inverse, inverse, gain_ref[...])
    out_ref[...] = (d_hidden + added_ref[...]).astype(jnp.bfloat16)


def packed_rows(sizes):
    starts, total = {}, 0
    for name, rows in sizes:
        starts[name] = slice(total, total + rows)
        total += rows
    return starts, total


def layout_rows(tokens_count, sequences, own_rows):
    wide = sequences * tokens_count // LANES
    return packed_rows(
        [
            ("key_cosine", tokens_count),
            ("key_sine", tokens_count),
            ("query_cosine", sequences),
            ("query_sine", sequences),
            ("inside", wide),
            ("chosen", wide),
            ("own_last", sequences),
            ("own_last_t", own_rows),
        ]
    )


def saved_rows(tokens_count, sequences):
    return packed_rows(
        [
            ("key_raw", tokens_count),
            ("key", tokens_count),
            ("value", tokens_count),
            ("query_raw", sequences),
            ("query", sequences),
            ("probs", sequences * tokens_count // LANES),
        ]
    )


def folded(block):
    parts = [block[:, LANES * k : LANES * (k + 1)] for k in range(block.shape[1] // LANES)]
    return jnp.concatenate(parts, axis=0)


def unfolded(block, rows):
    parts = [block[rows * k : rows * (k + 1)] for k in range(block.shape[0] // rows)]
    return jnp.concatenate(parts, axis=1)


def sequence_kernel(lengths_ref, out_ref, token_ref, *, tokens_count, own_rows):
    token_ref[0] = jnp.float32(0.0)
    sequences = lengths_ref.shape[1]
    at, _ = layout_rows(tokens_count, sequences, own_rows)
    lengths = lengths_ref[...].astype(jnp.float32)
    square = (sequences, sequences)
    ends = jnp.sum(
        jnp.where(iota(square, 1) <= iota(square, 0), lengths, 0.0), axis=1, keepdims=True
    )
    own_length = jnp.sum(
        jnp.where(iota(square, 1) == iota(square, 0), lengths, 0.0), axis=1, keepdims=True
    )
    starts = ends - own_length
    ends_row = jnp.sum(
        jnp.where(iota(square, 0) <= iota(square, 1), own_length, 0.0), axis=0, keepdims=True
    )
    starts_row = ends_row - lengths
    token = iota((sequences, tokens_count), 1).astype(jnp.float32)
    out_ref[at["inside"], :] = folded(((token >= starts) & (token < ends)).astype(jnp.float32))
    out_ref[at["chosen"], :] = folded((token == ends - 1.0).astype(jnp.float32))
    first = (lax.axis_index("tensor") * own_rows).astype(jnp.float32)
    own_token = iota((sequences, LANES), 1).astype(jnp.float32) + first
    own_token = jnp.where(iota((sequences, LANES), 1) < own_rows, own_token, -1.0)
    out_ref[at["own_last"], :] = (own_token == ends - 1.0).astype(jnp.float32)
    own_token = iota((own_rows, sequences), 0).astype(jnp.float32) + first
    own_last_t = (own_token == ends_row - 1.0).astype(jnp.float32)
    out_ref[at["own_last_t"], :] = jnp.concatenate(
        [own_last_t, jnp.zeros((own_rows, LANES - sequences), jnp.float32)], axis=1
    )
    token = iota((tokens_count, sequences), 0).astype(jnp.float32)
    held = (token >= starts_row) & (token < ends_row)
    position = jnp.sum(jnp.where(held, token - starts_row, 0.0), axis=1, keepdims=True)
    lane = iota((1, LANES), 1)
    halfway = LANES // 2
    pair = jnp.where(lane < halfway, lane, lane - halfway).astype(jnp.float32)
    frequency = jnp.exp(pair * (-2.0 / LANES * math.log(ROPE_BASE)))
    sign = jnp.where(lane < halfway, -1.0, 1.0)
    for name, place in (("key", position), ("query", own_length - 1.0)):
        angles = place * frequency
        out_ref[at[name + "_cosine"], :] = jnp.cos(angles)
        out_ref[at[name + "_sine"], :] = jnp.sin(angles) * sign


def on_device(
    hidden, lengths, positives, negatives, in_gain, wq, wkv, q_gain, k_gain, wo, out_gain
):
    tensor_count = lax.axis_size("tensor")
    z_count = lax.axis_size("z_far") * lax.axis_size("z_pair")
    own_rows, features = hidden.shape
    tokens_count = own_rows * tensor_count
    head_width = wq.shape[1]
    sequences = lengths.shape[1]
    query_count = positives.shape[0]
    total_rows = query_count // QDEV * sequences
    chunk = features // tensor_count
    f32, bf16 = jnp.float32, jnp.bfloat16
    head = (tokens_count, head_width)
    weights_shape = (head_width, features)
    flat = (tensor_count, own_rows * features // LANES, LANES)
    gain_rows = [q_gain[None, :], k_gain[None, :]]

    (copies,) = kernel_call(
        copied_norm_kernel, [(flat, bf16)], [hidden, in_gain[None, :]], near_outs=(0,)
    )
    piece = exchange(copies, "tensor")
    kv_own, query_all = kernel_call(
        projection_kernel,
        [(head, f32), (head, f32)],
        [piece, wkv, wq],
        near=(0,),
        near_outs=(0,),
    )
    kv_other = swapped(kv_own, "tensor", 0)
    def sequence_layout(after):
        return kernel_call(
            functools.partial(sequence_kernel, tokens_count=tokens_count, own_rows=own_rows),
            [((layout_rows(tokens_count, sequences, own_rows)[1], LANES), f32), ((1,), f32)],
            [lengths],
            after=[after],
        )

    layout, _ = sequence_layout(query_all)
    blocks, saved = kernel_call(
        attention_kernel,
        [
            ((tensor_count, sequences, chunk), bf16),
            ((saved_rows(tokens_count, sequences)[1], LANES), f32),
        ],
        [kv_own, kv_other, query_all, layout, *gain_rows, hidden, wo],
        near=(0, 1),
        near_outs=(0,),
    )
    (own_weights,) = kernel_call(
        transpose_kernel, [(weights_shape, bf16)], [wkv], after=[saved]
    )
    other_weights = swapped(own_weights, "tensor", 0)
    output_gain = out_gain[None, :]
    resid, scaled = kernel_call(
        resid_kernel,
        [((sequences, chunk), f32), ((z_count, sequences, chunk), bf16)],
        [exchange(blocks, "tensor"), output_gain],
        near=(0,),
        near_outs=(1,),
    )
    query_weights, wo_t, transposed = kernel_call(
        transpose_kernel,
        [(weights_shape, bf16), ((features, head_width), bf16), ((1,), f32)],
        [wq, wo],
        after=[resid],
    )
    both_weights, fetched = kernel_call(
        stack_kernel,
        [((2 * head_width, features), bf16), ((1,), f32)],
        [own_weights, other_weights],
    )
    layout_again, placed = sequence_layout(resid)
    tables = kernel_call(
        candidate_kernel,
        [
            ((16, query_count), jnp.int32),
            ((query_count, total_rows), bf16),
            ((query_count, total_rows), bf16),
        ],
        [positives[None, :], negatives.T],
        after=[resid],
    )
    everyone = lax.all_gather(exchange(scaled, ("z_far", "z_pair")), "core", axis=1)
    loss, d_resid16 = contrast(
        everyone, resid, output_gain, tables, [transposed, fetched, placed]
    )
    product, added = kernel_call(
        gradient_kernel,
        [(flat, bf16), ((own_rows, features), f32)],
        [
            d_resid16,
            wo_t,
            saved,
            layout_again,
            *gain_rows,
            both_weights,
            query_weights,
        ],
        near=(0,),
        near_outs=(0,),
    )
    terms = exchange(product, "tensor")
    (d_hidden,) = kernel_call(
        d_hidden_kernel,
        [((own_rows, features), bf16)],
        [terms, hidden, in_gain[None, :], added],
        near=(0,),
    )
    return (d_hidden, loss[0])


def solution(mesh):
    z_count = mesh.shape["dp"] // 2
    chips = mesh.devices.reshape(z_count // 2, 2, 2, mesh.shape["tensor"])
    mesh = jax.sharding.Mesh(chips, ("z_far", "z_pair", "core", "tensor"))
    everywhere = P(("z_far", "z_pair", "core", "tensor"), None)
    placed = (
        everywhere,
        P(("z_far", "z_pair", "core"), None),
        P(),
        P(),
        P(),
        P(None, "tensor"),
        P(None, "tensor"),
        P(),
        P(),
        P("tensor", None),
        P(),
    )
    return jax.shard_map(
        on_device, mesh=mesh, in_specs=placed, out_specs=(everywhere, P()), check_vma=False
    )
```

```python
import functools
import math

import jax
import jax.numpy as jnp
from jax import lax
from jax.experimental import pallas as pl
from jax.experimental.pallas import tpu as pltpu
from jax.sharding import PartitionSpec as P

QDEV = 8
LANES = 128
VMEM_BYTES = 32 * 2**20


EPSILON = 1e-06
SOFTMAX_TEMPER = 0.05
LOSS_MULTIPLIER = 8192.0
ROPE_BASE = 1000000.0


def swapped(value, axis, apart):
    mask = 2**apart
    pairs = [(source, source ^ mask) for source in range(lax.axis_size(axis))]
    return lax.ppermute(value, axis, pairs)


def rms_scale(tensor):
    return lax.rsqrt(jnp.mean(tensor * tensor, axis=-1, keepdims=True) + EPSILON)


def norm_backward(grad, unit_form, inverse, gain):
    scaled = grad * gain
    return inverse * (scaled - unit_form * jnp.mean(unit_form * scaled, axis=-1, keepdims=True))


def exchange(blocks, axis):
    return lax.all_to_all(blocks, axis, 0, 0, tiled=True)


def halves(value):
    high = value.astype(jnp.bfloat16).astype(jnp.float32)
    return high, value - high


def iota(shape, axis):
    return lax.broadcasted_iota(jnp.int32, shape, axis)


def columns_to_lanes(column, out_ref):
    diagonal = iota((LANES, LANES), 0) == iota((LANES, LANES), 1)
    for k in range(column.shape[0] // LANES):
        block = jnp.where(diagonal, column[LANES * k : LANES * (k + 1)], 0.0)
        out_ref[k : k + 1, :] = jnp.sum(block, axis=0, keepdims=True)


HALF = LANES // 2


def query_block():
    return lax.axis_index("z_pair"), lax.axis_index("core")


def block_lanes(block):
    return pl.ds(pl.multiple_of(block * LANES, LANES), LANES)


def in_first_half(shape):
    return iota(shape, len(shape) - 1) < HALF


def fold_half(first, second, half):
    is_first = in_first_half(first.shape)
    low = jnp.where(is_first, first, pltpu.roll(second, HALF, 1))
    high = jnp.where(is_first, pltpu.roll(first, HALF, 1), second)
    return jnp.where(half == 0, low, high)


def unfold_half(block):
    return block, pltpu.roll(block, HALF, 1)


def own_columns(gains_ref, width):
    start = pl.multiple_of(lax.axis_index("tensor") * width, width)
    return gains_ref[:, pl.ds(start, width)]


def partial_logits_kernel(
    rows_ref, query_hot_ref, positive_hot_ref, listed_all_ref, gains_ref, out_ref, held_ref
):
    rows = rows_ref[...]
    query_at, half = query_block()
    listed_ref = listed_all_ref[:8, block_lanes(query_at)]
    block_hot = query_hot_ref[block_lanes(query_at), :]
    queries = jnp.dot(block_hot, rows, preferred_element_type=jnp.float32)
    positives = jnp.dot(positive_hot_ref[...], rows, preferred_element_type=jnp.float32)
    queries = queries.astype(jnp.bfloat16)
    features = gains_ref.shape[1]
    rows32 = rows.astype(jnp.float32)
    plain = rows32 * (1.0 / own_columns(gains_ref, rows.shape[1]))
    squares = jnp.sum(rows32 * rows32, axis=1, keepdims=True) + jnp.sum(
        plain * plain, axis=1, keepdims=True
    ) * (EPSILON / features)
    against = (((1,), (1,)), ((), ()))
    with_positives = lax.dot_general(
        positives.astype(jnp.bfloat16), queries, against, preferred_element_type=jnp.float32
    )
    with_all = lax.dot_general(rows, queries, against, preferred_element_type=jnp.float32)
    row_index = iota(with_all.shape, 0)
    for j in range(8):
        listed = row_index == listed_ref[j : j + 1, :]
        held_ref[j : j + 1, :] = jnp.sum(jnp.where(listed, with_all, 0.0), axis=0, keepdims=True)
        held_ref[8 + j : 9 + j, :] = jnp.sum(
            jnp.where(listed, squares, 0.0), axis=0, keepdims=True
        )
    columns_to_lanes(squares, held_ref.at[16:24])
    count = with_positives.shape[0] // 2
    sent = fold_half(with_positives[:count], with_positives[count:], half).astype(jnp.bfloat16)
    high, low = halves(held_ref[0:16, :])
    listed16 = fold_half(high, low, half).astype(jnp.bfloat16)
    squares16 = jnp.concatenate(halves(held_ref[16:24, :])).astype(jnp.bfloat16)
    for t in range(out_ref.shape[0]):
        out_ref[t, :count, :] = sent
        out_ref[t, count : count + 16, :] = listed16
        out_ref[t, count + 16 : count + 32, :] = squares16


def softmax_kernel(arrived_ref, positive_hot_ref, out_ref, inverse_ref):
    count = positive_hot_ref.shape[0]
    summed = arrived_ref[0].astype(jnp.float32)
    for t in range(1, arrived_ref.shape[0]):
        summed = summed + arrived_ref[t].astype(jnp.float32)
    query_at, half = query_block()
    first_query = query_at * LANES + half * HALF
    start = count // 2
    with_positives = jnp.concatenate(unfold_half(summed[:start]), axis=0)
    high, low = unfold_half(summed[start : start + 16])
    hard, listed_squares = high[:8] + low[:8], high[8:] + low[8:]
    squares = summed[start + 16 : start + 24] + summed[start + 24 : start + 32]

    def valid(value, other):
        return jnp.where(in_first_half(value.shape), value, other)

    inverse_listed = lax.rsqrt(valid(listed_squares, 1.0) + EPSILON * EPSILON)
    inverse = lax.rsqrt(squares + EPSILON * EPSILON)
    inverse_ref[...] = inverse
    inverse_query = inverse_listed[7:8, :]
    picked = jnp.zeros((count, LANES), jnp.float32)
    for k in range(8):
        hot = positive_hot_ref[:, LANES * k : LANES * (k + 1)].astype(jnp.float32)
        picked = picked + hot * inverse[k : k + 1, :]
    inverse_positive = jnp.sum(picked, axis=1, keepdims=True)
    logits = valid(with_positives, 0.0) * inverse_positive * inverse_query / SOFTMAX_TEMPER
    hard = valid(hard, 0.0) * inverse_listed * inverse_query / SOFTMAX_TEMPER
    is_hard = iota(hard.shape, 0) < 7
    is_own = iota(logits.shape, 0) == iota(logits.shape, 1) + first_query
    is_own = is_own & in_first_half(logits.shape)
    weights = valid(jnp.exp(logits - 1.0 / SOFTMAX_TEMPER), 1.0)
    hard_weights = jnp.where(is_hard, jnp.exp(hard - 1.0 / SOFTMAX_TEMPER), 0.0)
    totals = jnp.sum(weights, axis=0, keepdims=True) + jnp.sum(hard_weights, axis=0, keepdims=True)
    target = jnp.sum(jnp.where(is_own, logits, 0.0), axis=0, keepdims=True)
    losses = jnp.log(totals) + 1.0 / SOFTMAX_TEMPER - target
    scaling_factor = LOSS_MULTIPLIER / (count * SOFTMAX_TEMPER)

    def rounded(value):
        return value.astype(jnp.bfloat16).astype(jnp.float32)

    coef = rounded(scaling_factor * (weights / totals - is_own.astype(jnp.float32)))
    hard_coef = rounded(scaling_factor * (hard_weights / totals))
    weighted = valid(coef * logits * SOFTMAX_TEMPER, 0.0)
    hard_weighted = jnp.where(is_hard, hard_coef * hard * SOFTMAX_TEMPER, 0.0)
    along_query = jnp.sum(weighted, axis=0, keepdims=True) + jnp.sum(
        hard_weighted, axis=0, keepdims=True
    )
    folded_coef = fold_half(coef[:start], coef[start:], 0)
    folded_hard = fold_half(
        jnp.where(is_hard, hard_coef, along_query), jnp.where(is_hard, hard_weighted, losses), 0
    )
    for k in range(out_ref.shape[0]):
        out_ref[k, :start, :] = folded_coef
        out_ref[k, start : start + 8, :] = folded_hard
        out_ref[k, start + 8 :, :] = jnp.zeros_like(out_ref[k, start + 8 :, :])
        columns_to_lanes(
            jnp.sum(weighted, axis=1, keepdims=True), out_ref.at[k, start + 8 : start + 16]
        )


def resid_grad_kernel(
    both_ref,
    inverse_ref,
    rows_ref,
    positive_hot_ref,
    query_hot_ref,
    listed_ref,
    resid_ref,
    gains_ref,
    out_ref,
    loss_ref,
):
    sequences = resid_ref.shape[0]
    count, total_rows = positive_hot_ref.shape
    z = lax.axis_index("z_far") * lax.axis_size("z_pair") + lax.axis_index("z_pair")
    group = z * lax.axis_size("core") + lax.axis_index("core")
    first_row = group * sequences
    first_query = group * QDEV
    across = (((1,), (1,)), ((), ()))

    def joined(start, stop):
        firsts, seconds = [], []
        for k in (0, 2):
            first, second = both_ref[k, start:stop, :], both_ref[k + 1, start:stop, :]
            firsts.append(fold_half(first, second, 0))
            seconds.append(fold_half(pltpu.roll(first, HALF, 1), pltpu.roll(second, HALF, 1), 0))
        return jnp.concatenate(firsts, axis=1), jnp.concatenate(seconds, axis=1)

    start = count // 2
    coef16 = jnp.concatenate(joined(0, start), axis=0).astype(jnp.bfloat16)
    hard, hard_weighted = joined(start, start + 8)
    along_passage = both_ref[0, start + 8 : start + 16, :]
    for k in range(1, both_ref.shape[0]):
        along_passage = along_passage + both_ref[k, start + 8 : start + 16, :]
    along_passage = jnp.concatenate([along_passage[0:1], along_passage[1:2]], axis=1)
    inverse = jnp.concatenate([inverse_ref[k : k + 1, :] for k in range(8)], axis=1)

    own_row = first_row + iota((sequences, count), 0)
    own_query = (iota((sequences, count), 0) < QDEV) & (
        iota((sequences, count), 1) == first_query + iota((sequences, count), 0)
    )
    own_positive = listed_ref[8:9, :] == own_row
    to_positives = lax.dot_general(
        own_query.astype(jnp.bfloat16), coef16, across, preferred_element_type=jnp.float32
    )
    to_queries = jnp.dot(
        own_positive.astype(jnp.bfloat16), coef16, preferred_element_type=jnp.float32
    )
    along = jnp.sum(
        jnp.where(own_query, hard[7:8, :], 0.0) + jnp.where(own_positive, along_passage, 0.0),
        axis=1,
        keepdims=True,
    )
    for j in range(7):
        listed = listed_ref[j : j + 1, :] == own_row
        to_queries = to_queries + jnp.where(listed, hard[j : j + 1, :], 0.0)
        along = along + jnp.sum(
            jnp.where(listed, hard_weighted[j : j + 1, :], 0.0), axis=1, keepdims=True
        )
    matrix = jnp.dot(
        to_positives.astype(jnp.bfloat16), positive_hot_ref[...], preferred_element_type=jnp.float32
    ) + jnp.dot(
        to_queries.astype(jnp.bfloat16), query_hot_ref[...], preferred_element_type=jnp.float32
    )
    row_index = iota((sequences, total_rows), 1)
    for j in range(7):
        own_hard = jnp.sum(jnp.where(own_query, hard[j : j + 1, :], 0.0), axis=1, keepdims=True)
        own_listed = jnp.where(own_query, listed_ref[j : j + 1, :].astype(jnp.float32), 0.0)
        own_listed = jnp.sum(own_listed, axis=1, keepdims=True).astype(jnp.int32)
        listed = row_index == own_listed
        matrix = matrix + jnp.where(listed, own_hard, 0.0)
    matrix = matrix * inverse
    high = matrix.astype(jnp.bfloat16)
    low = (matrix - high.astype(jnp.float32)).astype(jnp.bfloat16)
    rows = rows_ref[...]
    d_embed = jnp.dot(high, rows, preferred_element_type=jnp.float32) + jnp.dot(
        low, rows, preferred_element_type=jnp.float32
    )

    is_own_row = row_index == first_row + iota((sequences, total_rows), 0)
    own_inverse = jnp.sum(jnp.where(is_own_row, inverse, 0.0), axis=1, keepdims=True)
    resid = resid_ref[...]
    gain = own_columns(gains_ref, resid.shape[1])
    features = gains_ref.shape[1]
    d_resid = own_inverse * gain * (
        d_embed - resid * gain * own_inverse * along
    ) - resid * (along * own_inverse * own_inverse * (EPSILON / features))
    d_resid16 = d_resid.astype(jnp.bfloat16)
    for t in range(out_ref.shape[0]):
        out_ref[t] = d_resid16
    loss_ref[0] = jnp.sum(hard_weighted[7:8, :]) / count


def kernel_call(body, outs, arrays, after=(), scratch=()):
    count = len(arrays)

    def kernel(*refs):
        body(*refs[:count], *refs[count + len(after) :])

    def out_spec(shape):
        return pl.BlockSpec(memory_space=pltpu.SMEM if shape == (1,) else pltpu.VMEM)

    return pl.pallas_call(
        kernel,
        out_shape=[jax.ShapeDtypeStruct(shape, dtype) for shape, dtype in outs],
        in_specs=[pl.BlockSpec(memory_space=pltpu.VMEM)] * count
        + [pl.BlockSpec(memory_space=pl.ANY)] * len(after),
        out_specs=[out_spec(shape) for shape, _ in outs],
        scratch_shapes=list(scratch),
        compiler_params=pltpu.CompilerParams(vmem_limit_bytes=VMEM_BYTES),
    )(*arrays, *after)


def candidate_kernel(positives_ref, negatives_ref, listed_ref, query_hot_ref, positive_hot_ref):
    query_count, total_rows = query_hot_ref.shape
    groups = query_count // QDEV
    sequences = total_rows // groups
    others = sequences - QDEV

    def row_of(passage):
        at = ((passage.astype(jnp.float32) + 0.5) * (1.0 / others)).astype(jnp.int32)
        return passage + at * QDEV + QDEV

    def query_row(query):
        return query + query // QDEV * others

    positive_row = row_of(positives_ref[...])
    count = negatives_ref.shape[0]
    listed_ref[:count, :] = row_of(negatives_ref[...])
    listed_ref[count : count + 1, :] = query_row(iota((1, query_count), 1))
    listed_ref[count + 1 :, :] = jnp.broadcast_to(
        positive_row, (listed_ref.shape[0] - count - 1, query_count)
    )
    shape = (LANES, total_rows)
    diagonal = iota((LANES, LANES), 0) == iota((LANES, LANES), 1)
    for k in range(query_count // LANES):
        rows = slice(LANES * k, LANES * (k + 1))
        query = query_row(iota(shape, 0) + LANES * k)
        query_hot_ref[rows, :] = (query == iota(shape, 1)).astype(jnp.float32).astype(jnp.bfloat16)
        lanes = positive_row[:, rows].astype(jnp.float32)
        column = jnp.sum(jnp.where(diagonal, lanes, 0.0), axis=1, keepdims=True)
        positive_hot_ref[rows, :] = (
            (column.astype(jnp.int32) == iota(shape, 1)).astype(jnp.float32).astype(jnp.bfloat16)
        )


def transpose_kernel(*refs):
    half = len(refs) // 2
    for given_ref, out_ref in zip(refs[:half], refs[half:]):
        given = given_ref[...]
        out_ref[...] = given.T
    if len(refs) > 2 * half:
        refs[-1][0] = jnp.float32(0.0)


def stack_kernel(first_ref, second_ref, out_ref, token_ref):
    rows = first_ref.shape[0]
    out_ref[:rows, :] = first_ref[...]
    out_ref[rows:, :] = second_ref[...]
    token_ref[0] = jnp.float32(0.0)


def contrast(everyone, resid, gains, tables, after):
    tensor_count = lax.axis_size("tensor")
    sequences, width = resid.shape
    listed, query_hot, positive_hot = tables
    count, total_rows = positive_hot.shape
    rows = everyone.reshape(total_rows, width)
    (sent,) = kernel_call(
        partial_logits_kernel,
        [((tensor_count, count // 2 + 32, LANES), jnp.bfloat16)],
        [rows, query_hot, positive_hot, listed, gains],
        after=after,
        scratch=[pltpu.VMEM((24, LANES), jnp.float32)],
    )
    arrived = exchange(sent, "tensor")
    coefs, inverse = kernel_call(
        softmax_kernel,
        [((4, count // 2 + 16, LANES), jnp.float32), ((8, LANES), jnp.float32)],
        [arrived, positive_hot],
    )
    both = exchange(coefs, ("z_pair", "core"))
    d_resid16, loss = kernel_call(
        resid_grad_kernel,
        [((tensor_count, sequences, width), jnp.bfloat16), ((1,), jnp.float32)],
        [both, inverse, rows, positive_hot, query_hot, listed, resid, gains],
    )
    return loss, exchange(d_resid16, "tensor")


def copied_norm_kernel(hidden_ref, gain_ref, out_ref):
    hidden32 = hidden_ref[...].astype(jnp.float32)
    normed = (hidden32 * rms_scale(hidden32) * gain_ref[...]).astype(jnp.bfloat16)
    height = normed.shape[0]
    for c in range(normed.shape[1] // LANES):
        block = normed[:, LANES * c : LANES * (c + 1)]
        for t in range(out_ref.shape[0]):
            out_ref[t, height * c : height * (c + 1), :] = block


def projection_kernel(rows_ref, kv_weights_ref, query_weights_ref, kv_ref, sent_ref, query_ref):
    tensor_count, tall, _ = rows_ref.shape
    blocks = kv_weights_ref.shape[0] // LANES
    height = tall // blocks

    def block(c):
        part = rows_ref[:, height * c : height * (c + 1), :]
        return part.reshape(tensor_count * height, LANES)

    kv = jnp.zeros(kv_ref.shape, jnp.float32)
    query = jnp.zeros(query_ref.shape, jnp.float32)
    for c in range(0, blocks, 2):
        rows = jnp.concatenate([block(c), block(c + 1)], axis=1)
        columns = slice(LANES * c, LANES * (c + 2))
        kv = kv + jnp.dot(rows, kv_weights_ref[columns, :], preferred_element_type=jnp.float32)
        query = query + jnp.dot(
            rows, query_weights_ref[columns, :], preferred_element_type=jnp.float32
        )
    kv_ref[...] = kv
    sent_ref[...] = kv.astype(jnp.bfloat16)
    query_ref[...] = query


def half_turned(tensor, cosine, signed_sine):
    halfway = tensor.shape[1] // 2
    return tensor * cosine + pltpu.roll(tensor, halfway, 1) * signed_sine


def is_even_tensor():
    return lax.axis_index("tensor") % 2 == 0


def attention_kernel(
    own_ref,
    other_ref,
    query_all_ref,
    layout_ref,
    q_gain_ref,
    k_gain_ref,
    hidden_ref,
    wo_ref,
    out_ref,
    saved_ref,
):
    root = math.sqrt(own_ref.shape[1])
    tokens_count, sequences, own_rows = own_ref.shape[0], out_ref.shape[1], hidden_ref.shape[0]
    at, _ = layout_rows(tokens_count, sequences, own_rows)
    to, _ = saved_rows(tokens_count, sequences)
    is_even = is_even_tensor()
    own, other = own_ref[...], other_ref[...].astype(jnp.float32)
    key_raw = jnp.where(is_even, own, other)
    value16 = jnp.where(is_even, other, own).astype(jnp.bfloat16)
    query_raw = jnp.dot(
        unfolded(layout_ref[at["chosen"], :], sequences),
        query_all_ref[...],
        precision=lax.Precision.HIGHEST,
        preferred_element_type=jnp.float32,
    )
    q_gain, k_gain = q_gain_ref[...], k_gain_ref[...]
    key16 = half_turned(
        key_raw * rms_scale(key_raw) * k_gain,
        layout_ref[at["key_cosine"], :],
        layout_ref[at["key_sine"], :],
    ).astype(jnp.bfloat16)
    query16 = half_turned(
        query_raw * rms_scale(query_raw) * q_gain,
        layout_ref[at["query_cosine"], :],
        layout_ref[at["query_sine"], :],
    ).astype(jnp.bfloat16)
    shift = (
        root
        * jnp.max(q_gain, axis=1, keepdims=True)
        * jnp.max(k_gain, axis=1, keepdims=True)
    )
    scores = (
        lax.dot_general(
            query16, key16, (((1,), (1,)), ((), ())), preferred_element_type=jnp.float32
        )
        / root
    )
    inside = unfolded(layout_ref[at["inside"], :], sequences)
    weights = jnp.where(inside > 0.0, jnp.exp(scores - shift), 0.0)
    probs = weights / jnp.sum(weights, axis=1, keepdims=True)
    attn16 = jnp.dot(
        probs.astype(jnp.bfloat16), value16, preferred_element_type=jnp.float32
    ).astype(jnp.bfloat16)
    own_last = layout_ref[at["own_last"], :][:, :own_rows].astype(jnp.bfloat16)
    chunk = out_ref.shape[2]
    for t in range(out_ref.shape[0]):
        columns = slice(t * chunk, (t + 1) * chunk)
        block = jnp.dot(attn16, wo_ref[:, columns], preferred_element_type=jnp.float32)
        block = block + jnp.dot(
            own_last, hidden_ref[:, columns], preferred_element_type=jnp.float32
        )
        out_ref[t] = block.astype(jnp.bfloat16)
    saved_ref[to["key_raw"], :] = key_raw
    saved_ref[to["key"], :] = key16.astype(jnp.float32)
    saved_ref[to["value"], :] = value16.astype(jnp.float32)
    saved_ref[to["query_raw"], :] = query_raw
    saved_ref[to["query"], :] = query16.astype(jnp.float32)
    saved_ref[to["probs"], :] = folded(probs)


def resid_kernel(arrived_ref, gains_ref, resid_ref, out_ref):
    gain = own_columns(gains_ref, resid_ref.shape[1])
    resid = arrived_ref[0].astype(jnp.float32)
    for t in range(1, arrived_ref.shape[0]):
        resid = resid + arrived_ref[t].astype(jnp.float32)
    resid_ref[...] = resid
    scaled16 = (resid * gain).astype(jnp.bfloat16)
    for t in range(out_ref.shape[0]):
        out_ref[t] = scaled16


def gradient_kernel(
    d_resid_ref,
    wo_t_ref,
    saved_ref,
    layout_ref,
    q_gain_ref,
    k_gain_ref,
    both_weights_ref,
    query_weights_ref,
    out_ref,
    added_ref,
):
    head_width = saved_ref.shape[1]
    root = math.sqrt(head_width)
    sequences = d_resid_ref.shape[1]
    own_rows = added_ref.shape[0]
    tokens_count = own_rows * out_ref.shape[0]
    at, _ = layout_rows(tokens_count, sequences, own_rows)
    to, _ = saved_rows(tokens_count, sequences)
    is_even = is_even_tensor()
    chunk = d_resid_ref.shape[2]
    d_attn = jnp.dot(d_resid_ref[0], wo_t_ref[:chunk, :], preferred_element_type=jnp.float32)
    for t in range(1, d_resid_ref.shape[0]):
        d_attn = d_attn + jnp.dot(
            d_resid_ref[t],
            wo_t_ref[t * chunk : (t + 1) * chunk, :],
            preferred_element_type=jnp.float32,
        )
    d_attn16 = d_attn.astype(jnp.bfloat16)
    probs = unfolded(saved_ref[to["probs"], :], sequences)
    key16 = saved_ref[to["key"], :].astype(jnp.bfloat16)
    query16 = saved_ref[to["query"], :].astype(jnp.bfloat16)
    value16 = saved_ref[to["value"], :].astype(jnp.bfloat16)
    d_probs = lax.dot_general(
        d_attn16, value16, (((1,), (1,)), ((), ())), preferred_element_type=jnp.float32
    )
    d_scores16 = (
        probs * (d_probs - jnp.sum(probs * d_probs, axis=1, keepdims=True)) / root
    ).astype(jnp.bfloat16)
    down = (((0,), (0,)), ((), ()))
    d_query_rot = jnp.dot(d_scores16, key16, preferred_element_type=jnp.float32)
    d_key_rot = lax.dot_general(d_scores16, query16, down, preferred_element_type=jnp.float32)
    d_value = lax.dot_general(
        probs.astype(jnp.bfloat16), d_attn16, down, preferred_element_type=jnp.float32
    )

    def head_gradient(grad_rot, name, gain):
        raw = saved_ref[to[name + "_raw"], :]
        inverse = rms_scale(raw)
        turned_back = half_turned(
            grad_rot, layout_ref[at[name + "_cosine"], :], -layout_ref[at[name + "_sine"], :]
        )
        return norm_backward(turned_back, raw * inverse, inverse, gain)

    d_key = head_gradient(d_key_rot, "key", k_gain_ref[...])
    d_query = head_gradient(d_query_rot, "query", q_gain_ref[...])
    own_other16 = jnp.concatenate(
        [jnp.where(is_even, d_key, d_value), jnp.where(is_even, d_value, d_key)], axis=1
    ).astype(jnp.bfloat16)
    spread16 = lax.dot_general(
        unfolded(layout_ref[at["chosen"], :], sequences).astype(jnp.bfloat16),
        d_query.astype(jnp.bfloat16),
        down,
        preferred_element_type=jnp.float32,
    ).astype(jnp.bfloat16)
    last = layout_ref[at["own_last_t"], :][:, :sequences].astype(jnp.bfloat16)
    height = out_ref.shape[1] * LANES // added_ref.shape[1]
    for t in range(added_ref.shape[1] // chunk):
        columns = slice(t * chunk, (t + 1) * chunk)
        added_ref[:, columns] = jnp.dot(last, d_resid_ref[t], preferred_element_type=jnp.float32)
        term = jnp.dot(
            own_other16, both_weights_ref[:, columns], preferred_element_type=jnp.float32
        )
        term = term + jnp.dot(
            spread16, query_weights_ref[:, columns], preferred_element_type=jnp.float32
        )
        term16 = term.astype(jnp.bfloat16)
        for k in range(chunk // LANES):
            c = t * (chunk // LANES) + k
            block = term16[:, LANES * k : LANES * (k + 1)]
            out_ref[:, height * c : height * (c + 1), :] = block.reshape(-1, height, LANES)


def d_hidden_kernel(terms_ref, hidden_ref, gain_ref, added_ref, out_ref):
    d_normed = terms_ref[0].astype(jnp.float32)
    for t in range(1, terms_ref.shape[0]):
        d_normed = d_normed + terms_ref[t].astype(jnp.float32)
    hidden32 = hidden_ref[...].astype(jnp.float32)
    height = hidden32.shape[0]
    d_normed = jnp.concatenate(
        [d_normed[height * c : height * (c + 1)] for c in range(hidden32.shape[1] // LANES)],
        axis=1,
    )
    inverse = rms_scale(hidden32)
    d_hidden = norm_backward(d_normed, hidden32 * inverse, inverse, gain_ref[...])
    out_ref[...] = (d_hidden + added_ref[...]).astype(jnp.bfloat16)


def packed_rows(sizes):
    starts, total = {}, 0
    for name, rows in sizes:
        starts[name] = slice(total, total + rows)
        total += rows
    return starts, total


def layout_rows(tokens_count, sequences, own_rows):
    wide = sequences * tokens_count // LANES
    return packed_rows(
        [
            ("key_cosine", tokens_count),
            ("key_sine", tokens_count),
            ("query_cosine", sequences),
            ("query_sine", sequences),
            ("inside", wide),
            ("chosen", wide),
            ("own_last", sequences),
            ("own_last_t", own_rows),
        ]
    )


def saved_rows(tokens_count, sequences):
    return packed_rows(
        [
            ("key_raw", tokens_count),
            ("key", tokens_count),
            ("value", tokens_count),
            ("query_raw", sequences),
            ("query", sequences),
            ("probs", sequences * tokens_count // LANES),
        ]
    )


def folded(block):
    parts = [block[:, LANES * k : LANES * (k + 1)] for k in range(block.shape[1] // LANES)]
    return jnp.concatenate(parts, axis=0)


def unfolded(block, rows):
    parts = [block[rows * k : rows * (k + 1)] for k in range(block.shape[0] // rows)]
    return jnp.concatenate(parts, axis=1)


def sequence_kernel(lengths_ref, out_ref, token_ref, *, tokens_count, own_rows):
    token_ref[0] = jnp.float32(0.0)
    sequences = lengths_ref.shape[1]
    at, _ = layout_rows(tokens_count, sequences, own_rows)
    lengths = lengths_ref[...].astype(jnp.float32)
    square = (sequences, sequences)
    ends = jnp.sum(
        jnp.where(iota(square, 1) <= iota(square, 0), lengths, 0.0), axis=1, keepdims=True
    )
    own_length = jnp.sum(
        jnp.where(iota(square, 1) == iota(square, 0), lengths, 0.0), axis=1, keepdims=True
    )
    starts = ends - own_length
    ends_row = jnp.sum(
        jnp.where(iota(square, 0) <= iota(square, 1), own_length, 0.0), axis=0, keepdims=True
    )
    starts_row = ends_row - lengths
    token = iota((sequences, tokens_count), 1).astype(jnp.float32)
    out_ref[at["inside"], :] = folded(((token >= starts) & (token < ends)).astype(jnp.float32))
    out_ref[at["chosen"], :] = folded((token == ends - 1.0).astype(jnp.float32))
    first = (lax.axis_index("tensor") * own_rows).astype(jnp.float32)
    own_token = iota((sequences, LANES), 1).astype(jnp.float32) + first
    own_token = jnp.where(iota((sequences, LANES), 1) < own_rows, own_token, -1.0)
    out_ref[at["own_last"], :] = (own_token == ends - 1.0).astype(jnp.float32)
    own_token = iota((own_rows, sequences), 0).astype(jnp.float32) + first
    own_last_t = (own_token == ends_row - 1.0).astype(jnp.float32)
    out_ref[at["own_last_t"], :] = jnp.concatenate(
        [own_last_t, jnp.zeros((own_rows, LANES - sequences), jnp.float32)], axis=1
    )
    token = iota((tokens_count, sequences), 0).astype(jnp.float32)
    held = (token >= starts_row) & (token < ends_row)
    position = jnp.sum(jnp.where(held, token - starts_row, 0.0), axis=1, keepdims=True)
    lane = iota((1, LANES), 1)
    halfway = LANES // 2
    pair = jnp.where(lane < halfway, lane, lane - halfway).astype(jnp.float32)
    frequency = jnp.exp(pair * (-2.0 / LANES * math.log(ROPE_BASE)))
    sign = jnp.where(lane < halfway, -1.0, 1.0)
    for name, place in (("key", position), ("query", own_length - 1.0)):
        angles = place * frequency
        out_ref[at[name + "_cosine"], :] = jnp.cos(angles)
        out_ref[at[name + "_sine"], :] = jnp.sin(angles) * sign


def on_device(
    hidden, lengths, positives, negatives, in_gain, wq, wkv, q_gain, k_gain, wo, out_gain
):
    tensor_count = lax.axis_size("tensor")
    z_count = lax.axis_size("z_far") * lax.axis_size("z_pair")
    own_rows, features = hidden.shape
    tokens_count = own_rows * tensor_count
    head_width = wq.shape[1]
    sequences = lengths.shape[1]
    query_count = positives.shape[0]
    total_rows = query_count // QDEV * sequences
    chunk = features // tensor_count
    f32, bf16 = jnp.float32, jnp.bfloat16
    head = (tokens_count, head_width)
    weights_shape = (head_width, features)
    flat = (tensor_count, own_rows * features // LANES, LANES)
    gain_rows = [q_gain[None, :], k_gain[None, :]]

    (copies,) = kernel_call(
        copied_norm_kernel, [(flat, bf16)], [hidden, in_gain[None, :]]
    )
    piece = exchange(copies, "tensor")
    kv_own, kv_own16, query_all = kernel_call(
        projection_kernel, [(head, f32), (head, bf16), (head, f32)], [piece, wkv, wq]
    )
    kv_other = swapped(kv_own16, "tensor", 0)
    def sequence_layout(after):
        return kernel_call(
            functools.partial(sequence_kernel, tokens_count=tokens_count, own_rows=own_rows),
            [((layout_rows(tokens_count, sequences, own_rows)[1], LANES), f32), ((1,), f32)],
            [lengths],
            after=[after],
        )

    layout, _ = sequence_layout(query_all)
    blocks, saved = kernel_call(
        attention_kernel,
        [
            ((tensor_count, sequences, chunk), bf16),
            ((saved_rows(tokens_count, sequences)[1], LANES), f32),
        ],
        [kv_own, kv_other, query_all, layout, *gain_rows, hidden, wo],
    )
    (own_weights,) = kernel_call(
        transpose_kernel, [(weights_shape, bf16)], [wkv], after=[query_all]
    )
    other_weights = swapped(own_weights, "tensor", 0)
    output_gain = out_gain[None, :]
    resid, scaled = kernel_call(
        resid_kernel,
        [((sequences, chunk), f32), ((z_count, sequences, chunk), bf16)],
        [exchange(blocks, "tensor"), output_gain],
    )
    query_weights, wo_t, transposed = kernel_call(
        transpose_kernel,
        [(weights_shape, bf16), ((features, head_width), bf16), ((1,), f32)],
        [wq, wo],
        after=[resid],
    )
    both_weights, fetched = kernel_call(
        stack_kernel,
        [((2 * head_width, features), bf16), ((1,), f32)],
        [own_weights, other_weights],
    )
    layout_again, placed = sequence_layout(resid)
    tables = kernel_call(
        candidate_kernel,
        [
            ((16, query_count), jnp.int32),
            ((query_count, total_rows), bf16),
            ((query_count, total_rows), bf16),
        ],
        [positives[None, :], negatives.T],
        after=[resid],
    )
    everyone = lax.all_gather(exchange(scaled, ("z_far", "z_pair")), "core", axis=1)
    loss, d_resid16 = contrast(
        everyone, resid, output_gain, tables, [transposed, fetched, placed]
    )
    product, added = kernel_call(
        gradient_kernel,
        [(flat, bf16), ((own_rows, features), f32)],
        [
            d_resid16,
            wo_t,
            saved,
            layout_again,
            *gain_rows,
            both_weights,
            query_weights,
        ],
    )
    terms = exchange(product, "tensor")
    (d_hidden,) = kernel_call(
        d_hidden_kernel,
        [((own_rows, features), bf16)],
        [terms, hidden, in_gain[None, :], added],
    )
    return (d_hidden, loss[0])


def solution(mesh):
    z_count = mesh.shape["dp"] // 2
    chips = mesh.devices.reshape(z_count // 2, 2, 2, mesh.shape["tensor"])
    mesh = jax.sharding.Mesh(chips, ("z_far", "z_pair", "core", "tensor"))
    everywhere = P(("z_far", "z_pair", "core", "tensor"), None)
    placed = (
        everywhere,
        P(("z_far", "z_pair", "core"), None),
        P(),
        P(),
        P(),
        P(None, "tensor"),
        P(None, "tensor"),
        P(),
        P(),
        P("tensor", None),
        P(),
    )
    return jax.shard_map(
        on_device, mesh=mesh, in_specs=placed, out_specs=(everywhere, P()), check_vma=False
    )
```

```python
import functools
import math

import jax
import jax.numpy as jnp
from jax import lax
from jax.experimental import pallas as pl
from jax.experimental.pallas import tpu as pltpu
from jax.sharding import PartitionSpec as P

QDEV = 8
LANES = 128
VMEM_BYTES = 32 * 2**20


EPSILON = 1e-06
SOFTMAX_TEMPER = 0.05
LOSS_MULTIPLIER = 8192.0
ROPE_BASE = 1000000.0


def swapped(value, axis, apart):
    mask = 2**apart
    pairs = [(source, source ^ mask) for source in range(lax.axis_size(axis))]
    return lax.ppermute(value, axis, pairs)


def rms_scale(tensor):
    return lax.rsqrt(jnp.mean(tensor * tensor, axis=-1, keepdims=True) + EPSILON)


def norm_backward(grad, unit_form, inverse, gain):
    scaled = grad * gain
    return inverse * (scaled - unit_form * jnp.mean(unit_form * scaled, axis=-1, keepdims=True))


def exchange(blocks, axis):
    return lax.all_to_all(blocks, axis, 0, 0, tiled=True)


def halves(value):
    high = value.astype(jnp.bfloat16).astype(jnp.float32)
    return high, value - high


def iota(shape, axis):
    return lax.broadcasted_iota(jnp.int32, shape, axis)


def columns_to_lanes(column, out_ref):
    diagonal = iota((LANES, LANES), 0) == iota((LANES, LANES), 1)
    for k in range(column.shape[0] // LANES):
        block = jnp.where(diagonal, column[LANES * k : LANES * (k + 1)], 0.0)
        out_ref[k : k + 1, :] = jnp.sum(block, axis=0, keepdims=True)


HALF = LANES // 2


def query_block():
    return lax.axis_index("z_pair"), lax.axis_index("core")


def block_lanes(block):
    return pl.ds(pl.multiple_of(block * LANES, LANES), LANES)


def in_first_half(shape):
    return iota(shape, len(shape) - 1) < HALF


def fold_half(first, second, half):
    is_first = in_first_half(first.shape)
    low = jnp.where(is_first, first, pltpu.roll(second, HALF, 1))
    high = jnp.where(is_first, pltpu.roll(first, HALF, 1), second)
    return jnp.where(half == 0, low, high)


def unfold_half(block):
    return block, pltpu.roll(block, HALF, 1)


def own_columns(gains_ref, width):
    start = pl.multiple_of(lax.axis_index("tensor") * width, width)
    return gains_ref[:, pl.ds(start, width)]


def partial_logits_kernel(
    rows_ref, query_hot_ref, positive_hot_ref, listed_all_ref, gains_ref, out_ref, held_ref
):
    rows = rows_ref[...]
    query_at, half = query_block()
    listed_ref = listed_all_ref[:8, block_lanes(query_at)]
    block_hot = query_hot_ref[block_lanes(query_at), :]
    queries = jnp.dot(block_hot, rows, preferred_element_type=jnp.float32)
    positives = jnp.dot(positive_hot_ref[...], rows, preferred_element_type=jnp.float32)
    queries = queries.astype(jnp.bfloat16)
    features = gains_ref.shape[1]
    rows32 = rows.astype(jnp.float32)
    plain = rows32 * (1.0 / own_columns(gains_ref, rows.shape[1]))
    squares = jnp.sum(rows32 * rows32, axis=1, keepdims=True) + jnp.sum(
        plain * plain, axis=1, keepdims=True
    ) * (EPSILON / features)
    against = (((1,), (1,)), ((), ()))
    with_positives = lax.dot_general(
        positives.astype(jnp.bfloat16), queries, against, preferred_element_type=jnp.float32
    )
    with_all = lax.dot_general(rows, queries, against, preferred_element_type=jnp.float32)
    row_index = iota(with_all.shape, 0)
    for j in range(8):
        listed = row_index == listed_ref[j : j + 1, :]
        held_ref[j : j + 1, :] = jnp.sum(jnp.where(listed, with_all, 0.0), axis=0, keepdims=True)
        held_ref[8 + j : 9 + j, :] = jnp.sum(
            jnp.where(listed, squares, 0.0), axis=0, keepdims=True
        )
    columns_to_lanes(squares, held_ref.at[16:24])
    count = with_positives.shape[0] // 2
    sent = fold_half(with_positives[:count], with_positives[count:], half).astype(jnp.bfloat16)
    high, low = halves(held_ref[0:16, :])
    listed16 = fold_half(high, low, half).astype(jnp.bfloat16)
    squares16 = jnp.concatenate(halves(held_ref[16:24, :])).astype(jnp.bfloat16)
    for t in range(out_ref.shape[0]):
        out_ref[t, :count, :] = sent
        out_ref[t, count : count + 16, :] = listed16
        out_ref[t, count + 16 : count + 32, :] = squares16


def softmax_kernel(arrived_ref, positive_hot_ref, out_ref, inverse_ref):
    count = positive_hot_ref.shape[0]
    summed = arrived_ref[0].astype(jnp.float32)
    for t in range(1, arrived_ref.shape[0]):
        summed = summed + arrived_ref[t].astype(jnp.float32)
    query_at, half = query_block()
    first_query = query_at * LANES + half * HALF
    start = count // 2
    with_positives = jnp.concatenate(unfold_half(summed[:start]), axis=0)
    high, low = unfold_half(summed[start : start + 16])
    hard, listed_squares = high[:8] + low[:8], high[8:] + low[8:]
    squares = summed[start + 16 : start + 24] + summed[start + 24 : start + 32]

    def valid(value, other):
        return jnp.where(in_first_half(value.shape), value, other)

    inverse_listed = lax.rsqrt(valid(listed_squares, 1.0) + EPSILON * EPSILON)
    inverse = lax.rsqrt(squares + EPSILON * EPSILON)
    inverse_ref[...] = inverse
    inverse_query = inverse_listed[7:8, :]
    picked = jnp.zeros((count, LANES), jnp.float32)
    for k in range(8):
        hot = positive_hot_ref[:, LANES * k : LANES * (k + 1)].astype(jnp.float32)
        picked = picked + hot * inverse[k : k + 1, :]
    inverse_positive = jnp.sum(picked, axis=1, keepdims=True)
    logits = valid(with_positives, 0.0) * inverse_positive * inverse_query / SOFTMAX_TEMPER
    hard = valid(hard, 0.0) * inverse_listed * inverse_query / SOFTMAX_TEMPER
    is_hard = iota(hard.shape, 0) < 7
    is_own = iota(logits.shape, 0) == iota(logits.shape, 1) + first_query
    is_own = is_own & in_first_half(logits.shape)
    weights = valid(jnp.exp(logits - 1.0 / SOFTMAX_TEMPER), 1.0)
    hard_weights = jnp.where(is_hard, jnp.exp(hard - 1.0 / SOFTMAX_TEMPER), 0.0)
    totals = jnp.sum(weights, axis=0, keepdims=True) + jnp.sum(hard_weights, axis=0, keepdims=True)
    target = jnp.sum(jnp.where(is_own, logits, 0.0), axis=0, keepdims=True)
    losses = jnp.log(totals) + 1.0 / SOFTMAX_TEMPER - target
    scaling_factor = LOSS_MULTIPLIER / (count * SOFTMAX_TEMPER)

    def rounded(value):
        return value.astype(jnp.bfloat16).astype(jnp.float32)

    coef = rounded(scaling_factor * (weights / totals - is_own.astype(jnp.float32)))
    hard_coef = rounded(scaling_factor * (hard_weights / totals))
    weighted = valid(coef * logits * SOFTMAX_TEMPER, 0.0)
    hard_weighted = jnp.where(is_hard, hard_coef * hard * SOFTMAX_TEMPER, 0.0)
    along_query = jnp.sum(weighted, axis=0, keepdims=True) + jnp.sum(
        hard_weighted, axis=0, keepdims=True
    )
    folded_coef = fold_half(coef[:start], coef[start:], 0)
    folded_hard = fold_half(
        jnp.where(is_hard, hard_coef, along_query), jnp.where(is_hard, hard_weighted, losses), 0
    )
    for k in range(out_ref.shape[0]):
        out_ref[k, :start, :] = folded_coef
        out_ref[k, start : start + 8, :] = folded_hard
        out_ref[k, start + 8 :, :] = jnp.zeros_like(out_ref[k, start + 8 :, :])
        columns_to_lanes(
            jnp.sum(weighted, axis=1, keepdims=True), out_ref.at[k, start + 8 : start + 16]
        )


def resid_grad_kernel(
    both_ref,
    inverse_ref,
    rows_ref,
    positive_hot_ref,
    query_hot_ref,
    listed_ref,
    resid_ref,
    gains_ref,
    out_ref,
    loss_ref,
):
    sequences = resid_ref.shape[0]
    count, total_rows = positive_hot_ref.shape
    z = lax.axis_index("z_far") * lax.axis_size("z_pair") + lax.axis_index("z_pair")
    group = z * lax.axis_size("core") + lax.axis_index("core")
    first_row = group * sequences
    first_query = group * QDEV
    across = (((1,), (1,)), ((), ()))

    def joined(start, stop):
        firsts, seconds = [], []
        for k in (0, 2):
            first, second = both_ref[k, start:stop, :], both_ref[k + 1, start:stop, :]
            firsts.append(fold_half(first, second, 0))
            seconds.append(fold_half(pltpu.roll(first, HALF, 1), pltpu.roll(second, HALF, 1), 0))
        return jnp.concatenate(firsts, axis=1), jnp.concatenate(seconds, axis=1)

    start = count // 2
    coef16 = jnp.concatenate(joined(0, start), axis=0).astype(jnp.bfloat16)
    hard, hard_weighted = joined(start, start + 8)
    along_passage = both_ref[0, start + 8 : start + 16, :]
    for k in range(1, both_ref.shape[0]):
        along_passage = along_passage + both_ref[k, start + 8 : start + 16, :]
    along_passage = jnp.concatenate([along_passage[0:1], along_passage[1:2]], axis=1)
    inverse = jnp.concatenate([inverse_ref[k : k + 1, :] for k in range(8)], axis=1)

    own_row = first_row + iota((sequences, count), 0)
    own_query = (iota((sequences, count), 0) < QDEV) & (
        iota((sequences, count), 1) == first_query + iota((sequences, count), 0)
    )
    own_positive = listed_ref[8:9, :] == own_row
    to_positives = lax.dot_general(
        own_query.astype(jnp.bfloat16), coef16, across, preferred_element_type=jnp.float32
    )
    to_queries = jnp.dot(
        own_positive.astype(jnp.bfloat16), coef16, preferred_element_type=jnp.float32
    )
    along = jnp.sum(
        jnp.where(own_query, hard[7:8, :], 0.0) + jnp.where(own_positive, along_passage, 0.0),
        axis=1,
        keepdims=True,
    )
    for j in range(7):
        listed = listed_ref[j : j + 1, :] == own_row
        to_queries = to_queries + jnp.where(listed, hard[j : j + 1, :], 0.0)
        along = along + jnp.sum(
            jnp.where(listed, hard_weighted[j : j + 1, :], 0.0), axis=1, keepdims=True
        )
    matrix = jnp.dot(
        to_positives.astype(jnp.bfloat16), positive_hot_ref[...], preferred_element_type=jnp.float32
    ) + jnp.dot(
        to_queries.astype(jnp.bfloat16), query_hot_ref[...], preferred_element_type=jnp.float32
    )
    row_index = iota((sequences, total_rows), 1)
    for j in range(7):
        own_hard = jnp.sum(jnp.where(own_query, hard[j : j + 1, :], 0.0), axis=1, keepdims=True)
        own_listed = jnp.where(own_query, listed_ref[j : j + 1, :].astype(jnp.float32), 0.0)
        own_listed = jnp.sum(own_listed, axis=1, keepdims=True).astype(jnp.int32)
        listed = row_index == own_listed
        matrix = matrix + jnp.where(listed, own_hard, 0.0)
    matrix = matrix * inverse
    high = matrix.astype(jnp.bfloat16)
    low = (matrix - high.astype(jnp.float32)).astype(jnp.bfloat16)
    rows = rows_ref[...]
    d_embed = jnp.dot(high, rows, preferred_element_type=jnp.float32) + jnp.dot(
        low, rows, preferred_element_type=jnp.float32
    )

    is_own_row = row_index == first_row + iota((sequences, total_rows), 0)
    own_inverse = jnp.sum(jnp.where(is_own_row, inverse, 0.0), axis=1, keepdims=True)
    resid = resid_ref[...]
    gain = own_columns(gains_ref, resid.shape[1])
    features = gains_ref.shape[1]
    d_resid = own_inverse * gain * (
        d_embed - resid * gain * own_inverse * along
    ) - resid * (along * own_inverse * own_inverse * (EPSILON / features))
    d_resid16 = d_resid.astype(jnp.bfloat16)
    for t in range(out_ref.shape[0]):
        out_ref[t] = d_resid16
    loss_ref[0] = jnp.sum(hard_weighted[7:8, :]) / count


def kernel_call(body, outs, arrays, after=(), scratch=()):
    count = len(arrays)

    def kernel(*refs):
        body(*refs[:count], *refs[count + len(after) :])

    def out_spec(shape):
        return pl.BlockSpec(memory_space=pltpu.SMEM if shape == (1,) else pltpu.VMEM)

    return pl.pallas_call(
        kernel,
        out_shape=[jax.ShapeDtypeStruct(shape, dtype) for shape, dtype in outs],
        in_specs=[pl.BlockSpec(memory_space=pltpu.VMEM)] * count
        + [pl.BlockSpec(memory_space=pl.ANY)] * len(after),
        out_specs=[out_spec(shape) for shape, _ in outs],
        scratch_shapes=list(scratch),
        compiler_params=pltpu.CompilerParams(vmem_limit_bytes=VMEM_BYTES),
    )(*arrays, *after)


def candidate_kernel(positives_ref, negatives_ref, listed_ref, query_hot_ref, positive_hot_ref):
    query_count, total_rows = query_hot_ref.shape
    groups = query_count // QDEV
    sequences = total_rows // groups
    others = sequences - QDEV

    def row_of(passage):
        at = ((passage.astype(jnp.float32) + 0.5) * (1.0 / others)).astype(jnp.int32)
        return passage + at * QDEV + QDEV

    def query_row(query):
        return query + query // QDEV * others

    positive_row = row_of(positives_ref[...])
    count = negatives_ref.shape[0]
    listed_ref[:count, :] = row_of(negatives_ref[...])
    listed_ref[count : count + 1, :] = query_row(iota((1, query_count), 1))
    listed_ref[count + 1 :, :] = jnp.broadcast_to(
        positive_row, (listed_ref.shape[0] - count - 1, query_count)
    )
    shape = (LANES, total_rows)
    diagonal = iota((LANES, LANES), 0) == iota((LANES, LANES), 1)
    for k in range(query_count // LANES):
        rows = slice(LANES * k, LANES * (k + 1))
        query = query_row(iota(shape, 0) + LANES * k)
        query_hot_ref[rows, :] = (query == iota(shape, 1)).astype(jnp.float32).astype(jnp.bfloat16)
        lanes = positive_row[:, rows].astype(jnp.float32)
        column = jnp.sum(jnp.where(diagonal, lanes, 0.0), axis=1, keepdims=True)
        positive_hot_ref[rows, :] = (
            (column.astype(jnp.int32) == iota(shape, 1)).astype(jnp.float32).astype(jnp.bfloat16)
        )


def transpose_kernel(given_ref, out_ref, token_ref):
    out_ref[...] = given_ref[...].T
    token_ref[0] = jnp.float32(0.0)


def half_weights_kernel(kv_ref, query_ref, kept_ref, sent_ref):
    width, rows = kept_ref.shape[1], kv_ref.shape[1]
    parity = lax.axis_index("tensor") % 2
    for out_ref, half in ((kept_ref, parity), (sent_ref, 1 - parity)):
        features = pl.ds(pl.multiple_of(half * width, width), width)
        out_ref[:rows, :] = kv_ref[features, :].T
        out_ref[rows:, :] = query_ref[features, :].T


def stack_kernel(first_ref, second_ref, out_ref, token_ref):
    rows = first_ref.shape[0]
    out_ref[:rows, :] = first_ref[...]
    out_ref[rows:, :] = second_ref[...]
    token_ref[0] = jnp.float32(0.0)


def contrast(everyone, resid, gains, tables, after):
    tensor_count = lax.axis_size("tensor")
    sequences, width = resid.shape
    listed, query_hot, positive_hot = tables
    count, total_rows = positive_hot.shape
    rows = everyone.reshape(total_rows, width)
    (sent,) = kernel_call(
        partial_logits_kernel,
        [((tensor_count, count // 2 + 32, LANES), jnp.bfloat16)],
        [rows, query_hot, positive_hot, listed, gains],
        after=after,
        scratch=[pltpu.VMEM((24, LANES), jnp.float32)],
    )
    arrived = exchange(sent, "tensor")
    coefs, inverse = kernel_call(
        softmax_kernel,
        [((4, count // 2 + 16, LANES), jnp.float32), ((8, LANES), jnp.float32)],
        [arrived, positive_hot],
    )
    both = exchange(coefs, ("z_pair", "core"))
    d_resid16, loss = kernel_call(
        resid_grad_kernel,
        [((tensor_count, sequences, width), jnp.bfloat16), ((1,), jnp.float32)],
        [both, inverse, rows, positive_hot, query_hot, listed, resid, gains],
    )
    return loss, exchange(d_resid16, "tensor")


def copied_norm_kernel(hidden_ref, gain_ref, out_ref):
    hidden32 = hidden_ref[...].astype(jnp.float32)
    normed = (hidden32 * rms_scale(hidden32) * gain_ref[...]).astype(jnp.bfloat16)
    height = normed.shape[0]
    for c in range(normed.shape[1] // LANES):
        block = normed[:, LANES * c : LANES * (c + 1)]
        for t in range(out_ref.shape[0]):
            out_ref[t, height * c : height * (c + 1), :] = block


def projection_kernel(rows_ref, kv_weights_ref, query_weights_ref, kv_ref, sent_ref, query_ref):
    tensor_count, tall, _ = rows_ref.shape
    blocks = kv_weights_ref.shape[0] // LANES
    height = tall // blocks

    def block(c):
        part = rows_ref[:, height * c : height * (c + 1), :]
        return part.reshape(tensor_count * height, LANES)

    kv = jnp.zeros(kv_ref.shape, jnp.float32)
    query = jnp.zeros(query_ref.shape, jnp.float32)
    for c in range(0, blocks, 2):
        rows = jnp.concatenate([block(c), block(c + 1)], axis=1)
        columns = slice(LANES * c, LANES * (c + 2))
        kv = kv + jnp.dot(rows, kv_weights_ref[columns, :], preferred_element_type=jnp.float32)
        query = query + jnp.dot(
            rows, query_weights_ref[columns, :], preferred_element_type=jnp.float32
        )
    kv_ref[...] = kv
    sent_ref[...] = kv.astype(jnp.bfloat16)
    query_ref[...] = query


def half_turned(tensor, cosine, signed_sine):
    halfway = tensor.shape[1] // 2
    return tensor * cosine + pltpu.roll(tensor, halfway, 1) * signed_sine


def is_even_tensor():
    return lax.axis_index("tensor") % 2 == 0


def attention_kernel(
    own_ref,
    other_ref,
    query_all_ref,
    layout_ref,
    q_gain_ref,
    k_gain_ref,
    hidden_ref,
    wo_ref,
    out_ref,
    saved_ref,
):
    root = math.sqrt(own_ref.shape[1])
    tokens_count, sequences, own_rows = own_ref.shape[0], out_ref.shape[1], hidden_ref.shape[0]
    at, _ = layout_rows(tokens_count, sequences, own_rows)
    to, _ = saved_rows(tokens_count, sequences)
    is_even = is_even_tensor()
    own, other = own_ref[...], other_ref[...].astype(jnp.float32)
    key_raw = jnp.where(is_even, own, other)
    value16 = jnp.where(is_even, other, own).astype(jnp.bfloat16)
    query_raw = jnp.dot(
        unfolded(layout_ref[at["chosen"], :], sequences),
        query_all_ref[...],
        precision=lax.Precision.HIGHEST,
        preferred_element_type=jnp.float32,
    )
    q_gain, k_gain = q_gain_ref[...], k_gain_ref[...]
    key16 = half_turned(
        key_raw * rms_scale(key_raw) * k_gain,
        layout_ref[at["key_cosine"], :],
        layout_ref[at["key_sine"], :],
    ).astype(jnp.bfloat16)
    query16 = half_turned(
        query_raw * rms_scale(query_raw) * q_gain,
        layout_ref[at["query_cosine"], :],
        layout_ref[at["query_sine"], :],
    ).astype(jnp.bfloat16)
    shift = (
        root
        * jnp.max(q_gain, axis=1, keepdims=True)
        * jnp.max(k_gain, axis=1, keepdims=True)
    )
    scores = (
        lax.dot_general(
            query16, key16, (((1,), (1,)), ((), ())), preferred_element_type=jnp.float32
        )
        / root
    )
    inside = unfolded(layout_ref[at["inside"], :], sequences)
    weights = jnp.where(inside > 0.0, jnp.exp(scores - shift), 0.0)
    probs = weights / jnp.sum(weights, axis=1, keepdims=True)
    attn16 = jnp.dot(
        probs.astype(jnp.bfloat16), value16, preferred_element_type=jnp.float32
    ).astype(jnp.bfloat16)
    own_last = layout_ref[at["own_last"], :][:, :own_rows].astype(jnp.bfloat16)
    chunk = out_ref.shape[2]
    for t in range(out_ref.shape[0]):
        columns = slice(t * chunk, (t + 1) * chunk)
        block = jnp.dot(attn16, wo_ref[:, columns], preferred_element_type=jnp.float32)
        block = block + jnp.dot(
            own_last, hidden_ref[:, columns], preferred_element_type=jnp.float32
        )
        out_ref[t] = block.astype(jnp.bfloat16)
    saved_ref[to["key_raw"], :] = key_raw
    saved_ref[to["key"], :] = key16.astype(jnp.float32)
    saved_ref[to["value"], :] = value16.astype(jnp.float32)
    saved_ref[to["query_raw"], :] = query_raw
    saved_ref[to["query"], :] = query16.astype(jnp.float32)
    saved_ref[to["probs"], :] = folded(probs)


def resid_kernel(arrived_ref, gains_ref, resid_ref, out_ref):
    gain = own_columns(gains_ref, resid_ref.shape[1])
    resid = arrived_ref[0].astype(jnp.float32)
    for t in range(1, arrived_ref.shape[0]):
        resid = resid + arrived_ref[t].astype(jnp.float32)
    resid_ref[...] = resid
    scaled16 = (resid * gain).astype(jnp.bfloat16)
    for t in range(out_ref.shape[0]):
        out_ref[t] = scaled16


def gradient_kernel(
    d_resid_ref, wo_t_ref, saved_ref, layout_ref, q_gain_ref, k_gain_ref, own_ref, sent_ref
):
    head_width = saved_ref.shape[1]
    root = math.sqrt(head_width)
    sequences = d_resid_ref.shape[1]
    tensor_count = d_resid_ref.shape[0]
    tokens_count = (own_ref.shape[0] - sequences) // 2
    at, _ = layout_rows(tokens_count, sequences, tokens_count // tensor_count)
    to, _ = saved_rows(tokens_count, sequences)
    chunk = d_resid_ref.shape[2]
    d_attn = jnp.dot(d_resid_ref[0], wo_t_ref[:chunk, :], preferred_element_type=jnp.float32)
    for t in range(1, d_resid_ref.shape[0]):
        d_attn = d_attn + jnp.dot(
            d_resid_ref[t],
            wo_t_ref[t * chunk : (t + 1) * chunk, :],
            preferred_element_type=jnp.float32,
        )
    d_attn16 = d_attn.astype(jnp.bfloat16)
    probs = unfolded(saved_ref[to["probs"], :], sequences)
    key16 = saved_ref[to["key"], :].astype(jnp.bfloat16)
    query16 = saved_ref[to["query"], :].astype(jnp.bfloat16)
    value16 = saved_ref[to["value"], :].astype(jnp.bfloat16)
    d_probs = lax.dot_general(
        d_attn16, value16, (((1,), (1,)), ((), ())), preferred_element_type=jnp.float32
    )
    d_scores16 = (
        probs * (d_probs - jnp.sum(probs * d_probs, axis=1, keepdims=True)) / root
    ).astype(jnp.bfloat16)
    down = (((0,), (0,)), ((), ()))
    d_query_rot = jnp.dot(d_scores16, key16, preferred_element_type=jnp.float32)
    d_key_rot = lax.dot_general(d_scores16, query16, down, preferred_element_type=jnp.float32)
    d_value = lax.dot_general(
        probs.astype(jnp.bfloat16), d_attn16, down, preferred_element_type=jnp.float32
    )

    def head_gradient(grad_rot, name, gain):
        raw = saved_ref[to[name + "_raw"], :]
        inverse = rms_scale(raw)
        turned_back = half_turned(
            grad_rot, layout_ref[at[name + "_cosine"], :], -layout_ref[at[name + "_sine"], :]
        )
        return norm_backward(turned_back, raw * inverse, inverse, gain)

    d_key = head_gradient(d_key_rot, "key", k_gain_ref[...])
    d_query = head_gradient(d_query_rot, "query", q_gain_ref[...])
    own = jnp.concatenate([d_key, d_value, d_query], axis=0)
    own_ref[...] = own
    sent_ref[...] = own.astype(jnp.bfloat16)


def added_kernel(d_resid_ref, layout_ref, out_ref, token_ref):
    own_rows = out_ref.shape[0]
    tensor_count, sequences, chunk = d_resid_ref.shape
    at, _ = layout_rows(own_rows * tensor_count, sequences, own_rows)
    last = layout_ref[at["own_last_t"], :][:, :sequences].astype(jnp.bfloat16)
    for t in range(tensor_count):
        out_ref[:, t * chunk : (t + 1) * chunk] = jnp.dot(
            last, d_resid_ref[t], preferred_element_type=jnp.float32
        )
    token_ref[0] = jnp.float32(0.0)


def product_kernel(own_ref, other_ref, layout_ref, weights_ref, out_ref):
    tensor_count, tall, _ = out_ref.shape
    height = tall * LANES // weights_ref.shape[1]
    tokens_count = height * tensor_count
    sequences = own_ref.shape[0] - 2 * tokens_count
    at, _ = layout_rows(tokens_count, sequences, height)
    chosen = unfolded(layout_ref[at["chosen"], :], sequences).astype(jnp.bfloat16)

    def spread(d_query):
        return lax.dot_general(
            chosen,
            d_query.astype(jnp.bfloat16),
            (((0,), (0,)), ((), ())),
            preferred_element_type=jnp.float32,
        )

    own, other = own_ref[...], other_ref[...].astype(jnp.float32)
    d_key = own[:tokens_count] + other[:tokens_count]
    d_value = own[tokens_count : 2 * tokens_count] + other[tokens_count : 2 * tokens_count]
    is_even = is_even_tensor()
    gradients = jnp.concatenate(
        [
            jnp.where(is_even, d_key, d_value),
            spread(own[2 * tokens_count :]),
            jnp.where(is_even, d_value, d_key),
            spread(other[2 * tokens_count :]),
        ],
        axis=1,
    ).astype(jnp.bfloat16)
    wide = 2 * LANES
    for k in range(weights_ref.shape[1] // wide):
        term = jnp.dot(
            gradients, weights_ref[:, wide * k : wide * (k + 1)], preferred_element_type=jnp.float32
        ).astype(jnp.bfloat16)
        for c in (2 * k, 2 * k + 1):
            block = term[:, LANES * (c - 2 * k) : LANES * (c - 2 * k + 1)]
            out_ref[:, height * c : height * (c + 1), :] = block.reshape(-1, height, LANES)


def d_hidden_kernel(terms_ref, hidden_ref, gain_ref, added_ref, out_ref):
    hidden32 = hidden_ref[...].astype(jnp.float32)
    height = hidden32.shape[0]
    parts = []
    for parity in range(2):
        total = terms_ref[parity].astype(jnp.float32)
        for t in range(parity + 2, terms_ref.shape[0], 2):
            total = total + terms_ref[t].astype(jnp.float32)
        parts += [total[height * c : height * (c + 1)] for c in range(total.shape[0] // height)]
    d_normed = jnp.concatenate(parts, axis=1)
    inverse = rms_scale(hidden32)
    d_hidden = norm_backward(d_normed, hidden32 * inverse, inverse, gain_ref[...])
    out_ref[...] = (d_hidden + added_ref[...]).astype(jnp.bfloat16)


def packed_rows(sizes):
    starts, total = {}, 0
    for name, rows in sizes:
        starts[name] = slice(total, total + rows)
        total += rows
    return starts, total


def layout_rows(tokens_count, sequences, own_rows):
    wide = sequences * tokens_count // LANES
    return packed_rows(
        [
            ("key_cosine", tokens_count),
            ("key_sine", tokens_count),
            ("query_cosine", sequences),
            ("query_sine", sequences),
            ("inside", wide),
            ("chosen", wide),
            ("own_last", sequences),
            ("own_last_t", own_rows),
        ]
    )


def saved_rows(tokens_count, sequences):
    return packed_rows(
        [
            ("key_raw", tokens_count),
            ("key", tokens_count),
            ("value", tokens_count),
            ("query_raw", sequences),
            ("query", sequences),
            ("probs", sequences * tokens_count // LANES),
        ]
    )


def folded(block):
    parts = [block[:, LANES * k : LANES * (k + 1)] for k in range(block.shape[1] // LANES)]
    return jnp.concatenate(parts, axis=0)


def unfolded(block, rows):
    parts = [block[rows * k : rows * (k + 1)] for k in range(block.shape[0] // rows)]
    return jnp.concatenate(parts, axis=1)


def sequence_kernel(lengths_ref, out_ref, token_ref, *, tokens_count, own_rows):
    token_ref[0] = jnp.float32(0.0)
    sequences = lengths_ref.shape[1]
    at, _ = layout_rows(tokens_count, sequences, own_rows)
    lengths = lengths_ref[...].astype(jnp.float32)
    square = (sequences, sequences)
    ends = jnp.sum(
        jnp.where(iota(square, 1) <= iota(square, 0), lengths, 0.0), axis=1, keepdims=True
    )
    own_length = jnp.sum(
        jnp.where(iota(square, 1) == iota(square, 0), lengths, 0.0), axis=1, keepdims=True
    )
    starts = ends - own_length
    ends_row = jnp.sum(
        jnp.where(iota(square, 0) <= iota(square, 1), own_length, 0.0), axis=0, keepdims=True
    )
    starts_row = ends_row - lengths
    token = iota((sequences, tokens_count), 1).astype(jnp.float32)
    out_ref[at["inside"], :] = folded(((token >= starts) & (token < ends)).astype(jnp.float32))
    out_ref[at["chosen"], :] = folded((token == ends - 1.0).astype(jnp.float32))
    first = (lax.axis_index("tensor") * own_rows).astype(jnp.float32)
    own_token = iota((sequences, LANES), 1).astype(jnp.float32) + first
    own_token = jnp.where(iota((sequences, LANES), 1) < own_rows, own_token, -1.0)
    out_ref[at["own_last"], :] = (own_token == ends - 1.0).astype(jnp.float32)
    own_token = iota((own_rows, sequences), 0).astype(jnp.float32) + first
    own_last_t = (own_token == ends_row - 1.0).astype(jnp.float32)
    out_ref[at["own_last_t"], :] = jnp.concatenate(
        [own_last_t, jnp.zeros((own_rows, LANES - sequences), jnp.float32)], axis=1
    )
    token = iota((tokens_count, sequences), 0).astype(jnp.float32)
    held = (token >= starts_row) & (token < ends_row)
    position = jnp.sum(jnp.where(held, token - starts_row, 0.0), axis=1, keepdims=True)
    lane = iota((1, LANES), 1)
    halfway = LANES // 2
    pair = jnp.where(lane < halfway, lane, lane - halfway).astype(jnp.float32)
    frequency = jnp.exp(pair * (-2.0 / LANES * math.log(ROPE_BASE)))
    sign = jnp.where(lane < halfway, -1.0, 1.0)
    for name, place in (("key", position), ("query", own_length - 1.0)):
        angles = place * frequency
        out_ref[at[name + "_cosine"], :] = jnp.cos(angles)
        out_ref[at[name + "_sine"], :] = jnp.sin(angles) * sign


def on_device(
    hidden, lengths, positives, negatives, in_gain, wq, wkv, q_gain, k_gain, wo, out_gain
):
    tensor_count = lax.axis_size("tensor")
    z_count = lax.axis_size("z_far") * lax.axis_size("z_pair")
    own_rows, features = hidden.shape
    tokens_count = own_rows * tensor_count
    head_width = wq.shape[1]
    sequences = lengths.shape[1]
    query_count = positives.shape[0]
    total_rows = query_count // QDEV * sequences
    chunk = features // tensor_count
    f32, bf16 = jnp.float32, jnp.bfloat16
    head = (tokens_count, head_width)
    weights_shape = (head_width, features)
    flat = (tensor_count, own_rows * features // LANES, LANES)
    gain_rows = [q_gain[None, :], k_gain[None, :]]

    (copies,) = kernel_call(
        copied_norm_kernel, [(flat, bf16)], [hidden, in_gain[None, :]]
    )
    piece = exchange(copies, "tensor")
    kv_own, kv_own16, query_all = kernel_call(
        projection_kernel, [(head, f32), (head, bf16), (head, f32)], [piece, wkv, wq]
    )
    kv_other = swapped(kv_own16, "tensor", 0)
    def sequence_layout(after):
        return kernel_call(
            functools.partial(sequence_kernel, tokens_count=tokens_count, own_rows=own_rows),
            [((layout_rows(tokens_count, sequences, own_rows)[1], LANES), f32), ((1,), f32)],
            [lengths],
            after=[after],
        )

    layout, _ = sequence_layout(query_all)
    blocks, saved = kernel_call(
        attention_kernel,
        [
            ((tensor_count, sequences, chunk), bf16),
            ((saved_rows(tokens_count, sequences)[1], LANES), f32),
        ],
        [kv_own, kv_other, query_all, layout, *gain_rows, hidden, wo],
    )
    half_shape = (2 * head_width, features // 2)
    kept_weights, sent_weights = kernel_call(
        half_weights_kernel, [(half_shape, bf16), (half_shape, bf16)], [wkv, wq], after=[query_all]
    )
    other_weights = swapped(sent_weights, "tensor", 0)
    output_gain = out_gain[None, :]
    resid, scaled = kernel_call(
        resid_kernel,
        [((sequences, chunk), f32), ((z_count, sequences, chunk), bf16)],
        [exchange(blocks, "tensor"), output_gain],
    )
    wo_t, transposed = kernel_call(
        transpose_kernel, [((features, head_width), bf16), ((1,), f32)], [wo], after=[resid]
    )
    pair_weights, fetched = kernel_call(
        stack_kernel,
        [((4 * head_width, features // 2), bf16), ((1,), f32)],
        [kept_weights, other_weights],
    )
    layout_again, placed = sequence_layout(resid)
    tables = kernel_call(
        candidate_kernel,
        [
            ((16, query_count), jnp.int32),
            ((query_count, total_rows), bf16),
            ((query_count, total_rows), bf16),
        ],
        [positives[None, :], negatives.T],
        after=[resid],
    )
    everyone = lax.all_gather(exchange(scaled, ("z_far", "z_pair")), "core", axis=1)
    loss, d_resid16 = contrast(
        everyone, resid, output_gain, tables, [transposed, fetched, placed]
    )
    gradient_shape = (2 * tokens_count + sequences, head_width)
    own_gradients, sent_gradients = kernel_call(
        gradient_kernel,
        [(gradient_shape, f32), (gradient_shape, bf16)],
        [d_resid16, wo_t, saved, layout_again, *gain_rows],
        after=[loss],
    )
    other_gradients = swapped(sent_gradients, "tensor", 0)
    added, summed = kernel_call(
        added_kernel, [((own_rows, features), f32), ((1,), f32)], [d_resid16, layout_again]
    )
    (product,) = kernel_call(
        product_kernel,
        [((tensor_count, own_rows * features // LANES // 2, LANES), bf16)],
        [own_gradients, other_gradients, layout_again, pair_weights],
        after=[summed],
    )
    terms = exchange(product, "tensor")
    (d_hidden,) = kernel_call(
        d_hidden_kernel,
        [((own_rows, features), bf16)],
        [terms, hidden, in_gain[None, :], added],
    )
    return (d_hidden, loss[0])


def solution(mesh):
    z_count = mesh.shape["dp"] // 2
    chips = mesh.devices.reshape(z_count // 2, 2, 2, mesh.shape["tensor"])
    mesh = jax.sharding.Mesh(chips, ("z_far", "z_pair", "core", "tensor"))
    everywhere = P(("z_far", "z_pair", "core", "tensor"), None)
    placed = (
        everywhere,
        P(("z_far", "z_pair", "core"), None),
        P(),
        P(),
        P(),
        P(None, "tensor"),
        P(None, "tensor"),
        P(),
        P(),
        P("tensor", None),
        P(),
    )
    return jax.shard_map(
        on_device, mesh=mesh, in_specs=placed, out_specs=(everywhere, P()), check_vma=False
    )
```

```python
import functools
import math

import jax
import jax.numpy as jnp
from jax import lax
from jax.experimental import pallas as pl
from jax.experimental.pallas import tpu as pltpu
from jax.sharding import PartitionSpec as P

QDEV = 8
LANES = 128
VMEM_BYTES = 32 * 2**20


EPSILON = 1e-06
SOFTMAX_TEMPER = 0.05
LOSS_MULTIPLIER = 8192.0
ROPE_BASE = 1000000.0


def swapped(value, axis, apart):
    mask = 2**apart
    pairs = [(source, source ^ mask) for source in range(lax.axis_size(axis))]
    return lax.ppermute(value, axis, pairs)


def rms_scale(tensor):
    return lax.rsqrt(jnp.mean(tensor * tensor, axis=-1, keepdims=True) + EPSILON)


def norm_backward(grad, unit_form, inverse, gain):
    scaled = grad * gain
    return inverse * (scaled - unit_form * jnp.mean(unit_form * scaled, axis=-1, keepdims=True))


def exchange(blocks, axis):
    return lax.all_to_all(blocks, axis, 0, 0, tiled=True)


def halves(value):
    high = value.astype(jnp.bfloat16).astype(jnp.float32)
    return high, value - high


def iota(shape, axis):
    return lax.broadcasted_iota(jnp.int32, shape, axis)


def columns_to_lanes(column, out_ref):
    diagonal = iota((LANES, LANES), 0) == iota((LANES, LANES), 1)
    for k in range(column.shape[0] // LANES):
        block = jnp.where(diagonal, column[LANES * k : LANES * (k + 1)], 0.0)
        out_ref[k : k + 1, :] = jnp.sum(block, axis=0, keepdims=True)


HALF = LANES // 2


def query_block():
    return lax.axis_index("z_pair"), lax.axis_index("core")


def block_lanes(block):
    return pl.ds(pl.multiple_of(block * LANES, LANES), LANES)


def in_first_half(shape):
    return iota(shape, len(shape) - 1) < HALF


def fold_half(first, second, half):
    is_first = in_first_half(first.shape)
    low = jnp.where(is_first, first, pltpu.roll(second, HALF, 1))
    high = jnp.where(is_first, pltpu.roll(first, HALF, 1), second)
    return jnp.where(half == 0, low, high)


def unfold_half(block):
    return block, pltpu.roll(block, HALF, 1)


def own_columns(gains_ref, width):
    start = pl.multiple_of(lax.axis_index("tensor") * width, width)
    return gains_ref[:, pl.ds(start, width)]


def partial_logits_kernel(
    rows_ref, query_hot_ref, positive_hot_ref, listed_all_ref, gains_ref, out_ref, held_ref
):
    rows = rows_ref[...]
    query_at, half = query_block()
    listed_ref = listed_all_ref[:8, block_lanes(query_at)]
    block_hot = query_hot_ref[block_lanes(query_at), :]
    queries = jnp.dot(block_hot, rows, preferred_element_type=jnp.float32)
    positives = jnp.dot(positive_hot_ref[...], rows, preferred_element_type=jnp.float32)
    queries = queries.astype(jnp.bfloat16)
    features = gains_ref.shape[1]
    rows32 = rows.astype(jnp.float32)
    plain = rows32 * (1.0 / own_columns(gains_ref, rows.shape[1]))
    squares = jnp.sum(rows32 * rows32, axis=1, keepdims=True) + jnp.sum(
        plain * plain, axis=1, keepdims=True
    ) * (EPSILON / features)
    against = (((1,), (1,)), ((), ()))
    with_positives = lax.dot_general(
        positives.astype(jnp.bfloat16), queries, against, preferred_element_type=jnp.float32
    )
    with_all = lax.dot_general(rows, queries, against, preferred_element_type=jnp.float32)
    squares_all = jnp.broadcast_to(squares, with_all.shape)
    row_index = iota((LANES, LANES), 0)
    for j in range(8):
        product = jnp.zeros((LANES, LANES), jnp.float32)
        square = product
        for k in range(with_all.shape[0] // LANES):
            rows_at = slice(LANES * k, LANES * (k + 1))
            hit = row_index == listed_ref[j : j + 1, :] - LANES * k
            product = jnp.where(hit, with_all[rows_at], product)
            square = jnp.where(hit, squares_all[rows_at], square)
        held_ref[j : j + 1, :] = jnp.sum(product, axis=0, keepdims=True)
        held_ref[8 + j : 9 + j, :] = jnp.sum(square, axis=0, keepdims=True)
    columns_to_lanes(squares, held_ref.at[16:24])
    count = with_positives.shape[0] // 2
    sent = fold_half(with_positives[:count], with_positives[count:], half).astype(jnp.bfloat16)
    high, low = halves(held_ref[0:16, :])
    listed16 = fold_half(high, low, half).astype(jnp.bfloat16)
    squares16 = jnp.concatenate(halves(held_ref[16:24, :])).astype(jnp.bfloat16)
    for t in range(out_ref.shape[0]):
        out_ref[t, :count, :] = sent
        out_ref[t, count : count + 16, :] = listed16
        out_ref[t, count + 16 : count + 32, :] = squares16


def softmax_kernel(arrived_ref, positive_hot_ref, out_ref, inverse_ref):
    count = positive_hot_ref.shape[0]
    summed = arrived_ref[0].astype(jnp.float32)
    for t in range(1, arrived_ref.shape[0]):
        summed = summed + arrived_ref[t].astype(jnp.float32)
    query_at, half = query_block()
    first_query = query_at * LANES + half * HALF
    start = count // 2
    with_positives = jnp.concatenate(unfold_half(summed[:start]), axis=0)
    high, low = unfold_half(summed[start : start + 16])
    hard, listed_squares = high[:8] + low[:8], high[8:] + low[8:]
    squares = summed[start + 16 : start + 24] + summed[start + 24 : start + 32]

    def valid(value, other):
        return jnp.where(in_first_half(value.shape), value, other)

    inverse_listed = lax.rsqrt(valid(listed_squares, 1.0) + EPSILON * EPSILON)
    inverse = lax.rsqrt(squares + EPSILON * EPSILON)
    inverse_ref[...] = inverse
    inverse_query = inverse_listed[7:8, :]
    picked = jnp.zeros((count, LANES), jnp.float32)
    for k in range(8):
        hot = positive_hot_ref[:, LANES * k : LANES * (k + 1)].astype(jnp.float32)
        picked = picked + hot * inverse[k : k + 1, :]
    inverse_positive = jnp.sum(picked, axis=1, keepdims=True)
    logits = valid(with_positives, 0.0) * inverse_positive * inverse_query / SOFTMAX_TEMPER
    hard = valid(hard, 0.0) * inverse_listed * inverse_query / SOFTMAX_TEMPER
    is_hard = iota(hard.shape, 0) < 7
    is_own = iota(logits.shape, 0) == iota(logits.shape, 1) + first_query
    is_own = is_own & in_first_half(logits.shape)
    weights = valid(jnp.exp(logits - 1.0 / SOFTMAX_TEMPER), 1.0)
    hard_weights = jnp.where(is_hard, jnp.exp(hard - 1.0 / SOFTMAX_TEMPER), 0.0)
    totals = jnp.sum(weights, axis=0, keepdims=True) + jnp.sum(hard_weights, axis=0, keepdims=True)
    target = jnp.sum(jnp.where(is_own, logits, 0.0), axis=0, keepdims=True)
    losses = jnp.log(totals) + 1.0 / SOFTMAX_TEMPER - target
    scaling_factor = LOSS_MULTIPLIER / (count * SOFTMAX_TEMPER)

    def rounded(value):
        return value.astype(jnp.bfloat16).astype(jnp.float32)

    coef = rounded(scaling_factor * (weights / totals - is_own.astype(jnp.float32)))
    hard_coef = rounded(scaling_factor * (hard_weights / totals))
    weighted = valid(coef * logits * SOFTMAX_TEMPER, 0.0)
    hard_weighted = jnp.where(is_hard, hard_coef * hard * SOFTMAX_TEMPER, 0.0)
    along_query = jnp.sum(weighted, axis=0, keepdims=True) + jnp.sum(
        hard_weighted, axis=0, keepdims=True
    )
    folded_coef = fold_half(coef[:start], coef[start:], 0)
    folded_hard = fold_half(
        jnp.where(is_hard, hard_coef, along_query), jnp.where(is_hard, hard_weighted, losses), 0
    )
    for k in range(out_ref.shape[0]):
        out_ref[k, :start, :] = folded_coef
        out_ref[k, start : start + 8, :] = folded_hard
        out_ref[k, start + 8 :, :] = jnp.zeros_like(out_ref[k, start + 8 :, :])
        columns_to_lanes(
            jnp.sum(weighted, axis=1, keepdims=True), out_ref.at[k, start + 8 : start + 16]
        )


def resid_grad_kernel(
    both_ref,
    inverse_ref,
    rows_ref,
    positive_hot_ref,
    query_hot_ref,
    listed_ref,
    resid_ref,
    gains_ref,
    out_ref,
    loss_ref,
):
    sequences = resid_ref.shape[0]
    count, total_rows = positive_hot_ref.shape
    z = lax.axis_index("z_far") * lax.axis_size("z_pair") + lax.axis_index("z_pair")
    group = z * lax.axis_size("core") + lax.axis_index("core")
    first_row = group * sequences
    first_query = group * QDEV
    across = (((1,), (1,)), ((), ()))

    def joined(start, stop):
        firsts, seconds = [], []
        for k in (0, 2):
            first, second = both_ref[k, start:stop, :], both_ref[k + 1, start:stop, :]
            firsts.append(fold_half(first, second, 0))
            seconds.append(fold_half(pltpu.roll(first, HALF, 1), pltpu.roll(second, HALF, 1), 0))
        return jnp.concatenate(firsts, axis=1), jnp.concatenate(seconds, axis=1)

    start = count // 2
    coef16 = jnp.concatenate(joined(0, start), axis=0).astype(jnp.bfloat16)
    hard, hard_weighted = joined(start, start + 8)
    along_passage = both_ref[0, start + 8 : start + 16, :]
    for k in range(1, both_ref.shape[0]):
        along_passage = along_passage + both_ref[k, start + 8 : start + 16, :]
    along_passage = jnp.concatenate([along_passage[0:1], along_passage[1:2]], axis=1)
    inverse = jnp.concatenate([inverse_ref[k : k + 1, :] for k in range(8)], axis=1)

    own_row = first_row + iota((sequences, count), 0)
    own_query = (iota((sequences, count), 0) < QDEV) & (
        iota((sequences, count), 1) == first_query + iota((sequences, count), 0)
    )
    own_positive = listed_ref[8:9, :] == own_row
    to_positives = lax.dot_general(
        own_query.astype(jnp.bfloat16), coef16, across, preferred_element_type=jnp.float32
    )
    to_queries = jnp.dot(
        own_positive.astype(jnp.bfloat16), coef16, preferred_element_type=jnp.float32
    )
    along = jnp.sum(
        jnp.where(own_query, hard[7:8, :], 0.0) + jnp.where(own_positive, along_passage, 0.0),
        axis=1,
        keepdims=True,
    )
    for j in range(7):
        listed = listed_ref[j : j + 1, :] == own_row
        to_queries = to_queries + jnp.where(listed, hard[j : j + 1, :], 0.0)
        along = along + jnp.sum(
            jnp.where(listed, hard_weighted[j : j + 1, :], 0.0), axis=1, keepdims=True
        )
    matrix = jnp.dot(
        to_positives.astype(jnp.bfloat16), positive_hot_ref[...], preferred_element_type=jnp.float32
    ) + jnp.dot(
        to_queries.astype(jnp.bfloat16), query_hot_ref[...], preferred_element_type=jnp.float32
    )
    row_index = iota((sequences, total_rows), 1)
    for j in range(7):
        own_hard = jnp.sum(jnp.where(own_query, hard[j : j + 1, :], 0.0), axis=1, keepdims=True)
        own_listed = jnp.where(own_query, listed_ref[j : j + 1, :].astype(jnp.float32), 0.0)
        own_listed = jnp.sum(own_listed, axis=1, keepdims=True).astype(jnp.int32)
        listed = row_index == own_listed
        matrix = matrix + jnp.where(listed, own_hard, 0.0)
    matrix = matrix * inverse
    high = matrix.astype(jnp.bfloat16)
    low = (matrix - high.astype(jnp.float32)).astype(jnp.bfloat16)
    rows = rows_ref[...]
    d_embed = jnp.dot(high, rows, preferred_element_type=jnp.float32) + jnp.dot(
        low, rows, preferred_element_type=jnp.float32
    )

    is_own_row = row_index == first_row + iota((sequences, total_rows), 0)
    own_inverse = jnp.sum(jnp.where(is_own_row, inverse, 0.0), axis=1, keepdims=True)
    resid = resid_ref[...]
    gain = own_columns(gains_ref, resid.shape[1])
    features = gains_ref.shape[1]
    d_resid = own_inverse * gain * (
        d_embed - resid * gain * own_inverse * along
    ) - resid * (along * own_inverse * own_inverse * (EPSILON / features))
    d_resid16 = d_resid.astype(jnp.bfloat16)
    for t in range(out_ref.shape[0]):
        out_ref[t] = d_resid16
    loss_ref[0] = jnp.sum(hard_weighted[7:8, :]) / count


def kernel_call(body, outs, arrays, after=(), scratch=()):
    count = len(arrays)

    def kernel(*refs):
        body(*refs[:count], *refs[count + len(after) :])

    def out_spec(shape):
        return pl.BlockSpec(memory_space=pltpu.SMEM if shape == (1,) else pltpu.VMEM)

    return pl.pallas_call(
        kernel,
        out_shape=[jax.ShapeDtypeStruct(shape, dtype) for shape, dtype in outs],
        in_specs=[pl.BlockSpec(memory_space=pltpu.VMEM)] * count
        + [pl.BlockSpec(memory_space=pl.ANY)] * len(after),
        out_specs=[out_spec(shape) for shape, _ in outs],
        scratch_shapes=list(scratch),
        compiler_params=pltpu.CompilerParams(vmem_limit_bytes=VMEM_BYTES),
    )(*arrays, *after)


def candidate_kernel(positives_ref, negatives_ref, listed_ref, query_hot_ref, positive_hot_ref):
    query_count, total_rows = query_hot_ref.shape
    groups = query_count // QDEV
    sequences = total_rows // groups
    others = sequences - QDEV

    def row_of(passage):
        at = ((passage.astype(jnp.float32) + 0.5) * (1.0 / others)).astype(jnp.int32)
        return passage + at * QDEV + QDEV

    def query_row(query):
        return query + query // QDEV * others

    positive_row = row_of(positives_ref[...])
    count = negatives_ref.shape[0]
    listed_ref[:count, :] = row_of(negatives_ref[...])
    listed_ref[count : count + 1, :] = query_row(iota((1, query_count), 1))
    listed_ref[count + 1 :, :] = jnp.broadcast_to(
        positive_row, (listed_ref.shape[0] - count - 1, query_count)
    )
    shape = (LANES, total_rows)
    diagonal = iota((LANES, LANES), 0) == iota((LANES, LANES), 1)
    for k in range(query_count // LANES):
        rows = slice(LANES * k, LANES * (k + 1))
        query = query_row(iota(shape, 0) + LANES * k)
        query_hot_ref[rows, :] = (query == iota(shape, 1)).astype(jnp.float32).astype(jnp.bfloat16)
        lanes = positive_row[:, rows].astype(jnp.float32)
        column = jnp.sum(jnp.where(diagonal, lanes, 0.0), axis=1, keepdims=True)
        positive_hot_ref[rows, :] = (
            (column.astype(jnp.int32) == iota(shape, 1)).astype(jnp.float32).astype(jnp.bfloat16)
        )


def transpose_kernel(given_ref, out_ref, token_ref):
    out_ref[...] = given_ref[...].T
    token_ref[0] = jnp.float32(0.0)


def half_weights_kernel(kv_ref, query_ref, kept_ref, sent_ref):
    width, rows = kept_ref.shape[1], kv_ref.shape[1]
    parity = lax.axis_index("tensor") % 2
    for out_ref, half in ((kept_ref, parity), (sent_ref, 1 - parity)):
        features = pl.ds(pl.multiple_of(half * width, width), width)
        out_ref[:rows, :] = kv_ref[features, :].T
        out_ref[rows:, :] = query_ref[features, :].T


def stack_kernel(first_ref, second_ref, out_ref, token_ref):
    rows = first_ref.shape[0]
    out_ref[:rows, :] = first_ref[...]
    out_ref[rows:, :] = second_ref[...]
    token_ref[0] = jnp.float32(0.0)


def contrast(everyone, resid, gains, tables, after, after_logits):
    tensor_count = lax.axis_size("tensor")
    sequences, width = resid.shape
    listed, query_hot, positive_hot = tables
    count, total_rows = positive_hot.shape
    rows = everyone.reshape(total_rows, width)
    (sent,) = kernel_call(
        partial_logits_kernel,
        [((tensor_count, count // 2 + 32, LANES), jnp.bfloat16)],
        [rows, query_hot, positive_hot, listed, gains],
        after=after,
        scratch=[pltpu.VMEM((24, LANES), jnp.float32)],
    )
    arrived = exchange(sent, "tensor")
    coefs, inverse = kernel_call(
        softmax_kernel,
        [((4, count // 2 + 16, LANES), jnp.float32), ((8, LANES), jnp.float32)],
        [arrived, positive_hot],
        after=after_logits,
    )
    both = exchange(coefs, ("z_pair", "core"))
    d_resid16, loss = kernel_call(
        resid_grad_kernel,
        [((tensor_count, sequences, width), jnp.bfloat16), ((1,), jnp.float32)],
        [both, inverse, rows, positive_hot, query_hot, listed, resid, gains],
    )
    return loss, exchange(d_resid16, "tensor")


def copied_norm_kernel(hidden_ref, gain_ref, out_ref):
    hidden32 = hidden_ref[...].astype(jnp.float32)
    normed = (hidden32 * rms_scale(hidden32) * gain_ref[...]).astype(jnp.bfloat16)
    height = normed.shape[0]
    for c in range(normed.shape[1] // LANES):
        block = normed[:, LANES * c : LANES * (c + 1)]
        for t in range(out_ref.shape[0]):
            out_ref[t, height * c : height * (c + 1), :] = block


def projection_kernel(rows_ref, kv_weights_ref, query_weights_ref, kv_ref, sent_ref, query_ref):
    tensor_count, tall, _ = rows_ref.shape
    blocks = kv_weights_ref.shape[0] // LANES
    height = tall // blocks

    def block(c):
        part = rows_ref[:, height * c : height * (c + 1), :]
        return part.reshape(tensor_count * height, LANES)

    kv = jnp.zeros(kv_ref.shape, jnp.float32)
    query = jnp.zeros(query_ref.shape, jnp.float32)
    for c in range(0, blocks, 2):
        rows = jnp.concatenate([block(c), block(c + 1)], axis=1)
        columns = slice(LANES * c, LANES * (c + 2))
        kv = kv + jnp.dot(rows, kv_weights_ref[columns, :], preferred_element_type=jnp.float32)
        query = query + jnp.dot(
            rows, query_weights_ref[columns, :], preferred_element_type=jnp.float32
        )
    kv_ref[...] = kv
    sent_ref[...] = kv.astype(jnp.bfloat16)
    query_ref[...] = query


def half_turned(tensor, cosine, signed_sine):
    halfway = tensor.shape[1] // 2
    return tensor * cosine + pltpu.roll(tensor, halfway, 1) * signed_sine


def is_even_tensor():
    return lax.axis_index("tensor") % 2 == 0


def attention_kernel(
    own_ref,
    other_ref,
    query_all_ref,
    layout_ref,
    q_gain_ref,
    k_gain_ref,
    hidden_ref,
    wo_ref,
    out_ref,
    saved_ref,
):
    root = math.sqrt(own_ref.shape[1])
    tokens_count, sequences, own_rows = own_ref.shape[0], out_ref.shape[1], hidden_ref.shape[0]
    at, _ = layout_rows(tokens_count, sequences, own_rows)
    to, _ = saved_rows(tokens_count, sequences)
    is_even = is_even_tensor()
    own, other = own_ref[...], other_ref[...].astype(jnp.float32)
    key_raw = jnp.where(is_even, own, other)
    value16 = jnp.where(is_even, other, own).astype(jnp.bfloat16)
    query_raw = jnp.dot(
        unfolded(layout_ref[at["chosen"], :], sequences),
        query_all_ref[...],
        precision=lax.Precision.HIGHEST,
        preferred_element_type=jnp.float32,
    )
    q_gain, k_gain = q_gain_ref[...], k_gain_ref[...]
    key16 = half_turned(
        key_raw * rms_scale(key_raw) * k_gain,
        layout_ref[at["key_cosine"], :],
        layout_ref[at["key_sine"], :],
    ).astype(jnp.bfloat16)
    query16 = half_turned(
        query_raw * rms_scale(query_raw) * q_gain,
        layout_ref[at["query_cosine"], :],
        layout_ref[at["query_sine"], :],
    ).astype(jnp.bfloat16)
    shift = (
        root
        * jnp.max(q_gain, axis=1, keepdims=True)
        * jnp.max(k_gain, axis=1, keepdims=True)
    )
    scores = (
        lax.dot_general(
            query16, key16, (((1,), (1,)), ((), ())), preferred_element_type=jnp.float32
        )
        / root
    )
    inside = unfolded(layout_ref[at["inside"], :], sequences)
    weights = jnp.where(inside > 0.0, jnp.exp(scores - shift), 0.0)
    probs = weights / jnp.sum(weights, axis=1, keepdims=True)
    attn16 = jnp.dot(
        probs.astype(jnp.bfloat16), value16, preferred_element_type=jnp.float32
    ).astype(jnp.bfloat16)
    own_last = layout_ref[at["own_last"], :][:, :own_rows].astype(jnp.bfloat16)
    chunk = out_ref.shape[2]
    for t in range(out_ref.shape[0]):
        columns = slice(t * chunk, (t + 1) * chunk)
        block = jnp.dot(attn16, wo_ref[:, columns], preferred_element_type=jnp.float32)
        block = block + jnp.dot(
            own_last, hidden_ref[:, columns], preferred_element_type=jnp.float32
        )
        out_ref[t] = block.astype(jnp.bfloat16)
    saved_ref[to["key_raw"], :] = key_raw
    saved_ref[to["key"], :] = key16.astype(jnp.float32)
    saved_ref[to["value"], :] = value16.astype(jnp.float32)
    saved_ref[to["query_raw"], :] = query_raw
    saved_ref[to["query"], :] = query16.astype(jnp.float32)
    saved_ref[to["probs"], :] = folded(probs)


def resid_kernel(arrived_ref, gains_ref, resid_ref, out_ref):
    gain = own_columns(gains_ref, resid_ref.shape[1])
    resid = arrived_ref[0].astype(jnp.float32)
    for t in range(1, arrived_ref.shape[0]):
        resid = resid + arrived_ref[t].astype(jnp.float32)
    resid_ref[...] = resid
    scaled16 = (resid * gain).astype(jnp.bfloat16)
    for t in range(out_ref.shape[0]):
        out_ref[t] = scaled16


def gradient_kernel(
    d_resid_ref, wo_t_ref, saved_ref, layout_ref, q_gain_ref, k_gain_ref, own_ref, sent_ref
):
    head_width = saved_ref.shape[1]
    root = math.sqrt(head_width)
    sequences = d_resid_ref.shape[1]
    tensor_count = d_resid_ref.shape[0]
    tokens_count = (own_ref.shape[0] - sequences) // 2
    at, _ = layout_rows(tokens_count, sequences, tokens_count // tensor_count)
    to, _ = saved_rows(tokens_count, sequences)
    chunk = d_resid_ref.shape[2]
    d_attn = jnp.dot(d_resid_ref[0], wo_t_ref[:chunk, :], preferred_element_type=jnp.float32)
    for t in range(1, d_resid_ref.shape[0]):
        d_attn = d_attn + jnp.dot(
            d_resid_ref[t],
            wo_t_ref[t * chunk : (t + 1) * chunk, :],
            preferred_element_type=jnp.float32,
        )
    d_attn16 = d_attn.astype(jnp.bfloat16)
    probs = unfolded(saved_ref[to["probs"], :], sequences)
    key16 = saved_ref[to["key"], :].astype(jnp.bfloat16)
    query16 = saved_ref[to["query"], :].astype(jnp.bfloat16)
    value16 = saved_ref[to["value"], :].astype(jnp.bfloat16)
    d_probs = lax.dot_general(
        d_attn16, value16, (((1,), (1,)), ((), ())), preferred_element_type=jnp.float32
    )
    d_scores16 = (
        probs * (d_probs - jnp.sum(probs * d_probs, axis=1, keepdims=True)) / root
    ).astype(jnp.bfloat16)
    down = (((0,), (0,)), ((), ()))
    d_query_rot = jnp.dot(d_scores16, key16, preferred_element_type=jnp.float32)
    d_key_rot = lax.dot_general(d_scores16, query16, down, preferred_element_type=jnp.float32)
    d_value = lax.dot_general(
        probs.astype(jnp.bfloat16), d_attn16, down, preferred_element_type=jnp.float32
    )

    def head_gradient(grad_rot, name, gain):
        raw = saved_ref[to[name + "_raw"], :]
        inverse = rms_scale(raw)
        turned_back = half_turned(
            grad_rot, layout_ref[at[name + "_cosine"], :], -layout_ref[at[name + "_sine"], :]
        )
        return norm_backward(turned_back, raw * inverse, inverse, gain)

    d_key = head_gradient(d_key_rot, "key", k_gain_ref[...])
    d_query = head_gradient(d_query_rot, "query", q_gain_ref[...])
    own = jnp.concatenate([d_key, d_value, d_query], axis=0)
    own_ref[...] = own
    sent_ref[...] = own.astype(jnp.bfloat16)


def added_kernel(d_resid_ref, layout_ref, out_ref, token_ref):
    own_rows = out_ref.shape[0]
    tensor_count, sequences, chunk = d_resid_ref.shape
    at, _ = layout_rows(own_rows * tensor_count, sequences, own_rows)
    last = layout_ref[at["own_last_t"], :][:, :sequences].astype(jnp.bfloat16)
    for t in range(tensor_count):
        out_ref[:, t * chunk : (t + 1) * chunk] = jnp.dot(
            last, d_resid_ref[t], preferred_element_type=jnp.float32
        )
    token_ref[0] = jnp.float32(0.0)


def product_kernel(own_ref, other_ref, layout_ref, weights_ref, out_ref):
    tensor_count, tall, _ = out_ref.shape
    height = tall * LANES // weights_ref.shape[1]
    tokens_count = height * tensor_count
    sequences = own_ref.shape[0] - 2 * tokens_count
    at, _ = layout_rows(tokens_count, sequences, height)
    chosen = unfolded(layout_ref[at["chosen"], :], sequences).astype(jnp.bfloat16)

    def spread(d_query):
        return lax.dot_general(
            chosen,
            d_query.astype(jnp.bfloat16),
            (((0,), (0,)), ((), ())),
            preferred_element_type=jnp.float32,
        )

    own, other = own_ref[...], other_ref[...].astype(jnp.float32)
    d_key = own[:tokens_count] + other[:tokens_count]
    d_value = own[tokens_count : 2 * tokens_count] + other[tokens_count : 2 * tokens_count]
    is_even = is_even_tensor()
    gradients = jnp.concatenate(
        [
            jnp.where(is_even, d_key, d_value),
            spread(own[2 * tokens_count :]),
            jnp.where(is_even, d_value, d_key),
            spread(other[2 * tokens_count :]),
        ],
        axis=1,
    ).astype(jnp.bfloat16)
    wide = 2 * LANES
    for k in range(weights_ref.shape[1] // wide):
        term = jnp.dot(
            gradients, weights_ref[:, wide * k : wide * (k + 1)], preferred_element_type=jnp.float32
        ).astype(jnp.bfloat16)
        for c in (2 * k, 2 * k + 1):
            block = term[:, LANES * (c - 2 * k) : LANES * (c - 2 * k + 1)]
            out_ref[:, height * c : height * (c + 1), :] = block.reshape(-1, height, LANES)


def d_hidden_kernel(terms_ref, hidden_ref, gain_ref, added_ref, out_ref):
    hidden32 = hidden_ref[...].astype(jnp.float32)
    height = hidden32.shape[0]
    parts = []
    for parity in range(2):
        total = terms_ref[parity].astype(jnp.float32)
        for t in range(parity + 2, terms_ref.shape[0], 2):
            total = total + terms_ref[t].astype(jnp.float32)
        parts += [total[height * c : height * (c + 1)] for c in range(total.shape[0] // height)]
    d_normed = jnp.concatenate(parts, axis=1)
    inverse = rms_scale(hidden32)
    d_hidden = norm_backward(d_normed, hidden32 * inverse, inverse, gain_ref[...])
    out_ref[...] = (d_hidden + added_ref[...]).astype(jnp.bfloat16)


def packed_rows(sizes):
    starts, total = {}, 0
    for name, rows in sizes:
        starts[name] = slice(total, total + rows)
        total += rows
    return starts, total


def layout_rows(tokens_count, sequences, own_rows):
    wide = sequences * tokens_count // LANES
    return packed_rows(
        [
            ("key_cosine", tokens_count),
            ("key_sine", tokens_count),
            ("query_cosine", sequences),
            ("query_sine", sequences),
            ("inside", wide),
            ("chosen", wide),
            ("own_last", sequences),
            ("own_last_t", own_rows),
        ]
    )


def saved_rows(tokens_count, sequences):
    return packed_rows(
        [
            ("key_raw", tokens_count),
            ("key", tokens_count),
            ("value", tokens_count),
            ("query_raw", sequences),
            ("query", sequences),
            ("probs", sequences * tokens_count // LANES),
        ]
    )


def folded(block):
    parts = [block[:, LANES * k : LANES * (k + 1)] for k in range(block.shape[1] // LANES)]
    return jnp.concatenate(parts, axis=0)


def unfolded(block, rows):
    parts = [block[rows * k : rows * (k + 1)] for k in range(block.shape[0] // rows)]
    return jnp.concatenate(parts, axis=1)


def sequence_kernel(lengths_ref, out_ref, token_ref, *, tokens_count, own_rows):
    token_ref[0] = jnp.float32(0.0)
    sequences = lengths_ref.shape[1]
    at, _ = layout_rows(tokens_count, sequences, own_rows)
    lengths = lengths_ref[...].astype(jnp.float32)
    square = (sequences, sequences)
    ends = jnp.sum(
        jnp.where(iota(square, 1) <= iota(square, 0), lengths, 0.0), axis=1, keepdims=True
    )
    own_length = jnp.sum(
        jnp.where(iota(square, 1) == iota(square, 0), lengths, 0.0), axis=1, keepdims=True
    )
    starts = ends - own_length
    ends_row = jnp.sum(
        jnp.where(iota(square, 0) <= iota(square, 1), own_length, 0.0), axis=0, keepdims=True
    )
    starts_row = ends_row - lengths
    token = iota((sequences, tokens_count), 1).astype(jnp.float32)
    out_ref[at["inside"], :] = folded(((token >= starts) & (token < ends)).astype(jnp.float32))
    out_ref[at["chosen"], :] = folded((token == ends - 1.0).astype(jnp.float32))
    first = (lax.axis_index("tensor") * own_rows).astype(jnp.float32)
    own_token = iota((sequences, LANES), 1).astype(jnp.float32) + first
    own_token = jnp.where(iota((sequences, LANES), 1) < own_rows, own_token, -1.0)
    out_ref[at["own_last"], :] = (own_token == ends - 1.0).astype(jnp.float32)
    own_token = iota((own_rows, sequences), 0).astype(jnp.float32) + first
    own_last_t = (own_token == ends_row - 1.0).astype(jnp.float32)
    out_ref[at["own_last_t"], :] = jnp.concatenate(
        [own_last_t, jnp.zeros((own_rows, LANES - sequences), jnp.float32)], axis=1
    )
    token = iota((tokens_count, sequences), 0).astype(jnp.float32)
    held = (token >= starts_row) & (token < ends_row)
    position = jnp.sum(jnp.where(held, token - starts_row, 0.0), axis=1, keepdims=True)
    lane = iota((1, LANES), 1)
    halfway = LANES // 2
    pair = jnp.where(lane < halfway, lane, lane - halfway).astype(jnp.float32)
    frequency = jnp.exp(pair * (-2.0 / LANES * math.log(ROPE_BASE)))
    sign = jnp.where(lane < halfway, -1.0, 1.0)
    for name, place in (("key", position), ("query", own_length - 1.0)):
        angles = place * frequency
        out_ref[at[name + "_cosine"], :] = jnp.cos(angles)
        out_ref[at[name + "_sine"], :] = jnp.sin(angles) * sign


def on_device(
    hidden, lengths, positives, negatives, in_gain, wq, wkv, q_gain, k_gain, wo, out_gain
):
    tensor_count = lax.axis_size("tensor")
    z_count = lax.axis_size("z_far") * lax.axis_size("z_pair")
    own_rows, features = hidden.shape
    tokens_count = own_rows * tensor_count
    head_width = wq.shape[1]
    sequences = lengths.shape[1]
    query_count = positives.shape[0]
    total_rows = query_count // QDEV * sequences
    chunk = features // tensor_count
    f32, bf16 = jnp.float32, jnp.bfloat16
    head = (tokens_count, head_width)
    weights_shape = (head_width, features)
    flat = (tensor_count, own_rows * features // LANES, LANES)
    gain_rows = [q_gain[None, :], k_gain[None, :]]

    (copies,) = kernel_call(
        copied_norm_kernel, [(flat, bf16)], [hidden, in_gain[None, :]]
    )
    piece = exchange(copies, "tensor")
    kv_own, kv_own16, query_all = kernel_call(
        projection_kernel, [(head, f32), (head, bf16), (head, f32)], [piece, wkv, wq]
    )
    kv_other = swapped(kv_own16, "tensor", 0)
    def sequence_layout(after):
        return kernel_call(
            functools.partial(sequence_kernel, tokens_count=tokens_count, own_rows=own_rows),
            [((layout_rows(tokens_count, sequences, own_rows)[1], LANES), f32), ((1,), f32)],
            [lengths],
            after=[after],
        )

    layout, _ = sequence_layout(query_all)
    blocks, saved = kernel_call(
        attention_kernel,
        [
            ((tensor_count, sequences, chunk), bf16),
            ((saved_rows(tokens_count, sequences)[1], LANES), f32),
        ],
        [kv_own, kv_other, query_all, layout, *gain_rows, hidden, wo],
    )
    half_shape = (2 * head_width, features // 2)
    kept_weights, sent_weights = kernel_call(
        half_weights_kernel, [(half_shape, bf16), (half_shape, bf16)], [wkv, wq], after=[query_all]
    )
    other_weights = swapped(sent_weights, "tensor", 0)
    output_gain = out_gain[None, :]
    resid, scaled = kernel_call(
        resid_kernel,
        [((sequences, chunk), f32), ((z_count, sequences, chunk), bf16)],
        [exchange(blocks, "tensor"), output_gain],
    )
    wo_t, transposed = kernel_call(
        transpose_kernel, [((features, head_width), bf16), ((1,), f32)], [wo], after=[resid]
    )
    pair_weights, fetched = kernel_call(
        stack_kernel,
        [((4 * head_width, features // 2), bf16), ((1,), f32)],
        [kept_weights, other_weights],
    )
    layout_again, placed = sequence_layout(resid)
    tables = kernel_call(
        candidate_kernel,
        [
            ((16, query_count), jnp.int32),
            ((query_count, total_rows), bf16),
            ((query_count, total_rows), bf16),
        ],
        [positives[None, :], negatives.T],
        after=[resid],
    )
    everyone = lax.all_gather(exchange(scaled, ("z_far", "z_pair")), "core", axis=1)
    loss, d_resid16 = contrast(
        everyone, resid, output_gain, tables, [transposed, placed], [fetched]
    )
    gradient_shape = (2 * tokens_count + sequences, head_width)
    own_gradients, sent_gradients = kernel_call(
        gradient_kernel,
        [(gradient_shape, f32), (gradient_shape, bf16)],
        [d_resid16, wo_t, saved, layout_again, *gain_rows],
        after=[loss],
    )
    other_gradients = swapped(sent_gradients, "tensor", 0)
    added, summed = kernel_call(
        added_kernel, [((own_rows, features), f32), ((1,), f32)], [d_resid16, layout_again]
    )
    (product,) = kernel_call(
        product_kernel,
        [((tensor_count, own_rows * features // LANES // 2, LANES), bf16)],
        [own_gradients, other_gradients, layout_again, pair_weights],
        after=[summed],
    )
    terms = exchange(product, "tensor")
    (d_hidden,) = kernel_call(
        d_hidden_kernel,
        [((own_rows, features), bf16)],
        [terms, hidden, in_gain[None, :], added],
    )
    return (d_hidden, loss[0])


def solution(mesh):
    z_count = mesh.shape["dp"] // 2
    chips = mesh.devices.reshape(z_count // 2, 2, 2, mesh.shape["tensor"])
    mesh = jax.sharding.Mesh(chips, ("z_far", "z_pair", "core", "tensor"))
    everywhere = P(("z_far", "z_pair", "core", "tensor"), None)
    placed = (
        everywhere,
        P(("z_far", "z_pair", "core"), None),
        P(),
        P(),
        P(),
        P(None, "tensor"),
        P(None, "tensor"),
        P(),
        P(),
        P("tensor", None),
        P(),
    )
    return jax.shard_map(
        on_device, mesh=mesh, in_specs=placed, out_specs=(everywhere, P()), check_vma=False
    )
```

```python
import functools
import math

import jax
import jax.numpy as jnp
from jax import lax
from jax.experimental import pallas as pl
from jax.experimental.pallas import tpu as pltpu
from jax.sharding import PartitionSpec as P

QDEV = 8
LANES = 128
VMEM_BYTES = 32 * 2**20


EPSILON = 1e-06
SOFTMAX_TEMPER = 0.05
LOSS_MULTIPLIER = 8192.0
ROPE_BASE = 1000000.0


def swapped(value, axis, apart):
    mask = 2**apart
    pairs = [(source, source ^ mask) for source in range(lax.axis_size(axis))]
    return lax.ppermute(value, axis, pairs)


def rms_scale(tensor):
    return lax.rsqrt(jnp.mean(tensor * tensor, axis=-1, keepdims=True) + EPSILON)


def norm_backward(grad, unit_form, inverse, gain):
    scaled = grad * gain
    return inverse * (scaled - unit_form * jnp.mean(unit_form * scaled, axis=-1, keepdims=True))


def exchange(blocks, axis, groups=None):
    return lax.all_to_all(blocks, axis, 0, 0, axis_index_groups=groups, tiled=True)


def halves(value):
    high = value.astype(jnp.bfloat16).astype(jnp.float32)
    return high, value - high


def iota(shape, axis):
    return lax.broadcasted_iota(jnp.int32, shape, axis)


def columns_to_lanes(column, out_ref):
    diagonal = iota((LANES, LANES), 0) == iota((LANES, LANES), 1)
    for k in range(column.shape[0] // LANES):
        block = jnp.where(diagonal, column[LANES * k : LANES * (k + 1)], 0.0)
        out_ref[k : k + 1, :] = jnp.sum(block, axis=0, keepdims=True)


def core_rows():
    return pl.ds(pl.multiple_of(lax.axis_index("core") * LANES, LANES), LANES)


def own_columns(gains_ref, width):
    start = pl.multiple_of(lax.axis_index("tensor") * width, width)
    return gains_ref[:, pl.ds(start, width)]


def partial_logits_kernel(
    rows_ref, query_hot_ref, positive_hot_ref, listed_all_ref, gains_ref, out_ref, held_ref
):
    rows = rows_ref[...]
    listed_ref = listed_all_ref[:8, core_rows()]
    block_hot = query_hot_ref[core_rows(), :]
    queries = jnp.dot(block_hot, rows, preferred_element_type=jnp.float32)
    positives = jnp.dot(positive_hot_ref[...], rows, preferred_element_type=jnp.float32)
    queries = queries.astype(jnp.bfloat16)
    features = gains_ref.shape[1]
    rows32 = rows.astype(jnp.float32)
    plain = rows32 * (1.0 / own_columns(gains_ref, rows.shape[1]))
    squares = jnp.sum(rows32 * rows32, axis=1, keepdims=True) + jnp.sum(
        plain * plain, axis=1, keepdims=True
    ) * (EPSILON / features)
    against = (((1,), (1,)), ((), ()))
    with_positives = lax.dot_general(
        positives.astype(jnp.bfloat16), queries, against, preferred_element_type=jnp.float32
    )
    with_all = lax.dot_general(rows, queries, against, preferred_element_type=jnp.float32)
    squares_all = jnp.broadcast_to(squares, with_all.shape)
    row_index = iota((LANES, LANES), 0)
    for j in range(8):
        product = jnp.zeros((LANES, LANES), jnp.float32)
        square = product
        for k in range(with_all.shape[0] // LANES):
            rows_at = slice(LANES * k, LANES * (k + 1))
            hit = row_index == listed_ref[j : j + 1, :] - LANES * k
            product = jnp.where(hit, with_all[rows_at], product)
            square = jnp.where(hit, squares_all[rows_at], square)
        held_ref[j : j + 1, :] = jnp.sum(product, axis=0, keepdims=True)
        held_ref[8 + j : 9 + j, :] = jnp.sum(square, axis=0, keepdims=True)
    columns_to_lanes(squares, held_ref.at[16:24])
    send_logits(with_positives, [held_ref[8 * k : 8 * (k + 1), :] for k in range(3)], out_ref)


def send_logits(logits, others, out_ref):
    count = logits.shape[0]
    logits16 = logits.astype(jnp.bfloat16)
    others16 = [jnp.concatenate(halves(other), axis=0).astype(jnp.bfloat16) for other in others]
    for t in range(out_ref.shape[0]):
        out_ref[t, :count, :] = logits16
        for k, other16 in enumerate(others16):
            out_ref[t, count + 16 * k : count + 16 * (k + 1), :] = other16


def summed_logits(arrived_ref):
    summed = arrived_ref[0].astype(jnp.float32)
    for t in range(1, arrived_ref.shape[0]):
        summed = summed + arrived_ref[t].astype(jnp.float32)
    count = summed.shape[0] - 48
    blocks = [summed[count + 16 * k : count + 16 * (k + 1)] for k in range(3)]
    return summed[:count], [block[:8] + block[8:] for block in blocks]


def pass_logits_kernel(arrived_ref, out_ref):
    logits, others = summed_logits(arrived_ref)
    send_logits(logits, others, out_ref)


def softmax_kernel(arrived_ref, positive_hot_ref, out_ref, inverse_ref):
    count = positive_hot_ref.shape[0]
    with_positives, (hard, listed_squares, squares) = summed_logits(arrived_ref)
    first_query = lax.axis_index("core") * LANES
    inverse_listed = lax.rsqrt(listed_squares + EPSILON * EPSILON)
    inverse = lax.rsqrt(squares + EPSILON * EPSILON)
    inverse_ref[...] = inverse
    inverse_query = inverse_listed[7:8, :]
    picked = jnp.zeros((count, LANES), jnp.float32)
    for k in range(8):
        hot = positive_hot_ref[:, LANES * k : LANES * (k + 1)].astype(jnp.float32)
        picked = picked + hot * inverse[k : k + 1, :]
    inverse_positive = jnp.sum(picked, axis=1, keepdims=True)
    logits = with_positives * inverse_positive * inverse_query / SOFTMAX_TEMPER
    hard = hard * inverse_listed * inverse_query / SOFTMAX_TEMPER
    is_hard = iota(hard.shape, 0) < 7
    is_own = iota(logits.shape, 0) == iota(logits.shape, 1) + first_query
    weights = jnp.exp(logits - 1.0 / SOFTMAX_TEMPER)
    hard_weights = jnp.where(is_hard, jnp.exp(hard - 1.0 / SOFTMAX_TEMPER), 0.0)
    totals = jnp.sum(weights, axis=0, keepdims=True) + jnp.sum(hard_weights, axis=0, keepdims=True)
    target = jnp.sum(jnp.where(is_own, logits, 0.0), axis=0, keepdims=True)
    losses = jnp.log(totals) + 1.0 / SOFTMAX_TEMPER - target
    scaling_factor = LOSS_MULTIPLIER / (count * SOFTMAX_TEMPER)

    def rounded(value):
        return value.astype(jnp.bfloat16).astype(jnp.float32)

    coef = rounded(scaling_factor * (weights / totals - is_own.astype(jnp.float32)))
    hard_coef = rounded(scaling_factor * (hard_weights / totals))
    weighted = coef * logits * SOFTMAX_TEMPER
    hard_weighted = jnp.where(is_hard, hard_coef * hard * SOFTMAX_TEMPER, 0.0)
    along_query = jnp.sum(weighted, axis=0, keepdims=True) + jnp.sum(
        hard_weighted, axis=0, keepdims=True
    )
    out_ref[:count, :] = coef
    out_ref[count : count + 8, :] = jnp.where(is_hard, hard_coef, along_query)
    out_ref[count + 8 : count + 16, :] = jnp.where(is_hard, hard_weighted, losses)
    out_ref[count + 16 :, :] = jnp.zeros_like(out_ref[count + 16 :, :])
    columns_to_lanes(jnp.sum(weighted, axis=1, keepdims=True), out_ref.at[count + 16 :])


def resid_grad_kernel(
    both_ref,
    inverse_ref,
    rows_ref,
    positive_hot_ref,
    query_hot_ref,
    listed_ref,
    resid_ref,
    gains_ref,
    out_ref,
    loss_ref,
):
    sequences = resid_ref.shape[0]
    count, total_rows = positive_hot_ref.shape
    z = lax.axis_index("z_far") * lax.axis_size("z_pair") + lax.axis_index("z_pair")
    group = z * lax.axis_size("core") + lax.axis_index("core")
    first_row = group * sequences
    first_query = group * QDEV
    across = (((1,), (1,)), ((), ()))

    def joined(start, stop):
        return jnp.concatenate([both_ref[0, start:stop, :], both_ref[1, start:stop, :]], axis=1)

    coef16 = joined(0, count).astype(jnp.bfloat16)
    hard = joined(count, count + 8)
    hard_weighted = joined(count + 8, count + 16)
    along_passage = both_ref[0, count + 16 :, :] + both_ref[1, count + 16 :, :]
    along_passage = jnp.concatenate([along_passage[0:1], along_passage[1:2]], axis=1)
    inverse = jnp.concatenate([inverse_ref[k : k + 1, :] for k in range(8)], axis=1)

    own_row = first_row + iota((sequences, count), 0)
    own_query = (iota((sequences, count), 0) < QDEV) & (
        iota((sequences, count), 1) == first_query + iota((sequences, count), 0)
    )
    own_positive = listed_ref[8:9, :] == own_row
    to_positives = lax.dot_general(
        own_query.astype(jnp.bfloat16), coef16, across, preferred_element_type=jnp.float32
    )
    to_queries = jnp.dot(
        own_positive.astype(jnp.bfloat16), coef16, preferred_element_type=jnp.float32
    )
    along = jnp.sum(
        jnp.where(own_query, hard[7:8, :], 0.0) + jnp.where(own_positive, along_passage, 0.0),
        axis=1,
        keepdims=True,
    )
    for j in range(7):
        listed = listed_ref[j : j + 1, :] == own_row
        to_queries = to_queries + jnp.where(listed, hard[j : j + 1, :], 0.0)
        along = along + jnp.sum(
            jnp.where(listed, hard_weighted[j : j + 1, :], 0.0), axis=1, keepdims=True
        )
    matrix = jnp.dot(
        to_positives.astype(jnp.bfloat16), positive_hot_ref[...], preferred_element_type=jnp.float32
    ) + jnp.dot(
        to_queries.astype(jnp.bfloat16), query_hot_ref[...], preferred_element_type=jnp.float32
    )
    row_index = iota((sequences, total_rows), 1)
    for j in range(7):
        own_hard = jnp.sum(jnp.where(own_query, hard[j : j + 1, :], 0.0), axis=1, keepdims=True)
        own_listed = jnp.where(own_query, listed_ref[j : j + 1, :].astype(jnp.float32), 0.0)
        own_listed = jnp.sum(own_listed, axis=1, keepdims=True).astype(jnp.int32)
        listed = row_index == own_listed
        matrix = matrix + jnp.where(listed, own_hard, 0.0)
    matrix = matrix * inverse
    high = matrix.astype(jnp.bfloat16)
    low = (matrix - high.astype(jnp.float32)).astype(jnp.bfloat16)
    rows = rows_ref[...]
    d_embed = jnp.dot(high, rows, preferred_element_type=jnp.float32) + jnp.dot(
        low, rows, preferred_element_type=jnp.float32
    )

    is_own_row = row_index == first_row + iota((sequences, total_rows), 0)
    own_inverse = jnp.sum(jnp.where(is_own_row, inverse, 0.0), axis=1, keepdims=True)
    resid = resid_ref[...]
    gain = own_columns(gains_ref, resid.shape[1])
    features = gains_ref.shape[1]
    d_resid = own_inverse * gain * (
        d_embed - resid * gain * own_inverse * along
    ) - resid * (along * own_inverse * own_inverse * (EPSILON / features))
    d_resid16 = d_resid.astype(jnp.bfloat16)
    for t in range(out_ref.shape[0]):
        out_ref[t] = d_resid16
    loss_ref[0] = jnp.sum(hard_weighted[7:8, :]) / count


def kernel_call(body, outs, arrays, after=(), scratch=()):
    count = len(arrays)

    def kernel(*refs):
        body(*refs[:count], *refs[count + len(after) :])

    def out_spec(shape):
        return pl.BlockSpec(memory_space=pltpu.SMEM if shape == (1,) else pltpu.VMEM)

    return pl.pallas_call(
        kernel,
        out_shape=[jax.ShapeDtypeStruct(shape, dtype) for shape, dtype in outs],
        in_specs=[pl.BlockSpec(memory_space=pltpu.VMEM)] * count
        + [pl.BlockSpec(memory_space=pl.ANY)] * len(after),
        out_specs=[out_spec(shape) for shape, _ in outs],
        scratch_shapes=list(scratch),
        compiler_params=pltpu.CompilerParams(vmem_limit_bytes=VMEM_BYTES),
    )(*arrays, *after)


def candidate_kernel(positives_ref, negatives_ref, listed_ref, query_hot_ref, positive_hot_ref):
    query_count, total_rows = query_hot_ref.shape
    groups = query_count // QDEV
    sequences = total_rows // groups
    others = sequences - QDEV

    def row_of(passage):
        at = ((passage.astype(jnp.float32) + 0.5) * (1.0 / others)).astype(jnp.int32)
        return passage + at * QDEV + QDEV

    def query_row(query):
        return query + query // QDEV * others

    positive_row = row_of(positives_ref[...])
    count = negatives_ref.shape[0]
    listed_ref[:count, :] = row_of(negatives_ref[...])
    listed_ref[count : count + 1, :] = query_row(iota((1, query_count), 1))
    listed_ref[count + 1 :, :] = jnp.broadcast_to(
        positive_row, (listed_ref.shape[0] - count - 1, query_count)
    )
    shape = (LANES, total_rows)
    diagonal = iota((LANES, LANES), 0) == iota((LANES, LANES), 1)
    for k in range(query_count // LANES):
        rows = slice(LANES * k, LANES * (k + 1))
        query = query_row(iota(shape, 0) + LANES * k)
        query_hot_ref[rows, :] = (query == iota(shape, 1)).astype(jnp.float32).astype(jnp.bfloat16)
        lanes = positive_row[:, rows].astype(jnp.float32)
        column = jnp.sum(jnp.where(diagonal, lanes, 0.0), axis=1, keepdims=True)
        positive_hot_ref[rows, :] = (
            (column.astype(jnp.int32) == iota(shape, 1)).astype(jnp.float32).astype(jnp.bfloat16)
        )


def transpose_kernel(given_ref, out_ref, token_ref):
    out_ref[...] = given_ref[...].T
    token_ref[0] = jnp.float32(0.0)


def half_weights_kernel(kv_ref, query_ref, kept_ref, sent_ref):
    width, rows = kept_ref.shape[1], kv_ref.shape[1]
    parity = lax.axis_index("tensor") % 2
    for out_ref, half in ((kept_ref, parity), (sent_ref, 1 - parity)):
        features = pl.ds(pl.multiple_of(half * width, width), width)
        out_ref[:rows, :] = kv_ref[features, :].T
        out_ref[rows:, :] = query_ref[features, :].T


def contrast(everyone, resid, gains, tables, after, after_logits):
    tensor_count = lax.axis_size("tensor")
    sequences, width = resid.shape
    listed, query_hot, positive_hot = tables
    count, total_rows = positive_hot.shape
    rows = everyone.reshape(total_rows, width)
    lines = [[line * 4 + k for k in range(4)] for line in range(4)]
    across = [[k * 4 + line for k in range(4)] for line in range(4)]
    copies = ((4, count + 48, LANES), jnp.bfloat16)
    (sent,) = kernel_call(
        partial_logits_kernel,
        [copies],
        [rows, query_hot, positive_hot, listed, gains],
        after=after,
        scratch=[pltpu.VMEM((24, LANES), jnp.float32)],
    )
    (sent,) = kernel_call(pass_logits_kernel, [copies], [exchange(sent, "tensor", lines)])
    arrived = exchange(sent, "tensor", across)
    coefs, inverse = kernel_call(
        softmax_kernel,
        [((count + 24, LANES), jnp.float32), ((8, LANES), jnp.float32)],
        [arrived, positive_hot],
        after=after_logits,
    )
    both = lax.all_gather(coefs, "core", axis=0)
    d_resid16, loss = kernel_call(
        resid_grad_kernel,
        [((tensor_count, sequences, width), jnp.bfloat16), ((1,), jnp.float32)],
        [both, inverse, rows, positive_hot, query_hot, listed, resid, gains],
    )
    return loss, exchange(d_resid16, "tensor")


def copied_norm_kernel(hidden_ref, gain_ref, out_ref):
    hidden32 = hidden_ref[...].astype(jnp.float32)
    normed = (hidden32 * rms_scale(hidden32) * gain_ref[...]).astype(jnp.bfloat16)
    height = normed.shape[0]
    for c in range(normed.shape[1] // LANES):
        block = normed[:, LANES * c : LANES * (c + 1)]
        for t in range(out_ref.shape[0]):
            out_ref[t, height * c : height * (c + 1), :] = block


def projection_kernel(rows_ref, kv_weights_ref, query_weights_ref, kv_ref, sent_ref, query_ref):
    tensor_count, tall, _ = rows_ref.shape
    blocks = kv_weights_ref.shape[0] // LANES
    height = tall // blocks

    def block(c):
        part = rows_ref[:, height * c : height * (c + 1), :]
        return part.reshape(tensor_count * height, LANES)

    kv = jnp.zeros(kv_ref.shape, jnp.float32)
    query = jnp.zeros(query_ref.shape, jnp.float32)
    for c in range(0, blocks, 2):
        rows = jnp.concatenate([block(c), block(c + 1)], axis=1)
        columns = slice(LANES * c, LANES * (c + 2))
        kv = kv + jnp.dot(rows, kv_weights_ref[columns, :], preferred_element_type=jnp.float32)
        query = query + jnp.dot(
            rows, query_weights_ref[columns, :], preferred_element_type=jnp.float32
        )
    kv_ref[...] = kv
    sent_ref[...] = kv.astype(jnp.bfloat16)
    query_ref[...] = query


def half_turned(tensor, cosine, signed_sine):
    halfway = tensor.shape[1] // 2
    return tensor * cosine + pltpu.roll(tensor, halfway, 1) * signed_sine


def is_even_tensor():
    return lax.axis_index("tensor") % 2 == 0


def attention_kernel(
    own_ref,
    other_ref,
    query_all_ref,
    layout_ref,
    q_gain_ref,
    k_gain_ref,
    hidden_ref,
    wo_ref,
    out_ref,
    saved_ref,
):
    root = math.sqrt(own_ref.shape[1])
    tokens_count, sequences, own_rows = own_ref.shape[0], out_ref.shape[1], hidden_ref.shape[0]
    at, _ = layout_rows(tokens_count, sequences, own_rows)
    to, _ = saved_rows(tokens_count, sequences)
    is_even = is_even_tensor()
    own, other = own_ref[...], other_ref[...].astype(jnp.float32)
    key_raw = jnp.where(is_even, own, other)
    value16 = jnp.where(is_even, other, own).astype(jnp.bfloat16)
    query_raw = jnp.dot(
        unfolded(layout_ref[at["chosen"], :], sequences),
        query_all_ref[...],
        precision=lax.Precision.HIGHEST,
        preferred_element_type=jnp.float32,
    )
    q_gain, k_gain = q_gain_ref[...], k_gain_ref[...]
    key16 = half_turned(
        key_raw * rms_scale(key_raw) * k_gain,
        layout_ref[at["key_cosine"], :],
        layout_ref[at["key_sine"], :],
    ).astype(jnp.bfloat16)
    query16 = half_turned(
        query_raw * rms_scale(query_raw) * q_gain,
        layout_ref[at["query_cosine"], :],
        layout_ref[at["query_sine"], :],
    ).astype(jnp.bfloat16)
    shift = (
        root
        * jnp.max(q_gain, axis=1, keepdims=True)
        * jnp.max(k_gain, axis=1, keepdims=True)
    )
    scores = (
        lax.dot_general(
            query16, key16, (((1,), (1,)), ((), ())), preferred_element_type=jnp.float32
        )
        / root
    )
    inside = unfolded(layout_ref[at["inside"], :], sequences)
    weights = jnp.where(inside > 0.0, jnp.exp(scores - shift), 0.0)
    probs = weights / jnp.sum(weights, axis=1, keepdims=True)
    attn16 = jnp.dot(
        probs.astype(jnp.bfloat16), value16, preferred_element_type=jnp.float32
    ).astype(jnp.bfloat16)
    own_last = layout_ref[at["own_last"], :][:, :own_rows].astype(jnp.bfloat16)
    chunk = out_ref.shape[2]
    for t in range(out_ref.shape[0]):
        columns = slice(t * chunk, (t + 1) * chunk)
        block = jnp.dot(attn16, wo_ref[:, columns], preferred_element_type=jnp.float32)
        block = block + jnp.dot(
            own_last, hidden_ref[:, columns], preferred_element_type=jnp.float32
        )
        out_ref[t] = block.astype(jnp.bfloat16)
    saved_ref[to["key_raw"], :] = key_raw
    saved_ref[to["key"], :] = key16.astype(jnp.float32)
    saved_ref[to["value"], :] = value16.astype(jnp.float32)
    saved_ref[to["query_raw"], :] = query_raw
    saved_ref[to["query"], :] = query16.astype(jnp.float32)
    saved_ref[to["probs"], :] = folded(probs)


def resid_kernel(arrived_ref, gains_ref, resid_ref, out_ref):
    gain = own_columns(gains_ref, resid_ref.shape[1])
    resid = arrived_ref[0].astype(jnp.float32)
    for t in range(1, arrived_ref.shape[0]):
        resid = resid + arrived_ref[t].astype(jnp.float32)
    resid_ref[...] = resid
    scaled16 = (resid * gain).astype(jnp.bfloat16)
    for t in range(out_ref.shape[0]):
        out_ref[t] = scaled16


def gradient_kernel(
    d_resid_ref, wo_t_ref, saved_ref, layout_ref, q_gain_ref, k_gain_ref, own_ref, sent_ref
):
    head_width = saved_ref.shape[1]
    root = math.sqrt(head_width)
    sequences = d_resid_ref.shape[1]
    tensor_count = d_resid_ref.shape[0]
    tokens_count = (own_ref.shape[0] - sequences) // 2
    at, _ = layout_rows(tokens_count, sequences, tokens_count // tensor_count)
    to, _ = saved_rows(tokens_count, sequences)
    chunk = d_resid_ref.shape[2]
    d_attn = jnp.dot(d_resid_ref[0], wo_t_ref[:chunk, :], preferred_element_type=jnp.float32)
    for t in range(1, d_resid_ref.shape[0]):
        d_attn = d_attn + jnp.dot(
            d_resid_ref[t],
            wo_t_ref[t * chunk : (t + 1) * chunk, :],
            preferred_element_type=jnp.float32,
        )
    d_attn16 = d_attn.astype(jnp.bfloat16)
    probs = unfolded(saved_ref[to["probs"], :], sequences)
    key16 = saved_ref[to["key"], :].astype(jnp.bfloat16)
    query16 = saved_ref[to["query"], :].astype(jnp.bfloat16)
    value16 = saved_ref[to["value"], :].astype(jnp.bfloat16)
    d_probs = lax.dot_general(
        d_attn16, value16, (((1,), (1,)), ((), ())), preferred_element_type=jnp.float32
    )
    d_scores16 = (
        probs * (d_probs - jnp.sum(probs * d_probs, axis=1, keepdims=True)) / root
    ).astype(jnp.bfloat16)
    down = (((0,), (0,)), ((), ()))
    d_query_rot = jnp.dot(d_scores16, key16, preferred_element_type=jnp.float32)
    d_key_rot = lax.dot_general(d_scores16, query16, down, preferred_element_type=jnp.float32)
    d_value = lax.dot_general(
        probs.astype(jnp.bfloat16), d_attn16, down, preferred_element_type=jnp.float32
    )

    def head_gradient(grad_rot, name, gain):
        raw = saved_ref[to[name + "_raw"], :]
        inverse = rms_scale(raw)
        turned_back = half_turned(
            grad_rot, layout_ref[at[name + "_cosine"], :], -layout_ref[at[name + "_sine"], :]
        )
        return norm_backward(turned_back, raw * inverse, inverse, gain)

    d_key = head_gradient(d_key_rot, "key", k_gain_ref[...])
    d_query = head_gradient(d_query_rot, "query", q_gain_ref[...])
    own = jnp.concatenate([d_key, d_value, d_query], axis=0)
    own_ref[...] = own
    sent_ref[...] = own.astype(jnp.bfloat16)


def added_kernel(d_resid_ref, layout_ref, out_ref, token_ref):
    own_rows = out_ref.shape[0]
    tensor_count, sequences, chunk = d_resid_ref.shape
    at, _ = layout_rows(own_rows * tensor_count, sequences, own_rows)
    last = layout_ref[at["own_last_t"], :][:, :sequences].astype(jnp.bfloat16)
    for t in range(tensor_count):
        out_ref[:, t * chunk : (t + 1) * chunk] = jnp.dot(
            last, d_resid_ref[t], preferred_element_type=jnp.float32
        )
    token_ref[0] = jnp.float32(0.0)


def product_kernel(own_ref, other_ref, layout_ref, kept_ref, fetched_ref, out_ref):
    tensor_count, tall, _ = out_ref.shape
    height = tall * LANES // kept_ref.shape[1]
    tokens_count = height * tensor_count
    sequences = own_ref.shape[0] - 2 * tokens_count
    at, _ = layout_rows(tokens_count, sequences, height)
    chosen = unfolded(layout_ref[at["chosen"], :], sequences).astype(jnp.bfloat16)

    def spread(d_query):
        return lax.dot_general(
            chosen,
            d_query.astype(jnp.bfloat16),
            (((0,), (0,)), ((), ())),
            preferred_element_type=jnp.float32,
        )

    own, other = own_ref[...], other_ref[...].astype(jnp.float32)
    d_key = own[:tokens_count] + other[:tokens_count]
    d_value = own[tokens_count : 2 * tokens_count] + other[tokens_count : 2 * tokens_count]
    is_even = is_even_tensor()
    own16 = jnp.concatenate(
        [jnp.where(is_even, d_key, d_value), spread(own[2 * tokens_count :])], axis=1
    ).astype(jnp.bfloat16)
    other16 = jnp.concatenate(
        [jnp.where(is_even, d_value, d_key), spread(other[2 * tokens_count :])], axis=1
    ).astype(jnp.bfloat16)
    wide = 2 * LANES
    for k in range(kept_ref.shape[1] // wide):
        columns = slice(wide * k, wide * (k + 1))
        term = jnp.dot(own16, kept_ref[:, columns], preferred_element_type=jnp.float32)
        term = term + jnp.dot(
            other16, fetched_ref[:, columns], preferred_element_type=jnp.float32
        )
        term = term.astype(jnp.bfloat16)
        for c in (2 * k, 2 * k + 1):
            block = term[:, LANES * (c - 2 * k) : LANES * (c - 2 * k + 1)]
            out_ref[:, height * c : height * (c + 1), :] = block.reshape(-1, height, LANES)


def d_hidden_kernel(terms_ref, hidden_ref, gain_ref, added_ref, out_ref):
    hidden32 = hidden_ref[...].astype(jnp.float32)
    height = hidden32.shape[0]
    parts = []
    for parity in range(2):
        total = terms_ref[parity].astype(jnp.float32)
        for t in range(parity + 2, terms_ref.shape[0], 2):
            total = total + terms_ref[t].astype(jnp.float32)
        parts += [total[height * c : height * (c + 1)] for c in range(total.shape[0] // height)]
    d_normed = jnp.concatenate(parts, axis=1)
    inverse = rms_scale(hidden32)
    d_hidden = norm_backward(d_normed, hidden32 * inverse, inverse, gain_ref[...])
    out_ref[...] = (d_hidden + added_ref[...]).astype(jnp.bfloat16)


def packed_rows(sizes):
    starts, total = {}, 0
    for name, rows in sizes:
        starts[name] = slice(total, total + rows)
        total += rows
    return starts, total


def layout_rows(tokens_count, sequences, own_rows):
    wide = sequences * tokens_count // LANES
    return packed_rows(
        [
            ("key_cosine", tokens_count),
            ("key_sine", tokens_count),
            ("query_cosine", sequences),
            ("query_sine", sequences),
            ("inside", wide),
            ("chosen", wide),
            ("own_last", sequences),
            ("own_last_t", own_rows),
        ]
    )


def saved_rows(tokens_count, sequences):
    return packed_rows(
        [
            ("key_raw", tokens_count),
            ("key", tokens_count),
            ("value", tokens_count),
            ("query_raw", sequences),
            ("query", sequences),
            ("probs", sequences * tokens_count // LANES),
        ]
    )


def folded(block):
    parts = [block[:, LANES * k : LANES * (k + 1)] for k in range(block.shape[1] // LANES)]
    return jnp.concatenate(parts, axis=0)


def unfolded(block, rows):
    parts = [block[rows * k : rows * (k + 1)] for k in range(block.shape[0] // rows)]
    return jnp.concatenate(parts, axis=1)


def sequence_kernel(lengths_ref, out_ref, token_ref, *, tokens_count, own_rows):
    token_ref[0] = jnp.float32(0.0)
    sequences = lengths_ref.shape[1]
    at, _ = layout_rows(tokens_count, sequences, own_rows)
    lengths = lengths_ref[...].astype(jnp.float32)
    square = (sequences, sequences)
    ends = jnp.sum(
        jnp.where(iota(square, 1) <= iota(square, 0), lengths, 0.0), axis=1, keepdims=True
    )
    own_length = jnp.sum(
        jnp.where(iota(square, 1) == iota(square, 0), lengths, 0.0), axis=1, keepdims=True
    )
    starts = ends - own_length
    ends_row = jnp.sum(
        jnp.where(iota(square, 0) <= iota(square, 1), own_length, 0.0), axis=0, keepdims=True
    )
    starts_row = ends_row - lengths
    token = iota((sequences, tokens_count), 1).astype(jnp.float32)
    out_ref[at["inside"], :] = folded(((token >= starts) & (token < ends)).astype(jnp.float32))
    out_ref[at["chosen"], :] = folded((token == ends - 1.0).astype(jnp.float32))
    first = (lax.axis_index("tensor") * own_rows).astype(jnp.float32)
    own_token = iota((sequences, LANES), 1).astype(jnp.float32) + first
    own_token = jnp.where(iota((sequences, LANES), 1) < own_rows, own_token, -1.0)
    out_ref[at["own_last"], :] = (own_token == ends - 1.0).astype(jnp.float32)
    own_token = iota((own_rows, sequences), 0).astype(jnp.float32) + first
    own_last_t = (own_token == ends_row - 1.0).astype(jnp.float32)
    out_ref[at["own_last_t"], :] = jnp.concatenate(
        [own_last_t, jnp.zeros((own_rows, LANES - sequences), jnp.float32)], axis=1
    )
    token = iota((tokens_count, sequences), 0).astype(jnp.float32)
    held = (token >= starts_row) & (token < ends_row)
    position = jnp.sum(jnp.where(held, token - starts_row, 0.0), axis=1, keepdims=True)
    lane = iota((1, LANES), 1)
    halfway = LANES // 2
    pair = jnp.where(lane < halfway, lane, lane - halfway).astype(jnp.float32)
    frequency = jnp.exp(pair * (-2.0 / LANES * math.log(ROPE_BASE)))
    sign = jnp.where(lane < halfway, -1.0, 1.0)
    for name, place in (("key", position), ("query", own_length - 1.0)):
        angles = place * frequency
        out_ref[at[name + "_cosine"], :] = jnp.cos(angles)
        out_ref[at[name + "_sine"], :] = jnp.sin(angles) * sign


def on_device(
    hidden, lengths, positives, negatives, in_gain, wq, wkv, q_gain, k_gain, wo, out_gain
):
    tensor_count = lax.axis_size("tensor")
    z_count = lax.axis_size("z_far") * lax.axis_size("z_pair")
    own_rows, features = hidden.shape
    tokens_count = own_rows * tensor_count
    head_width = wq.shape[1]
    sequences = lengths.shape[1]
    query_count = positives.shape[0]
    total_rows = query_count // QDEV * sequences
    chunk = features // tensor_count
    f32, bf16 = jnp.float32, jnp.bfloat16
    head = (tokens_count, head_width)
    weights_shape = (head_width, features)
    flat = (tensor_count, own_rows * features // LANES, LANES)
    gain_rows = [q_gain[None, :], k_gain[None, :]]

    (copies,) = kernel_call(
        copied_norm_kernel, [(flat, bf16)], [hidden, in_gain[None, :]]
    )
    piece = exchange(copies, "tensor")
    kv_own, kv_own16, query_all = kernel_call(
        projection_kernel, [(head, f32), (head, bf16), (head, f32)], [piece, wkv, wq]
    )
    kv_other = swapped(kv_own16, "tensor", 0)
    def sequence_layout(after):
        return kernel_call(
            functools.partial(sequence_kernel, tokens_count=tokens_count, own_rows=own_rows),
            [((layout_rows(tokens_count, sequences, own_rows)[1], LANES), f32), ((1,), f32)],
            [lengths],
            after=[after],
        )

    layout, _ = sequence_layout(query_all)
    blocks, saved = kernel_call(
        attention_kernel,
        [
            ((tensor_count, sequences, chunk), bf16),
            ((saved_rows(tokens_count, sequences)[1], LANES), f32),
        ],
        [kv_own, kv_other, query_all, layout, *gain_rows, hidden, wo],
    )
    half_shape = (2 * head_width, features // 2)
    kept_weights, sent_weights = kernel_call(
        half_weights_kernel, [(half_shape, bf16), (half_shape, bf16)], [wkv, wq], after=[query_all]
    )
    other_weights = swapped(sent_weights, "tensor", 0)
    output_gain = out_gain[None, :]
    resid, scaled = kernel_call(
        resid_kernel,
        [((sequences, chunk), f32), ((z_count, sequences, chunk), bf16)],
        [exchange(blocks, "tensor"), output_gain],
    )
    wo_t, transposed = kernel_call(
        transpose_kernel, [((features, head_width), bf16), ((1,), f32)], [wo], after=[resid]
    )
    layout_again, placed = sequence_layout(resid)
    tables = kernel_call(
        candidate_kernel,
        [
            ((16, query_count), jnp.int32),
            ((query_count, total_rows), bf16),
            ((query_count, total_rows), bf16),
        ],
        [positives[None, :], negatives.T],
        after=[resid],
    )
    everyone = lax.all_gather(exchange(scaled, ("z_far", "z_pair")), "core", axis=1)
    loss, d_resid16 = contrast(
        everyone, resid, output_gain, tables, [transposed, placed], [other_weights]
    )
    gradient_shape = (2 * tokens_count + sequences, head_width)
    own_gradients, sent_gradients = kernel_call(
        gradient_kernel,
        [(gradient_shape, f32), (gradient_shape, bf16)],
        [d_resid16, wo_t, saved, layout_again, *gain_rows],
        after=[loss],
    )
    other_gradients = swapped(sent_gradients, "tensor", 0)
    added, summed = kernel_call(
        added_kernel, [((own_rows, features), f32), ((1,), f32)], [d_resid16, layout_again]
    )
    (product,) = kernel_call(
        product_kernel,
        [((tensor_count, own_rows * features // LANES // 2, LANES), bf16)],
        [own_gradients, other_gradients, layout_again, kept_weights, other_weights],
        after=[summed],
    )
    terms = exchange(product, "tensor")
    (d_hidden,) = kernel_call(
        d_hidden_kernel,
        [((own_rows, features), bf16)],
        [terms, hidden, in_gain[None, :], added],
    )
    return (d_hidden, loss[0])


def solution(mesh):
    z_count = mesh.shape["dp"] // 2
    chips = mesh.devices.reshape(z_count // 2, 2, 2, mesh.shape["tensor"])
    mesh = jax.sharding.Mesh(chips, ("z_far", "z_pair", "core", "tensor"))
    everywhere = P(("z_far", "z_pair", "core", "tensor"), None)
    placed = (
        everywhere,
        P(("z_far", "z_pair", "core"), None),
        P(),
        P(),
        P(),
        P(None, "tensor"),
        P(None, "tensor"),
        P(),
        P(),
        P("tensor", None),
        P(),
    )
    return jax.shard_map(
        on_device, mesh=mesh, in_specs=placed, out_specs=(everywhere, P()), check_vma=False
    )
```

```python
import functools
import math

import jax
import jax.numpy as jnp
from jax import lax
from jax.experimental import pallas as pl
from jax.experimental.pallas import tpu as pltpu
from jax.sharding import PartitionSpec as P

QDEV = 8
LANES = 128
VMEM_BYTES = 32 * 2**20


EPSILON = 1e-06
SOFTMAX_TEMPER = 0.05
LOSS_MULTIPLIER = 8192.0
ROPE_BASE = 1000000.0


def swapped(value, axis, apart):
    mask = 2**apart
    pairs = [(source, source ^ mask) for source in range(lax.axis_size(axis))]
    return lax.ppermute(value, axis, pairs)


def rms_scale(tensor):
    return lax.rsqrt(jnp.mean(tensor * tensor, axis=-1, keepdims=True) + EPSILON)


def norm_backward(grad, unit_form, inverse, gain):
    scaled = grad * gain
    return inverse * (scaled - unit_form * jnp.mean(unit_form * scaled, axis=-1, keepdims=True))


def exchange(blocks, axis, groups=None):
    return lax.all_to_all(blocks, axis, 0, 0, axis_index_groups=groups, tiled=True)


def halves(value):
    high = value.astype(jnp.bfloat16).astype(jnp.float32)
    return high, value - high


def iota(shape, axis):
    return lax.broadcasted_iota(jnp.int32, shape, axis)


def columns_to_lanes(column, out_ref):
    diagonal = iota((LANES, LANES), 0) == iota((LANES, LANES), 1)
    for k in range(column.shape[0] // LANES):
        block = jnp.where(diagonal, column[LANES * k : LANES * (k + 1)], 0.0)
        out_ref[k : k + 1, :] = jnp.sum(block, axis=0, keepdims=True)


def core_rows():
    return pl.ds(pl.multiple_of(lax.axis_index("core") * LANES, LANES), LANES)


def own_columns(gains_ref, width):
    start = pl.multiple_of(lax.axis_index("tensor") * width, width)
    return gains_ref[:, pl.ds(start, width)]


def partial_logits_kernel(
    rows_ref, query_hot_ref, positive_hot_ref, listed_all_ref, gains_ref, out_ref, held_ref
):
    rows = rows_ref[...]
    listed_ref = listed_all_ref[:8, core_rows()]
    block_hot = query_hot_ref[core_rows(), :]
    queries = jnp.dot(block_hot, rows, preferred_element_type=jnp.float32)
    positives = jnp.dot(positive_hot_ref[...], rows, preferred_element_type=jnp.float32)
    queries = queries.astype(jnp.bfloat16)
    features = gains_ref.shape[1]
    rows32 = rows.astype(jnp.float32)
    plain = rows32 * (1.0 / own_columns(gains_ref, rows.shape[1]))
    squares = jnp.sum(rows32 * rows32, axis=1, keepdims=True) + jnp.sum(
        plain * plain, axis=1, keepdims=True
    ) * (EPSILON / features)
    against = (((1,), (1,)), ((), ()))
    with_positives = lax.dot_general(
        positives.astype(jnp.bfloat16), queries, against, preferred_element_type=jnp.float32
    )
    with_all = lax.dot_general(rows, queries, against, preferred_element_type=jnp.float32)
    squares_all = jnp.broadcast_to(squares, with_all.shape)
    row_index = iota((LANES, LANES), 0)
    for j in range(8):
        product = jnp.zeros((LANES, LANES), jnp.float32)
        square = product
        for k in range(with_all.shape[0] // LANES):
            rows_at = slice(LANES * k, LANES * (k + 1))
            hit = row_index == listed_ref[j : j + 1, :] - LANES * k
            product = jnp.where(hit, with_all[rows_at], product)
            square = jnp.where(hit, squares_all[rows_at], square)
        held_ref[j : j + 1, :] = jnp.sum(product, axis=0, keepdims=True)
        held_ref[8 + j : 9 + j, :] = jnp.sum(square, axis=0, keepdims=True)
    columns_to_lanes(squares, held_ref.at[16:24])
    send_logits(with_positives, [held_ref[8 * k : 8 * (k + 1), :] for k in range(3)], out_ref)


def send_logits(logits, others, out_ref):
    count = logits.shape[0]
    logits16 = logits.astype(jnp.bfloat16)
    others16 = [jnp.concatenate(halves(other), axis=0).astype(jnp.bfloat16) for other in others]
    for t in range(out_ref.shape[0]):
        out_ref[t, :count, :] = logits16
        for k, other16 in enumerate(others16):
            out_ref[t, count + 16 * k : count + 16 * (k + 1), :] = other16


def summed_logits(arrived_ref):
    summed = arrived_ref[0].astype(jnp.float32)
    for t in range(1, arrived_ref.shape[0]):
        summed = summed + arrived_ref[t].astype(jnp.float32)
    count = summed.shape[0] - 48
    blocks = [summed[count + 16 * k : count + 16 * (k + 1)] for k in range(3)]
    return summed[:count], [block[:8] + block[8:] for block in blocks]


def pass_logits_kernel(arrived_ref, out_ref):
    logits, others = summed_logits(arrived_ref)
    send_logits(logits, others, out_ref)


def softmax_kernel(arrived_ref, positive_hot_ref, out_ref, inverse_ref):
    count = positive_hot_ref.shape[0]
    with_positives, (hard, listed_squares, squares) = summed_logits(arrived_ref)
    first_query = lax.axis_index("core") * LANES
    inverse_listed = lax.rsqrt(listed_squares + EPSILON * EPSILON)
    inverse = lax.rsqrt(squares + EPSILON * EPSILON)
    inverse_ref[...] = inverse
    inverse_query = inverse_listed[7:8, :]
    picked = jnp.zeros((count, LANES), jnp.float32)
    for k in range(8):
        hot = positive_hot_ref[:, LANES * k : LANES * (k + 1)].astype(jnp.float32)
        picked = picked + hot * inverse[k : k + 1, :]
    inverse_positive = jnp.sum(picked, axis=1, keepdims=True)
    logits = with_positives * inverse_positive * inverse_query / SOFTMAX_TEMPER
    hard = hard * inverse_listed * inverse_query / SOFTMAX_TEMPER
    is_hard = iota(hard.shape, 0) < 7
    is_own = iota(logits.shape, 0) == iota(logits.shape, 1) + first_query
    weights = jnp.exp(logits - 1.0 / SOFTMAX_TEMPER)
    hard_weights = jnp.where(is_hard, jnp.exp(hard - 1.0 / SOFTMAX_TEMPER), 0.0)
    totals = jnp.sum(weights, axis=0, keepdims=True) + jnp.sum(hard_weights, axis=0, keepdims=True)
    target = jnp.sum(jnp.where(is_own, logits, 0.0), axis=0, keepdims=True)
    losses = jnp.log(totals) + 1.0 / SOFTMAX_TEMPER - target
    scaling_factor = LOSS_MULTIPLIER / (count * SOFTMAX_TEMPER)

    def rounded(value):
        return value.astype(jnp.bfloat16).astype(jnp.float32)

    coef = rounded(scaling_factor * (weights / totals - is_own.astype(jnp.float32)))
    hard_coef = rounded(scaling_factor * (hard_weights / totals))
    weighted = coef * logits * SOFTMAX_TEMPER
    hard_weighted = jnp.where(is_hard, hard_coef * hard * SOFTMAX_TEMPER, 0.0)
    along_query = jnp.sum(weighted, axis=0, keepdims=True) + jnp.sum(
        hard_weighted, axis=0, keepdims=True
    )
    out_ref[:count, :] = coef
    out_ref[count : count + 8, :] = jnp.where(is_hard, hard_coef, along_query)
    out_ref[count + 8 : count + 16, :] = jnp.where(is_hard, hard_weighted, losses)
    out_ref[count + 16 :, :] = jnp.zeros_like(out_ref[count + 16 :, :])
    columns_to_lanes(jnp.sum(weighted, axis=1, keepdims=True), out_ref.at[count + 16 :])


def resid_grad_kernel(
    both_ref,
    inverse_ref,
    rows_ref,
    positive_hot_ref,
    query_hot_ref,
    listed_ref,
    resid_ref,
    gains_ref,
    out_ref,
    loss_ref,
):
    sequences = resid_ref.shape[0]
    count, total_rows = positive_hot_ref.shape
    z = lax.axis_index("z_far") * lax.axis_size("z_pair") + lax.axis_index("z_pair")
    group = z * lax.axis_size("core") + lax.axis_index("core")
    first_row = group * sequences
    first_query = group * QDEV
    across = (((1,), (1,)), ((), ()))

    def joined(start, stop):
        return jnp.concatenate([both_ref[0, start:stop, :], both_ref[1, start:stop, :]], axis=1)

    coef16 = joined(0, count).astype(jnp.bfloat16)
    hard = joined(count, count + 8)
    hard_weighted = joined(count + 8, count + 16)
    along_passage = both_ref[0, count + 16 :, :] + both_ref[1, count + 16 :, :]
    along_passage = jnp.concatenate([along_passage[0:1], along_passage[1:2]], axis=1)
    inverse = jnp.concatenate([inverse_ref[k : k + 1, :] for k in range(8)], axis=1)

    own_row = first_row + iota((sequences, count), 0)
    own_query = (iota((sequences, count), 0) < QDEV) & (
        iota((sequences, count), 1) == first_query + iota((sequences, count), 0)
    )
    own_positive = listed_ref[8:9, :] == own_row
    to_positives = lax.dot_general(
        own_query.astype(jnp.bfloat16), coef16, across, preferred_element_type=jnp.float32
    )
    to_queries = jnp.dot(
        own_positive.astype(jnp.bfloat16), coef16, preferred_element_type=jnp.float32
    )
    along = jnp.sum(
        jnp.where(own_query, hard[7:8, :], 0.0) + jnp.where(own_positive, along_passage, 0.0),
        axis=1,
        keepdims=True,
    )
    for j in range(7):
        listed = listed_ref[j : j + 1, :] == own_row
        to_queries = to_queries + jnp.where(listed, hard[j : j + 1, :], 0.0)
        along = along + jnp.sum(
            jnp.where(listed, hard_weighted[j : j + 1, :], 0.0), axis=1, keepdims=True
        )
    matrix = jnp.dot(
        to_positives.astype(jnp.bfloat16), positive_hot_ref[...], preferred_element_type=jnp.float32
    ) + jnp.dot(
        to_queries.astype(jnp.bfloat16), query_hot_ref[...], preferred_element_type=jnp.float32
    )
    row_index = iota((sequences, total_rows), 1)
    for j in range(7):
        own_hard = jnp.sum(jnp.where(own_query, hard[j : j + 1, :], 0.0), axis=1, keepdims=True)
        own_listed = jnp.where(own_query, listed_ref[j : j + 1, :].astype(jnp.float32), 0.0)
        own_listed = jnp.sum(own_listed, axis=1, keepdims=True).astype(jnp.int32)
        listed = row_index == own_listed
        matrix = matrix + jnp.where(listed, own_hard, 0.0)
    matrix = matrix * inverse
    high = matrix.astype(jnp.bfloat16)
    low = (matrix - high.astype(jnp.float32)).astype(jnp.bfloat16)
    rows = rows_ref[...]
    d_embed = jnp.dot(high, rows, preferred_element_type=jnp.float32) + jnp.dot(
        low, rows, preferred_element_type=jnp.float32
    )

    is_own_row = row_index == first_row + iota((sequences, total_rows), 0)
    own_inverse = jnp.sum(jnp.where(is_own_row, inverse, 0.0), axis=1, keepdims=True)
    resid = resid_ref[...]
    gain = own_columns(gains_ref, resid.shape[1])
    features = gains_ref.shape[1]
    d_resid = own_inverse * gain * (
        d_embed - resid * gain * own_inverse * along
    ) - resid * (along * own_inverse * own_inverse * (EPSILON / features))
    d_resid16 = d_resid.astype(jnp.bfloat16)
    for t in range(out_ref.shape[0]):
        out_ref[t] = d_resid16
    loss_ref[0] = jnp.sum(hard_weighted[7:8, :]) / count


def kernel_call(body, outs, arrays, after=(), scratch=()):
    count = len(arrays)

    def kernel(*refs):
        body(*refs[:count], *refs[count + len(after) :])

    def out_spec(shape):
        return pl.BlockSpec(memory_space=pltpu.SMEM if shape == (1,) else pltpu.VMEM)

    return pl.pallas_call(
        kernel,
        out_shape=[jax.ShapeDtypeStruct(shape, dtype) for shape, dtype in outs],
        in_specs=[pl.BlockSpec(memory_space=pltpu.VMEM)] * count
        + [pl.BlockSpec(memory_space=pl.ANY)] * len(after),
        out_specs=[out_spec(shape) for shape, _ in outs],
        scratch_shapes=list(scratch),
        compiler_params=pltpu.CompilerParams(vmem_limit_bytes=VMEM_BYTES),
    )(*arrays, *after)


def candidate_kernel(positives_ref, negatives_ref, listed_ref, query_hot_ref, positive_hot_ref):
    query_count, total_rows = query_hot_ref.shape
    groups = query_count // QDEV
    sequences = total_rows // groups
    others = sequences - QDEV

    def row_of(passage):
        at = ((passage.astype(jnp.float32) + 0.5) * (1.0 / others)).astype(jnp.int32)
        return passage + at * QDEV + QDEV

    def query_row(query):
        return query + query // QDEV * others

    positive_row = row_of(positives_ref[...])
    count = negatives_ref.shape[0]
    listed_ref[:count, :] = row_of(negatives_ref[...])
    listed_ref[count : count + 1, :] = query_row(iota((1, query_count), 1))
    listed_ref[count + 1 :, :] = jnp.broadcast_to(
        positive_row, (listed_ref.shape[0] - count - 1, query_count)
    )
    shape = (LANES, total_rows)
    diagonal = iota((LANES, LANES), 0) == iota((LANES, LANES), 1)
    for k in range(query_count // LANES):
        rows = slice(LANES * k, LANES * (k + 1))
        query = query_row(iota(shape, 0) + LANES * k)
        query_hot_ref[rows, :] = (query == iota(shape, 1)).astype(jnp.float32).astype(jnp.bfloat16)
        lanes = positive_row[:, rows].astype(jnp.float32)
        column = jnp.sum(jnp.where(diagonal, lanes, 0.0), axis=1, keepdims=True)
        positive_hot_ref[rows, :] = (
            (column.astype(jnp.int32) == iota(shape, 1)).astype(jnp.float32).astype(jnp.bfloat16)
        )


def transpose_kernel(given_ref, out_ref, token_ref):
    out_ref[...] = given_ref[...].T
    token_ref[0] = jnp.float32(0.0)


def half_weights_kernel(kv_ref, query_ref, kept_ref, sent_ref):
    width, rows = kept_ref.shape[1], kv_ref.shape[1]
    parity = lax.axis_index("tensor") % 2
    for out_ref, half in ((kept_ref, parity), (sent_ref, 1 - parity)):
        features = pl.ds(pl.multiple_of(half * width, width), width)
        out_ref[:rows, :] = kv_ref[features, :].T
        out_ref[rows:, :] = query_ref[features, :].T


def contrast(everyone, resid, gains, tables, after, after_logits):
    tensor_count = lax.axis_size("tensor")
    sequences, width = resid.shape
    listed, query_hot, positive_hot = tables
    count, total_rows = positive_hot.shape
    rows = everyone.reshape(total_rows, width)
    axes = ("z_far", "z_pair", "core", "tensor")
    lines = [[line * 4 + k for k in range(4)] for line in range(4)]
    across = [[k * 4 + line for k in range(4)] for line in range(4)]

    def everywhere(of_cores):
        planes = lax.axis_size("z_far") * lax.axis_size("z_pair") * lax.axis_size("core")
        return [
            [plane * tensor_count + t for t in line]
            for plane in range(planes)
            for line in of_cores[plane % 2]
        ]

    copies = ((4, count + 48, LANES), jnp.bfloat16)
    (sent,) = kernel_call(
        partial_logits_kernel,
        [copies],
        [rows, query_hot, positive_hot, listed, gains],
        after=after,
        scratch=[pltpu.VMEM((24, LANES), jnp.float32)],
    )
    (sent,) = kernel_call(pass_logits_kernel, [copies], [exchange(sent, axes, everywhere([lines, across]))])
    arrived = exchange(sent, axes, everywhere([across, lines]))
    coefs, inverse = kernel_call(
        softmax_kernel,
        [((count + 24, LANES), jnp.float32), ((8, LANES), jnp.float32)],
        [arrived, positive_hot],
        after=after_logits,
    )
    both = lax.all_gather(coefs, "core", axis=0)
    d_resid16, loss = kernel_call(
        resid_grad_kernel,
        [((tensor_count, sequences, width), jnp.bfloat16), ((1,), jnp.float32)],
        [both, inverse, rows, positive_hot, query_hot, listed, resid, gains],
    )
    return loss, exchange(d_resid16, "tensor")


def copied_norm_kernel(hidden_ref, gain_ref, out_ref):
    hidden32 = hidden_ref[...].astype(jnp.float32)
    normed = (hidden32 * rms_scale(hidden32) * gain_ref[...]).astype(jnp.bfloat16)
    height = normed.shape[0]
    for c in range(normed.shape[1] // LANES):
        block = normed[:, LANES * c : LANES * (c + 1)]
        for t in range(out_ref.shape[0]):
            out_ref[t, height * c : height * (c + 1), :] = block


def projection_kernel(rows_ref, kv_weights_ref, query_weights_ref, kv_ref, sent_ref, query_ref):
    tensor_count, tall, _ = rows_ref.shape
    blocks = kv_weights_ref.shape[0] // LANES
    height = tall // blocks

    def block(c):
        part = rows_ref[:, height * c : height * (c + 1), :]
        return part.reshape(tensor_count * height, LANES)

    kv = jnp.zeros(kv_ref.shape, jnp.float32)
    query = jnp.zeros(query_ref.shape, jnp.float32)
    for c in range(0, blocks, 2):
        rows = jnp.concatenate([block(c), block(c + 1)], axis=1)
        columns = slice(LANES * c, LANES * (c + 2))
        kv = kv + jnp.dot(rows, kv_weights_ref[columns, :], preferred_element_type=jnp.float32)
        query = query + jnp.dot(
            rows, query_weights_ref[columns, :], preferred_element_type=jnp.float32
        )
    kv_ref[...] = kv
    sent_ref[...] = kv.astype(jnp.bfloat16)
    query_ref[...] = query


def half_turned(tensor, cosine, signed_sine):
    halfway = tensor.shape[1] // 2
    return tensor * cosine + pltpu.roll(tensor, halfway, 1) * signed_sine


def is_even_tensor():
    return lax.axis_index("tensor") % 2 == 0


def attention_kernel(
    own_ref,
    other_ref,
    query_all_ref,
    layout_ref,
    q_gain_ref,
    k_gain_ref,
    hidden_ref,
    wo_ref,
    out_ref,
    saved_ref,
):
    root = math.sqrt(own_ref.shape[1])
    tokens_count, sequences, own_rows = own_ref.shape[0], out_ref.shape[1], hidden_ref.shape[0]
    at, _ = layout_rows(tokens_count, sequences, own_rows)
    to, _ = saved_rows(tokens_count, sequences)
    is_even = is_even_tensor()
    own, other = own_ref[...], other_ref[...].astype(jnp.float32)
    key_raw = jnp.where(is_even, own, other)
    value16 = jnp.where(is_even, other, own).astype(jnp.bfloat16)
    query_raw = jnp.dot(
        unfolded(layout_ref[at["chosen"], :], sequences),
        query_all_ref[...],
        precision=lax.Precision.HIGHEST,
        preferred_element_type=jnp.float32,
    )
    q_gain, k_gain = q_gain_ref[...], k_gain_ref[...]
    key16 = half_turned(
        key_raw * rms_scale(key_raw) * k_gain,
        layout_ref[at["key_cosine"], :],
        layout_ref[at["key_sine"], :],
    ).astype(jnp.bfloat16)
    query16 = half_turned(
        query_raw * rms_scale(query_raw) * q_gain,
        layout_ref[at["query_cosine"], :],
        layout_ref[at["query_sine"], :],
    ).astype(jnp.bfloat16)
    shift = (
        root
        * jnp.max(q_gain, axis=1, keepdims=True)
        * jnp.max(k_gain, axis=1, keepdims=True)
    )
    scores = (
        lax.dot_general(
            query16, key16, (((1,), (1,)), ((), ())), preferred_element_type=jnp.float32
        )
        / root
    )
    inside = unfolded(layout_ref[at["inside"], :], sequences)
    weights = jnp.where(inside > 0.0, jnp.exp(scores - shift), 0.0)
    probs = weights / jnp.sum(weights, axis=1, keepdims=True)
    attn16 = jnp.dot(
        probs.astype(jnp.bfloat16), value16, preferred_element_type=jnp.float32
    ).astype(jnp.bfloat16)
    own_last = layout_ref[at["own_last"], :][:, :own_rows].astype(jnp.bfloat16)
    chunk = out_ref.shape[2]
    for t in range(out_ref.shape[0]):
        columns = slice(t * chunk, (t + 1) * chunk)
        block = jnp.dot(attn16, wo_ref[:, columns], preferred_element_type=jnp.float32)
        block = block + jnp.dot(
            own_last, hidden_ref[:, columns], preferred_element_type=jnp.float32
        )
        out_ref[t] = block.astype(jnp.bfloat16)
    saved_ref[to["key_raw"], :] = key_raw
    saved_ref[to["key"], :] = key16.astype(jnp.float32)
    saved_ref[to["value"], :] = value16.astype(jnp.float32)
    saved_ref[to["query_raw"], :] = query_raw
    saved_ref[to["query"], :] = query16.astype(jnp.float32)
    saved_ref[to["probs"], :] = folded(probs)


def resid_kernel(arrived_ref, gains_ref, resid_ref, out_ref):
    gain = own_columns(gains_ref, resid_ref.shape[1])
    resid = arrived_ref[0].astype(jnp.float32)
    for t in range(1, arrived_ref.shape[0]):
        resid = resid + arrived_ref[t].astype(jnp.float32)
    resid_ref[...] = resid
    scaled16 = (resid * gain).astype(jnp.bfloat16)
    for t in range(out_ref.shape[0]):
        out_ref[t] = scaled16


def gradient_kernel(
    d_resid_ref, wo_t_ref, saved_ref, layout_ref, q_gain_ref, k_gain_ref, own_ref, sent_ref
):
    head_width = saved_ref.shape[1]
    root = math.sqrt(head_width)
    sequences = d_resid_ref.shape[1]
    tensor_count = d_resid_ref.shape[0]
    tokens_count = (own_ref.shape[0] - sequences) // 2
    at, _ = layout_rows(tokens_count, sequences, tokens_count // tensor_count)
    to, _ = saved_rows(tokens_count, sequences)
    chunk = d_resid_ref.shape[2]
    d_attn = jnp.dot(d_resid_ref[0], wo_t_ref[:chunk, :], preferred_element_type=jnp.float32)
    for t in range(1, d_resid_ref.shape[0]):
        d_attn = d_attn + jnp.dot(
            d_resid_ref[t],
            wo_t_ref[t * chunk : (t + 1) * chunk, :],
            preferred_element_type=jnp.float32,
        )
    d_attn16 = d_attn.astype(jnp.bfloat16)
    probs = unfolded(saved_ref[to["probs"], :], sequences)
    key16 = saved_ref[to["key"], :].astype(jnp.bfloat16)
    query16 = saved_ref[to["query"], :].astype(jnp.bfloat16)
    value16 = saved_ref[to["value"], :].astype(jnp.bfloat16)
    d_probs = lax.dot_general(
        d_attn16, value16, (((1,), (1,)), ((), ())), preferred_element_type=jnp.float32
    )
    d_scores16 = (
        probs * (d_probs - jnp.sum(probs * d_probs, axis=1, keepdims=True)) / root
    ).astype(jnp.bfloat16)
    down = (((0,), (0,)), ((), ()))
    d_query_rot = jnp.dot(d_scores16, key16, preferred_element_type=jnp.float32)
    d_key_rot = lax.dot_general(d_scores16, query16, down, preferred_element_type=jnp.float32)
    d_value = lax.dot_general(
        probs.astype(jnp.bfloat16), d_attn16, down, preferred_element_type=jnp.float32
    )

    def head_gradient(grad_rot, name, gain):
        raw = saved_ref[to[name + "_raw"], :]
        inverse = rms_scale(raw)
        turned_back = half_turned(
            grad_rot, layout_ref[at[name + "_cosine"], :], -layout_ref[at[name + "_sine"], :]
        )
        return norm_backward(turned_back, raw * inverse, inverse, gain)

    d_key = head_gradient(d_key_rot, "key", k_gain_ref[...])
    d_query = head_gradient(d_query_rot, "query", q_gain_ref[...])
    own = jnp.concatenate([d_key, d_value, d_query], axis=0)
    own_ref[...] = own
    sent_ref[...] = own.astype(jnp.bfloat16)


def added_kernel(d_resid_ref, layout_ref, out_ref, token_ref):
    own_rows = out_ref.shape[0]
    tensor_count, sequences, chunk = d_resid_ref.shape
    at, _ = layout_rows(own_rows * tensor_count, sequences, own_rows)
    last = layout_ref[at["own_last_t"], :][:, :sequences].astype(jnp.bfloat16)
    for t in range(tensor_count):
        out_ref[:, t * chunk : (t + 1) * chunk] = jnp.dot(
            last, d_resid_ref[t], preferred_element_type=jnp.float32
        )
    token_ref[0] = jnp.float32(0.0)


def product_kernel(own_ref, other_ref, layout_ref, kept_ref, fetched_ref, out_ref):
    tensor_count, tall, _ = out_ref.shape
    height = tall * LANES // kept_ref.shape[1]
    tokens_count = height * tensor_count
    sequences = own_ref.shape[0] - 2 * tokens_count
    at, _ = layout_rows(tokens_count, sequences, height)
    chosen = unfolded(layout_ref[at["chosen"], :], sequences).astype(jnp.bfloat16)

    def spread(d_query):
        return lax.dot_general(
            chosen,
            d_query.astype(jnp.bfloat16),
            (((0,), (0,)), ((), ())),
            preferred_element_type=jnp.float32,
        )

    own, other = own_ref[...], other_ref[...].astype(jnp.float32)
    d_key = own[:tokens_count] + other[:tokens_count]
    d_value = own[tokens_count : 2 * tokens_count] + other[tokens_count : 2 * tokens_count]
    is_even = is_even_tensor()
    own16 = jnp.concatenate(
        [jnp.where(is_even, d_key, d_value), spread(own[2 * tokens_count :])], axis=1
    ).astype(jnp.bfloat16)
    other16 = jnp.concatenate(
        [jnp.where(is_even, d_value, d_key), spread(other[2 * tokens_count :])], axis=1
    ).astype(jnp.bfloat16)
    wide = 2 * LANES
    for k in range(kept_ref.shape[1] // wide):
        columns = slice(wide * k, wide * (k + 1))
        term = jnp.dot(own16, kept_ref[:, columns], preferred_element_type=jnp.float32)
        term = term + jnp.dot(
            other16, fetched_ref[:, columns], preferred_element_type=jnp.float32
        )
        term = term.astype(jnp.bfloat16)
        for c in (2 * k, 2 * k + 1):
            block = term[:, LANES * (c - 2 * k) : LANES * (c - 2 * k + 1)]
            out_ref[:, height * c : height * (c + 1), :] = block.reshape(-1, height, LANES)


def d_hidden_kernel(terms_ref, hidden_ref, gain_ref, added_ref, out_ref):
    hidden32 = hidden_ref[...].astype(jnp.float32)
    height = hidden32.shape[0]
    parts = []
    for parity in range(2):
        total = terms_ref[parity].astype(jnp.float32)
        for t in range(parity + 2, terms_ref.shape[0], 2):
            total = total + terms_ref[t].astype(jnp.float32)
        parts += [total[height * c : height * (c + 1)] for c in range(total.shape[0] // height)]
    d_normed = jnp.concatenate(parts, axis=1)
    inverse = rms_scale(hidden32)
    d_hidden = norm_backward(d_normed, hidden32 * inverse, inverse, gain_ref[...])
    out_ref[...] = (d_hidden + added_ref[...]).astype(jnp.bfloat16)


def packed_rows(sizes):
    starts, total = {}, 0
    for name, rows in sizes:
        starts[name] = slice(total, total + rows)
        total += rows
    return starts, total


def layout_rows(tokens_count, sequences, own_rows):
    wide = sequences * tokens_count // LANES
    return packed_rows(
        [
            ("key_cosine", tokens_count),
            ("key_sine", tokens_count),
            ("query_cosine", sequences),
            ("query_sine", sequences),
            ("inside", wide),
            ("chosen", wide),
            ("own_last", sequences),
            ("own_last_t", own_rows),
        ]
    )


def saved_rows(tokens_count, sequences):
    return packed_rows(
        [
            ("key_raw", tokens_count),
            ("key", tokens_count),
            ("value", tokens_count),
            ("query_raw", sequences),
            ("query", sequences),
            ("probs", sequences * tokens_count // LANES),
        ]
    )


def folded(block):
    parts = [block[:, LANES * k : LANES * (k + 1)] for k in range(block.shape[1] // LANES)]
    return jnp.concatenate(parts, axis=0)


def unfolded(block, rows):
    parts = [block[rows * k : rows * (k + 1)] for k in range(block.shape[0] // rows)]
    return jnp.concatenate(parts, axis=1)


def sequence_kernel(lengths_ref, out_ref, token_ref, *, tokens_count, own_rows):
    token_ref[0] = jnp.float32(0.0)
    sequences = lengths_ref.shape[1]
    at, _ = layout_rows(tokens_count, sequences, own_rows)
    lengths = lengths_ref[...].astype(jnp.float32)
    square = (sequences, sequences)
    ends = jnp.sum(
        jnp.where(iota(square, 1) <= iota(square, 0), lengths, 0.0), axis=1, keepdims=True
    )
    own_length = jnp.sum(
        jnp.where(iota(square, 1) == iota(square, 0), lengths, 0.0), axis=1, keepdims=True
    )
    starts = ends - own_length
    ends_row = jnp.sum(
        jnp.where(iota(square, 0) <= iota(square, 1), own_length, 0.0), axis=0, keepdims=True
    )
    starts_row = ends_row - lengths
    token = iota((sequences, tokens_count), 1).astype(jnp.float32)
    out_ref[at["inside"], :] = folded(((token >= starts) & (token < ends)).astype(jnp.float32))
    out_ref[at["chosen"], :] = folded((token == ends - 1.0).astype(jnp.float32))
    first = (lax.axis_index("tensor") * own_rows).astype(jnp.float32)
    own_token = iota((sequences, LANES), 1).astype(jnp.float32) + first
    own_token = jnp.where(iota((sequences, LANES), 1) < own_rows, own_token, -1.0)
    out_ref[at["own_last"], :] = (own_token == ends - 1.0).astype(jnp.float32)
    own_token = iota((own_rows, sequences), 0).astype(jnp.float32) + first
    own_last_t = (own_token == ends_row - 1.0).astype(jnp.float32)
    out_ref[at["own_last_t"], :] = jnp.concatenate(
        [own_last_t, jnp.zeros((own_rows, LANES - sequences), jnp.float32)], axis=1
    )
    token = iota((tokens_count, sequences), 0).astype(jnp.float32)
    held = (token >= starts_row) & (token < ends_row)
    position = jnp.sum(jnp.where(held, token - starts_row, 0.0), axis=1, keepdims=True)
    lane = iota((1, LANES), 1)
    halfway = LANES // 2
    pair = jnp.where(lane < halfway, lane, lane - halfway).astype(jnp.float32)
    frequency = jnp.exp(pair * (-2.0 / LANES * math.log(ROPE_BASE)))
    sign = jnp.where(lane < halfway, -1.0, 1.0)
    for name, place in (("key", position), ("query", own_length - 1.0)):
        angles = place * frequency
        out_ref[at[name + "_cosine"], :] = jnp.cos(angles)
        out_ref[at[name + "_sine"], :] = jnp.sin(angles) * sign


def on_device(
    hidden, lengths, positives, negatives, in_gain, wq, wkv, q_gain, k_gain, wo, out_gain
):
    tensor_count = lax.axis_size("tensor")
    z_count = lax.axis_size("z_far") * lax.axis_size("z_pair")
    own_rows, features = hidden.shape
    tokens_count = own_rows * tensor_count
    head_width = wq.shape[1]
    sequences = lengths.shape[1]
    query_count = positives.shape[0]
    total_rows = query_count // QDEV * sequences
    chunk = features // tensor_count
    f32, bf16 = jnp.float32, jnp.bfloat16
    head = (tokens_count, head_width)
    weights_shape = (head_width, features)
    flat = (tensor_count, own_rows * features // LANES, LANES)
    gain_rows = [q_gain[None, :], k_gain[None, :]]

    (copies,) = kernel_call(
        copied_norm_kernel, [(flat, bf16)], [hidden, in_gain[None, :]]
    )
    piece = exchange(copies, "tensor")
    kv_own, kv_own16, query_all = kernel_call(
        projection_kernel, [(head, f32), (head, bf16), (head, f32)], [piece, wkv, wq]
    )
    kv_other = swapped(kv_own16, "tensor", 0)
    def sequence_layout(after):
        return kernel_call(
            functools.partial(sequence_kernel, tokens_count=tokens_count, own_rows=own_rows),
            [((layout_rows(tokens_count, sequences, own_rows)[1], LANES), f32), ((1,), f32)],
            [lengths],
            after=[after],
        )

    layout, _ = sequence_layout(query_all)
    blocks, saved = kernel_call(
        attention_kernel,
        [
            ((tensor_count, sequences, chunk), bf16),
            ((saved_rows(tokens_count, sequences)[1], LANES), f32),
        ],
        [kv_own, kv_other, query_all, layout, *gain_rows, hidden, wo],
    )
    half_shape = (2 * head_width, features // 2)
    kept_weights, sent_weights = kernel_call(
        half_weights_kernel, [(half_shape, bf16), (half_shape, bf16)], [wkv, wq], after=[query_all]
    )
    other_weights = swapped(sent_weights, "tensor", 0)
    output_gain = out_gain[None, :]
    resid, scaled = kernel_call(
        resid_kernel,
        [((sequences, chunk), f32), ((z_count, sequences, chunk), bf16)],
        [exchange(blocks, "tensor"), output_gain],
    )
    wo_t, transposed = kernel_call(
        transpose_kernel, [((features, head_width), bf16), ((1,), f32)], [wo], after=[resid]
    )
    layout_again, placed = sequence_layout(resid)
    tables = kernel_call(
        candidate_kernel,
        [
            ((16, query_count), jnp.int32),
            ((query_count, total_rows), bf16),
            ((query_count, total_rows), bf16),
        ],
        [positives[None, :], negatives.T],
        after=[resid],
    )
    everyone = lax.all_gather(exchange(scaled, ("z_far", "z_pair")), "core", axis=1)
    loss, d_resid16 = contrast(
        everyone, resid, output_gain, tables, [transposed, placed], [other_weights]
    )
    gradient_shape = (2 * tokens_count + sequences, head_width)
    own_gradients, sent_gradients = kernel_call(
        gradient_kernel,
        [(gradient_shape, f32), (gradient_shape, bf16)],
        [d_resid16, wo_t, saved, layout_again, *gain_rows],
        after=[loss],
    )
    other_gradients = swapped(sent_gradients, "tensor", 0)
    added, summed = kernel_call(
        added_kernel, [((own_rows, features), f32), ((1,), f32)], [d_resid16, layout_again]
    )
    (product,) = kernel_call(
        product_kernel,
        [((tensor_count, own_rows * features // LANES // 2, LANES), bf16)],
        [own_gradients, other_gradients, layout_again, kept_weights, other_weights],
        after=[summed],
    )
    terms = exchange(product, "tensor")
    (d_hidden,) = kernel_call(
        d_hidden_kernel,
        [((own_rows, features), bf16)],
        [terms, hidden, in_gain[None, :], added],
    )
    return (d_hidden, loss[0])


def solution(mesh):
    z_count = mesh.shape["dp"] // 2
    chips = mesh.devices.reshape(z_count // 2, 2, 2, mesh.shape["tensor"])
    mesh = jax.sharding.Mesh(chips, ("z_far", "z_pair", "core", "tensor"))
    everywhere = P(("z_far", "z_pair", "core", "tensor"), None)
    placed = (
        everywhere,
        P(("z_far", "z_pair", "core"), None),
        P(),
        P(),
        P(),
        P(None, "tensor"),
        P(None, "tensor"),
        P(),
        P(),
        P("tensor", None),
        P(),
    )
    return jax.shard_map(
        on_device, mesh=mesh, in_specs=placed, out_specs=(everywhere, P()), check_vma=False
    )
```

```python
import functools
import math

import jax
import jax.numpy as jnp
from jax import lax
from jax.experimental import pallas as pl
from jax.experimental.pallas import tpu as pltpu
from jax.sharding import PartitionSpec as P

QDEV = 8
LANES = 128
VMEM_BYTES = 32 * 2**20


EPSILON = 1e-06
SOFTMAX_TEMPER = 0.05
LOSS_MULTIPLIER = 8192.0
ROPE_BASE = 1000000.0


def swapped(value, axis, apart):
    mask = 2**apart
    pairs = [(source, source ^ mask) for source in range(lax.axis_size(axis))]
    return lax.ppermute(value, axis, pairs)


def rms_scale(tensor):
    return lax.rsqrt(jnp.mean(tensor * tensor, axis=-1, keepdims=True) + EPSILON)


def norm_backward(grad, unit_form, inverse, gain):
    scaled = grad * gain
    return inverse * (scaled - unit_form * jnp.mean(unit_form * scaled, axis=-1, keepdims=True))


def exchange(blocks, axis, groups=None):
    return lax.all_to_all(blocks, axis, 0, 0, axis_index_groups=groups, tiled=True)


def halves(value):
    high = value.astype(jnp.bfloat16).astype(jnp.float32)
    return high, value - high


def iota(shape, axis):
    return lax.broadcasted_iota(jnp.int32, shape, axis)


def columns_to_lanes(column, out_ref):
    diagonal = iota((LANES, LANES), 0) == iota((LANES, LANES), 1)
    for k in range(column.shape[0] // LANES):
        block = jnp.where(diagonal, column[LANES * k : LANES * (k + 1)], 0.0)
        out_ref[k : k + 1, :] = jnp.sum(block, axis=0, keepdims=True)


def core_rows():
    return pl.ds(pl.multiple_of(lax.axis_index("core") * LANES, LANES), LANES)


def own_columns(gains_ref, width):
    start = pl.multiple_of(lax.axis_index("tensor") * width, width)
    return gains_ref[:, pl.ds(start, width)]


def partial_logits_kernel(
    rows_ref, query_hot_ref, positive_hot_ref, listed_all_ref, gains_ref, out_ref, held_ref
):
    rows = rows_ref[...]
    listed_ref = listed_all_ref[:8, core_rows()]
    block_hot = query_hot_ref[core_rows(), :]
    queries = jnp.dot(block_hot, rows, preferred_element_type=jnp.float32)
    positives = jnp.dot(positive_hot_ref[...], rows, preferred_element_type=jnp.float32)
    queries = queries.astype(jnp.bfloat16)
    features = gains_ref.shape[1]
    rows32 = rows.astype(jnp.float32)
    plain = rows32 * (1.0 / own_columns(gains_ref, rows.shape[1]))
    squares = jnp.sum(rows32 * rows32, axis=1, keepdims=True) + jnp.sum(
        plain * plain, axis=1, keepdims=True
    ) * (EPSILON / features)
    against = (((1,), (1,)), ((), ()))
    with_positives = lax.dot_general(
        positives.astype(jnp.bfloat16), queries, against, preferred_element_type=jnp.float32
    )
    with_all = lax.dot_general(rows, queries, against, preferred_element_type=jnp.float32)
    squares_all = jnp.broadcast_to(squares, with_all.shape)
    row_index = iota((LANES, LANES), 0)
    for j in range(8):
        product = jnp.zeros((LANES, LANES), jnp.float32)
        square = product
        for k in range(with_all.shape[0] // LANES):
            rows_at = slice(LANES * k, LANES * (k + 1))
            hit = row_index == listed_ref[j : j + 1, :] - LANES * k
            product = jnp.where(hit, with_all[rows_at], product)
            square = jnp.where(hit, squares_all[rows_at], square)
        held_ref[j : j + 1, :] = jnp.sum(product, axis=0, keepdims=True)
        held_ref[8 + j : 9 + j, :] = jnp.sum(square, axis=0, keepdims=True)
    columns_to_lanes(squares, held_ref.at[16:24])
    send_logits(with_positives, [held_ref[8 * k : 8 * (k + 1), :] for k in range(3)], out_ref)


def send_logits(logits, others, out_ref):
    count = logits.shape[0]
    logits16 = logits.astype(jnp.bfloat16)
    others16 = [jnp.concatenate(halves(other), axis=0).astype(jnp.bfloat16) for other in others]
    for t in range(out_ref.shape[0]):
        out_ref[t, :count, :] = logits16
        for k, other16 in enumerate(others16):
            out_ref[t, count + 16 * k : count + 16 * (k + 1), :] = other16


def summed_logits(arrived_ref):
    summed = arrived_ref[0].astype(jnp.float32)
    for t in range(1, arrived_ref.shape[0]):
        summed = summed + arrived_ref[t].astype(jnp.float32)
    count = summed.shape[0] - 48
    blocks = [summed[count + 16 * k : count + 16 * (k + 1)] for k in range(3)]
    return summed[:count], [block[:8] + block[8:] for block in blocks]


def pass_logits_kernel(arrived_ref, out_ref):
    logits, others = summed_logits(arrived_ref)
    send_logits(logits, others, out_ref)


def softmax_kernel(arrived_ref, positive_hot_ref, out_ref, inverse_ref):
    count = positive_hot_ref.shape[0]
    with_positives, (hard, listed_squares, squares) = summed_logits(arrived_ref)
    first_query = lax.axis_index("core") * LANES
    inverse_listed = lax.rsqrt(listed_squares + EPSILON * EPSILON)
    inverse = lax.rsqrt(squares + EPSILON * EPSILON)
    inverse_ref[...] = inverse
    inverse_query = inverse_listed[7:8, :]
    picked = jnp.zeros((count, LANES), jnp.float32)
    for k in range(8):
        hot = positive_hot_ref[:, LANES * k : LANES * (k + 1)].astype(jnp.float32)
        picked = picked + hot * inverse[k : k + 1, :]
    inverse_positive = jnp.sum(picked, axis=1, keepdims=True)
    logits = with_positives * inverse_positive * inverse_query / SOFTMAX_TEMPER
    hard = hard * inverse_listed * inverse_query / SOFTMAX_TEMPER
    is_hard = iota(hard.shape, 0) < 7
    is_own = iota(logits.shape, 0) == iota(logits.shape, 1) + first_query
    weights = jnp.exp(logits - 1.0 / SOFTMAX_TEMPER)
    hard_weights = jnp.where(is_hard, jnp.exp(hard - 1.0 / SOFTMAX_TEMPER), 0.0)
    totals = jnp.sum(weights, axis=0, keepdims=True) + jnp.sum(hard_weights, axis=0, keepdims=True)
    target = jnp.sum(jnp.where(is_own, logits, 0.0), axis=0, keepdims=True)
    losses = jnp.log(totals) + 1.0 / SOFTMAX_TEMPER - target
    scaling_factor = LOSS_MULTIPLIER / (count * SOFTMAX_TEMPER)

    def rounded(value):
        return value.astype(jnp.bfloat16).astype(jnp.float32)

    coef = rounded(scaling_factor * (weights / totals - is_own.astype(jnp.float32)))
    hard_coef = rounded(scaling_factor * (hard_weights / totals))
    weighted = coef * logits * SOFTMAX_TEMPER
    hard_weighted = jnp.where(is_hard, hard_coef * hard * SOFTMAX_TEMPER, 0.0)
    along_query = jnp.sum(weighted, axis=0, keepdims=True) + jnp.sum(
        hard_weighted, axis=0, keepdims=True
    )
    out_ref[:count, :] = coef
    out_ref[count : count + 8, :] = jnp.where(is_hard, hard_coef, along_query)
    out_ref[count + 8 : count + 16, :] = jnp.where(is_hard, hard_weighted, losses)
    out_ref[count + 16 :, :] = jnp.zeros_like(out_ref[count + 16 :, :])
    columns_to_lanes(jnp.sum(weighted, axis=1, keepdims=True), out_ref.at[count + 16 :])


def resid_grad_kernel(
    both_ref,
    inverse_ref,
    rows_ref,
    positive_hot_ref,
    query_hot_ref,
    listed_ref,
    resid_ref,
    gains_ref,
    out_ref,
    loss_ref,
):
    sequences = resid_ref.shape[0]
    count, total_rows = positive_hot_ref.shape
    z = lax.axis_index("z_far") * lax.axis_size("z_pair") + lax.axis_index("z_pair")
    group = z * lax.axis_size("core") + lax.axis_index("core")
    first_row = group * sequences
    first_query = group * QDEV
    across = (((1,), (1,)), ((), ()))

    def joined(start, stop):
        return jnp.concatenate([both_ref[0, start:stop, :], both_ref[1, start:stop, :]], axis=1)

    coef16 = joined(0, count).astype(jnp.bfloat16)
    hard = joined(count, count + 8)
    hard_weighted = joined(count + 8, count + 16)
    along_passage = both_ref[0, count + 16 :, :] + both_ref[1, count + 16 :, :]
    along_passage = jnp.concatenate([along_passage[0:1], along_passage[1:2]], axis=1)
    inverse = jnp.concatenate([inverse_ref[k : k + 1, :] for k in range(8)], axis=1)

    own_row = first_row + iota((sequences, count), 0)
    own_query = (iota((sequences, count), 0) < QDEV) & (
        iota((sequences, count), 1) == first_query + iota((sequences, count), 0)
    )
    own_positive = listed_ref[8:9, :] == own_row
    to_positives = lax.dot_general(
        own_query.astype(jnp.bfloat16), coef16, across, preferred_element_type=jnp.float32
    )
    to_queries = jnp.dot(
        own_positive.astype(jnp.bfloat16), coef16, preferred_element_type=jnp.float32
    )
    along = jnp.sum(
        jnp.where(own_query, hard[7:8, :], 0.0) + jnp.where(own_positive, along_passage, 0.0),
        axis=1,
        keepdims=True,
    )
    for j in range(7):
        listed = listed_ref[j : j + 1, :] == own_row
        to_queries = to_queries + jnp.where(listed, hard[j : j + 1, :], 0.0)
        along = along + jnp.sum(
            jnp.where(listed, hard_weighted[j : j + 1, :], 0.0), axis=1, keepdims=True
        )
    matrix = jnp.dot(
        to_positives.astype(jnp.bfloat16), positive_hot_ref[...], preferred_element_type=jnp.float32
    ) + jnp.dot(
        to_queries.astype(jnp.bfloat16), query_hot_ref[...], preferred_element_type=jnp.float32
    )
    row_index = iota((sequences, total_rows), 1)
    for j in range(7):
        own_hard = jnp.sum(jnp.where(own_query, hard[j : j + 1, :], 0.0), axis=1, keepdims=True)
        own_listed = jnp.where(own_query, listed_ref[j : j + 1, :].astype(jnp.float32), 0.0)
        own_listed = jnp.sum(own_listed, axis=1, keepdims=True).astype(jnp.int32)
        listed = row_index == own_listed
        matrix = matrix + jnp.where(listed, own_hard, 0.0)
    matrix = matrix * inverse
    high = matrix.astype(jnp.bfloat16)
    low = (matrix - high.astype(jnp.float32)).astype(jnp.bfloat16)
    rows = rows_ref[...]
    d_embed = jnp.dot(high, rows, preferred_element_type=jnp.float32) + jnp.dot(
        low, rows, preferred_element_type=jnp.float32
    )

    is_own_row = row_index == first_row + iota((sequences, total_rows), 0)
    own_inverse = jnp.sum(jnp.where(is_own_row, inverse, 0.0), axis=1, keepdims=True)
    resid = resid_ref[...]
    gain = own_columns(gains_ref, resid.shape[1])
    features = gains_ref.shape[1]
    d_resid = own_inverse * gain * (
        d_embed - resid * gain * own_inverse * along
    ) - resid * (along * own_inverse * own_inverse * (EPSILON / features))
    d_resid16 = d_resid.astype(jnp.bfloat16)
    for t in range(out_ref.shape[0]):
        out_ref[t] = d_resid16
    loss_ref[0] = jnp.sum(hard_weighted[7:8, :]) / count


def kernel_call(body, outs, arrays, after=(), scratch=()):
    count = len(arrays)

    def kernel(*refs):
        body(*refs[:count], *refs[count + len(after) :])

    def out_spec(shape):
        return pl.BlockSpec(memory_space=pltpu.SMEM if shape == (1,) else pltpu.VMEM)

    return pl.pallas_call(
        kernel,
        out_shape=[jax.ShapeDtypeStruct(shape, dtype) for shape, dtype in outs],
        in_specs=[pl.BlockSpec(memory_space=pltpu.VMEM)] * count
        + [pl.BlockSpec(memory_space=pl.ANY)] * len(after),
        out_specs=[out_spec(shape) for shape, _ in outs],
        scratch_shapes=list(scratch),
        compiler_params=pltpu.CompilerParams(vmem_limit_bytes=VMEM_BYTES),
    )(*arrays, *after)


def candidate_kernel(positives_ref, negatives_ref, listed_ref, query_hot_ref, positive_hot_ref):
    query_count, total_rows = query_hot_ref.shape
    groups = query_count // QDEV
    sequences = total_rows // groups
    others = sequences - QDEV

    def row_of(passage):
        at = ((passage.astype(jnp.float32) + 0.5) * (1.0 / others)).astype(jnp.int32)
        return passage + at * QDEV + QDEV

    def query_row(query):
        return query + query // QDEV * others

    positive_row = row_of(positives_ref[...])
    count = negatives_ref.shape[0]
    listed_ref[:count, :] = row_of(negatives_ref[...])
    listed_ref[count : count + 1, :] = query_row(iota((1, query_count), 1))
    listed_ref[count + 1 :, :] = jnp.broadcast_to(
        positive_row, (listed_ref.shape[0] - count - 1, query_count)
    )
    shape = (LANES, total_rows)
    diagonal = iota((LANES, LANES), 0) == iota((LANES, LANES), 1)
    for k in range(query_count // LANES):
        rows = slice(LANES * k, LANES * (k + 1))
        query = query_row(iota(shape, 0) + LANES * k)
        query_hot_ref[rows, :] = (query == iota(shape, 1)).astype(jnp.float32).astype(jnp.bfloat16)
        lanes = positive_row[:, rows].astype(jnp.float32)
        column = jnp.sum(jnp.where(diagonal, lanes, 0.0), axis=1, keepdims=True)
        positive_hot_ref[rows, :] = (
            (column.astype(jnp.int32) == iota(shape, 1)).astype(jnp.float32).astype(jnp.bfloat16)
        )


def transpose_kernel(given_ref, out_ref, token_ref):
    out_ref[...] = given_ref[...].T
    token_ref[0] = jnp.float32(0.0)


def half_weights_kernel(kv_ref, query_ref, kept_ref, sent_ref):
    width, rows = kept_ref.shape[1], kv_ref.shape[1]
    parity = lax.axis_index("tensor") % 2
    for out_ref, half in ((kept_ref, parity), (sent_ref, 1 - parity)):
        features = pl.ds(pl.multiple_of(half * width, width), width)
        out_ref[:rows, :] = kv_ref[features, :].T
        out_ref[rows:, :] = query_ref[features, :].T


def contrast(everyone, resid, gains, tables, after, after_logits):
    tensor_count = lax.axis_size("tensor")
    sequences, width = resid.shape
    listed, query_hot, positive_hot = tables
    count, total_rows = positive_hot.shape
    rows = everyone.reshape(total_rows, width)
    axes = ("z_far", "z_pair", "core", "tensor")
    lines = [[line * 4 + k for k in range(4)] for line in range(4)]
    across = [[k * 4 + line for k in range(4)] for line in range(4)]

    def everywhere(of_cores):
        planes = lax.axis_size("z_far") * lax.axis_size("z_pair") * lax.axis_size("core")
        return [
            [plane * tensor_count + t for t in line]
            for plane in range(planes)
            for line in of_cores[plane % 2]
        ]

    copies = ((4, count + 48, LANES), jnp.bfloat16)
    (sent,) = kernel_call(
        partial_logits_kernel,
        [copies],
        [rows, query_hot, positive_hot, listed, gains],
        after=after,
        scratch=[pltpu.VMEM((24, LANES), jnp.float32)],
    )
    (sent,) = kernel_call(pass_logits_kernel, [copies], [exchange(sent, axes, everywhere([lines, across]))], after=after_logits)
    arrived = exchange(sent, axes, everywhere([across, lines]))
    coefs, inverse = kernel_call(
        softmax_kernel,
        [((count + 24, LANES), jnp.float32), ((8, LANES), jnp.float32)],
        [arrived, positive_hot],
    )
    both = lax.all_gather(coefs, "core", axis=0)
    d_resid16, loss = kernel_call(
        resid_grad_kernel,
        [((tensor_count, sequences, width), jnp.bfloat16), ((1,), jnp.float32)],
        [both, inverse, rows, positive_hot, query_hot, listed, resid, gains],
    )
    return loss, exchange(d_resid16, "tensor")


def copied_norm_kernel(hidden_ref, gain_ref, out_ref):
    hidden32 = hidden_ref[...].astype(jnp.float32)
    normed = (hidden32 * rms_scale(hidden32) * gain_ref[...]).astype(jnp.bfloat16)
    height = normed.shape[0]
    for c in range(normed.shape[1] // LANES):
        block = normed[:, LANES * c : LANES * (c + 1)]
        for t in range(out_ref.shape[0]):
            out_ref[t, height * c : height * (c + 1), :] = block


def projection_kernel(rows_ref, kv_weights_ref, query_weights_ref, kv_ref, sent_ref, query_ref):
    tensor_count, tall, _ = rows_ref.shape
    blocks = kv_weights_ref.shape[0] // LANES
    height = tall // blocks

    def block(c):
        part = rows_ref[:, height * c : height * (c + 1), :]
        return part.reshape(tensor_count * height, LANES)

    kv = jnp.zeros(kv_ref.shape, jnp.float32)
    query = jnp.zeros(query_ref.shape, jnp.float32)
    for c in range(0, blocks, 2):
        rows = jnp.concatenate([block(c), block(c + 1)], axis=1)
        columns = slice(LANES * c, LANES * (c + 2))
        kv = kv + jnp.dot(rows, kv_weights_ref[columns, :], preferred_element_type=jnp.float32)
        query = query + jnp.dot(
            rows, query_weights_ref[columns, :], preferred_element_type=jnp.float32
        )
    kv_ref[...] = kv
    sent_ref[...] = kv.astype(jnp.bfloat16)
    query_ref[...] = query


def half_turned(tensor, cosine, signed_sine):
    halfway = tensor.shape[1] // 2
    return tensor * cosine + pltpu.roll(tensor, halfway, 1) * signed_sine


def is_even_tensor():
    return lax.axis_index("tensor") % 2 == 0


def attention_kernel(
    own_ref,
    other_ref,
    query_all_ref,
    layout_ref,
    q_gain_ref,
    k_gain_ref,
    hidden_ref,
    wo_ref,
    out_ref,
    saved_ref,
):
    root = math.sqrt(own_ref.shape[1])
    tokens_count, sequences, own_rows = own_ref.shape[0], out_ref.shape[1], hidden_ref.shape[0]
    at, _ = layout_rows(tokens_count, sequences, own_rows)
    to, _ = saved_rows(tokens_count, sequences)
    is_even = is_even_tensor()
    own, other = own_ref[...], other_ref[...].astype(jnp.float32)
    key_raw = jnp.where(is_even, own, other)
    value16 = jnp.where(is_even, other, own).astype(jnp.bfloat16)
    query_raw = jnp.dot(
        unfolded(layout_ref[at["chosen"], :], sequences),
        query_all_ref[...],
        precision=lax.Precision.HIGHEST,
        preferred_element_type=jnp.float32,
    )
    q_gain, k_gain = q_gain_ref[...], k_gain_ref[...]
    key16 = half_turned(
        key_raw * rms_scale(key_raw) * k_gain,
        layout_ref[at["key_cosine"], :],
        layout_ref[at["key_sine"], :],
    ).astype(jnp.bfloat16)
    query16 = half_turned(
        query_raw * rms_scale(query_raw) * q_gain,
        layout_ref[at["query_cosine"], :],
        layout_ref[at["query_sine"], :],
    ).astype(jnp.bfloat16)
    shift = (
        root
        * jnp.max(q_gain, axis=1, keepdims=True)
        * jnp.max(k_gain, axis=1, keepdims=True)
    )
    scores = (
        lax.dot_general(
            query16, key16, (((1,), (1,)), ((), ())), preferred_element_type=jnp.float32
        )
        / root
    )
    inside = unfolded(layout_ref[at["inside"], :], sequences)
    weights = jnp.where(inside > 0.0, jnp.exp(scores - shift), 0.0)
    probs = weights / jnp.sum(weights, axis=1, keepdims=True)
    attn16 = jnp.dot(
        probs.astype(jnp.bfloat16), value16, preferred_element_type=jnp.float32
    ).astype(jnp.bfloat16)
    own_last = layout_ref[at["own_last"], :][:, :own_rows].astype(jnp.bfloat16)
    chunk = out_ref.shape[2]
    for t in range(out_ref.shape[0]):
        columns = slice(t * chunk, (t + 1) * chunk)
        block = jnp.dot(attn16, wo_ref[:, columns], preferred_element_type=jnp.float32)
        block = block + jnp.dot(
            own_last, hidden_ref[:, columns], preferred_element_type=jnp.float32
        )
        out_ref[t] = block.astype(jnp.bfloat16)
    saved_ref[to["key_raw"], :] = key_raw
    saved_ref[to["key"], :] = key16.astype(jnp.float32)
    saved_ref[to["value"], :] = value16.astype(jnp.float32)
    saved_ref[to["query_raw"], :] = query_raw
    saved_ref[to["query"], :] = query16.astype(jnp.float32)
    saved_ref[to["probs"], :] = folded(probs)


def resid_kernel(arrived_ref, gains_ref, resid_ref, out_ref):
    gain = own_columns(gains_ref, resid_ref.shape[1])
    resid = arrived_ref[0].astype(jnp.float32)
    for t in range(1, arrived_ref.shape[0]):
        resid = resid + arrived_ref[t].astype(jnp.float32)
    resid_ref[...] = resid
    scaled16 = (resid * gain).astype(jnp.bfloat16)
    for t in range(out_ref.shape[0]):
        out_ref[t] = scaled16


def gradient_kernel(
    d_resid_ref, wo_t_ref, saved_ref, layout_ref, q_gain_ref, k_gain_ref, own_ref, sent_ref
):
    head_width = saved_ref.shape[1]
    root = math.sqrt(head_width)
    sequences = d_resid_ref.shape[1]
    tensor_count = d_resid_ref.shape[0]
    tokens_count = (own_ref.shape[0] - sequences) // 2
    at, _ = layout_rows(tokens_count, sequences, tokens_count // tensor_count)
    to, _ = saved_rows(tokens_count, sequences)
    chunk = d_resid_ref.shape[2]
    d_attn = jnp.dot(d_resid_ref[0], wo_t_ref[:chunk, :], preferred_element_type=jnp.float32)
    for t in range(1, d_resid_ref.shape[0]):
        d_attn = d_attn + jnp.dot(
            d_resid_ref[t],
            wo_t_ref[t * chunk : (t + 1) * chunk, :],
            preferred_element_type=jnp.float32,
        )
    d_attn16 = d_attn.astype(jnp.bfloat16)
    probs = unfolded(saved_ref[to["probs"], :], sequences)
    key16 = saved_ref[to["key"], :].astype(jnp.bfloat16)
    query16 = saved_ref[to["query"], :].astype(jnp.bfloat16)
    value16 = saved_ref[to["value"], :].astype(jnp.bfloat16)
    d_probs = lax.dot_general(
        d_attn16, value16, (((1,), (1,)), ((), ())), preferred_element_type=jnp.float32
    )
    d_scores16 = (
        probs * (d_probs - jnp.sum(probs * d_probs, axis=1, keepdims=True)) / root
    ).astype(jnp.bfloat16)
    down = (((0,), (0,)), ((), ()))
    d_query_rot = jnp.dot(d_scores16, key16, preferred_element_type=jnp.float32)
    d_key_rot = lax.dot_general(d_scores16, query16, down, preferred_element_type=jnp.float32)
    d_value = lax.dot_general(
        probs.astype(jnp.bfloat16), d_attn16, down, preferred_element_type=jnp.float32
    )

    def head_gradient(grad_rot, name, gain):
        raw = saved_ref[to[name + "_raw"], :]
        inverse = rms_scale(raw)
        turned_back = half_turned(
            grad_rot, layout_ref[at[name + "_cosine"], :], -layout_ref[at[name + "_sine"], :]
        )
        return norm_backward(turned_back, raw * inverse, inverse, gain)

    d_key = head_gradient(d_key_rot, "key", k_gain_ref[...])
    d_query = head_gradient(d_query_rot, "query", q_gain_ref[...])
    own = jnp.concatenate([d_key, d_value, d_query], axis=0)
    own_ref[...] = own
    sent_ref[...] = own.astype(jnp.bfloat16)


def added_kernel(d_resid_ref, layout_ref, out_ref, token_ref):
    own_rows = out_ref.shape[0]
    tensor_count, sequences, chunk = d_resid_ref.shape
    at, _ = layout_rows(own_rows * tensor_count, sequences, own_rows)
    last = layout_ref[at["own_last_t"], :][:, :sequences].astype(jnp.bfloat16)
    for t in range(tensor_count):
        out_ref[:, t * chunk : (t + 1) * chunk] = jnp.dot(
            last, d_resid_ref[t], preferred_element_type=jnp.float32
        )
    token_ref[0] = jnp.float32(0.0)


def product_kernel(own_ref, other_ref, layout_ref, kept_ref, fetched_ref, out_ref):
    tensor_count, tall, _ = out_ref.shape
    height = tall * LANES // kept_ref.shape[1]
    tokens_count = height * tensor_count
    sequences = own_ref.shape[0] - 2 * tokens_count
    at, _ = layout_rows(tokens_count, sequences, height)
    chosen = unfolded(layout_ref[at["chosen"], :], sequences).astype(jnp.bfloat16)

    def spread(d_query):
        return lax.dot_general(
            chosen,
            d_query.astype(jnp.bfloat16),
            (((0,), (0,)), ((), ())),
            preferred_element_type=jnp.float32,
        )

    own, other = own_ref[...], other_ref[...].astype(jnp.float32)
    d_key = own[:tokens_count] + other[:tokens_count]
    d_value = own[tokens_count : 2 * tokens_count] + other[tokens_count : 2 * tokens_count]
    is_even = is_even_tensor()
    own16 = jnp.concatenate(
        [jnp.where(is_even, d_key, d_value), spread(own[2 * tokens_count :])], axis=1
    ).astype(jnp.bfloat16)
    other16 = jnp.concatenate(
        [jnp.where(is_even, d_value, d_key), spread(other[2 * tokens_count :])], axis=1
    ).astype(jnp.bfloat16)
    wide = 2 * LANES
    for k in range(kept_ref.shape[1] // wide):
        columns = slice(wide * k, wide * (k + 1))
        term = jnp.dot(own16, kept_ref[:, columns], preferred_element_type=jnp.float32)
        term = term + jnp.dot(
            other16, fetched_ref[:, columns], preferred_element_type=jnp.float32
        )
        term = term.astype(jnp.bfloat16)
        for c in (2 * k, 2 * k + 1):
            block = term[:, LANES * (c - 2 * k) : LANES * (c - 2 * k + 1)]
            out_ref[:, height * c : height * (c + 1), :] = block.reshape(-1, height, LANES)


def d_hidden_kernel(terms_ref, hidden_ref, gain_ref, added_ref, out_ref):
    hidden32 = hidden_ref[...].astype(jnp.float32)
    height = hidden32.shape[0]
    parts = []
    for parity in range(2):
        total = terms_ref[parity].astype(jnp.float32)
        for t in range(parity + 2, terms_ref.shape[0], 2):
            total = total + terms_ref[t].astype(jnp.float32)
        parts += [total[height * c : height * (c + 1)] for c in range(total.shape[0] // height)]
    d_normed = jnp.concatenate(parts, axis=1)
    inverse = rms_scale(hidden32)
    d_hidden = norm_backward(d_normed, hidden32 * inverse, inverse, gain_ref[...])
    out_ref[...] = (d_hidden + added_ref[...]).astype(jnp.bfloat16)


def packed_rows(sizes):
    starts, total = {}, 0
    for name, rows in sizes:
        starts[name] = slice(total, total + rows)
        total += rows
    return starts, total


def layout_rows(tokens_count, sequences, own_rows):
    wide = sequences * tokens_count // LANES
    return packed_rows(
        [
            ("key_cosine", tokens_count),
            ("key_sine", tokens_count),
            ("query_cosine", sequences),
            ("query_sine", sequences),
            ("inside", wide),
            ("chosen", wide),
            ("own_last", sequences),
            ("own_last_t", own_rows),
        ]
    )


def saved_rows(tokens_count, sequences):
    return packed_rows(
        [
            ("key_raw", tokens_count),
            ("key", tokens_count),
            ("value", tokens_count),
            ("query_raw", sequences),
            ("query", sequences),
            ("probs", sequences * tokens_count // LANES),
        ]
    )


def folded(block):
    parts = [block[:, LANES * k : LANES * (k + 1)] for k in range(block.shape[1] // LANES)]
    return jnp.concatenate(parts, axis=0)


def unfolded(block, rows):
    parts = [block[rows * k : rows * (k + 1)] for k in range(block.shape[0] // rows)]
    return jnp.concatenate(parts, axis=1)


def sequence_kernel(lengths_ref, out_ref, token_ref, *, tokens_count, own_rows):
    token_ref[0] = jnp.float32(0.0)
    sequences = lengths_ref.shape[1]
    at, _ = layout_rows(tokens_count, sequences, own_rows)
    lengths = lengths_ref[...].astype(jnp.float32)
    square = (sequences, sequences)
    ends = jnp.sum(
        jnp.where(iota(square, 1) <= iota(square, 0), lengths, 0.0), axis=1, keepdims=True
    )
    own_length = jnp.sum(
        jnp.where(iota(square, 1) == iota(square, 0), lengths, 0.0), axis=1, keepdims=True
    )
    starts = ends - own_length
    ends_row = jnp.sum(
        jnp.where(iota(square, 0) <= iota(square, 1), own_length, 0.0), axis=0, keepdims=True
    )
    starts_row = ends_row - lengths
    token = iota((sequences, tokens_count), 1).astype(jnp.float32)
    out_ref[at["inside"], :] = folded(((token >= starts) & (token < ends)).astype(jnp.float32))
    out_ref[at["chosen"], :] = folded((token == ends - 1.0).astype(jnp.float32))
    first = (lax.axis_index("tensor") * own_rows).astype(jnp.float32)
    own_token = iota((sequences, LANES), 1).astype(jnp.float32) + first
    own_token = jnp.where(iota((sequences, LANES), 1) < own_rows, own_token, -1.0)
    out_ref[at["own_last"], :] = (own_token == ends - 1.0).astype(jnp.float32)
    own_token = iota((own_rows, sequences), 0).astype(jnp.float32) + first
    own_last_t = (own_token == ends_row - 1.0).astype(jnp.float32)
    out_ref[at["own_last_t"], :] = jnp.concatenate(
        [own_last_t, jnp.zeros((own_rows, LANES - sequences), jnp.float32)], axis=1
    )
    token = iota((tokens_count, sequences), 0).astype(jnp.float32)
    held = (token >= starts_row) & (token < ends_row)
    position = jnp.sum(jnp.where(held, token - starts_row, 0.0), axis=1, keepdims=True)
    lane = iota((1, LANES), 1)
    halfway = LANES // 2
    pair = jnp.where(lane < halfway, lane, lane - halfway).astype(jnp.float32)
    frequency = jnp.exp(pair * (-2.0 / LANES * math.log(ROPE_BASE)))
    sign = jnp.where(lane < halfway, -1.0, 1.0)
    for name, place in (("key", position), ("query", own_length - 1.0)):
        angles = place * frequency
        out_ref[at[name + "_cosine"], :] = jnp.cos(angles)
        out_ref[at[name + "_sine"], :] = jnp.sin(angles) * sign


def on_device(
    hidden, lengths, positives, negatives, in_gain, wq, wkv, q_gain, k_gain, wo, out_gain
):
    tensor_count = lax.axis_size("tensor")
    z_count = lax.axis_size("z_far") * lax.axis_size("z_pair")
    own_rows, features = hidden.shape
    tokens_count = own_rows * tensor_count
    head_width = wq.shape[1]
    sequences = lengths.shape[1]
    query_count = positives.shape[0]
    total_rows = query_count // QDEV * sequences
    chunk = features // tensor_count
    f32, bf16 = jnp.float32, jnp.bfloat16
    head = (tokens_count, head_width)
    weights_shape = (head_width, features)
    flat = (tensor_count, own_rows * features // LANES, LANES)
    gain_rows = [q_gain[None, :], k_gain[None, :]]

    (copies,) = kernel_call(
        copied_norm_kernel, [(flat, bf16)], [hidden, in_gain[None, :]]
    )
    piece = exchange(copies, "tensor")
    kv_own, kv_own16, query_all = kernel_call(
        projection_kernel, [(head, f32), (head, bf16), (head, f32)], [piece, wkv, wq]
    )
    kv_other = swapped(kv_own16, "tensor", 0)
    def sequence_layout(after):
        return kernel_call(
            functools.partial(sequence_kernel, tokens_count=tokens_count, own_rows=own_rows),
            [((layout_rows(tokens_count, sequences, own_rows)[1], LANES), f32), ((1,), f32)],
            [lengths],
            after=[after],
        )

    layout, _ = sequence_layout(query_all)
    blocks, saved = kernel_call(
        attention_kernel,
        [
            ((tensor_count, sequences, chunk), bf16),
            ((saved_rows(tokens_count, sequences)[1], LANES), f32),
        ],
        [kv_own, kv_other, query_all, layout, *gain_rows, hidden, wo],
    )
    half_shape = (2 * head_width, features // 2)
    kept_weights, sent_weights = kernel_call(
        half_weights_kernel, [(half_shape, bf16), (half_shape, bf16)], [wkv, wq], after=[query_all]
    )
    other_weights = swapped(sent_weights, "tensor", 0)
    output_gain = out_gain[None, :]
    resid, scaled = kernel_call(
        resid_kernel,
        [((sequences, chunk), f32), ((z_count, sequences, chunk), bf16)],
        [exchange(blocks, "tensor"), output_gain],
    )
    wo_t, transposed = kernel_call(
        transpose_kernel, [((features, head_width), bf16), ((1,), f32)], [wo], after=[resid]
    )
    layout_again, placed = sequence_layout(resid)
    tables = kernel_call(
        candidate_kernel,
        [
            ((16, query_count), jnp.int32),
            ((query_count, total_rows), bf16),
            ((query_count, total_rows), bf16),
        ],
        [positives[None, :], negatives.T],
        after=[resid],
    )
    everyone = lax.all_gather(exchange(scaled, ("z_far", "z_pair")), "core", axis=1)
    loss, d_resid16 = contrast(
        everyone, resid, output_gain, tables, [transposed, placed], [other_weights]
    )
    gradient_shape = (2 * tokens_count + sequences, head_width)
    own_gradients, sent_gradients = kernel_call(
        gradient_kernel,
        [(gradient_shape, f32), (gradient_shape, bf16)],
        [d_resid16, wo_t, saved, layout_again, *gain_rows],
        after=[loss],
    )
    other_gradients = swapped(sent_gradients, "tensor", 0)
    added, summed = kernel_call(
        added_kernel, [((own_rows, features), f32), ((1,), f32)], [d_resid16, layout_again]
    )
    (product,) = kernel_call(
        product_kernel,
        [((tensor_count, own_rows * features // LANES // 2, LANES), bf16)],
        [own_gradients, other_gradients, layout_again, kept_weights, other_weights],
        after=[summed],
    )
    terms = exchange(product, "tensor")
    (d_hidden,) = kernel_call(
        d_hidden_kernel,
        [((own_rows, features), bf16)],
        [terms, hidden, in_gain[None, :], added],
    )
    return (d_hidden, loss[0])


def solution(mesh):
    z_count = mesh.shape["dp"] // 2
    chips = mesh.devices.reshape(z_count // 2, 2, 2, mesh.shape["tensor"])
    mesh = jax.sharding.Mesh(chips, ("z_far", "z_pair", "core", "tensor"))
    everywhere = P(("z_far", "z_pair", "core", "tensor"), None)
    placed = (
        everywhere,
        P(("z_far", "z_pair", "core"), None),
        P(),
        P(),
        P(),
        P(None, "tensor"),
        P(None, "tensor"),
        P(),
        P(),
        P("tensor", None),
        P(),
    )
    return jax.shard_map(
        on_device, mesh=mesh, in_specs=placed, out_specs=(everywhere, P()), check_vma=False
    )
```

```python
import functools
import math

import jax
import jax.numpy as jnp
from jax import lax
from jax.experimental import pallas as pl
from jax.experimental.pallas import tpu as pltpu
from jax.sharding import PartitionSpec as P

QDEV = 8
LANES = 128
VMEM_BYTES = 32 * 2**20


EPSILON = 1e-06
SOFTMAX_TEMPER = 0.05
LOSS_MULTIPLIER = 8192.0
ROPE_BASE = 1000000.0


def swapped(value, axis, apart):
    mask = 2**apart
    pairs = [(source, source ^ mask) for source in range(lax.axis_size(axis))]
    return lax.ppermute(value, axis, pairs)


def rms_scale(tensor):
    return lax.rsqrt(jnp.mean(tensor * tensor, axis=-1, keepdims=True) + EPSILON)


def norm_backward(grad, unit_form, inverse, gain):
    scaled = grad * gain
    return inverse * (scaled - unit_form * jnp.mean(unit_form * scaled, axis=-1, keepdims=True))


def exchange(blocks, axis, groups=None):
    return lax.all_to_all(blocks, axis, 0, 0, axis_index_groups=groups, tiled=True)


def halves(value):
    high = value.astype(jnp.bfloat16).astype(jnp.float32)
    return high, value - high


def iota(shape, axis):
    return lax.broadcasted_iota(jnp.int32, shape, axis)


def columns_to_lanes(column, out_ref):
    diagonal = iota((LANES, LANES), 0) == iota((LANES, LANES), 1)
    for k in range(column.shape[0] // LANES):
        block = jnp.where(diagonal, column[LANES * k : LANES * (k + 1)], 0.0)
        out_ref[k : k + 1, :] = jnp.sum(block, axis=0, keepdims=True)


def core_rows():
    return pl.ds(pl.multiple_of(lax.axis_index("core") * LANES, LANES), LANES)


def own_columns(gains_ref, width):
    start = pl.multiple_of(lax.axis_index("tensor") * width, width)
    return gains_ref[:, pl.ds(start, width)]


def partial_logits_kernel(
    rows_ref, query_hot_ref, positive_hot_ref, listed_all_ref, gains_ref, out_ref, held_ref
):
    rows = rows_ref[...]
    listed_ref = listed_all_ref[:8, core_rows()]
    block_hot = query_hot_ref[core_rows(), :]
    queries = jnp.dot(block_hot, rows, preferred_element_type=jnp.float32)
    positives = jnp.dot(positive_hot_ref[...], rows, preferred_element_type=jnp.float32)
    queries = queries.astype(jnp.bfloat16)
    features = gains_ref.shape[1]
    rows32 = rows.astype(jnp.float32)
    plain = rows32 * (1.0 / own_columns(gains_ref, rows.shape[1]))
    squares = jnp.sum(rows32 * rows32, axis=1, keepdims=True) + jnp.sum(
        plain * plain, axis=1, keepdims=True
    ) * (EPSILON / features)
    against = (((1,), (1,)), ((), ()))
    with_positives = lax.dot_general(
        positives.astype(jnp.bfloat16), queries, against, preferred_element_type=jnp.float32
    )
    with_all = lax.dot_general(rows, queries, against, preferred_element_type=jnp.float32)
    squares_all = jnp.broadcast_to(squares, with_all.shape)
    row_index = iota((LANES, LANES), 0)
    for j in range(8):
        product = jnp.zeros((LANES, LANES), jnp.float32)
        square = product
        for k in range(with_all.shape[0] // LANES):
            rows_at = slice(LANES * k, LANES * (k + 1))
            hit = row_index == listed_ref[j : j + 1, :] - LANES * k
            product = jnp.where(hit, with_all[rows_at], product)
            square = jnp.where(hit, squares_all[rows_at], square)
        held_ref[j : j + 1, :] = jnp.sum(product, axis=0, keepdims=True)
        held_ref[8 + j : 9 + j, :] = jnp.sum(square, axis=0, keepdims=True)
    columns_to_lanes(squares, held_ref.at[16:24])
    send_logits(with_positives, [held_ref[8 * k : 8 * (k + 1), :] for k in range(3)], out_ref)


def send_logits(logits, others, out_ref):
    count = logits.shape[0]
    logits16 = logits.astype(jnp.bfloat16)
    others16 = [jnp.concatenate(halves(other), axis=0).astype(jnp.bfloat16) for other in others]
    for t in range(out_ref.shape[0]):
        out_ref[t, :count, :] = logits16
        for k, other16 in enumerate(others16):
            out_ref[t, count + 16 * k : count + 16 * (k + 1), :] = other16


def summed_logits(arrived_ref):
    summed = arrived_ref[0].astype(jnp.float32)
    for t in range(1, arrived_ref.shape[0]):
        summed = summed + arrived_ref[t].astype(jnp.float32)
    count = summed.shape[0] - 48
    blocks = [summed[count + 16 * k : count + 16 * (k + 1)] for k in range(3)]
    return summed[:count], [block[:8] + block[8:] for block in blocks]


def pass_logits_kernel(arrived_ref, out_ref):
    logits, others = summed_logits(arrived_ref)
    send_logits(logits, others, out_ref)


def softmax_kernel(arrived_ref, positive_hot_ref, out_ref, inverse_ref):
    count = positive_hot_ref.shape[0]
    with_positives, (hard, listed_squares, squares) = summed_logits(arrived_ref)
    first_query = lax.axis_index("core") * LANES
    inverse_listed = lax.rsqrt(listed_squares + EPSILON * EPSILON)
    inverse = lax.rsqrt(squares + EPSILON * EPSILON)
    inverse_ref[...] = inverse
    inverse_query = inverse_listed[7:8, :]
    picked = jnp.zeros((count, LANES), jnp.float32)
    for k in range(8):
        hot = positive_hot_ref[:, LANES * k : LANES * (k + 1)].astype(jnp.float32)
        picked = picked + hot * inverse[k : k + 1, :]
    inverse_positive = jnp.sum(picked, axis=1, keepdims=True)
    logits = with_positives * inverse_positive * inverse_query / SOFTMAX_TEMPER
    hard = hard * inverse_listed * inverse_query / SOFTMAX_TEMPER
    is_hard = iota(hard.shape, 0) < 7
    is_own = iota(logits.shape, 0) == iota(logits.shape, 1) + first_query
    weights = jnp.exp(logits - 1.0 / SOFTMAX_TEMPER)
    hard_weights = jnp.where(is_hard, jnp.exp(hard - 1.0 / SOFTMAX_TEMPER), 0.0)
    totals = jnp.sum(weights, axis=0, keepdims=True) + jnp.sum(hard_weights, axis=0, keepdims=True)
    target = jnp.sum(jnp.where(is_own, logits, 0.0), axis=0, keepdims=True)
    losses = jnp.log(totals) + 1.0 / SOFTMAX_TEMPER - target
    scaling_factor = LOSS_MULTIPLIER / (count * SOFTMAX_TEMPER)

    def rounded(value):
        return value.astype(jnp.bfloat16).astype(jnp.float32)

    coef = rounded(scaling_factor * (weights / totals - is_own.astype(jnp.float32)))
    hard_coef = rounded(scaling_factor * (hard_weights / totals))
    weighted = coef * logits * SOFTMAX_TEMPER
    hard_weighted = jnp.where(is_hard, hard_coef * hard * SOFTMAX_TEMPER, 0.0)
    along_query = jnp.sum(weighted, axis=0, keepdims=True) + jnp.sum(
        hard_weighted, axis=0, keepdims=True
    )
    out_ref[:count, :] = coef
    out_ref[count : count + 8, :] = jnp.where(is_hard, hard_coef, along_query)
    out_ref[count + 8 : count + 16, :] = jnp.where(is_hard, hard_weighted, losses)
    out_ref[count + 16 :, :] = jnp.zeros_like(out_ref[count + 16 :, :])
    columns_to_lanes(jnp.sum(weighted, axis=1, keepdims=True), out_ref.at[count + 16 :])


def resid_grad_kernel(
    both_ref,
    inverse_ref,
    rows_ref,
    positive_hot_ref,
    query_hot_ref,
    listed_ref,
    resid_ref,
    gains_ref,
    out_ref,
    loss_ref,
):
    sequences = resid_ref.shape[0]
    count, total_rows = positive_hot_ref.shape
    z = lax.axis_index("z_far") * lax.axis_size("z_pair") + lax.axis_index("z_pair")
    group = z * lax.axis_size("core") + lax.axis_index("core")
    first_row = group * sequences
    first_query = group * QDEV
    across = (((1,), (1,)), ((), ()))

    def joined(start, stop):
        return jnp.concatenate([both_ref[0, start:stop, :], both_ref[1, start:stop, :]], axis=1)

    coef16 = joined(0, count).astype(jnp.bfloat16)
    hard = joined(count, count + 8)
    hard_weighted = joined(count + 8, count + 16)
    along_passage = both_ref[0, count + 16 :, :] + both_ref[1, count + 16 :, :]
    along_passage = jnp.concatenate([along_passage[0:1], along_passage[1:2]], axis=1)
    inverse = jnp.concatenate([inverse_ref[k : k + 1, :] for k in range(8)], axis=1)

    own_row = first_row + iota((sequences, count), 0)
    own_query = (iota((sequences, count), 0) < QDEV) & (
        iota((sequences, count), 1) == first_query + iota((sequences, count), 0)
    )
    own_positive = listed_ref[8:9, :] == own_row
    to_positives = lax.dot_general(
        own_query.astype(jnp.bfloat16), coef16, across, preferred_element_type=jnp.float32
    )
    to_queries = jnp.dot(
        own_positive.astype(jnp.bfloat16), coef16, preferred_element_type=jnp.float32
    )
    along = jnp.sum(
        jnp.where(own_query, hard[7:8, :], 0.0) + jnp.where(own_positive, along_passage, 0.0),
        axis=1,
        keepdims=True,
    )
    for j in range(7):
        listed = listed_ref[j : j + 1, :] == own_row
        to_queries = to_queries + jnp.where(listed, hard[j : j + 1, :], 0.0)
        along = along + jnp.sum(
            jnp.where(listed, hard_weighted[j : j + 1, :], 0.0), axis=1, keepdims=True
        )
    matrix = jnp.dot(
        to_positives.astype(jnp.bfloat16), positive_hot_ref[...], preferred_element_type=jnp.float32
    ) + jnp.dot(
        to_queries.astype(jnp.bfloat16), query_hot_ref[...], preferred_element_type=jnp.float32
    )
    row_index = iota((sequences, total_rows), 1)
    for j in range(7):
        own_hard = jnp.sum(jnp.where(own_query, hard[j : j + 1, :], 0.0), axis=1, keepdims=True)
        own_listed = jnp.where(own_query, listed_ref[j : j + 1, :].astype(jnp.float32), 0.0)
        own_listed = jnp.sum(own_listed, axis=1, keepdims=True).astype(jnp.int32)
        listed = row_index == own_listed
        matrix = matrix + jnp.where(listed, own_hard, 0.0)
    matrix = matrix * inverse
    high = matrix.astype(jnp.bfloat16)
    low = (matrix - high.astype(jnp.float32)).astype(jnp.bfloat16)
    rows = rows_ref[...]
    d_embed = jnp.dot(high, rows, preferred_element_type=jnp.float32) + jnp.dot(
        low, rows, preferred_element_type=jnp.float32
    )

    is_own_row = row_index == first_row + iota((sequences, total_rows), 0)
    own_inverse = jnp.sum(jnp.where(is_own_row, inverse, 0.0), axis=1, keepdims=True)
    resid = resid_ref[...]
    gain = own_columns(gains_ref, resid.shape[1])
    features = gains_ref.shape[1]
    d_resid = own_inverse * gain * (
        d_embed - resid * gain * own_inverse * along
    ) - resid * (along * own_inverse * own_inverse * (EPSILON / features))
    d_resid16 = d_resid.astype(jnp.bfloat16)
    for t in range(out_ref.shape[0]):
        out_ref[t] = d_resid16
    loss_ref[0] = jnp.sum(hard_weighted[7:8, :]) / count


def kernel_call(body, outs, arrays, after=(), scratch=()):
    count = len(arrays)

    def kernel(*refs):
        body(*refs[:count], *refs[count + len(after) :])

    def out_spec(shape):
        return pl.BlockSpec(memory_space=pltpu.SMEM if shape == (1,) else pltpu.VMEM)

    return pl.pallas_call(
        kernel,
        out_shape=[jax.ShapeDtypeStruct(shape, dtype) for shape, dtype in outs],
        in_specs=[pl.BlockSpec(memory_space=pltpu.VMEM)] * count
        + [pl.BlockSpec(memory_space=pl.ANY)] * len(after),
        out_specs=[out_spec(shape) for shape, _ in outs],
        scratch_shapes=list(scratch),
        compiler_params=pltpu.CompilerParams(vmem_limit_bytes=VMEM_BYTES),
    )(*arrays, *after)


def candidate_kernel(positives_ref, negatives_ref, listed_ref, query_hot_ref, positive_hot_ref):
    query_count, total_rows = query_hot_ref.shape
    groups = query_count // QDEV
    sequences = total_rows // groups
    others = sequences - QDEV

    def row_of(passage):
        at = ((passage.astype(jnp.float32) + 0.5) * (1.0 / others)).astype(jnp.int32)
        return passage + at * QDEV + QDEV

    def query_row(query):
        return query + query // QDEV * others

    positive_row = row_of(positives_ref[...])
    count = negatives_ref.shape[0]
    listed_ref[:count, :] = row_of(negatives_ref[...])
    listed_ref[count : count + 1, :] = query_row(iota((1, query_count), 1))
    listed_ref[count + 1 :, :] = jnp.broadcast_to(
        positive_row, (listed_ref.shape[0] - count - 1, query_count)
    )
    shape = (LANES, total_rows)
    diagonal = iota((LANES, LANES), 0) == iota((LANES, LANES), 1)
    for k in range(query_count // LANES):
        rows = slice(LANES * k, LANES * (k + 1))
        query = query_row(iota(shape, 0) + LANES * k)
        query_hot_ref[rows, :] = (query == iota(shape, 1)).astype(jnp.float32).astype(jnp.bfloat16)
        lanes = positive_row[:, rows].astype(jnp.float32)
        column = jnp.sum(jnp.where(diagonal, lanes, 0.0), axis=1, keepdims=True)
        positive_hot_ref[rows, :] = (
            (column.astype(jnp.int32) == iota(shape, 1)).astype(jnp.float32).astype(jnp.bfloat16)
        )


def transpose_kernel(given_ref, out_ref, token_ref):
    out_ref[...] = given_ref[...].T
    token_ref[0] = jnp.float32(0.0)


def half_weights_kernel(kv_ref, query_ref, kept_ref, sent_ref):
    width, rows = kept_ref.shape[1], kv_ref.shape[1]
    parity = lax.axis_index("tensor") % 2
    for out_ref, half in ((kept_ref, parity), (sent_ref, 1 - parity)):
        features = pl.ds(pl.multiple_of(half * width, width), width)
        out_ref[:rows, :] = kv_ref[features, :].T
        out_ref[rows:, :] = query_ref[features, :].T


def contrast(everyone, resid, gains, tables, after, after_logits):
    tensor_count = lax.axis_size("tensor")
    sequences, width = resid.shape
    listed, query_hot, positive_hot = tables
    count, total_rows = positive_hot.shape
    rows = everyone.reshape(total_rows, width)
    axes = ("z_far", "z_pair", "core", "tensor")
    lines = [[line * 4 + k for k in range(4)] for line in range(4)]
    across = [[k * 4 + line for k in range(4)] for line in range(4)]

    def everywhere(of_cores):
        planes = lax.axis_size("z_far") * lax.axis_size("z_pair") * lax.axis_size("core")
        return [
            [plane * tensor_count + t for t in line]
            for plane in range(planes)
            for line in of_cores[plane % 2]
        ]

    copies = ((4, count + 48, LANES), jnp.bfloat16)
    (sent,) = kernel_call(
        partial_logits_kernel,
        [copies],
        [rows, query_hot, positive_hot, listed, gains],
        after=after,
        scratch=[pltpu.VMEM((24, LANES), jnp.float32)],
    )
    (sent,) = kernel_call(pass_logits_kernel, [copies], [exchange(sent, axes, everywhere([lines, across]))])
    arrived = exchange(sent, axes, everywhere([across, lines]))
    coefs, inverse = kernel_call(
        softmax_kernel,
        [((count + 24, LANES), jnp.float32), ((8, LANES), jnp.float32)],
        [arrived, positive_hot],
        after=after_logits,
    )
    both = lax.all_gather(coefs, "core", axis=0)
    d_resid16, loss = kernel_call(
        resid_grad_kernel,
        [((tensor_count, sequences, width), jnp.bfloat16), ((1,), jnp.float32)],
        [both, inverse, rows, positive_hot, query_hot, listed, resid, gains],
    )
    return loss, exchange(d_resid16, "tensor")


def unit_rows_kernel(hidden_ref, out_ref):
    hidden32 = hidden_ref[...].astype(jnp.float32)
    out_ref[...] = hidden32 * rms_scale(hidden32)


def copied_norm_kernel(unit_ref, gain_ref, out_ref):
    normed = (unit_ref[...] * gain_ref[...]).astype(jnp.bfloat16)
    height = normed.shape[0]
    for c in range(normed.shape[1] // LANES):
        block = normed[:, LANES * c : LANES * (c + 1)]
        for t in range(out_ref.shape[0]):
            out_ref[t, height * c : height * (c + 1), :] = block


def projection_kernel(rows_ref, kv_weights_ref, query_weights_ref, kv_ref, sent_ref, query_ref):
    tensor_count, tall, _ = rows_ref.shape
    blocks = kv_weights_ref.shape[0] // LANES
    height = tall // blocks

    def block(c):
        part = rows_ref[:, height * c : height * (c + 1), :]
        return part.reshape(tensor_count * height, LANES)

    kv = jnp.zeros(kv_ref.shape, jnp.float32)
    query = jnp.zeros(query_ref.shape, jnp.float32)
    for c in range(0, blocks, 2):
        rows = jnp.concatenate([block(c), block(c + 1)], axis=1)
        columns = slice(LANES * c, LANES * (c + 2))
        kv = kv + jnp.dot(rows, kv_weights_ref[columns, :], preferred_element_type=jnp.float32)
        query = query + jnp.dot(
            rows, query_weights_ref[columns, :], preferred_element_type=jnp.float32
        )
    kv_ref[...] = kv
    sent_ref[...] = kv.astype(jnp.bfloat16)
    query_ref[...] = query


def half_turned(tensor, cosine, signed_sine):
    halfway = tensor.shape[1] // 2
    return tensor * cosine + pltpu.roll(tensor, halfway, 1) * signed_sine


def is_even_tensor():
    return lax.axis_index("tensor") % 2 == 0


def attention_kernel(
    own_ref,
    other_ref,
    query_all_ref,
    layout_ref,
    q_gain_ref,
    k_gain_ref,
    hidden_ref,
    wo_ref,
    out_ref,
    saved_ref,
):
    root = math.sqrt(own_ref.shape[1])
    tokens_count, sequences, own_rows = own_ref.shape[0], out_ref.shape[1], hidden_ref.shape[0]
    at, _ = layout_rows(tokens_count, sequences, own_rows)
    to, _ = saved_rows(tokens_count, sequences)
    is_even = is_even_tensor()
    own, other = own_ref[...], other_ref[...].astype(jnp.float32)
    key_raw = jnp.where(is_even, own, other)
    value16 = jnp.where(is_even, other, own).astype(jnp.bfloat16)
    query_raw = jnp.dot(
        unfolded(layout_ref[at["chosen"], :], sequences),
        query_all_ref[...],
        precision=lax.Precision.HIGHEST,
        preferred_element_type=jnp.float32,
    )
    q_gain, k_gain = q_gain_ref[...], k_gain_ref[...]
    key16 = half_turned(
        key_raw * rms_scale(key_raw) * k_gain,
        layout_ref[at["key_cosine"], :],
        layout_ref[at["key_sine"], :],
    ).astype(jnp.bfloat16)
    query16 = half_turned(
        query_raw * rms_scale(query_raw) * q_gain,
        layout_ref[at["query_cosine"], :],
        layout_ref[at["query_sine"], :],
    ).astype(jnp.bfloat16)
    shift = (
        root
        * jnp.max(q_gain, axis=1, keepdims=True)
        * jnp.max(k_gain, axis=1, keepdims=True)
    )
    scores = (
        lax.dot_general(
            query16, key16, (((1,), (1,)), ((), ())), preferred_element_type=jnp.float32
        )
        / root
    )
    inside = unfolded(layout_ref[at["inside"], :], sequences)
    weights = jnp.where(inside > 0.0, jnp.exp(scores - shift), 0.0)
    probs = weights / jnp.sum(weights, axis=1, keepdims=True)
    attn16 = jnp.dot(
        probs.astype(jnp.bfloat16), value16, preferred_element_type=jnp.float32
    ).astype(jnp.bfloat16)
    own_last = layout_ref[at["own_last"], :][:, :own_rows].astype(jnp.bfloat16)
    chunk = out_ref.shape[2]
    for t in range(out_ref.shape[0]):
        columns = slice(t * chunk, (t + 1) * chunk)
        block = jnp.dot(attn16, wo_ref[:, columns], preferred_element_type=jnp.float32)
        block = block + jnp.dot(
            own_last, hidden_ref[:, columns], preferred_element_type=jnp.float32
        )
        out_ref[t] = block.astype(jnp.bfloat16)
    saved_ref[to["key_raw"], :] = key_raw
    saved_ref[to["key"], :] = key16.astype(jnp.float32)
    saved_ref[to["value"], :] = value16.astype(jnp.float32)
    saved_ref[to["query_raw"], :] = query_raw
    saved_ref[to["query"], :] = query16.astype(jnp.float32)
    saved_ref[to["probs"], :] = folded(probs)


def resid_kernel(arrived_ref, gains_ref, resid_ref, out_ref):
    gain = own_columns(gains_ref, resid_ref.shape[1])
    resid = arrived_ref[0].astype(jnp.float32)
    for t in range(1, arrived_ref.shape[0]):
        resid = resid + arrived_ref[t].astype(jnp.float32)
    resid_ref[...] = resid
    scaled16 = (resid * gain).astype(jnp.bfloat16)
    for t in range(out_ref.shape[0]):
        out_ref[t] = scaled16


def gradient_kernel(
    d_resid_ref, wo_t_ref, saved_ref, layout_ref, q_gain_ref, k_gain_ref, own_ref, sent_ref
):
    head_width = saved_ref.shape[1]
    root = math.sqrt(head_width)
    sequences = d_resid_ref.shape[1]
    tensor_count = d_resid_ref.shape[0]
    tokens_count = (own_ref.shape[0] - sequences) // 2
    at, _ = layout_rows(tokens_count, sequences, tokens_count // tensor_count)
    to, _ = saved_rows(tokens_count, sequences)
    chunk = d_resid_ref.shape[2]
    d_attn = jnp.dot(d_resid_ref[0], wo_t_ref[:chunk, :], preferred_element_type=jnp.float32)
    for t in range(1, d_resid_ref.shape[0]):
        d_attn = d_attn + jnp.dot(
            d_resid_ref[t],
            wo_t_ref[t * chunk : (t + 1) * chunk, :],
            preferred_element_type=jnp.float32,
        )
    d_attn16 = d_attn.astype(jnp.bfloat16)
    probs = unfolded(saved_ref[to["probs"], :], sequences)
    key16 = saved_ref[to["key"], :].astype(jnp.bfloat16)
    query16 = saved_ref[to["query"], :].astype(jnp.bfloat16)
    value16 = saved_ref[to["value"], :].astype(jnp.bfloat16)
    d_probs = lax.dot_general(
        d_attn16, value16, (((1,), (1,)), ((), ())), preferred_element_type=jnp.float32
    )
    d_scores16 = (
        probs * (d_probs - jnp.sum(probs * d_probs, axis=1, keepdims=True)) / root
    ).astype(jnp.bfloat16)
    down = (((0,), (0,)), ((), ()))
    d_query_rot = jnp.dot(d_scores16, key16, preferred_element_type=jnp.float32)
    d_key_rot = lax.dot_general(d_scores16, query16, down, preferred_element_type=jnp.float32)
    d_value = lax.dot_general(
        probs.astype(jnp.bfloat16), d_attn16, down, preferred_element_type=jnp.float32
    )

    def head_gradient(grad_rot, name, gain):
        raw = saved_ref[to[name + "_raw"], :]
        inverse = rms_scale(raw)
        turned_back = half_turned(
            grad_rot, layout_ref[at[name + "_cosine"], :], -layout_ref[at[name + "_sine"], :]
        )
        return norm_backward(turned_back, raw * inverse, inverse, gain)

    d_key = head_gradient(d_key_rot, "key", k_gain_ref[...])
    d_query = head_gradient(d_query_rot, "query", q_gain_ref[...])
    own = jnp.concatenate([d_key, d_value, d_query], axis=0)
    own_ref[...] = own
    sent_ref[...] = own.astype(jnp.bfloat16)


def added_kernel(d_resid_ref, layout_ref, out_ref, token_ref):
    own_rows = out_ref.shape[0]
    tensor_count, sequences, chunk = d_resid_ref.shape
    at, _ = layout_rows(own_rows * tensor_count, sequences, own_rows)
    last = layout_ref[at["own_last_t"], :][:, :sequences].astype(jnp.bfloat16)
    for t in range(tensor_count):
        out_ref[:, t * chunk : (t + 1) * chunk] = jnp.dot(
            last, d_resid_ref[t], preferred_element_type=jnp.float32
        )
    token_ref[0] = jnp.float32(0.0)


def product_kernel(own_ref, other_ref, layout_ref, kept_ref, fetched_ref, out_ref):
    tensor_count, tall, _ = out_ref.shape
    height = tall * LANES // kept_ref.shape[1]
    tokens_count = height * tensor_count
    sequences = own_ref.shape[0] - 2 * tokens_count
    at, _ = layout_rows(tokens_count, sequences, height)
    chosen = unfolded(layout_ref[at["chosen"], :], sequences).astype(jnp.bfloat16)

    def spread(d_query):
        return lax.dot_general(
            chosen,
            d_query.astype(jnp.bfloat16),
            (((0,), (0,)), ((), ())),
            preferred_element_type=jnp.float32,
        )

    own, other = own_ref[...], other_ref[...].astype(jnp.float32)
    d_key = own[:tokens_count] + other[:tokens_count]
    d_value = own[tokens_count : 2 * tokens_count] + other[tokens_count : 2 * tokens_count]
    is_even = is_even_tensor()
    own16 = jnp.concatenate(
        [jnp.where(is_even, d_key, d_value), spread(own[2 * tokens_count :])], axis=1
    ).astype(jnp.bfloat16)
    other16 = jnp.concatenate(
        [jnp.where(is_even, d_value, d_key), spread(other[2 * tokens_count :])], axis=1
    ).astype(jnp.bfloat16)
    wide = 2 * LANES
    for k in range(kept_ref.shape[1] // wide):
        columns = slice(wide * k, wide * (k + 1))
        term = jnp.dot(own16, kept_ref[:, columns], preferred_element_type=jnp.float32)
        term = term + jnp.dot(
            other16, fetched_ref[:, columns], preferred_element_type=jnp.float32
        )
        term = term.astype(jnp.bfloat16)
        for c in (2 * k, 2 * k + 1):
            block = term[:, LANES * (c - 2 * k) : LANES * (c - 2 * k + 1)]
            out_ref[:, height * c : height * (c + 1), :] = block.reshape(-1, height, LANES)


def d_hidden_kernel(terms_ref, hidden_ref, gain_ref, added_ref, out_ref):
    hidden32 = hidden_ref[...].astype(jnp.float32)
    height = hidden32.shape[0]
    parts = []
    for parity in range(2):
        total = terms_ref[parity].astype(jnp.float32)
        for t in range(parity + 2, terms_ref.shape[0], 2):
            total = total + terms_ref[t].astype(jnp.float32)
        parts += [total[height * c : height * (c + 1)] for c in range(total.shape[0] // height)]
    d_normed = jnp.concatenate(parts, axis=1)
    inverse = rms_scale(hidden32)
    d_hidden = norm_backward(d_normed, hidden32 * inverse, inverse, gain_ref[...])
    out_ref[...] = (d_hidden + added_ref[...]).astype(jnp.bfloat16)


def packed_rows(sizes):
    starts, total = {}, 0
    for name, rows in sizes:
        starts[name] = slice(total, total + rows)
        total += rows
    return starts, total


def layout_rows(tokens_count, sequences, own_rows):
    wide = sequences * tokens_count // LANES
    return packed_rows(
        [
            ("key_cosine", tokens_count),
            ("key_sine", tokens_count),
            ("query_cosine", sequences),
            ("query_sine", sequences),
            ("inside", wide),
            ("chosen", wide),
            ("own_last", sequences),
            ("own_last_t", own_rows),
        ]
    )


def saved_rows(tokens_count, sequences):
    return packed_rows(
        [
            ("key_raw", tokens_count),
            ("key", tokens_count),
            ("value", tokens_count),
            ("query_raw", sequences),
            ("query", sequences),
            ("probs", sequences * tokens_count // LANES),
        ]
    )


def folded(block):
    parts = [block[:, LANES * k : LANES * (k + 1)] for k in range(block.shape[1] // LANES)]
    return jnp.concatenate(parts, axis=0)


def unfolded(block, rows):
    parts = [block[rows * k : rows * (k + 1)] for k in range(block.shape[0] // rows)]
    return jnp.concatenate(parts, axis=1)


def sequence_kernel(lengths_ref, out_ref, token_ref, *, tokens_count, own_rows):
    token_ref[0] = jnp.float32(0.0)
    sequences = lengths_ref.shape[1]
    at, _ = layout_rows(tokens_count, sequences, own_rows)
    lengths = lengths_ref[...].astype(jnp.float32)
    square = (sequences, sequences)
    ends = jnp.sum(
        jnp.where(iota(square, 1) <= iota(square, 0), lengths, 0.0), axis=1, keepdims=True
    )
    own_length = jnp.sum(
        jnp.where(iota(square, 1) == iota(square, 0), lengths, 0.0), axis=1, keepdims=True
    )
    starts = ends - own_length
    ends_row = jnp.sum(
        jnp.where(iota(square, 0) <= iota(square, 1), own_length, 0.0), axis=0, keepdims=True
    )
    starts_row = ends_row - lengths
    token = iota((sequences, tokens_count), 1).astype(jnp.float32)
    out_ref[at["inside"], :] = folded(((token >= starts) & (token < ends)).astype(jnp.float32))
    out_ref[at["chosen"], :] = folded((token == ends - 1.0).astype(jnp.float32))
    first = (lax.axis_index("tensor") * own_rows).astype(jnp.float32)
    own_token = iota((sequences, LANES), 1).astype(jnp.float32) + first
    own_token = jnp.where(iota((sequences, LANES), 1) < own_rows, own_token, -1.0)
    out_ref[at["own_last"], :] = (own_token == ends - 1.0).astype(jnp.float32)
    own_token = iota((own_rows, sequences), 0).astype(jnp.float32) + first
    own_last_t = (own_token == ends_row - 1.0).astype(jnp.float32)
    out_ref[at["own_last_t"], :] = jnp.concatenate(
        [own_last_t, jnp.zeros((own_rows, LANES - sequences), jnp.float32)], axis=1
    )
    token = iota((tokens_count, sequences), 0).astype(jnp.float32)
    held = (token >= starts_row) & (token < ends_row)
    position = jnp.sum(jnp.where(held, token - starts_row, 0.0), axis=1, keepdims=True)
    lane = iota((1, LANES), 1)
    halfway = LANES // 2
    pair = jnp.where(lane < halfway, lane, lane - halfway).astype(jnp.float32)
    frequency = jnp.exp(pair * (-2.0 / LANES * math.log(ROPE_BASE)))
    sign = jnp.where(lane < halfway, -1.0, 1.0)
    for name, place in (("key", position), ("query", own_length - 1.0)):
        angles = place * frequency
        out_ref[at[name + "_cosine"], :] = jnp.cos(angles)
        out_ref[at[name + "_sine"], :] = jnp.sin(angles) * sign


def on_device(
    hidden, lengths, positives, negatives, in_gain, wq, wkv, q_gain, k_gain, wo, out_gain
):
    tensor_count = lax.axis_size("tensor")
    z_count = lax.axis_size("z_far") * lax.axis_size("z_pair")
    own_rows, features = hidden.shape
    tokens_count = own_rows * tensor_count
    head_width = wq.shape[1]
    sequences = lengths.shape[1]
    query_count = positives.shape[0]
    total_rows = query_count // QDEV * sequences
    chunk = features // tensor_count
    f32, bf16 = jnp.float32, jnp.bfloat16
    head = (tokens_count, head_width)
    weights_shape = (head_width, features)
    flat = (tensor_count, own_rows * features // LANES, LANES)
    gain_rows = [q_gain[None, :], k_gain[None, :]]

    (unit_rows,) = kernel_call(unit_rows_kernel, [((own_rows, features), f32)], [hidden])
    (copies,) = kernel_call(
        copied_norm_kernel, [(flat, bf16)], [unit_rows, in_gain[None, :]]
    )
    piece = exchange(copies, "tensor")
    kv_own, kv_own16, query_all = kernel_call(
        projection_kernel, [(head, f32), (head, bf16), (head, f32)], [piece, wkv, wq]
    )
    kv_other = swapped(kv_own16, "tensor", 0)
    def sequence_layout(after):
        return kernel_call(
            functools.partial(sequence_kernel, tokens_count=tokens_count, own_rows=own_rows),
            [((layout_rows(tokens_count, sequences, own_rows)[1], LANES), f32), ((1,), f32)],
            [lengths],
            after=[after],
        )

    layout, _ = sequence_layout(query_all)
    blocks, saved = kernel_call(
        attention_kernel,
        [
            ((tensor_count, sequences, chunk), bf16),
            ((saved_rows(tokens_count, sequences)[1], LANES), f32),
        ],
        [kv_own, kv_other, query_all, layout, *gain_rows, hidden, wo],
    )
    half_shape = (2 * head_width, features // 2)
    kept_weights, sent_weights = kernel_call(
        half_weights_kernel, [(half_shape, bf16), (half_shape, bf16)], [wkv, wq], after=[query_all]
    )
    other_weights = swapped(sent_weights, "tensor", 0)
    output_gain = out_gain[None, :]
    resid, scaled = kernel_call(
        resid_kernel,
        [((sequences, chunk), f32), ((z_count, sequences, chunk), bf16)],
        [exchange(blocks, "tensor"), output_gain],
    )
    wo_t, transposed = kernel_call(
        transpose_kernel, [((features, head_width), bf16), ((1,), f32)], [wo], after=[resid]
    )
    layout_again, placed = sequence_layout(resid)
    tables = kernel_call(
        candidate_kernel,
        [
            ((16, query_count), jnp.int32),
            ((query_count, total_rows), bf16),
            ((query_count, total_rows), bf16),
        ],
        [positives[None, :], negatives.T],
        after=[resid],
    )
    everyone = lax.all_gather(exchange(scaled, ("z_far", "z_pair")), "core", axis=1)
    loss, d_resid16 = contrast(
        everyone, resid, output_gain, tables, [transposed, placed], [other_weights]
    )
    gradient_shape = (2 * tokens_count + sequences, head_width)
    own_gradients, sent_gradients = kernel_call(
        gradient_kernel,
        [(gradient_shape, f32), (gradient_shape, bf16)],
        [d_resid16, wo_t, saved, layout_again, *gain_rows],
        after=[loss],
    )
    other_gradients = swapped(sent_gradients, "tensor", 0)
    added, summed = kernel_call(
        added_kernel, [((own_rows, features), f32), ((1,), f32)], [d_resid16, layout_again]
    )
    (product,) = kernel_call(
        product_kernel,
        [((tensor_count, own_rows * features // LANES // 2, LANES), bf16)],
        [own_gradients, other_gradients, layout_again, kept_weights, other_weights],
        after=[summed],
    )
    terms = exchange(product, "tensor")
    (d_hidden,) = kernel_call(
        d_hidden_kernel,
        [((own_rows, features), bf16)],
        [terms, hidden, in_gain[None, :], added],
    )
    return (d_hidden, loss[0])


def solution(mesh):
    z_count = mesh.shape["dp"] // 2
    chips = mesh.devices.reshape(z_count // 2, 2, 2, mesh.shape["tensor"])
    mesh = jax.sharding.Mesh(chips, ("z_far", "z_pair", "core", "tensor"))
    everywhere = P(("z_far", "z_pair", "core", "tensor"), None)
    placed = (
        everywhere,
        P(("z_far", "z_pair", "core"), None),
        P(),
        P(),
        P(),
        P(None, "tensor"),
        P(None, "tensor"),
        P(),
        P(),
        P("tensor", None),
        P(),
    )
    return jax.shard_map(
        on_device, mesh=mesh, in_specs=placed, out_specs=(everywhere, P()), check_vma=False
    )
```
